32 devices in a mesh: ctx: 16 (over z, x, core), fsdp: 2 (over y).
Axes of the slice: x: 2, y: 2, z: 4, core: 2. Of those that a mesh axis runs over, the one named last changes fastest.
Arguments:
- tokens: bfloat16 [4096, 1152], P(('ctx', 'fsdp')), may hold values from -6 to 6
- query_weight: bfloat16 [1152, 1152], P('fsdp'), may hold values from -0.4375 to 0.4375
- key_projection: bfloat16 [1152, 384], P('fsdp'), may hold values from -0.1875 to 0.1875
- value_projection: bfloat16 [1152, 384], P('fsdp'), may hold values from -0.1875 to 0.1875
- output_weight: bfloat16 [1152, 1152], P('fsdp'), may hold values from -1 to 1
- gate_weight: bfloat16 [1152, 3072], P('fsdp'), may hold values from -0.1875 to 0.1875
- up_weight: bfloat16 [1152, 3072], P('fsdp'), may hold values from -0.1875 to 0.1875
- down_weight: bfloat16 [3072, 1152], P('fsdp'), may hold values from -0.109375 to 0.109375
- norm_attn: bfloat16 [1152], P('fsdp'), may hold values from 0.5 to 1.5
- norm_mlp: bfloat16 [1152], P('fsdp'), may hold values from 0.5 to 1.5
- doc_starts: int32 [4], replicated, may hold values from 0 to 4095, as said below
- cotangent: bfloat16 [4096, 1152], P(('ctx', 'fsdp')), may hold values from -6 to 6
Outputs:
- result: bfloat16 [4096, 1152], P(('ctx', 'fsdp'))
- tokens_grad: float32 [4096, 1152], P(('ctx', 'fsdp'))
- query_grad: float32 [1152, 1152], P('fsdp', 'ctx')
- key_grad: float32 [1152, 384], P('fsdp', 'ctx')
- value_grad: float32 [1152, 384], P('fsdp', 'ctx')
- output_grad: float32 [1152, 1152], P('fsdp', 'ctx')
- gate_grad: float32 [1152, 3072], P('fsdp', 'ctx')
- up_grad: float32 [1152, 3072], P('fsdp', 'ctx')
- down_grad: float32 [3072, 1152], P('fsdp', 'ctx')
- norm_attn_grad: float32 [1152], replicated
- norm_mlp_grad: float32 [1152], replicated
The draws below stay inside these ranges and needn't reach their ends.
Inputs may be any that keep to these rules, and one draw needn't show every extreme that they name: `doc_starts`: strictly increasing positions where documents begin, the first 0 and the last 4095; the second is one of positions 1 to 64 and the third one of positions 4032 to 4094, so one document runs from the first device's tokens to the last device's.
All inputs are finite; a program needn't handle non-finite values.
Results may differ from the reference program's by a relative error of at most 0.02.
Values may be sent and summed in bfloat16 or wider, within the bound.
A program may use at most 384 MiB of HBM per device.

```python
import math
import jax
import jax.numpy as jnp
from jax import lax

MODEL_WIDTH = 1152
QUERY_HEADS = 18
KEY_VALUE_HEADS = 6
HEAD_SIZE = 64
FF = 3072
TOK_DEV = 128
TOKENS = 4096


def draw_doc_starts(key, part):
    key = jax.random.fold_in(key, 11)
    first_key, second_key = jax.random.split(key, 2)
    first_cut = jax.random.randint(first_key, (), 1, TOK_DEV // 2 + 1)
    tail_rows = jax.random.randint(second_key, (), 2, TOK_DEV // 2 + 1)
    last_doc = TOKENS - tail_rows
    final_doc = jnp.full((), TOKENS - 1, jnp.int32)
    return jnp.stack([jnp.zeros((), jnp.int32), first_cut.astype(jnp.int32), last_doc.astype(jnp.int32), final_doc]).astype(jnp.int32)


def spiked(values, stream_key, source, target, shards_of, factor):
    def block_of(dim):
        return (jnp.arange(values.shape[dim]) // (values.shape[dim] // shards_of)).reshape((-1,) + (1,) * (values.ndim - 1 - dim))

    first = jax.random.permutation(stream_key, shards_of)[block_of(target)]
    other_side = (block_of(target) + shards_of // 2) % shards_of
    return jnp.where((block_of(source) == first) | (block_of(source) == other_side), factor * values, values)


def shard_levels(own_key, extent, shards, smallest, largest):
    def one(position, blocks):
        draws = jax.random.uniform(jax.random.fold_in(jax.random.fold_in(own_key, 6), position), (blocks,), jnp.float32, smallest / len(shards), largest / len(shards))
        return jnp.repeat(jnp.exp(draws), extent[position] // blocks).reshape((-1,) + (1,) * (len(extent) - position - 1))

    factor_of = one(*shards[0])
    for cut in shards[1:]:
        factor_of = factor_of * one(*cut)
    return factor_of


def scatter_about(rng, extent, scale, most, shards=(), kind=jnp.bfloat16):
    entries = scale * jax.random.normal(rng, extent, jnp.float32)
    if shards:
        entries = entries * shard_levels(rng, extent, shards, -0.22, 0.18)
    return jnp.clip(entries, -most, most).astype(kind)


def gaussian_with(stream_key, extent, spread, bound, cuts, heavy, kind=jnp.bfloat16):
    values = spread * jax.random.normal(stream_key, extent, jnp.float32)
    if cuts:
        values = values * shard_levels(stream_key, extent, cuts, -0.22, 0.18)
    return jnp.clip(spiked(values, jax.random.fold_in(stream_key, 3), *heavy), -bound, bound).astype(kind)


def setup_inputs(seed: int = 0) -> dict:
    seeds = jax.random.split(jax.random.key(seed), 13)
    tokens = scatter_about(seeds[0], (TOKENS, MODEL_WIDTH), 1.0, 6.0, ((0, 32),))
    query_weight = scatter_about(seeds[1], (MODEL_WIDTH, QUERY_HEADS * HEAD_SIZE), (MODEL_WIDTH // 6) ** -0.5, 0.4375, ((0, 2),))
    key_projection = scatter_about(seeds[2], (MODEL_WIDTH, KEY_VALUE_HEADS * HEAD_SIZE), MODEL_WIDTH ** -0.5, 0.1875, ((0, 2),))
    value_projection = scatter_about(seeds[3], (MODEL_WIDTH, KEY_VALUE_HEADS * HEAD_SIZE), MODEL_WIDTH ** -0.5, 0.1875, ((0, 2),))
    output_weight = scatter_about(seeds[4], (QUERY_HEADS * HEAD_SIZE, MODEL_WIDTH), (QUERY_HEADS * HEAD_SIZE // 36) ** -0.5, 1.0, ((0, 2),))
    gate_weight = scatter_about(seeds[5], (MODEL_WIDTH, FF), MODEL_WIDTH ** -0.5, 0.1875, ((0, 2),))
    up_weight = scatter_about(seeds[6], (MODEL_WIDTH, FF), MODEL_WIDTH ** -0.5, 0.1875, ((0, 2),))
    down_weight = scatter_about(seeds[7], (FF, MODEL_WIDTH), FF ** -0.5, 0.109375, ((0, 2),))
    norm_attn = jnp.clip(1.0 + 0.1 * jax.random.normal(seeds[8], (MODEL_WIDTH,), jnp.float32), 0.5, 1.5).astype(jnp.bfloat16)
    norm_mlp = jnp.clip(1.0 + 0.1 * jax.random.normal(seeds[9], (MODEL_WIDTH,), jnp.float32), 0.5, 1.5).astype(jnp.bfloat16)
    doc_starts = draw_doc_starts(jax.random.fold_in(seeds[12], 71), 0)
    cotangent = gaussian_with(seeds[11], (TOKENS, MODEL_WIDTH), 1.0, 6.0, ((0, 32),), (0, 1, 32, 2.75))
    return dict(tokens=tokens, query_weight=query_weight, key_projection=key_projection, value_projection=value_projection, output_weight=output_weight, gate_weight=gate_weight, up_weight=up_weight, down_weight=down_weight, norm_attn=norm_attn, norm_mlp=norm_mlp, doc_starts=doc_starts, cotangent=cotangent)


EPS = 1e-05
THETA = 10000.0
EXACT_MATMUL = lax.Precision.HIGHEST

@jax.custom_vjp
def reduced_precision(v):
    return lax.optimization_barrier(v.astype(jnp.bfloat16)).astype(jnp.float32)

@jax.custom_vjp
def reduced_backward(v):
    return v

def low_keep(v):
    return (reduced_precision(v), None)

def low_pass(kept, grad):
    return (grad,)

def back_keep(v):
    return (v, None)

def back_low(kept, grad):
    return (reduced_precision(grad),)
reduced_precision.defvjp(low_keep, low_pass)
reduced_backward.defvjp(back_keep, back_low)

def rope_tables(positions):
    half_dim = HEAD_SIZE // 2
    frequency = jnp.exp(-math.log(THETA) * jnp.arange(half_dim, dtype=jnp.float32) / half_dim)
    angles = positions.astype(jnp.float32)[:, None] * frequency[None, :]
    return (jnp.cos(angles), jnp.sin(angles))

def apply_rotary(values, cosine_table, sine_table):
    half_dim = values.shape[-1] // 2
    first_half = values[..., :half_dim]
    second_half = values[..., half_dim:]
    cos_rows = cosine_table[:, None, :]
    sin_rows = sine_table[:, None, :]
    return jnp.concatenate([first_half * cos_rows - second_half * sin_rows, second_half * cos_rows + first_half * sin_rows], axis=-1)

def doc_begin(indices, doc_starts):
    marked = jnp.where(indices[:, None] >= doc_starts[None, :], doc_starts[None, :], 0)
    return lax.optimization_barrier(jnp.max(marked, axis=1)).astype(jnp.int32)

def normalize(values):
    return values * lax.rsqrt(lax.optimization_barrier(jnp.mean(values * values, axis=-1, keepdims=True)) + EPS)

def attention(query_rot, key_rotated, value_reduced, positions, begins):
    overall_rows = query_rot.shape[0]
    rows_per_block = math.gcd(overall_rows, 512)
    block_count = overall_rows // rows_per_block
    queries_per_group = QUERY_HEADS // KEY_VALUE_HEADS
    key_row_matrix = key_rotated.reshape(overall_rows, KEY_VALUE_HEADS, HEAD_SIZE)
    value_row_matrix = value_reduced.reshape(overall_rows, KEY_VALUE_HEADS, HEAD_SIZE)
    key_index = jnp.arange(overall_rows, dtype=jnp.int32)

    def one_block(inputs):
        query_tile_block, index_block, begin_block = inputs
        query_rows = query_tile_block.reshape(rows_per_block, KEY_VALUE_HEADS, queries_per_group, HEAD_SIZE)
        scores = jnp.einsum('rgjd,kgd->gjrk', query_rows, key_row_matrix, precision=EXACT_MATMUL) * (1.0 / math.sqrt(HEAD_SIZE))
        scores = reduced_backward(scores)
        allowed = (key_index[None, :] <= index_block[:, None]) & (key_index[None, :] >= begin_block[:, None])
        scores = jnp.where(allowed[None, None], scores, -jnp.inf)
        probabilities = reduced_precision(jax.nn.softmax(scores, axis=-1))
        mixed_heads = jnp.einsum('gjrk,kgd->rgjd', probabilities, value_row_matrix, precision=EXACT_MATMUL)
        return mixed_heads.reshape(rows_per_block, QUERY_HEADS * HEAD_SIZE)
    outputs = lax.map(jax.checkpoint(one_block), (query_rot.reshape(block_count, rows_per_block, QUERY_HEADS * HEAD_SIZE), positions.reshape(block_count, rows_per_block), begins.reshape(block_count, rows_per_block)))
    return outputs.reshape(overall_rows, QUERY_HEADS * HEAD_SIZE)

def forward_layer(params, cosine_table, sine_table, positions, begins):
    hidden, query_w, key_matrix, value_w, output_w, gate_w, up_w, down_w, gain_attn, gain_mlp = params
    overall_rows = hidden.shape[0]
    attention_input = reduced_precision(normalize(hidden) * gain_attn)
    query_pre = reduced_backward(jnp.dot(attention_input, query_w, precision=EXACT_MATMUL)).reshape(overall_rows, QUERY_HEADS, HEAD_SIZE)
    key_unrotated = reduced_backward(jnp.dot(attention_input, key_matrix, precision=EXACT_MATMUL)).reshape(overall_rows, KEY_VALUE_HEADS, HEAD_SIZE)
    value_reduced = reduced_precision(reduced_backward(jnp.dot(attention_input, value_w, precision=EXACT_MATMUL)))
    query_rot = reduced_precision(apply_rotary(query_pre, cosine_table, sine_table)).reshape(overall_rows, QUERY_HEADS * HEAD_SIZE)
    key_rotated = reduced_precision(apply_rotary(key_unrotated, cosine_table, sine_table)).reshape(overall_rows, KEY_VALUE_HEADS * HEAD_SIZE)
    attn_exact = attention(query_rot, key_rotated, value_reduced, positions, begins)
    attn_rows = reduced_precision(reduced_backward(attn_exact))
    resid = hidden + reduced_backward(jnp.dot(attn_rows, output_w, precision=EXACT_MATMUL))
    mlp_in = reduced_precision(normalize(resid) * gain_mlp)
    gate_pre = reduced_backward(jnp.dot(mlp_in, gate_w, precision=EXACT_MATMUL))
    up_pre = reduced_backward(jnp.dot(mlp_in, up_w, precision=EXACT_MATMUL))
    mixed = reduced_precision(jax.nn.silu(gate_pre) * up_pre)
    return resid + jnp.dot(mixed, down_w, precision=EXACT_MATMUL)

def reference(tokens, query_weight, key_projection, value_projection, output_weight, gate_weight, up_weight, down_weight, norm_attn, norm_mlp, doc_starts, cotangent):
    positions = jnp.arange(TOKENS, dtype=jnp.int32)
    begins = doc_begin(positions, doc_starts)
    cosine_table, sine_table = rope_tables(positions - begins)

    def forward(*params):
        return forward_layer(params, cosine_table, sine_table, positions, begins)
    params = tuple((argument.astype(jnp.float32) for argument in (tokens, query_weight, key_projection, value_projection, output_weight, gate_weight, up_weight, down_weight, norm_attn, norm_mlp)))
    result, pullback = jax.vjp(forward, *params)
    gradients = pullback(cotangent.astype(jnp.float32))
    return (result.astype(jnp.bfloat16), gradients[0], gradients[1], gradients[2], gradients[3], gradients[4], gradients[5], gradients[6], gradients[7], gradients[8], gradients[9])
```

```python
import functools
import math

import jax
import jax.numpy as jnp
from jax import lax
from jax.experimental import pallas as pl
from jax.experimental.pallas import tpu as pltpu
from jax.sharding import PartitionSpec as P

QUERY_HEADS = 18
KEY_VALUE_HEADS = 6
HEAD_SIZE = 64
HS = HEAD_SIZE

EPS = 1e-05
THETA = 10000.0
NEG = -1e30
AXES = ("ctx", "fsdp")


def rope_tables(positions):
    half_dim = HEAD_SIZE // 2
    frequency = jnp.exp(-math.log(THETA) * jnp.arange(half_dim, dtype=jnp.float32) / half_dim)
    angles = positions.astype(jnp.float32)[:, None] * frequency[None, :]
    return (jnp.cos(angles), jnp.sin(angles))


def apply_rotary(values, cosine_table, sine_table):
    half_dim = values.shape[-1] // 2
    first_half = values[..., :half_dim]
    second_half = values[..., half_dim:]
    cos_rows = cosine_table[:, None, :]
    sin_rows = sine_table[:, None, :]
    return jnp.concatenate(
        [
            first_half * cos_rows - second_half * sin_rows,
            second_half * cos_rows + first_half * sin_rows,
        ],
        axis=-1,
    )


def unrotate(values, cosine_table, sine_table):
    half_dim = values.shape[-1] // 2
    first_half = values[..., :half_dim]
    second_half = values[..., half_dim:]
    cos_rows = cosine_table[:, None, :]
    sin_rows = sine_table[:, None, :]
    return jnp.concatenate(
        [
            first_half * cos_rows + second_half * sin_rows,
            second_half * cos_rows - first_half * sin_rows,
        ],
        axis=-1,
    )


def doc_begin(indices, doc_starts):
    marked = jnp.where(indices[:, None] >= doc_starts[None, :], doc_starts[None, :], 0)
    return jnp.max(marked, axis=1)


def layout_rows(device, row_count):
    return device * row_count + jnp.arange(row_count, dtype=jnp.int32)


def heads_rows(natural):
    return jnp.transpose(natural.astype(jnp.float32))
def padded(rows, heads, g):
    top = jnp.concatenate([rows[HS*(heads*g+j):HS*(heads*g+j+1)] for j in range(heads)], axis=1)
    z = jnp.zeros_like(top)
    return jnp.concatenate([top, z] if g == 0 else [z, top], axis=0)
def head_lanes(per_group, heads, tq):
    return jnp.transpose(jnp.concatenate([per_group[g][:, tq*j:tq*(j+1)] for g in range(2) for j in range(heads)], axis=0))
def bias_tile(info, docs, first, bk, tq):
    query = info[0] + lax.broadcasted_iota(jnp.int32, (1, tq), 1)
    begin = jnp.zeros((1, tq), jnp.int32)
    for i in range(docs.shape[0]):
        begin = jnp.maximum(begin, jnp.where(query >= docs[i], docs[i], 0))
    key = first + lax.broadcasted_iota(jnp.int32, (bk, 1), 0)
    return jnp.where((key <= query) & (key >= begin), 0.0, NEG)

def fwd_kernel(info, docs, q_ref, k_ref, v_ref, o_ref, ot_ref, lse_ref, *, bk, heads, tq):
    rows = heads*tq
    qt = heads_rows(q_ref[...]) * (1.0/8.0)
    qg = [padded(qt, heads, g).astype(jnp.bfloat16) for g in range(2)]
    def body(j, carry):
        first = pl.multiple_of(j*bk, bk)
        kb = k_ref[pl.ds(first, bk), :]
        vt = jnp.transpose(v_ref[pl.ds(first, bk), :])
        bias = bias_tile(info, docs, first, bk, tq)
        bias = jnp.concatenate([bias]*heads, axis=1)
        out = []
        for g in range(2):
            m, l, acc = carry[g]
            s = jnp.dot(kb, qg[g], preferred_element_type=jnp.float32) + bias
            mn = jnp.maximum(m, jnp.max(s, axis=0, keepdims=True))
            p = jnp.exp(s - mn)
            a = jnp.exp(m - mn)
            l = l*a + jnp.sum(p, axis=0, keepdims=True)
            acc = acc*a + jnp.dot(vt[HS*g:HS*(g+1)], p.astype(jnp.bfloat16), preferred_element_type=jnp.float32)
            out.append((mn, l, acc))
        return tuple(out)
    init = tuple((jnp.full((1, rows), NEG, jnp.float32), jnp.zeros((1, rows), jnp.float32), jnp.zeros((HS, rows), jnp.float32)) for _ in range(2))
    res = lax.fori_loop(info[1], info[2], body, init)
    ots = []
    for g in range(2):
        m, l, acc = res[g]
        o = acc / l
        ots.append(o)
        ot_ref[g] = o
        lse_ref[g] = m + jnp.log(l)
    o_ref[...] = head_lanes(ots, heads, tq).astype(o_ref.dtype)

def bwd_kernel(info, docs, q_ref, do_ref, ot_ref, lse_ref, k_ref, v_ref, dq_ref, dk_ref, dv_ref, acc_ref, *, bk, heads, tq):
    rows = heads*tq
    n = k_ref.shape[0]
    qt = heads_rows(q_ref[...]) * (1.0/8.0)
    dt = heads_rows(do_ref[...])
    qg = [padded(qt, heads, g) for g in range(2)]
    dg = [padded(dt, heads, g) for g in range(2)]
    qrows = jnp.concatenate([jnp.transpose(x) for x in qg], axis=0).astype(jnp.bfloat16)
    drows = jnp.concatenate([jnp.transpose(x) for x in dg], axis=0).astype(jnp.bfloat16)
    delta = [jnp.sum(dg[g][HS*g:HS*(g+1)] * ot_ref[g], axis=0, keepdims=True) for g in range(2)]
    lse = [lse_ref[g] for g in range(2)]
    qg = [x.astype(jnp.bfloat16) for x in qg]
    dg = [x.astype(jnp.bfloat16) for x in dg]
    acc_ref[...] = jnp.zeros_like(acc_ref)
    def zero(j, _):
        first = pl.multiple_of(j*bk, bk)
        dk_ref[pl.ds(first, bk), :] = jnp.zeros((bk, 2*HS), dk_ref.dtype)
        dv_ref[pl.ds(first, bk), :] = jnp.zeros((bk, 2*HS), dv_ref.dtype)
        return _
    lax.fori_loop(0, info[1], zero, 0)
    lax.fori_loop(info[2], n//bk, zero, 0)
    def body(j, _):
        first = pl.multiple_of(j*bk, bk)
        kb = k_ref[pl.ds(first, bk), :]
        vb = v_ref[pl.ds(first, bk), :]
        kt = jnp.transpose(kb)
        bias = bias_tile(info, docs, first, bk, tq)
        bias = jnp.concatenate([bias]*heads, axis=1)
        ps = []; dss = []
        for g in range(2):
            s = jnp.dot(kb, qg[g], preferred_element_type=jnp.float32)
            p = jnp.exp(s + (bias - lse[g]))
            dp = jnp.dot(vb, dg[g], preferred_element_type=jnp.float32)
            ds = (p * (dp - delta[g])).astype(jnp.bfloat16)
            ps.append(p.astype(jnp.bfloat16)); dss.append(ds)
            acc_ref[g] += jnp.dot(kt[HS*g:HS*(g+1)], ds, preferred_element_type=jnp.float32)
        dv = jnp.dot(jnp.concatenate(ps, axis=1), drows, preferred_element_type=jnp.float32)
        dk = jnp.dot(jnp.concatenate(dss, axis=1), qrows, preferred_element_type=jnp.float32)
        dk_ref[pl.ds(first, bk), :] = dk.astype(dk_ref.dtype)
        dv_ref[pl.ds(first, bk), :] = dv.astype(dv_ref.dtype)
        return _
    lax.fori_loop(info[1], info[2], body, 0)
    dq_ref[...] = head_lanes([acc_ref[g] for g in range(2)], heads, tq) * (1.0/8.0)

def attention_forward(info, docs, q, kv, bk=512):
    tq, width = q.shape
    n = kv.shape[0]
    parts = kv.shape[1]//(4*HS)
    heads = width//HS//(2*parts)
    smem = pl.BlockSpec(memory_space=pltpu.SMEM)
    return pl.pallas_call(
        functools.partial(fwd_kernel, bk=bk, heads=heads, tq=tq),
        grid=(parts,),
        out_shape=[jax.ShapeDtypeStruct((tq, width), jnp.bfloat16), jax.ShapeDtypeStruct((2*parts, HS, heads*tq), jnp.float32), jax.ShapeDtypeStruct((2*parts, 1, heads*tq), jnp.float32)],
        in_specs=[smem, smem, pl.BlockSpec((tq, 2*heads*HS), lambda p: (0, p)), pl.BlockSpec((n, 2*HS), lambda p: (0, p)), pl.BlockSpec((n, 2*HS), lambda p: (0, parts + p))],
        out_specs=[pl.BlockSpec((tq, 2*heads*HS), lambda p: (0, p)), pl.BlockSpec((2, HS, heads*tq), lambda p: (p, 0, 0)), pl.BlockSpec((2, 1, heads*tq), lambda p: (p, 0, 0))],
        compiler_params=pltpu.CompilerParams(vmem_limit_bytes=60*2**20),
        name="attention_forward",
    )(info, docs, q, kv, kv)

def attention_backward(info, docs, q, do, ot, lse, kv, bk=512):
    tq, width = q.shape
    n = kv.shape[0]
    parts = kv.shape[1]//(4*HS)
    heads = width//HS//(2*parts)
    buffers = 2 if 32 * n * HS <= 40*2**20 else 1
    smem = pl.BlockSpec(memory_space=pltpu.SMEM)
    return pl.pallas_call(
        functools.partial(bwd_kernel, bk=bk, heads=heads, tq=tq),
        grid=(parts,),
        out_shape=[jax.ShapeDtypeStruct((tq, width), jnp.float32), jax.ShapeDtypeStruct((n, 2*parts*HS), jnp.bfloat16), jax.ShapeDtypeStruct((n, 2*parts*HS), jnp.bfloat16)],
        in_specs=[smem, smem, pl.BlockSpec((tq, 2*heads*HS), lambda p: (0, p)), pl.BlockSpec((tq, 2*heads*HS), lambda p: (0, p)),
                  pl.BlockSpec((2, HS, heads*tq), lambda p: (p, 0, 0)), pl.BlockSpec((2, 1, heads*tq), lambda p: (p, 0, 0)),
                  pl.BlockSpec((n, 2*HS), lambda p: (0, p), pipeline_mode=pl.Buffered(buffers)), pl.BlockSpec((n, 2*HS), lambda p: (0, parts + p), pipeline_mode=pl.Buffered(buffers))],
        out_specs=[pl.BlockSpec((tq, 2*heads*HS), lambda p: (0, p)), pl.BlockSpec((n, 2*HS), lambda p: (0, p)), pl.BlockSpec((n, 2*HS), lambda p: (0, p))],
        scratch_shapes=[pltpu.VMEM((2, HS, heads*tq), jnp.float32)],
        compiler_params=pltpu.CompilerParams(vmem_limit_bytes=60*2**20),
        name="attention_backward",
    )(info, docs, q, do, ot, lse, kv, kv)


def exchange_kernel(nctx, nf, blocks, small, out, small_out, own_sem, send_sem, recv_sem):
    me_c, me_f = lax.axis_index("ctx"), lax.axis_index("fsdp")
    me = me_c * nf + me_f
    n = nctx * nf
    barrier = pltpu.get_barrier_semaphore()

    def target(k):
        other = lax.rem(me + k, n)
        return other, {"ctx": other // nf, "fsdp": lax.rem(other, nf)}

    def greet(k, carry):
        _, where = target(k)
        pl.semaphore_signal(barrier, inc=1, device_id=where, device_id_type=pl.DeviceIdType.MESH)
        return carry

    lax.fori_loop(1, n, greet, 0)
    own = pltpu.make_async_copy(blocks.at[me_c], out.at[me], own_sem.at[0])
    own.start()
    own_small = pltpu.make_async_copy(small, small_out.at[me], own_sem.at[1])
    own_small.start()
    pl.semaphore_wait(barrier, n - 1)

    def copies(k):
        other, where = target(k)
        return (
            pltpu.make_async_remote_copy(
                src_ref=blocks.at[other // nf], dst_ref=out.at[me],
                send_sem=send_sem.at[0, k], recv_sem=recv_sem.at[0, k],
                device_id=where, device_id_type=pl.DeviceIdType.MESH,
            ),
            pltpu.make_async_remote_copy(
                src_ref=small, dst_ref=small_out.at[me],
                send_sem=send_sem.at[1, k], recv_sem=recv_sem.at[1, k],
                device_id=where, device_id_type=pl.DeviceIdType.MESH,
            ),
        )

    def begin(k, carry):
        for copy in copies(k):
            copy.start()
        return carry

    def finish(k, carry):
        for copy in copies(k):
            copy.wait()
        return carry

    lax.fori_loop(1, n, begin, 0)
    lax.fori_loop(1, n, finish, 0)
    own.wait()
    own_small.wait()


def exchange(blocks, small, nctx, nf):
    n = nctx * nf
    vmem = pl.BlockSpec(memory_space=pltpu.VMEM)
    return pl.pallas_call(
        functools.partial(exchange_kernel, nctx, nf),
        out_shape=[
            jax.ShapeDtypeStruct((n,) + blocks.shape[1:], blocks.dtype),
            jax.ShapeDtypeStruct((n,) + small.shape, small.dtype),
        ],
        in_specs=[vmem, vmem],
        out_specs=[vmem, vmem],
        scratch_shapes=[
            pltpu.SemaphoreType.DMA((2,)),
            pltpu.SemaphoreType.DMA((2, n)),
            pltpu.SemaphoreType.DMA((2, n)),
        ],
        compiler_params=pltpu.CompilerParams(
            collective_id=0, has_side_effects=True, vmem_limit_bytes=48 * 2**20
        ),
        name="exchange",
    )(blocks, small)


def line_dims(count):
    fours = 0
    while count % 4 == 0:
        count //= 4
        fours += 1
    return ([count] if count > 1 else []) + [4] * fours


class Layout:
    def __init__(self, nctx, nf):
        self.nctx, self.nf, self.plane = nctx, nf, nctx // 2
        self.ctx = lax.axis_index("ctx")
        self.f = lax.axis_index("fsdp")
        self.core = lax.rem(self.ctx, 2)
        self.place = self.ctx // 2

    def send(self, value, move):
        pairs = []
        for ctx in range(self.nctx):
            for f in range(self.nf):
                place, core, side = move(ctx // 2, ctx % 2, f)
                pairs.append((ctx * self.nf + f, (place * 2 + core) * self.nf + side))
        return lax.ppermute(value, AXES, pairs)

    def to_core(self, value):
        return self.send(value, lambda r, c, f: (r, 1 - c, f))

    def to_side(self, value):
        return self.send(value, lambda r, c, f: (r, c, 1 - f))

    def in_order(self, which, own, other, axis=0):
        return jnp.where(
            which == 0,
            jnp.concatenate([own, other], axis=axis),
            jnp.concatenate([other, own], axis=axis),
        )

    def plane_scatter(self, data):
        stride = 1
        for size in line_dims(self.plane):
            coord = lax.rem(self.place // stride, size)
            data = data.reshape((data.shape[0] // size, size) + data.shape[1:])
            total = lax.dynamic_index_in_dim(data, coord, 1, keepdims=False).astype(jnp.float32)
            for k in range(1, size):
                part = lax.dynamic_index_in_dim(data, lax.rem(coord + k, size), 1, keepdims=False)

                def move(r, c, f, k=k, size=size, stride=stride):
                    at = r // stride % size
                    return r + ((at + k) % size - at) * stride, c, f

                total = total + self.send(part, move).astype(jnp.float32)
            stride *= size
            data = total if data.shape[0] == 1 else total.astype(jnp.bfloat16)
        return data[0]


def pair_weight(lay, local):
    half = local.shape[0] // 2
    mine = lax.dynamic_slice_in_dim(local, lay.core * half, half, 0)
    got = lay.to_side(mine)
    other = lay.to_core(got)
    return lay.in_order(lay.f, local, lay.in_order(lay.core, got, other))


def gather_group(lay, own):
    two = jnp.concatenate([own, lay.to_side(own)], axis=0)
    return jnp.concatenate([two, lay.to_core(two)], axis=0)


def scatter_group(lay, partial, rows):
    got = lay.to_core(partial[2 * rows :].astype(jnp.bfloat16))
    total = partial[: 2 * rows] + got.astype(jnp.float32)
    last = lay.to_side(total[rows:].astype(jnp.bfloat16))
    return total[:rows] + last.astype(jnp.float32)


def column_blocks(values, count):
    rows, width = values.shape
    return values.reshape(rows, count, width // count)


def per_device(
    nctx,
    nf,
    tokens,
    query_weight,
    key_projection,
    value_projection,
    output_weight,
    gate_weight,
    up_weight,
    down_weight,
    norm_attn,
    norm_mlp,
    doc_starts,
    cotangent,
):
    lay = Layout(nctx, nf)
    f, core = lay.f, lay.core
    token_rows, width = tokens.shape
    half = width // nf
    n_tokens = token_rows * nctx * nf
    hidden_units = gate_weight.shape[1]
    quarter = hidden_units // (2 * nf)
    bf16, f32 = jnp.bfloat16, jnp.float32

    gains = jnp.stack([norm_attn, norm_mlp])
    gains = lay.in_order(f, gains, lay.to_side(gains), axis=1).astype(f32)
    gain_attn, gain_mlp = gains[0], gains[1]
    qkv_full = pair_weight(
        lay, jnp.concatenate([query_weight, key_projection, value_projection], axis=1)
    )
    output_full = pair_weight(lay, output_weight)

    def quarter_columns(index):
        at = index * quarter
        return jnp.concatenate(
            [
                lax.dynamic_slice_in_dim(gate_weight, at, quarter, 1),
                lax.dynamic_slice_in_dim(up_weight, at, quarter, 1),
            ],
            axis=1,
        )

    mine = 2 * f + core
    gate_up = lay.in_order(
        f, quarter_columns(mine), lay.to_side(quarter_columns(2 * (1 - f) + core))
    )
    down = lax.dynamic_slice_in_dim(down_weight, core * quarter, quarter, 0)
    cotangents = gather_group(lay, cotangent)

    hidden = tokens.astype(f32)
    inv_attn = lax.rsqrt(jnp.mean(hidden * hidden, axis=-1, keepdims=True) + EPS)
    normed_attn = hidden * inv_attn
    attention_input = (normed_attn * gain_attn).astype(bf16)

    def pair_side(values):
        halves = values.reshape(token_rows, nf, half)
        own = lax.dynamic_index_in_dim(halves, f, 1, keepdims=False)
        other = lax.dynamic_index_in_dim(halves, 1 - f, 1, keepdims=False)
        return lay.in_order(f, own, lay.to_side(other))

    own_device = lax.axis_index(AXES)
    own_index = layout_rows(own_device, token_rows)
    own_begin = doc_begin(own_index, doc_starts)
    cosine_table, sine_table = rope_tables(own_index - own_begin)

    qkv = jnp.dot(attention_input, qkv_full, preferred_element_type=f32)
    query_width = QUERY_HEADS * HEAD_SIZE
    key_width = KEY_VALUE_HEADS * HEAD_SIZE
    rotated = apply_rotary(
        qkv[:, : query_width + key_width].reshape(
            token_rows, QUERY_HEADS + KEY_VALUE_HEADS, HEAD_SIZE
        ),
        cosine_table,
        sine_table,
    ).astype(bf16).reshape(token_rows, query_width + key_width)
    query_rot = rotated[:, :query_width]
    key_value = jnp.concatenate(
        [rotated[:, query_width:], qkv[:, query_width + key_width :].astype(bf16)], axis=1
    )
    key_values = lax.all_gather(key_value, AXES, axis=0, tiled=True)
    block = math.gcd(n_tokens, 512)
    start = own_device * token_rows
    info = jnp.stack(
        [start, jnp.min(own_begin) // block, (start + token_rows - 1) // block + 1]
    ).astype(jnp.int32)
    attn_low, attn_exact, log_total = attention_forward(
        info, doc_starts, query_rot, key_values, block
    )

    resid = hidden + jnp.dot(attn_low, output_full, preferred_element_type=f32)
    inv_mlp = lax.rsqrt(jnp.mean(resid * resid, axis=-1, keepdims=True) + EPS)
    normed_mlp = resid * inv_mlp
    mlp_in = (normed_mlp * gain_mlp).astype(bf16)
    mlp_ins = gather_group(lay, mlp_in)
    gate_up_pre = jnp.dot(mlp_ins, gate_up, preferred_element_type=f32)
    gate_pre, up_pre = gate_up_pre[:, :quarter], gate_up_pre[:, quarter:]
    sigmoid_gate = jax.nn.sigmoid(gate_pre)
    gate_act = jax.nn.silu(gate_pre)
    mixed = (gate_act * up_pre).astype(bf16)
    grad_mixed = jnp.einsum("td,fd->tf", cotangents, down, preferred_element_type=f32)
    grad_gate = (grad_mixed * up_pre * sigmoid_gate * (1.0 + gate_pre * (1.0 - sigmoid_gate))).astype(bf16)
    grad_up = (grad_mixed * gate_act).astype(bf16)
    grads = jnp.concatenate([grad_gate, grad_up], axis=1)
    grad_mlp_in = scatter_group(
        lay, jnp.einsum("tf,df->td", grads, gate_up, preferred_element_type=f32), token_rows
    )
    result = (
        resid
        + scatter_group(lay, jnp.dot(mixed, down, preferred_element_type=f32), token_rows)
    ).astype(bf16)

    gain_mlp_partial = jnp.sum(grad_mlp_in * normed_mlp, axis=0)
    scaled_mlp = grad_mlp_in * gain_mlp
    grad_resid = cotangent.astype(f32) + inv_mlp * (
        scaled_mlp - normed_mlp * jnp.mean(scaled_mlp * normed_mlp, axis=-1, keepdims=True)
    )
    grad_branch = grad_resid.astype(bf16)
    grad_attn = jnp.einsum(
        "td,hd->th", grad_branch, output_full, preferred_element_type=f32
    ).astype(bf16)

    grad_query_rot, grad_key_rot, grad_value_all = attention_backward(
        info, doc_starts, query_rot, grad_attn, attn_exact, log_total, key_values, block
    )
    grad_kv = jnp.concatenate([grad_key_rot, grad_value_all], axis=1).reshape(
        lay.plane, 2, nf, token_rows, 2 * key_width
    )
    own = lax.dynamic_index_in_dim(grad_kv, core, 1, keepdims=False).astype(f32)
    own = own + lay.to_core(
        lax.dynamic_index_in_dim(grad_kv, 1 - core, 1, keepdims=False)
    ).astype(f32)
    own = own.astype(bf16)
    both = lax.dynamic_index_in_dim(own, f, 1, keepdims=False).astype(f32)
    both = both + lay.to_side(lax.dynamic_index_in_dim(own, 1 - f, 1, keepdims=False)).astype(f32)
    grad_kv = lay.plane_scatter(both.astype(bf16))

    gate_up_partial = jnp.einsum("tf,td->fd", grads, mlp_ins, preferred_element_type=f32).astype(bf16)
    down_partial = jnp.einsum("td,tf->df", cotangents, mixed, preferred_element_type=f32).astype(bf16)
    gate_up_piece = lay.plane_scatter(
        gate_up_partial.reshape(2, lay.plane, quarter // lay.plane, width).transpose(1, 0, 2, 3)
    ).astype(bf16)
    down_piece = lay.plane_scatter(
        down_partial.reshape(lay.plane, width // lay.plane, quarter)
    )
    parity = lax.rem(lay.place, 2)
    left, right = gate_up_piece[..., :half], gate_up_piece[..., half:]
    per_side = lay.plane // 2

    def home(flip):
        def move(r, c, side):
            at = (2 * side + c) * per_side + r // 2
            return at // 2, at % 2, (r + flip) % 2

        return move

    same = lay.send(jnp.where(parity == 0, left, right), home(0))
    cross = lay.send(jnp.where(parity == 0, right, left), home(1))
    gate_up_sum = lay.in_order(f, same, cross, axis=1).astype(f32)
    gate_sum, up_sum = gate_up_sum[0].T, gate_up_sum[1].T
    down_piece = down_piece.reshape(2, width // nctx, quarter)
    down_own = lax.dynamic_index_in_dim(down_piece, core, 0, keepdims=False)
    down_other = lay.to_core(
        lax.dynamic_index_in_dim(down_piece, 1 - core, 0, keepdims=False).astype(bf16)
    ).astype(f32)
    down_sum = lay.in_order(core, down_own, down_other, axis=1).T

    grad_query = unrotate(
        grad_query_rot.reshape(token_rows, QUERY_HEADS, HEAD_SIZE), cosine_table, sine_table
    ).astype(bf16).reshape(token_rows, query_width)
    grad_key = unrotate(
        grad_kv[:, :key_width].reshape(token_rows, KEY_VALUE_HEADS, HEAD_SIZE),
        cosine_table,
        sine_table,
    ).astype(bf16).reshape(token_rows, key_width)
    grad_value = grad_kv[:, key_width:].astype(bf16)
    grad_qkv = jnp.concatenate([grad_query, grad_key, grad_value], axis=1)
    grad_attn_in = jnp.einsum("th,dh->td", grad_qkv, qkv_full, preferred_element_type=f32)
    gain_attn_partial = jnp.sum(grad_attn_in * normed_attn, axis=0)
    scaled_attn = grad_attn_in * gain_attn
    tokens_grad = grad_resid + inv_attn * (
        scaled_attn - normed_attn * jnp.mean(scaled_attn * normed_attn, axis=-1, keepdims=True)
    )

    inputs_all = lax.all_gather(pair_side(attention_input), "ctx", axis=0, tiled=True)
    attn_all = lax.all_gather(pair_side(attn_low), "ctx", axis=0, tiled=True)
    blocks = jnp.concatenate(
        [column_blocks(v, nctx) for v in (grad_query, grad_key, grad_value, grad_branch)], axis=2
    )
    used = blocks.shape[2]
    blocks = jnp.pad(blocks, ((0, 0), (0, 0), (0, -used % 128))).transpose(1, 0, 2)
    small = jnp.stack([gain_attn_partial, gain_mlp_partial])
    small = jnp.pad(small, ((0, 6), (0, 0)))
    columns, gain_parts = exchange(blocks, small, nctx, nf)
    columns = columns.reshape(n_tokens, -1)
    gain_sums = jnp.sum(gain_parts, axis=0)
    sizes = [query_width // nctx, key_width // nctx, key_width // nctx]
    qkv_cols = sum(sizes)
    qkv_sum = jnp.einsum("td,th->dh", inputs_all, columns[:, :qkv_cols], preferred_element_type=f32)
    output_sum = jnp.einsum(
        "th,td->hd", attn_all, columns[:, qkv_cols:used], preferred_element_type=f32
    )
    query_sum = qkv_sum[:, : sizes[0]]
    key_sum = qkv_sum[:, sizes[0] : sizes[0] + sizes[1]]
    value_sum = qkv_sum[:, sizes[0] + sizes[1] :]
    return (
        result,
        tokens_grad,
        query_sum,
        key_sum,
        value_sum,
        output_sum,
        gate_sum,
        up_sum,
        down_sum,
        gain_sums[0],
        gain_sums[1],
    )


def solution(mesh):
    return jax.shard_map(
        functools.partial(per_device, mesh.shape["ctx"], mesh.shape["fsdp"]),
        mesh=mesh,
        in_specs=(
            P(("ctx", "fsdp"), None),
            P("fsdp", None),
            P("fsdp", None),
            P("fsdp", None),
            P("fsdp", None),
            P("fsdp", None),
            P("fsdp", None),
            P("fsdp", None),
            P("fsdp"),
            P("fsdp"),
            P(),
            P(("ctx", "fsdp"), None),
        ),
        out_specs=(
            P(("ctx", "fsdp"), None),
            P(("ctx", "fsdp"), None),
            P("fsdp", "ctx"),
            P("fsdp", "ctx"),
            P("fsdp", "ctx"),
            P("fsdp", "ctx"),
            P("fsdp", "ctx"),
            P("fsdp", "ctx"),
            P("fsdp", "ctx"),
            P(),
            P(),
        ),
        check_vma=False,
    )
```

```python
import functools
import math

import jax
import jax.numpy as jnp
from jax import lax
from jax.experimental import pallas as pl
from jax.experimental.pallas import tpu as pltpu
from jax.sharding import PartitionSpec as P

QUERY_HEADS = 18
KEY_VALUE_HEADS = 6
HEAD_SIZE = 64
HS = HEAD_SIZE

EPS = 1e-05
THETA = 10000.0
NEG = -1e30
AXES = ("ctx", "fsdp")


def rope_tables(positions):
    half_dim = HEAD_SIZE // 2
    frequency = jnp.exp(-math.log(THETA) * jnp.arange(half_dim, dtype=jnp.float32) / half_dim)
    angles = positions.astype(jnp.float32)[:, None] * frequency[None, :]
    return (jnp.cos(angles), jnp.sin(angles))


def apply_rotary(values, cosine_table, sine_table):
    half_dim = values.shape[-1] // 2
    first_half = values[..., :half_dim]
    second_half = values[..., half_dim:]
    cos_rows = cosine_table[:, None, :]
    sin_rows = sine_table[:, None, :]
    return jnp.concatenate(
        [
            first_half * cos_rows - second_half * sin_rows,
            second_half * cos_rows + first_half * sin_rows,
        ],
        axis=-1,
    )


def unrotate(values, cosine_table, sine_table):
    half_dim = values.shape[-1] // 2
    first_half = values[..., :half_dim]
    second_half = values[..., half_dim:]
    cos_rows = cosine_table[:, None, :]
    sin_rows = sine_table[:, None, :]
    return jnp.concatenate(
        [
            first_half * cos_rows + second_half * sin_rows,
            second_half * cos_rows - first_half * sin_rows,
        ],
        axis=-1,
    )


def doc_begin(indices, doc_starts):
    marked = jnp.where(indices[:, None] >= doc_starts[None, :], doc_starts[None, :], 0)
    return jnp.max(marked, axis=1)


def layout_rows(device, row_count):
    return device * row_count + jnp.arange(row_count, dtype=jnp.int32)


def heads_rows(natural):
    return jnp.transpose(natural.astype(jnp.float32))
def padded(rows, heads, g):
    top = jnp.concatenate([rows[HS*(heads*g+j):HS*(heads*g+j+1)] for j in range(heads)], axis=1)
    z = jnp.zeros_like(top)
    return jnp.concatenate([top, z] if g == 0 else [z, top], axis=0)
def head_lanes(per_group, heads, tq):
    return jnp.transpose(jnp.concatenate([per_group[g][:, tq*j:tq*(j+1)] for g in range(2) for j in range(heads)], axis=0))
def bias_tile(info, docs, first, bk, tq):
    query = info[0] + lax.broadcasted_iota(jnp.int32, (1, tq), 1)
    begin = jnp.zeros((1, tq), jnp.int32)
    for i in range(docs.shape[0]):
        begin = jnp.maximum(begin, jnp.where(query >= docs[i], docs[i], 0))
    key = first + lax.broadcasted_iota(jnp.int32, (bk, 1), 0)
    return jnp.where((key <= query) & (key >= begin), 0.0, NEG)


def line_dims(count):
    fours = 0
    while count % 4 == 0:
        count //= 4
        fours += 1
    return ([count] if count > 1 else []) + [4] * fours


def rotate_back(rows, cos_rows, sin_rows):
    half_dim = HS // 2
    first, second = rows[:half_dim], rows[half_dim:]
    return jnp.concatenate(
        [first * cos_rows + second * sin_rows, second * cos_rows - first * sin_rows], axis=0
    )


def round_up(value, unit):
    return -(-value // unit) * unit


def backward_kernel(plan, docs, q_ref, do_ref, ot_ref, lse_ref, kv_hbm, w_ref, cos_ref, sin_ref,
                    normed_ref, inv_ref, gain_ref, gres_ref, gmlp_ref,
                    tokens_ref, colq_ref, colkv_ref, gains_ref,
                    kvbuf, dkv, acc_ref, gqt_ref, ga_ref, qblk, kvblk, small,
                    load_sem, send_sem, recv_sem, col_send, col_recv, own_sem, credit, *recvs):
    nctx, nf, parts, heads, tq, slots = plan
    plane = nctx // 2
    n = nctx * nf
    dims = line_dims(plane)
    nd = len(dims)
    bk = 2 * nf * tq
    me_c, me_f = lax.axis_index("ctx"), lax.axis_index("fsdp")
    me = me_c * nf + me_f
    core, place = lax.rem(me_c, 2), me_c // 2
    mesh_id = pl.DeviceIdType.MESH
    half_dim = HS // 2

    def target(k):
        other = lax.rem(me + k, n)
        return other, {"ctx": other // nf, "fsdp": lax.rem(other, nf)}

    barrier = pltpu.get_barrier_semaphore()

    def greet(k, carry):
        pl.semaphore_signal(barrier, inc=1, device_id=target(k)[1], device_id_type=mesh_id)
        return carry

    lax.fori_loop(1, n, greet, 0)

    def loads(p):
        s = p % slots
        return [
            pltpu.make_async_copy(
                kv_hbm.at[:, pl.ds((kind * parts + p) * 2 * HS, 2 * HS)],
                kvbuf.at[s, kind], load_sem.at[s, kind],
            )
            for kind in range(2)
        ]

    resident = slots == parts

    def block_loads(p, j):
        slot = lax.rem(j, 2)
        return [
            pltpu.make_async_copy(
                kv_hbm.at[pl.ds(pl.multiple_of(j * bk, bk), bk), pl.ds((kind * parts + p) * 2 * HS, 2 * HS)],
                kvbuf.at[slot, kind], load_sem.at[slot, kind],
            )
            for kind in range(2)
        ]

    if resident:
        for p in range(parts):
            for copy in loads(p):
                copy.start()

    def dim_axis(i):
        stride = math.prod(dims[:i])
        size = dims[i]
        own = lax.rem(place // stride, size)

        def peer(k):
            there = lax.rem(own + k, size)
            return there, {"ctx": (place + (there - own) * stride) * 2 + core, "fsdp": me_f}

        return (nd - 1 - i, size, own, peer)

    core_axis = (nd, 2, core, lambda k: (1 - core, {"ctx": place * 2 + 1 - core, "fsdp": me_f}))
    side_axis = (nd + 1, 2, me_f, lambda k: (1 - me_f, {"ctx": me_c, "fsdp": 1 - me_f}))
    lines = [dim_axis(i) for i in range(nd)]
    orders = [[core_axis, side_axis] + lines, [core_axis, lines[0], side_axis] + lines[1:]]
    stages = nd + 2

    def region(kind, stage, at):
        index = [slice(None)] * (nd + 2)
        for axis in orders[kind][:stage]:
            index[axis[0]] = axis[2]
        index[orders[kind][stage][0]] = at
        return tuple(index)

    def stage_copies(p, kind, stage):
        s = p % slots
        axis = orders[kind][stage]
        copies = []
        for k in range(1, axis[1]):
            there, where = axis[3](k)
            copies.append(
                pltpu.make_async_remote_copy(
                    src_ref=dkv.at[(s, kind) + region(kind, stage, there)],
                    dst_ref=recvs[kind * stages + stage].at[s, k - 1],
                    send_sem=send_sem.at[s, kind, stage, k - 1],
                    recv_sem=recv_sem.at[s, kind, stage, k - 1],
                    device_id=where, device_id_type=mesh_id,
                )
            )
        return copies

    def stage_start(p, stage):
        for kind in range(2):
            for copy in stage_copies(p, kind, stage):
                copy.start()

    finals = {}

    def stage_finish(p, stage):
        s = p % slots
        for kind in range(2):
            axis = orders[kind][stage]
            for copy in stage_copies(p, kind, stage):
                copy.wait()
            where = region(kind, stage, axis[2])
            got = recvs[kind * stages + stage]
            free = [i for i in range(nd + 2) if isinstance(where[i], slice)]

            def add(index, lead):
                total = dkv[(s, kind) + index].astype(jnp.float32)
                for k in range(axis[1] - 1):
                    total = total + got[(s, k) + lead].astype(jnp.float32)
                return total

            if not free:
                finals[p, kind] = add(where, ())
            else:
                size = dkv.shape[2 + free[0]]

                def one(i, carry):
                    index = list(where)
                    index[free[0]] = i
                    index = tuple(index)
                    dkv[(s, kind) + index] = add(index, (i,)).astype(dkv.dtype)
                    return carry

                lax.fori_loop(0, size, one, 0)

    def place_index(j):
        index = []
        for i in reversed(range(nd)):
            index.append(lax.rem(j // math.prod(dims[:i]), dims[i]))
        return tuple(index)

    start = me * tq
    last = (start + tq - 1) // bk + 1

    def compute(p):
        s = p % slots
        span = slice(2 * heads * HS * p, 2 * heads * HS * (p + 1))
        qt = q_ref[span, :].astype(jnp.float32) * (1.0 / 8.0)
        dt = heads_rows(do_ref[:, span])
        qg = [padded(qt, heads, g) for g in range(2)]
        dg = [padded(dt, heads, g) for g in range(2)]
        qrows = jnp.concatenate([jnp.transpose(x) for x in qg], axis=0).astype(jnp.bfloat16)
        drows = jnp.concatenate([jnp.transpose(x) for x in dg], axis=0).astype(jnp.bfloat16)
        delta = [
            jnp.sum(dg[g][HS * g : HS * (g + 1)] * ot_ref[2 * p + g], axis=0, keepdims=True)
            for g in range(2)
        ]
        lse = [lse_ref[2 * p + g] for g in range(2)]
        qg = [x.astype(jnp.bfloat16) for x in qg]
        dg = [x.astype(jnp.bfloat16) for x in dg]
        acc_ref[...] = jnp.zeros_like(acc_ref)
        for copy in loads(p) if resident else block_loads(p, 0):
            if not resident:
                copy.start()
            else:
                copy.wait()

        def zero(j, carry):
            at = place_index(j)
            for kind in range(2):
                dkv[(s, kind) + at] = jnp.zeros((2, nf, tq, 2 * HS), dkv.dtype)
            return carry

        def body(j, carry):
            first = pl.multiple_of(j * bk, bk)
            if resident:
                kb = kvbuf[s, 0, pl.ds(first, bk), :]
                vb = kvbuf[s, 1, pl.ds(first, bk), :]
            else:
                for copy in block_loads(p, j):
                    copy.wait()

                @pl.when(j + 1 < last)
                def _():
                    for copy in block_loads(p, j + 1):
                        copy.start()

                kb, vb = kvbuf[lax.rem(j, 2), 0], kvbuf[lax.rem(j, 2), 1]
            kt = jnp.transpose(kb)
            bias = bias_tile((start,), docs, first, bk, tq)
            bias = jnp.concatenate([bias] * heads, axis=1)
            ps = []
            dss = []
            for g in range(2):
                score = jnp.dot(kb, qg[g], preferred_element_type=jnp.float32)
                prob = jnp.exp(score + (bias - lse[g]))
                dp = jnp.dot(vb, dg[g], preferred_element_type=jnp.float32)
                ds = (prob * (dp - delta[g])).astype(jnp.bfloat16)
                ps.append(prob.astype(jnp.bfloat16))
                dss.append(ds)
                acc_ref[g] += jnp.dot(kt[HS * g : HS * (g + 1)], ds, preferred_element_type=jnp.float32)
            dv = jnp.dot(jnp.concatenate(ps, axis=1), drows, preferred_element_type=jnp.float32)
            dk = jnp.dot(jnp.concatenate(dss, axis=1), qrows, preferred_element_type=jnp.float32)
            at = place_index(j)
            dkv[(s, 0) + at] = dk.astype(dkv.dtype).reshape(2, nf, tq, 2 * HS)
            dkv[(s, 1) + at] = dv.astype(dkv.dtype).reshape(2, nf, tq, 2 * HS)
            return carry

        lax.fori_loop(last, plane, zero, 0)
        lax.fori_loop(0, last, body, 0)
        cos_rows = jnp.concatenate([cos_ref[...]] * heads, axis=1) * (1.0 / 8.0)
        sin_rows = jnp.concatenate([sin_ref[...]] * heads, axis=1) * (1.0 / 8.0)
        for g in range(2):
            back = rotate_back(acc_ref[g], cos_rows, sin_rows).astype(gqt_ref.dtype)
            for j in range(heads):
                h = (2 * p + g) * heads + j
                gqt_ref[HS * h : HS * (h + 1), :] = back[:, tq * j : tq * (j + 1)]

    peers = 2 + sum(size - 1 for size in dims)

    def all_peers():
        found = [core_axis[3](1)[1], side_axis[3](1)[1]]
        for axis in lines:
            found += [axis[3](k)[1] for k in range(1, axis[1])]
        return found

    progress = {}

    def advance(p):
        stage = progress[p]
        stage_finish(p, stage)
        progress[p] = stage + 1
        if stage + 1 < stages:
            stage_start(p, stage + 1)
        else:
            del progress[p]
            if p + slots < parts:
                for where in all_peers():
                    pl.semaphore_signal(credit, inc=1, device_id=where, device_id_type=mesh_id)

    for p in range(parts):
        if p >= slots:
            while p - slots in progress:
                advance(p - slots)
        compute(p)
        if p == 0:
            pl.semaphore_wait(barrier, n - 1)
        if p >= slots:
            pl.semaphore_wait(credit, peers)
        stage_start(p, 0)
        progress[p] = 0
        for older in [o for o in progress if o < p]:
            advance(older)

    def copies_to(k, which):
        other, where = target(k)
        block, out = ((qblk, colq_ref), (kvblk, colkv_ref), (small, gains_ref))[which]
        return pltpu.make_async_remote_copy(
            src_ref=block if which == 2 else block.at[other // nf], dst_ref=out.at[me],
            send_sem=col_send.at[which, k], recv_sem=col_recv.at[which, k],
            device_id=where, device_id_type=mesh_id,
        )

    def share(which):
        def one(k, carry):
            copies_to(k, which).start()
            return carry

        block, out = ((qblk, colq_ref), (kvblk, colkv_ref), (small, gains_ref))[which]
        pltpu.make_async_copy(block if which == 2 else block.at[me_c], out.at[me], own_sem.at[which]).start()
        lax.fori_loop(1, n, one, 0)

    def share_wait(which):
        def one(k, carry):
            copies_to(k, which).wait()
            return carry

        block, out = ((qblk, colq_ref), (kvblk, colkv_ref), (small, gains_ref))[which]
        pltpu.make_async_copy(block if which == 2 else block.at[me_c], out.at[me], own_sem.at[which]).wait()
        lax.fori_loop(1, n, one, 0)

    width_q = 2 * parts * heads * HS
    width_k = 2 * parts * HS
    cq, ck = width_q // nctx, width_k // nctx
    qblk[...] = jnp.zeros_like(qblk)
    kvblk[...] = jnp.zeros_like(kvblk)
    for i in range(nctx):
        qblk[i, 0:cq, :] = gqt_ref[cq * i : cq * (i + 1), :]
    share(0)
    ga_ref[...] = jnp.dot(w_ref[:, :width_q], gqt_ref[...], preferred_element_type=jnp.float32)
    while progress:
        for p in list(progress):
            advance(p)

    cos_rows, sin_rows = cos_ref[...], sin_ref[...]
    grads = []
    for kind in range(2):
        rows = []
        for p in range(parts):
            both = jnp.transpose(finals[p, kind])
            for g in range(2):
                one = both[HS * g : HS * (g + 1)]
                rows.append(rotate_back(one, cos_rows, sin_rows) if kind == 0 else one)
        grads.append(jnp.concatenate(rows, axis=0).astype(jnp.bfloat16))
    for i in range(nctx):
        kvblk[i, 0:ck, :] = grads[0][ck * i : ck * (i + 1)]
        kvblk[i, ck : 2 * ck, :] = grads[1][ck * i : ck * (i + 1)]
    share(1)
    grad_t = (
        ga_ref[...]
        + jnp.dot(w_ref[:, width_q : width_q + width_k], grads[0], preferred_element_type=jnp.float32)
        + jnp.dot(w_ref[:, width_q + width_k :], grads[1], preferred_element_type=jnp.float32)
    )
    grad = jnp.transpose(grad_t)
    normed = normed_ref[...].astype(jnp.float32) * inv_ref[...]
    product = grad * normed
    gain_sum = jnp.sum(product, axis=0, keepdims=True)
    lanes = 128
    tiles = gain_sum.shape[1] // lanes
    rows = [gain_sum[:, lanes * i : lanes * (i + 1)] for i in range(tiles)]
    rows += [gmlp_ref[:, lanes * i : lanes * (i + 1)] for i in range(tiles)]
    rows += [jnp.zeros((small.shape[0] - 2 * tiles, lanes), jnp.float32)]
    small[...] = jnp.concatenate(rows, axis=0)
    share(2)
    gain = gain_ref[0:1, :]
    scaled = grad * gain
    mean = jnp.mean(scaled * normed, axis=1, keepdims=True)
    tokens_ref[...] = gres_ref[...] + inv_ref[...] * (scaled - normed * mean)
    share_wait(0)
    share_wait(1)
    share_wait(2)


def backward(nctx, nf, docs, q, do, ot, lse, kv, w, cos_t, sin_t, normed, inv, gain, gres, gmlp):
    width_q, tq = q.shape
    n_tokens, width_kv = kv.shape
    n = nctx * nf
    parts = width_kv // (4 * HS)
    heads = width_q // HS // (2 * parts)
    dims = line_dims(nctx // 2)
    lead = tuple(reversed(dims))
    part_bytes = n_tokens * 2 * HS * 2
    slots = parts if parts * part_bytes * 5 <= 24 * 2**20 else 1
    nd = len(dims)
    bf16, f32 = jnp.bfloat16, jnp.float32
    axes = {"core": (nd, 2), "side": (nd + 1, nf)}
    line = [(nd - 1 - i, dims[i]) for i in range(nd)]
    orders = [
        [axes["core"], axes["side"]] + line,
        [axes["core"], line[0], axes["side"]] + line[1:],
    ]
    recvs = []
    for order in orders:
        left = list(lead) + [2, nf]
        for position, size in order:
            left[position] = None
            recvs.append(
                pltpu.VMEM((slots, size - 1) + tuple(x for x in left if x) + (tq, 2 * HS), bf16)
            )
    stages = nd + 2
    most = max(dims + [2])
    pq = round_up(width_q // nctx, 16)
    pk = round_up(2 * (2 * parts * HS) // nctx, 16)
    model = w.shape[0]
    sr = round_up(2 * model // 128, 8)
    vmem = pl.BlockSpec(memory_space=pltpu.VMEM)
    smem = pl.BlockSpec(memory_space=pltpu.SMEM)
    hbm = pl.BlockSpec(memory_space=pl.ANY)
    return pl.pallas_call(
        functools.partial(backward_kernel, (nctx, nf, parts, heads, tq, slots)),
        out_shape=[
            jax.ShapeDtypeStruct((tq, model), f32),
            jax.ShapeDtypeStruct((n, pq, tq), bf16),
            jax.ShapeDtypeStruct((n, pk, tq), bf16),
            jax.ShapeDtypeStruct((n, sr, 128), f32),
        ],
        in_specs=[smem, vmem, vmem, vmem, vmem, hbm] + [vmem] * 8,
        out_specs=[vmem] * 4,
        scratch_shapes=[
            pltpu.VMEM((slots, 2, n_tokens, 2 * HS) if slots == parts else (2, 2, 2 * nf * tq, 2 * HS), bf16),
            pltpu.VMEM((slots, 2) + lead + (2, nf, tq, 2 * HS), bf16),
            pltpu.VMEM((2, HS, heads * tq), f32),
            pltpu.VMEM((width_q, tq), bf16),
            pltpu.VMEM((model, tq), f32),
            pltpu.VMEM((nctx, pq, tq), bf16),
            pltpu.VMEM((nctx, pk, tq), bf16),
            pltpu.VMEM((sr, 128), f32),
            pltpu.SemaphoreType.DMA((max(slots, 2), 2)),
            pltpu.SemaphoreType.DMA((slots, 2, stages, most - 1)),
            pltpu.SemaphoreType.DMA((slots, 2, stages, most - 1)),
            pltpu.SemaphoreType.DMA((3, n)),
            pltpu.SemaphoreType.DMA((3, n)),
            pltpu.SemaphoreType.DMA((3,)),
            pltpu.SemaphoreType.REGULAR,
        ]
        + recvs,
        compiler_params=pltpu.CompilerParams(
            collective_id=1, has_side_effects=True, vmem_limit_bytes=60 * 2**20
        ),
        cost_estimate=pl.CostEstimate(flops=10**10, bytes_accessed=3 * 10**7, transcendentals=10**7),
        name="backward",
    )(docs, q, do, ot, lse, kv, w, cos_t, sin_t, normed, inv, gain, gres, gmlp)


def rotate(rows, cos_rows, sin_rows):
    half_dim = HS // 2
    first, second = rows[:half_dim], rows[half_dim:]
    return jnp.concatenate(
        [first * cos_rows - second * sin_rows, second * cos_rows + first * sin_rows], axis=0
    )


class Axes:
    def __init__(self, nctx, nf):
        self.ctx, self.f = lax.axis_index("ctx"), lax.axis_index("fsdp")
        self.core, self.place = lax.rem(self.ctx, 2), self.ctx // 2
        self.me = self.ctx * nf + self.f
        self.dims = line_dims(nctx // 2)
        self.nd = len(self.dims)
        ctx, f, core, place = self.ctx, self.f, self.core, self.place
        self.core_axis = (self.nd, 2, core, lambda k: (1 - core, {"ctx": place * 2 + 1 - core, "fsdp": f}))
        self.side_axis = (self.nd + 1, 2, f, lambda k: (1 - f, {"ctx": ctx, "fsdp": 1 - f}))
        self.lines = [self.line(i) for i in range(self.nd)]
        self.peer_count = 2 + sum(size - 1 for size in self.dims)

    def at_line(self, i, there):
        stride = math.prod(self.dims[:i])
        own = lax.rem(self.place // stride, self.dims[i])
        return {"ctx": (self.place + (there - own) * stride) * 2 + self.core, "fsdp": self.f}

    def line(self, i):
        size = self.dims[i]
        own = lax.rem(self.place // math.prod(self.dims[:i]), size)

        def peer(k):
            there = lax.rem(own + k, size)
            return there, self.at_line(i, there)

        return (self.nd - 1 - i, size, own, peer)

    def peers(self):
        found = [self.core_axis[3](1)[1], self.side_axis[3](1)[1]]
        for axis in self.lines:
            found += [axis[3](k)[1] for k in range(1, axis[1])]
        return found

    def place_index(self, j):
        return tuple(
            lax.rem(j // math.prod(self.dims[:i]), self.dims[i]) for i in reversed(range(self.nd))
        )


def forward_kernel(plan, docs, tokens_ref, gains_ref, cos_ref, sin_ref, wq, wk, wv, wo, wg, wu, cot,
                   qt_ref, kv_out, low_ref, ot_ref, lse_ref, wqkv_out, wo_out, gu_out, cots_out,
                   attn_in_ref, inv_ref, gain_ref,
                   wbuf, obuf, gubuf, cbuf, gain_far, own_kv, kvb, m_ref, l_ref, acc_ref,
                   load_sem, w_send, w_recv, top_send, top_recv, ag_send, ag_recv, blk_sem, out_sem):
    nctx, nf, parts, heads, tq = plan
    ax = Axes(nctx, nf)
    f, core, place = ax.f, ax.core, ax.place
    mesh_id = pl.DeviceIdType.MESH
    bf16, f32 = jnp.bfloat16, jnp.float32
    width = tokens_ref.shape[1]
    half = width // nf
    width_q, width_k = 2 * parts * heads * HS, 2 * parts * HS
    rows4, rows2 = half // 4, half // 2
    quarter = gu_out.shape[1] // 2
    side = ax.side_axis[3](1)[1]
    mate = ax.core_axis[3](1)[1]
    low = ax.lines[0]
    bit = lax.rem(low[2], 2)
    across = ax.at_line(0, low[2] + 1 - 2 * bit)
    top = ax.nd - 1
    chunks = ax.dims[top]
    z = ax.lines[top][2]

    barrier = pltpu.get_barrier_semaphore()
    for where in ax.peers():
        pl.semaphore_signal(barrier, inc=1, device_id=where, device_id_type=mesh_id)

    def local(src, dst, i):
        return pltpu.make_async_copy(src, dst, load_sem.at[i])

    own_rows = pl.ds(pl.multiple_of(f * half, half), half)
    own_quarter = pl.ds(pl.multiple_of((2 * f + core) * quarter, quarter), quarter)
    loads = [
        local(wk, wbuf.at[own_rows, pl.ds(width_q, width_k)], 0),
        local(wv, wbuf.at[own_rows, pl.ds(width_q + width_k, width_k)], 1),
        local(wq, wbuf.at[own_rows, pl.ds(0, width_q)], 2),
        local(wo, obuf.at[own_rows], 3),
        local(wg.at[:, own_quarter], gubuf.at[own_rows, pl.ds(0, quarter)], 4),
        local(wu.at[:, own_quarter], gubuf.at[own_rows, pl.ds(quarter, quarter)], 5),
        local(cot, cbuf.at[0], 6),
    ]
    for copy in loads:
        copy.start()

    def remote(src, dst, i, where):
        return pltpu.make_async_remote_copy(
            src_ref=src, dst_ref=dst, send_sem=w_send.at[i], recv_sem=w_recv.at[i],
            device_id=where, device_id_type=mesh_id,
        )

    near = pl.multiple_of(core * rows2 + bit * rows4, 16)
    far_x = pl.multiple_of(core * rows2 + (1 - bit) * rows4, 16)
    there = (1 - f) * half

    def piece(base, offset):
        return pl.ds(pl.multiple_of(base + offset, 16), rows4)

    kv_cols, q_cols = pl.ds(width_q, 2 * width_k), pl.ds(0, width_q)
    mine = f * half
    gains_copy = remote(gains_ref, gain_far, 0, side)
    kv_y = [
        remote(wk.at[piece(0, near)], wbuf.at[piece(mine, near), pl.ds(width_q, width_k)], 1, side),
        remote(wv.at[piece(0, near)], wbuf.at[piece(mine, near), pl.ds(width_q + width_k, width_k)], 2, side),
    ]
    q_y = [remote(wq.at[piece(0, near)], wbuf.at[piece(mine, near), q_cols], 3, side)]
    o_y = [remote(wo.at[piece(0, near)], obuf.at[piece(mine, near)], 4, side)]

    def forwards(buf, cols, first):
        def part(offset):
            return buf.at[piece(there, offset), cols] if cols is not None else buf.at[piece(there, offset)]

        return [
            remote(part(near), part(near), first, across),
            remote(part(near), part(near), first + 1, mate),
            remote(part(far_x), part(far_x), first + 2, mate),
        ]

    kv_f = forwards(wbuf, kv_cols, 5)
    q_f = forwards(wbuf, q_cols, 8)
    o_f = forwards(obuf, None, 11)
    far_quarter = pl.ds(pl.multiple_of((2 * (1 - f) + core) * quarter, quarter), quarter)

    deep = lax.rem(z, 2)
    above = ax.at_line(top, z + 1 - 2 * deep)

    def gu_rows(base, which=bit):
        return pl.ds(pl.multiple_of(base + which * rows2 + deep * rows4, 16), rows4)

    gu_y = [
        remote(wg.at[gu_rows(0), far_quarter], gubuf.at[gu_rows(mine), pl.ds(0, quarter)], 14, side),
        remote(wu.at[gu_rows(0), far_quarter], gubuf.at[gu_rows(mine), pl.ds(quarter, quarter)], 15, side),
    ]
    gu_x = remote(gubuf.at[gu_rows(there)], gubuf.at[gu_rows(there)], 16, across)
    gu_z = [
        remote(gubuf.at[gu_rows(there, which)], gubuf.at[gu_rows(there, which)], 19 + i, above)
        for i, which in enumerate((bit, 1 - bit))
    ]
    cot_y = remote(cot, cbuf.at[1], 17, side)
    cot_c = remote(cbuf.at[pl.ds(0, 2)], cbuf.at[pl.ds(2, 2)], 18, mate)

    pl.semaphore_wait(barrier, ax.peer_count)
    gains_copy.start()
    for copy in kv_y + q_y:
        copy.start()

    hidden = tokens_ref[...].astype(f32)
    inv = lax.rsqrt(jnp.mean(hidden * hidden, axis=1, keepdims=True) + EPS)
    inv_ref[...] = inv
    gains_copy.wait()
    near_gain, far_gain = gains_ref[0:1, :], gain_far[0:1, :]
    gain = jnp.where(
        f == 0,
        jnp.concatenate([near_gain, far_gain], axis=1),
        jnp.concatenate([far_gain, near_gain], axis=1),
    )
    near_mlp, far_mlp = gains_ref[1:2, :], gain_far[1:2, :]
    gain_ref[0:1, :] = gain
    gain_ref[1:2, :] = jnp.where(
        f == 0,
        jnp.concatenate([near_mlp, far_mlp], axis=1),
        jnp.concatenate([far_mlp, near_mlp], axis=1),
    )
    attn_in = (hidden * inv * gain).astype(bf16)
    attn_in_ref[...] = attn_in

    for copy in kv_y:
        copy.wait()
    kv_f[0].start()
    kv_f[1].start()
    for copy in q_y:
        copy.wait()
    for copy in o_y + gu_y:
        copy.start()
    kv_f[0].wait()
    kv_f[2].start()
    q_f[0].start()
    q_f[1].start()
    for copy in loads[:3]:
        copy.wait()
    kv_f[1].wait()
    kv_f[2].wait()
    kv = jnp.dot(attn_in, wbuf[:, width_q:], preferred_element_type=f32)
    cos_rows, sin_rows = cos_ref[...], sin_ref[...]
    kt = jnp.transpose(kv[:, :width_k])
    k_rot = jnp.concatenate(
        [rotate(kt[HS * g : HS * (g + 1)], cos_rows, sin_rows) for g in range(2 * parts)], axis=0
    )
    own_kv[:, :width_k] = jnp.transpose(k_rot).astype(bf16)
    own_kv[:, width_k:] = kv[:, width_k:].astype(bf16)
    own_at = ax.place_index(place) + (core, f)
    put = pltpu.make_async_copy(own_kv, kv_out.at[own_at], out_sem.at[0])
    put.start()

    def top_copy(k):
        return pltpu.make_async_remote_copy(
            src_ref=own_kv, dst_ref=kv_out.at[own_at],
            send_sem=top_send.at[k - 1], recv_sem=top_recv.at[k - 1],
            device_id=ax.at_line(top, lax.rem(z + k, chunks)), device_id_type=mesh_id,
        )

    for k in range(1, chunks):
        @pl.when(z + k < chunks)
        def _():
            top_copy(k).start()

    lower = ax.lines[:top]
    orders = [lower + [ax.side_axis, ax.core_axis], [ax.side_axis] + lower + [ax.core_axis]]
    stages = len(orders[0])

    def ag_copies(k, stage):
        copies = []
        for kind in range(2):
            index = [None] * (ax.nd + 2)
            index[0] = z - k
            for i, axis in enumerate(orders[kind]):
                index[axis[0]] = slice(None) if i < stage else axis[2]
            region = kv_out.at[tuple(index) + (slice(None), pl.ds(kind * width_k, width_k))]
            axis = orders[kind][stage]
            for i in range(1, axis[1]):
                copies.append(
                    pltpu.make_async_remote_copy(
                        src_ref=region, dst_ref=region,
                        send_sem=ag_send.at[k, kind, stage, i - 1],
                        recv_sem=ag_recv.at[k, kind, stage, i - 1],
                        device_id=axis[3](i)[1], device_id_type=mesh_id,
                    )
                )
        return copies

    def tick(k, stage):
        @pl.when(z >= k)
        def _():
            if stage == 0:
                if k > 0:
                    top_copy(k).wait_recv()
            else:
                for copy in ag_copies(k, stage - 1):
                    copy.wait()
            if stage < stages:
                for copy in ag_copies(k, stage):
                    copy.start()

    put.wait()
    tick(0, 0)
    q_f[0].wait()
    q_f[2].start()
    q_f[1].wait()
    q_f[2].wait()
    back = pltpu.make_async_copy(wbuf, wqkv_out, out_sem.at[1])
    back.start()
    query = jnp.dot(attn_in, wbuf[:, :width_q], preferred_element_type=f32)
    query_t = jnp.transpose(query)
    for h in range(2 * parts * heads):
        qt_ref[HS * h : HS * (h + 1), :] = rotate(
            query_t[HS * h : HS * (h + 1)], cos_rows, sin_rows
        ).astype(bf16)
    m_ref[...] = jnp.full_like(m_ref, NEG)
    l_ref[...] = jnp.zeros_like(l_ref)
    acc_ref[...] = jnp.zeros_like(acc_ref)

    bk = 2 * nf * tq
    per_chunk = math.prod(ax.dims[:top])
    start = ax.me * tq

    def block_copy(j, slot):
        return pltpu.make_async_copy(kv_out.at[ax.place_index(j)], kvb.at[slot], blk_sem.at[slot])

    def attend(k):
        first_block = (z - k) * per_chunk
        count = jnp.minimum(place - first_block + 1, per_chunk)

        @pl.when(z >= k)
        def _():
            block_copy(first_block, 0).start()

            def block(i, carry):
                j = first_block + i
                slot = lax.rem(i, 2)

                @pl.when(i + 1 < count)
                def _():
                    block_copy(j + 1, 1 - slot).start()

                block_copy(j, slot).wait()
                bias = bias_tile((start,), docs, j * bk, bk, tq)
                bias = jnp.concatenate([bias] * heads, axis=1)
                for p in range(parts):
                    kb = kvb[slot, :, :, :, 2 * HS * p : 2 * HS * (p + 1)].reshape(bk, 2 * HS)
                    vb = kvb[slot, :, :, :, width_k + 2 * HS * p : width_k + 2 * HS * (p + 1)]
                    vt = jnp.transpose(vb.reshape(bk, 2 * HS))
                    rows = qt_ref[2 * heads * HS * p : 2 * heads * HS * (p + 1), :] * bf16(1.0 / 8.0)
                    for g in range(2):
                        at = 2 * p + g
                        s = jnp.dot(kb, padded(rows, heads, g), preferred_element_type=f32) + bias
                        m = m_ref[at]
                        new = jnp.maximum(m, jnp.max(s, axis=0, keepdims=True))
                        prob = jnp.exp(s - new)
                        decay = jnp.exp(m - new)
                        m_ref[at] = new
                        l_ref[at] = l_ref[at] * decay + jnp.sum(prob, axis=0, keepdims=True)
                        acc_ref[at] = acc_ref[at] * decay + jnp.dot(
                            vt[HS * g : HS * (g + 1)], prob.astype(bf16), preferred_element_type=f32
                        )
                return carry

            lax.fori_loop(0, count, block, 0)

    for turn in range(1, chunks + stages):
        for k in range(chunks):
            stage = turn - k
            if (k, stage) != (0, 0) and 0 <= stage <= stages:
                tick(k, stage)
        if turn == 4:
            for copy in o_y + gu_y:
                copy.wait()
            o_f[0].start()
            o_f[1].start()
            gu_x.start()
            gu_z[0].start()
        if turn == 3:
            cot_y.start()
        if turn == 6:
            o_f[0].wait()
            o_f[2].start()
            gu_x.wait()
            gu_z[1].start()
        if turn == 5:
            cot_y.wait()
            loads[6].wait()
            cot_c.start()
        if turn >= stages:
            attend(turn - stages)
    for p in range(parts):
        outs = []
        for g in range(2):
            at = 2 * p + g
            out = acc_ref[at] / l_ref[at]
            outs.append(out)
            ot_ref[at] = out
            lse_ref[at] = m_ref[at] + jnp.log(l_ref[at])
        low_ref[:, 2 * heads * HS * p : 2 * heads * HS * (p + 1)] = head_lanes(outs, heads, tq).astype(bf16)

    for k in range(1, chunks):
        @pl.when(z + k < chunks)
        def _():
            top_copy(k).wait_send()
    for copy in loads[3:6]:
        copy.wait()
    backs = [back]
    for waits, src, dst in (
        (o_f[1:], obuf, wo_out), ([cot_c], cbuf, cots_out), (gu_z, gubuf, gu_out)
    ):
        for copy in waits:
            copy.wait()
        backs.append(pltpu.make_async_copy(src, dst, out_sem.at[1 + len(backs)]))
        backs[-1].start()
    for copy in backs:
        copy.wait()


def forward(nctx, nf, docs, tokens, gains, cos_t, sin_t, wq, wk, wv, wo, wg, wu, cot):
    tq, width = tokens.shape
    width_q, width_k = wq.shape[1], wk.shape[1]
    parts = width_k // (2 * HS)
    heads = width_q // HS // (2 * parts)
    hidden_units = wg.shape[1]
    quarter = hidden_units // (2 * nf)
    dims = line_dims(nctx // 2)
    lead = tuple(reversed(dims))
    most = max(dims + [2])
    chunks = dims[-1]
    stages = len(dims) + 1
    bf16, f32 = jnp.bfloat16, jnp.float32
    vmem = pl.BlockSpec(memory_space=pltpu.VMEM)
    smem = pl.BlockSpec(memory_space=pltpu.SMEM)
    hbm = pl.BlockSpec(memory_space=pl.ANY)
    dma = pltpu.SemaphoreType.DMA
    return pl.pallas_call(
        functools.partial(forward_kernel, (nctx, nf, parts, heads, tq)),
        out_shape=[
            jax.ShapeDtypeStruct((width_q, tq), bf16),
            jax.ShapeDtypeStruct(lead + (2, nf, tq, 2 * width_k), bf16),
            jax.ShapeDtypeStruct((tq, width_q), bf16),
            jax.ShapeDtypeStruct((2 * parts, HS, heads * tq), f32),
            jax.ShapeDtypeStruct((2 * parts, 1, heads * tq), f32),
            jax.ShapeDtypeStruct((width, width_q + 2 * width_k), bf16),
            jax.ShapeDtypeStruct((nf * wo.shape[0], wo.shape[1]), bf16),
            jax.ShapeDtypeStruct((width, 2 * quarter), bf16),
            jax.ShapeDtypeStruct((2 * nf, tq, width), bf16),
            jax.ShapeDtypeStruct((tq, width), bf16),
            jax.ShapeDtypeStruct((tq, 1), f32),
            jax.ShapeDtypeStruct((2, width), f32),
        ],
        in_specs=[smem, vmem, vmem, vmem, vmem] + [hbm] * 7,
        out_specs=[vmem, hbm, vmem, vmem, vmem, hbm, hbm, hbm, hbm, vmem, vmem, vmem],
        scratch_shapes=[
            pltpu.VMEM((width, width_q + 2 * width_k), bf16),
            pltpu.VMEM((nf * wo.shape[0], wo.shape[1]), bf16),
            pltpu.VMEM((width, 2 * quarter), bf16),
            pltpu.VMEM((2 * nf, tq, width), bf16),
            pltpu.VMEM(gains.shape, f32),
            pltpu.VMEM((tq, 2 * width_k), bf16),
            pltpu.VMEM((2, 2, nf, tq, 2 * width_k), bf16),
            pltpu.VMEM((2 * parts, 1, heads * tq), f32),
            pltpu.VMEM((2 * parts, 1, heads * tq), f32),
            pltpu.VMEM((2 * parts, HS, heads * tq), f32),
            dma((7,)),
            dma((21,)),
            dma((21,)),
            dma((chunks - 1,)),
            dma((chunks - 1,)),
            dma((chunks, 2, stages, most - 1)),
            dma((chunks, 2, stages, most - 1)),
            dma((2,)),
            dma((5,)),
        ],
        compiler_params=pltpu.CompilerParams(
            collective_id=0, has_side_effects=True, vmem_limit_bytes=60 * 2**20
        ),
        name="forward",
    )(docs, tokens, gains, cos_t, sin_t, wq, wk, wv, wo, wg, wu, cot)


class Layout:
    def __init__(self, nctx, nf):
        self.nctx, self.nf, self.plane = nctx, nf, nctx // 2
        self.ctx = lax.axis_index("ctx")
        self.f = lax.axis_index("fsdp")
        self.core = lax.rem(self.ctx, 2)
        self.place = self.ctx // 2

    def send(self, value, move):
        pairs = []
        for ctx in range(self.nctx):
            for f in range(self.nf):
                place, core, side = move(ctx // 2, ctx % 2, f)
                pairs.append((ctx * self.nf + f, (place * 2 + core) * self.nf + side))
        return lax.ppermute(value, AXES, pairs)

    def to_core(self, value):
        return self.send(value, lambda r, c, f: (r, 1 - c, f))

    def to_side(self, value):
        return self.send(value, lambda r, c, f: (r, c, 1 - f))

    def in_order(self, which, own, other, axis=0):
        return jnp.where(
            which == 0,
            jnp.concatenate([own, other], axis=axis),
            jnp.concatenate([other, own], axis=axis),
        )

    def plane_scatter(self, data):
        stride = 1
        for size in line_dims(self.plane):
            coord = lax.rem(self.place // stride, size)
            data = data.reshape((data.shape[0] // size, size) + data.shape[1:])
            total = lax.dynamic_index_in_dim(data, coord, 1, keepdims=False).astype(jnp.float32)
            for k in range(1, size):
                part = lax.dynamic_index_in_dim(data, lax.rem(coord + k, size), 1, keepdims=False)

                def move(r, c, f, k=k, size=size, stride=stride):
                    at = r // stride % size
                    return r + ((at + k) % size - at) * stride, c, f

                total = total + self.send(part, move).astype(jnp.float32)
            stride *= size
            data = total if data.shape[0] == 1 else total.astype(jnp.bfloat16)
        return data[0]


def pair_weight(lay, local):
    half = local.shape[0] // 2
    mine = lax.dynamic_slice_in_dim(local, lay.core * half, half, 0)
    got = lay.to_side(mine)
    other = lay.to_core(got)
    return lay.in_order(lay.f, local, lay.in_order(lay.core, got, other))


def gather_group(lay, own):
    two = jnp.concatenate([own, lay.to_side(own)], axis=0)
    return jnp.concatenate([two, lay.to_core(two)], axis=0)


def scatter_group(lay, partial, rows):
    got = lay.to_core(partial[2 * rows :].astype(jnp.bfloat16))
    total = partial[: 2 * rows] + got.astype(jnp.float32)
    last = lay.to_side(total[rows:].astype(jnp.bfloat16))
    return total[:rows] + last.astype(jnp.float32)


def column_blocks(values, count):
    rows, width = values.shape
    return values.reshape(rows, count, width // count)


def per_device(
    nctx,
    nf,
    tokens,
    query_weight,
    key_projection,
    value_projection,
    output_weight,
    gate_weight,
    up_weight,
    down_weight,
    norm_attn,
    norm_mlp,
    doc_starts,
    cotangent,
):
    lay = Layout(nctx, nf)
    f, core = lay.f, lay.core
    token_rows, width = tokens.shape
    half = width // nf
    n_tokens = token_rows * nctx * nf
    hidden_units = gate_weight.shape[1]
    quarter = hidden_units // (2 * nf)
    bf16, f32 = jnp.bfloat16, jnp.float32

    own_device = lax.axis_index(AXES)
    own_index = layout_rows(own_device, token_rows)
    own_begin = doc_begin(own_index, doc_starts)
    cosine_table, sine_table = rope_tables(own_index - own_begin)
    cosine_table, sine_table = cosine_table.T, sine_table.T
    gains = jnp.pad(jnp.stack([norm_attn, norm_mlp]).astype(f32), ((0, 6), (0, 0)))
    (
        query_rot, key_values, attn_low, attn_exact, log_total, qkv_full, output_full, gate_up,
        cotangents, attention_input, inv_attn, gains,
    ) = forward(
        nctx, nf, doc_starts, tokens, gains, cosine_table, sine_table, query_weight, key_projection,
        value_projection, output_weight, gate_weight, up_weight, cotangent,
    )
    query_width = QUERY_HEADS * HEAD_SIZE
    key_width = KEY_VALUE_HEADS * HEAD_SIZE
    key_values = key_values.reshape(n_tokens, 2 * key_width)
    cotangents = cotangents.reshape(2 * nf * token_rows, width)
    gain_mlp = gains[1]
    down = lax.dynamic_slice_in_dim(down_weight, core * quarter, quarter, 0)
    hidden = tokens.astype(f32)

    def pair_side(values):
        halves = values.reshape(token_rows, nf, half)
        own = lax.dynamic_index_in_dim(halves, f, 1, keepdims=False)
        other = lax.dynamic_index_in_dim(halves, 1 - f, 1, keepdims=False)
        return lay.in_order(f, own, lay.to_side(other))

    resid = hidden + jnp.dot(attn_low, output_full, preferred_element_type=f32)
    inv_mlp = lax.rsqrt(jnp.mean(resid * resid, axis=-1, keepdims=True) + EPS)
    normed_mlp = resid * inv_mlp
    mlp_in = (normed_mlp * gain_mlp).astype(bf16)
    mlp_ins = gather_group(lay, mlp_in)
    gate_up_pre = jnp.dot(mlp_ins, gate_up, preferred_element_type=f32)
    gate_pre, up_pre = gate_up_pre[:, :quarter], gate_up_pre[:, quarter:]
    sigmoid_gate = jax.nn.sigmoid(gate_pre)
    gate_act = jax.nn.silu(gate_pre)
    mixed = (gate_act * up_pre).astype(bf16)
    grad_mixed = jnp.einsum("td,fd->tf", cotangents, down, preferred_element_type=f32)
    grad_gate = (grad_mixed * up_pre * sigmoid_gate * (1.0 + gate_pre * (1.0 - sigmoid_gate))).astype(bf16)
    grad_up = (grad_mixed * gate_act).astype(bf16)
    grads = jnp.concatenate([grad_gate, grad_up], axis=1)
    grad_mlp_in = scatter_group(
        lay, jnp.einsum("tf,df->td", grads, gate_up, preferred_element_type=f32), token_rows
    )
    result = (
        resid
        + scatter_group(lay, jnp.dot(mixed, down, preferred_element_type=f32), token_rows)
    ).astype(bf16)

    gain_mlp_partial = jnp.sum(grad_mlp_in * normed_mlp, axis=0)
    scaled_mlp = grad_mlp_in * gain_mlp
    grad_resid = cotangent.astype(f32) + inv_mlp * (
        scaled_mlp - normed_mlp * jnp.mean(scaled_mlp * normed_mlp, axis=-1, keepdims=True)
    )
    grad_branch = grad_resid.astype(bf16)
    grad_attn = jnp.einsum(
        "td,hd->th", grad_branch, output_full, preferred_element_type=f32
    ).astype(bf16)

    tokens_grad, columns_q, columns_kv, gain_parts = backward(
        nctx, nf, doc_starts, query_rot, grad_attn, attn_exact, log_total, key_values, qkv_full,
        cosine_table, sine_table, tokens, inv_attn, gains, grad_resid,
        gain_mlp_partial[None],
    )

    gate_up_partial = jnp.einsum("tf,td->fd", grads, mlp_ins, preferred_element_type=f32).astype(bf16)
    down_partial = jnp.einsum("td,tf->df", cotangents, mixed, preferred_element_type=f32).astype(bf16)
    gate_up_piece = lay.plane_scatter(
        gate_up_partial.reshape(2, lay.plane, quarter // lay.plane, width).transpose(1, 0, 2, 3)
    ).astype(bf16)
    down_piece = lay.plane_scatter(
        down_partial.reshape(lay.plane, width // lay.plane, quarter)
    )
    parity = lax.rem(lay.place, 2)
    left, right = gate_up_piece[..., :half], gate_up_piece[..., half:]
    per_side = lay.plane // 2

    def home(flip):
        def move(r, c, side):
            at = (2 * side + c) * per_side + r // 2
            return at // 2, at % 2, (r + flip) % 2

        return move

    same = lay.send(jnp.where(parity == 0, left, right), home(0))
    cross = lay.send(jnp.where(parity == 0, right, left), home(1))
    gate_up_sum = lay.in_order(f, same, cross, axis=1).astype(f32)
    gate_sum, up_sum = gate_up_sum[0].T, gate_up_sum[1].T
    down_piece = down_piece.reshape(2, width // nctx, quarter)
    down_own = lax.dynamic_index_in_dim(down_piece, core, 0, keepdims=False)
    down_other = lay.to_core(
        lax.dynamic_index_in_dim(down_piece, 1 - core, 0, keepdims=False).astype(bf16)
    ).astype(f32)
    down_sum = lay.in_order(core, down_own, down_other, axis=1).T

    inputs_all = lax.all_gather(pair_side(attention_input), "ctx", axis=0, tiled=True)
    cq, ck = query_width // nctx, key_width // nctx
    columns = jnp.concatenate([columns_q[:, :cq], columns_kv[:, : 2 * ck]], axis=1)
    qkv_sum = jnp.einsum(
        "nct,ntd->dc", columns, inputs_all.reshape(nctx * nf, token_rows, half),
        preferred_element_type=f32,
    )
    sizes = [cq, ck, ck]
    gain_sums = jnp.sum(gain_parts, axis=0)[: 2 * width // 128].reshape(2, width)
    attn_lows = pair_side(attn_low)
    attn_lows = jnp.concatenate([attn_lows, lay.to_core(attn_lows)], axis=0)
    branches = lay.in_order(f, grad_branch, lay.to_side(grad_branch))
    branches = jnp.concatenate([branches, lay.to_core(branches)], axis=0)
    output_partial = jnp.einsum("td,th->dh", branches, attn_lows, preferred_element_type=f32)
    output_partial = lax.dynamic_index_in_dim(
        output_partial.astype(bf16).reshape(lay.plane, 2, width // nctx, half), core, 1, keepdims=False
    )
    output_sum = lay.plane_scatter(output_partial).T
    query_sum = qkv_sum[:, : sizes[0]]
    key_sum = qkv_sum[:, sizes[0] : sizes[0] + sizes[1]]
    value_sum = qkv_sum[:, sizes[0] + sizes[1] :]
    return (
        result,
        tokens_grad,
        query_sum,
        key_sum,
        value_sum,
        output_sum,
        gate_sum,
        up_sum,
        down_sum,
        gain_sums[0],
        gain_sums[1],
    )


def solution(mesh):
    return jax.shard_map(
        functools.partial(per_device, mesh.shape["ctx"], mesh.shape["fsdp"]),
        mesh=mesh,
        in_specs=(
            P(("ctx", "fsdp"), None),
            P("fsdp", None),
            P("fsdp", None),
            P("fsdp", None),
            P("fsdp", None),
            P("fsdp", None),
            P("fsdp", None),
            P("fsdp", None),
            P("fsdp"),
            P("fsdp"),
            P(),
            P(("ctx", "fsdp"), None),
        ),
        out_specs=(
            P(("ctx", "fsdp"), None),
            P(("ctx", "fsdp"), None),
            P("fsdp", "ctx"),
            P("fsdp", "ctx"),
            P("fsdp", "ctx"),
            P("fsdp", "ctx"),
            P("fsdp", "ctx"),
            P("fsdp", "ctx"),
            P("fsdp", "ctx"),
            P(),
            P(),
        ),
        check_vma=False,
    )
```

```python
import functools
import math

import jax
import jax.numpy as jnp
from jax import lax
from jax.experimental import pallas as pl
from jax.experimental.pallas import tpu as pltpu
from jax.sharding import PartitionSpec as P

QUERY_HEADS = 18
KEY_VALUE_HEADS = 6
HEAD_SIZE = 64
HS = HEAD_SIZE

EPS = 1e-05
THETA = 10000.0
NEG = -1e30
AXES = ("ctx", "fsdp")


def rope_tables(positions):
    half_dim = HEAD_SIZE // 2
    frequency = jnp.exp(-math.log(THETA) * jnp.arange(half_dim, dtype=jnp.float32) / half_dim)
    angles = positions.astype(jnp.float32)[:, None] * frequency[None, :]
    return (jnp.cos(angles), jnp.sin(angles))


def apply_rotary(values, cosine_table, sine_table):
    half_dim = values.shape[-1] // 2
    first_half = values[..., :half_dim]
    second_half = values[..., half_dim:]
    cos_rows = cosine_table[:, None, :]
    sin_rows = sine_table[:, None, :]
    return jnp.concatenate(
        [
            first_half * cos_rows - second_half * sin_rows,
            second_half * cos_rows + first_half * sin_rows,
        ],
        axis=-1,
    )


def unrotate(values, cosine_table, sine_table):
    half_dim = values.shape[-1] // 2
    first_half = values[..., :half_dim]
    second_half = values[..., half_dim:]
    cos_rows = cosine_table[:, None, :]
    sin_rows = sine_table[:, None, :]
    return jnp.concatenate(
        [
            first_half * cos_rows + second_half * sin_rows,
            second_half * cos_rows - first_half * sin_rows,
        ],
        axis=-1,
    )


def doc_begin(indices, doc_starts):
    marked = jnp.where(indices[:, None] >= doc_starts[None, :], doc_starts[None, :], 0)
    return jnp.max(marked, axis=1)


def layout_rows(device, row_count):
    return device * row_count + jnp.arange(row_count, dtype=jnp.int32)


def heads_rows(natural):
    return jnp.transpose(natural.astype(jnp.float32))
def padded(rows, heads, g):
    top = jnp.concatenate([rows[HS*(heads*g+j):HS*(heads*g+j+1)] for j in range(heads)], axis=1)
    z = jnp.zeros_like(top)
    return jnp.concatenate([top, z] if g == 0 else [z, top], axis=0)
def head_lanes(per_group, heads, tq):
    return jnp.transpose(jnp.concatenate([per_group[g][:, tq*j:tq*(j+1)] for g in range(2) for j in range(heads)], axis=0))
def bias_tile(info, docs, first, bk, tq):
    query = info[0] + lax.broadcasted_iota(jnp.int32, (1, tq), 1)
    begin = jnp.zeros((1, tq), jnp.int32)
    for i in range(docs.shape[0]):
        begin = jnp.maximum(begin, jnp.where(query >= docs[i], docs[i], 0))
    key = first + lax.broadcasted_iota(jnp.int32, (bk, 1), 0)
    return jnp.where((key <= query) & (key >= begin), 0.0, NEG)


def line_dims(count):
    fours = 0
    while count % 4 == 0:
        count //= 4
        fours += 1
    return ([count] if count > 1 else []) + [4] * fours


def rotate_back(rows, cos_rows, sin_rows):
    half_dim = HS // 2
    first, second = rows[:half_dim], rows[half_dim:]
    return jnp.concatenate(
        [first * cos_rows + second * sin_rows, second * cos_rows - first * sin_rows], axis=0
    )


def round_up(value, unit):
    return -(-value // unit) * unit


def backward_kernel(plan, docs, q_ref, do_ref, ot_ref, lse_ref, kv_hbm, w_ref, cos_ref, sin_ref,
                    normed_ref, inv_ref, gain_ref, gres_ref, gmlp_ref, low_ref, branch_ref, gup_hbm, dnp_hbm,
                    tokens_ref, colq_ref, colkv_ref, gains_ref, gate_ref, up_ref, down_ref, out_ref,
                    kvbuf, dkv, acc_ref, gqt_ref, ga_ref, qblk, kvblk, small,
                    load_sem, send_sem, recv_sem, col_send, col_recv, own_sem, credit,
                    wg, wd, wo, brs, lows, halves, fin, fin_in, dsend, din,
                    g_send, g_recv, w_load, w_send, w_recv, top_send, top_recv, fin_send, fin_recv, *recvs):
    nctx, nf, parts, heads, tq, slots = plan
    plane = nctx // 2
    n = nctx * nf
    dims = line_dims(plane)
    nd = len(dims)
    bk = 2 * nf * tq
    me_c, me_f = lax.axis_index("ctx"), lax.axis_index("fsdp")
    me = me_c * nf + me_f
    core, place = lax.rem(me_c, 2), me_c // 2
    mesh_id = pl.DeviceIdType.MESH
    half_dim = HS // 2

    def target(k):
        other = lax.rem(me + k, n)
        return other, {"ctx": other // nf, "fsdp": lax.rem(other, nf)}

    barrier = pltpu.get_barrier_semaphore()

    def greet(k, carry):
        pl.semaphore_signal(barrier, inc=1, device_id=target(k)[1], device_id_type=mesh_id)
        return carry

    lax.fori_loop(1, n, greet, 0)

    def loads(p):
        s = p % slots
        return [
            pltpu.make_async_copy(
                kv_hbm.at[:, pl.ds((kind * parts + p) * 2 * HS, 2 * HS)],
                kvbuf.at[s, kind], load_sem.at[s, kind],
            )
            for kind in range(2)
        ]

    resident = slots == parts

    def block_loads(p, j):
        slot = lax.rem(j, 2)
        return [
            pltpu.make_async_copy(
                kv_hbm.at[pl.ds(pl.multiple_of(j * bk, bk), bk), pl.ds((kind * parts + p) * 2 * HS, 2 * HS)],
                kvbuf.at[slot, kind], load_sem.at[slot, kind],
            )
            for kind in range(2)
        ]

    if resident:
        for p in range(parts):
            for copy in loads(p):
                copy.start()

    def dim_axis(i):
        stride = math.prod(dims[:i])
        size = dims[i]
        own = lax.rem(place // stride, size)

        def peer(k):
            there = lax.rem(own + k, size)
            return there, {"ctx": (place + (there - own) * stride) * 2 + core, "fsdp": me_f}

        return (nd - 1 - i, size, own, peer)

    core_axis = (nd, 2, core, lambda k: (1 - core, {"ctx": place * 2 + 1 - core, "fsdp": me_f}))
    side_axis = (nd + 1, 2, me_f, lambda k: (1 - me_f, {"ctx": me_c, "fsdp": 1 - me_f}))
    lines = [dim_axis(i) for i in range(nd)]
    orders = [[core_axis, side_axis] + lines, [core_axis, lines[0], side_axis] + lines[1:]]
    stages = nd + 2
    wrecvs = recvs[2 * stages :]
    side_at, mate_at = side_axis[3](1)[1], core_axis[3](1)[1]

    top = nd - 1
    chunks, z = dims[top], lines[top][2]
    arrays = ((wg, gup_hbm), (wd, dnp_hbm), (wo, None))

    def chunk_at(k):
        return lax.rem(z + k, chunks)

    def w_region(k, stage, at):
        index = [slice(None)] * nd
        index[0] = chunk_at(k)
        for axis in lines[:stage]:
            index[axis[0]] = axis[2]
        index[lines[stage][0]] = at
        return tuple(index)

    def held(a, index):
        return index if a == 2 else index[: nd - 1]

    def w_copies(a, k, stage):
        axis = lines[stage]
        buf, far = arrays[a]
        copies = []
        for i in range(1, axis[1]):
            there, where = axis[3](i)
            copies.append(
                pltpu.make_async_remote_copy(
                    src_ref=far.at[w_region(k, stage, there)] if stage == 0 and a < 2
                    else buf.at[held(a, w_region(k, stage, there))],
                    dst_ref=wrecvs[a * nd + stage].at[i - 1, chunk_at(k)],
                    send_sem=w_send.at[a, k, stage, i - 1], recv_sem=w_recv.at[a, k, stage, i - 1],
                    device_id=where, device_id_type=mesh_id,
                )
            )
        return copies

    def top_copy(a, k):
        return pltpu.make_async_remote_copy(
            src_ref=arrays[a][0].at[held(a, w_region(k, top, chunk_at(k)))], dst_ref=wrecvs[a * nd + top].at[k - 1],
            send_sem=top_send.at[a, k - 1], recv_sem=top_recv.at[a, k - 1],
            device_id=lines[top][3](k)[1], device_id_type=mesh_id,
        )

    def w_start(which, k):
        for a in which:
            for copy in w_copies(a, k, 0):
                copy.start()

    def w_finish(which, k):
        for a in which:
            buf = arrays[a][0]
            for stage in range(top):
                for copy in w_copies(a, k, stage):
                    copy.wait()
                where = held(a, w_region(k, stage, lines[stage][2]))
                got = wrecvs[a * nd + stage]
                total = buf[where].astype(jnp.float32)
                for i in range(lines[stage][1] - 1):
                    total = total + got[i, chunk_at(k)].astype(jnp.float32)
                buf[where] = total.astype(buf.dtype)
                if stage + 1 < top:
                    for copy in w_copies(a, k, stage + 1):
                        copy.start()
            if k > 0:
                top_copy(a, k).start()

    def w_total(a):
        buf = arrays[a][0]
        total = buf[held(a, w_region(0, top, z))].astype(jnp.float32)
        for k in range(1, chunks):
            top_copy(a, k).wait()
            total = total + wrecvs[a * nd + top][k - 1].astype(jnp.float32)
        return total

    w_loads = [
        pltpu.make_async_copy(far.at[(slice(None),) * (nd - 1) + (lines[0][2],)], buf, w_load.at[i])
        for i, (buf, far) in enumerate(arrays[:2])
    ]
    for copy in w_loads:
        copy.start()
    half = low_ref.shape[1] // nf
    low_all = low_ref[...]
    halves[0] = low_all[:, :half]
    halves[1] = low_all[:, half:]
    lows[0] = halves[me_f]
    brs[0] = branch_ref[...]

    def g_copy(i, src, dst, where):
        return pltpu.make_async_remote_copy(
            src_ref=src, dst_ref=dst, send_sem=g_send.at[i], recv_sem=g_recv.at[i],
            device_id=where, device_id_type=mesh_id,
        )

    low_side = g_copy(0, halves.at[1 - me_f], lows.at[1], side_at)
    br_side = g_copy(1, brs.at[0], brs.at[1], side_at)
    low_core = g_copy(2, lows.at[pl.ds(0, 2)], lows.at[pl.ds(2, 2)], mate_at)
    br_core = g_copy(3, brs.at[pl.ds(0, 2)], brs.at[pl.ds(2, 2)], mate_at)

    def output_partial():
        low_core.wait()
        br_core.wait()
        rows = jnp.transpose(brs[...].reshape(4 * tq, brs.shape[2]))
        part = jnp.dot(rows, lows[...].reshape(4 * tq, half), preferred_element_type=jnp.float32)
        unit = brs.shape[2] // nctx
        wo[...] = jnp.zeros_like(wo)
        for r in range(plane):
            first = 2 * unit * r
            piece = jnp.where(core == 0, part[first : first + unit], part[first + unit : first + 2 * unit])
            wo[static_index(dims, r) + (slice(0, unit), slice(0, half))] = piece.astype(wo.dtype)

    pl.semaphore_wait(barrier, n - 1)
    low_side.start()
    br_side.start()
    w_start((0, 1), 1)
    w_start((0, 1), 2 % chunks)

    def region(kind, stage, at):
        index = [slice(None)] * (nd + 2)
        for axis in orders[kind][:stage]:
            index[axis[0]] = axis[2]
        index[orders[kind][stage][0]] = at
        return tuple(index)

    def stage_copies(p, kind, stage):
        s = p % slots
        axis = orders[kind][stage]
        copies = []
        for k in range(1, axis[1]):
            there, where = axis[3](k)
            copies.append(
                pltpu.make_async_remote_copy(
                    src_ref=dkv.at[(s, kind) + region(kind, stage, there)],
                    dst_ref=recvs[kind * stages + stage].at[s, k - 1],
                    send_sem=send_sem.at[s, kind, stage, k - 1],
                    recv_sem=recv_sem.at[s, kind, stage, k - 1],
                    device_id=where, device_id_type=mesh_id,
                )
            )
        return copies

    def stage_start(p, stage):
        for kind in range(2):
            for copy in stage_copies(p, kind, stage):
                copy.start()

    finals = {}

    def stage_finish(p, stage):
        s = p % slots
        for kind in range(2):
            axis = orders[kind][stage]
            for copy in stage_copies(p, kind, stage):
                copy.wait()
            where = region(kind, stage, axis[2])
            got = recvs[kind * stages + stage]
            free = [i for i in range(nd + 2) if isinstance(where[i], slice)]

            def add(index, lead):
                total = dkv[(s, kind) + index].astype(jnp.float32)
                for k in range(axis[1] - 1):
                    total = total + got[(s, k) + lead].astype(jnp.float32)
                return total

            if not free:
                finals[p, kind] = add(where, ())
            else:
                size = dkv.shape[2 + free[0]]

                def one(i, carry):
                    index = list(where)
                    index[free[0]] = i
                    index = tuple(index)
                    dkv[(s, kind) + index] = add(index, (i,)).astype(dkv.dtype)
                    return carry

                lax.fori_loop(0, size, one, 0)

    def place_index(j):
        index = []
        for i in reversed(range(nd)):
            index.append(lax.rem(j // math.prod(dims[:i]), dims[i]))
        return tuple(index)

    start = me * tq
    last = (start + tq - 1) // bk + 1

    def compute(p):
        s = p % slots
        span = slice(2 * heads * HS * p, 2 * heads * HS * (p + 1))
        qt = q_ref[span, :].astype(jnp.float32) * (1.0 / 8.0)
        dt = heads_rows(do_ref[:, span])
        qg = [padded(qt, heads, g) for g in range(2)]
        dg = [padded(dt, heads, g) for g in range(2)]
        qrows = jnp.concatenate([jnp.transpose(x) for x in qg], axis=0).astype(jnp.bfloat16)
        drows = jnp.concatenate([jnp.transpose(x) for x in dg], axis=0).astype(jnp.bfloat16)
        delta = [
            jnp.sum(dg[g][HS * g : HS * (g + 1)] * ot_ref[2 * p + g], axis=0, keepdims=True)
            for g in range(2)
        ]
        lse = [lse_ref[2 * p + g] for g in range(2)]
        qg = [x.astype(jnp.bfloat16) for x in qg]
        dg = [x.astype(jnp.bfloat16) for x in dg]
        acc_ref[...] = jnp.zeros_like(acc_ref)
        for copy in loads(p) if resident else block_loads(p, 0):
            if not resident:
                copy.start()
            else:
                copy.wait()

        def zero(j, carry):
            at = place_index(j)
            for kind in range(2):
                dkv[(s, kind) + at] = jnp.zeros((2, nf, tq, 2 * HS), dkv.dtype)
            return carry

        def body(j, carry):
            first = pl.multiple_of(j * bk, bk)
            if resident:
                kb = kvbuf[s, 0, pl.ds(first, bk), :]
                vb = kvbuf[s, 1, pl.ds(first, bk), :]
            else:
                for copy in block_loads(p, j):
                    copy.wait()

                @pl.when(j + 1 < last)
                def _():
                    for copy in block_loads(p, j + 1):
                        copy.start()

                kb, vb = kvbuf[lax.rem(j, 2), 0], kvbuf[lax.rem(j, 2), 1]
            kt = jnp.transpose(kb)
            bias = bias_tile((start,), docs, first, bk, tq)
            bias = jnp.concatenate([bias] * heads, axis=1)
            ps = []
            dss = []
            for g in range(2):
                score = jnp.dot(kb, qg[g], preferred_element_type=jnp.float32)
                prob = jnp.exp(score + (bias - lse[g]))
                dp = jnp.dot(vb, dg[g], preferred_element_type=jnp.float32)
                ds = (prob * (dp - delta[g])).astype(jnp.bfloat16)
                ps.append(prob.astype(jnp.bfloat16))
                dss.append(ds)
                acc_ref[g] += jnp.dot(kt[HS * g : HS * (g + 1)], ds, preferred_element_type=jnp.float32)
            dv = jnp.dot(jnp.concatenate(ps, axis=1), drows, preferred_element_type=jnp.float32)
            dk = jnp.dot(jnp.concatenate(dss, axis=1), qrows, preferred_element_type=jnp.float32)
            at = place_index(j)
            dkv[(s, 0) + at] = dk.astype(dkv.dtype).reshape(2, nf, tq, 2 * HS)
            dkv[(s, 1) + at] = dv.astype(dkv.dtype).reshape(2, nf, tq, 2 * HS)
            return carry

        lax.fori_loop(last, plane, zero, 0)
        lax.fori_loop(0, last, body, 0)
        cos_rows = jnp.concatenate([cos_ref[...]] * heads, axis=1) * (1.0 / 8.0)
        sin_rows = jnp.concatenate([sin_ref[...]] * heads, axis=1) * (1.0 / 8.0)
        for g in range(2):
            back = rotate_back(acc_ref[g], cos_rows, sin_rows).astype(gqt_ref.dtype)
            for j in range(heads):
                h = (2 * p + g) * heads + j
                gqt_ref[HS * h : HS * (h + 1), :] = back[:, tq * j : tq * (j + 1)]

    peers = 2 + sum(size - 1 for size in dims)

    def all_peers():
        found = [core_axis[3](1)[1], side_axis[3](1)[1]]
        for axis in lines:
            found += [axis[3](k)[1] for k in range(1, axis[1])]
        return found

    progress = {}

    def advance(p):
        stage = progress[p]
        stage_finish(p, stage)
        progress[p] = stage + 1
        if stage + 1 < stages:
            stage_start(p, stage + 1)
        else:
            del progress[p]
            if p + slots < parts:
                for where in all_peers():
                    pl.semaphore_signal(credit, inc=1, device_id=where, device_id_type=mesh_id)

    for p in range(parts):
        if p >= slots:
            while p - slots in progress:
                advance(p - slots)
        compute(p)
        if p >= slots:
            pl.semaphore_wait(credit, peers)
        stage_start(p, 0)
        progress[p] = 0
        for older in [o for o in progress if o < p]:
            advance(older)
        if p == 0:
            low_side.wait()
            br_side.wait()
            low_core.start()
            br_core.start()
        if p == 1:
            for copy in w_loads:
                copy.wait()
            w_finish((0, 1), 1)
            if chunks > 3:
                w_start((0, 1), 3)
            output_partial()
            for k in list(range(1, chunks)) + [0]:
                w_start((2,), k)
    w_finish((0, 1), 2)
    w_start((0, 1), 0)

    def copies_to(k, which):
        other, where = target(k)
        block, out = ((qblk, colq_ref), (kvblk, colkv_ref), (small, gains_ref))[which]
        return pltpu.make_async_remote_copy(
            src_ref=block if which == 2 else block.at[other // nf], dst_ref=out.at[me],
            send_sem=col_send.at[which, k], recv_sem=col_recv.at[which, k],
            device_id=where, device_id_type=mesh_id,
        )

    def share(which):
        def one(k, carry):
            copies_to(k, which).start()
            return carry

        block, out = ((qblk, colq_ref), (kvblk, colkv_ref), (small, gains_ref))[which]
        pltpu.make_async_copy(block if which == 2 else block.at[me_c], out.at[me], own_sem.at[which]).start()
        lax.fori_loop(1, n, one, 0)

    def share_wait(which):
        def one(k, carry):
            copies_to(k, which).wait()
            return carry

        block, out = ((qblk, colq_ref), (kvblk, colkv_ref), (small, gains_ref))[which]
        pltpu.make_async_copy(block if which == 2 else block.at[me_c], out.at[me], own_sem.at[which]).wait()
        lax.fori_loop(1, n, one, 0)

    width_q = 2 * parts * heads * HS
    width_k = 2 * parts * HS
    cq, ck = width_q // nctx, width_k // nctx
    qblk[...] = jnp.zeros_like(qblk)
    kvblk[...] = jnp.zeros_like(kvblk)
    for i in range(nctx):
        qblk[i, 0:cq, :] = gqt_ref[cq * i : cq * (i + 1), :]
    share(0)
    ga_ref[...] = jnp.dot(w_ref[:, :width_q], gqt_ref[...], preferred_element_type=jnp.float32)
    for k in list(range(1, chunks)):
        w_finish((2,), k)
    while progress:
        for p in list(progress):
            advance(p)

    cos_rows, sin_rows = cos_ref[...], sin_ref[...]
    grads = []
    for kind in range(2):
        rows = []
        for p in range(parts):
            both = jnp.transpose(finals[p, kind])
            for g in range(2):
                one = both[HS * g : HS * (g + 1)]
                rows.append(rotate_back(one, cos_rows, sin_rows) if kind == 0 else one)
        grads.append(jnp.concatenate(rows, axis=0).astype(jnp.bfloat16))
    for i in range(nctx):
        kvblk[i, 0:ck, :] = grads[0][ck * i : ck * (i + 1)]
        kvblk[i, ck : 2 * ck, :] = grads[1][ck * i : ck * (i + 1)]
    share(1)
    grad_t = (
        ga_ref[...]
        + jnp.dot(w_ref[:, width_q : width_q + width_k], grads[0], preferred_element_type=jnp.float32)
        + jnp.dot(w_ref[:, width_q + width_k :], grads[1], preferred_element_type=jnp.float32)
    )
    grad = jnp.transpose(grad_t)
    normed = normed_ref[...].astype(jnp.float32) * inv_ref[...]
    product = grad * normed
    gain_sum = jnp.sum(product, axis=0, keepdims=True)
    lanes = 128
    tiles = gain_sum.shape[1] // lanes
    rows = [gain_sum[:, lanes * i : lanes * (i + 1)] for i in range(tiles)]
    rows += [gmlp_ref[:, lanes * i : lanes * (i + 1)] for i in range(tiles)]
    rows += [jnp.zeros((small.shape[0] - 2 * tiles, lanes), jnp.float32)]
    small[...] = jnp.concatenate(rows, axis=0)
    share(2)
    gain = gain_ref[0:1, :]
    scaled = grad * gain
    mean = jnp.mean(scaled * normed, axis=1, keepdims=True)
    tokens_ref[...] = gres_ref[...] + inv_ref[...] * (scaled - normed * mean)
    for k in range(3, chunks):
        w_finish((0, 1), k)
    w_finish((0, 1, 2), 0)

    total = w_total(0)
    unit, lanes = fin.shape[2], fin.shape[3]
    blank = jnp.zeros((2, unit, lanes - half), fin.dtype)
    for s in range(2):
        fin[s] = jnp.concatenate([total[:, :, half * s : half * (s + 1)].astype(fin.dtype), blank], axis=2)
    dsum = w_total(1)
    dsend[...] = dsum.astype(dsend.dtype)
    down_copy = g_copy(4, dsend, din, mate_at)
    down_copy.start()
    per_side = plane // 2
    home = (2 * me_f + core) * per_side + place // 2
    slot = lax.rem(place, 2)

    def home_copy(s):
        return pltpu.make_async_remote_copy(
            src_ref=fin.at[s], dst_ref=fin_in.at[slot], send_sem=fin_send.at[s], recv_sem=fin_recv.at[slot],
            device_id={"ctx": home, "fsdp": jnp.int32(s)}, device_id_type=mesh_id,
        )

    def self_copy(s):
        return pltpu.make_async_copy(fin.at[s], fin_in.at[slot], fin_send.at[s])

    for s in range(2):
        at_home = (home == me_c) & (me_f == s)

        @pl.when(jnp.logical_not(at_home))
        def _():
            home_copy(s).start()

        @pl.when(at_home)
        def _():
            self_copy(s).start()

    osum = w_total(2)
    out_ref[...] = jnp.transpose(osum)[:half, : out_ref.shape[1]]
    share_wait(0)
    share_wait(1)
    share_wait(2)
    down_copy.wait()
    cols = down_ref.shape[1]
    got = din[...].astype(jnp.float32)
    own_cols = jnp.where(core == 0, dsum[:cols], dsum[cols:])
    far_cols = jnp.where(core == 0, got[:cols], got[cols:])
    down_ref[...] = jnp.transpose(
        jnp.where(
            core == 0,
            jnp.concatenate([own_cols, far_cols], axis=1),
            jnp.concatenate([far_cols, own_cols], axis=1),
        )
    )
    for s in range(2):
        at_home = (home == me_c) & (me_f == s)

        @pl.when(jnp.logical_not(at_home))
        def _():
            home_copy(s).wait_send()

        @pl.when(at_home)
        def _():
            self_copy(s).wait()

    owner = me_c // per_side
    for h in range(2):
        holder = (2 * lax.rem(me_c, per_side) + h) * 2 + lax.rem(owner, 2)

        @pl.when(jnp.logical_not((holder == me_c) & (owner // 2 == me_f)))
        def _():
            pltpu.make_async_remote_copy(
                src_ref=fin.at[0], dst_ref=fin_in.at[h], send_sem=fin_send.at[0], recv_sem=fin_recv.at[h],
                device_id={"ctx": home, "fsdp": me_f}, device_id_type=mesh_id,
            ).wait_recv()

    for kind, ref in ((0, gate_ref), (1, up_ref)):
        rows = jnp.concatenate([fin_in[0, kind], fin_in[1, kind]], axis=0).astype(jnp.float32)
        ref[...] = jnp.transpose(rows)[:half, :]


def backward(nctx, nf, docs, q, do, ot, lse, kv, w, cos_t, sin_t, normed, inv, gain, gres, gmlp, low, branch, gup, dnp):
    width_q, tq = q.shape
    n_tokens, width_kv = kv.shape
    n = nctx * nf
    parts = width_kv // (4 * HS)
    heads = width_q // HS // (2 * parts)
    dims = line_dims(nctx // 2)
    lead = tuple(reversed(dims))
    part_bytes = n_tokens * 2 * HS * 2
    slots = parts if parts * part_bytes * 5 <= 24 * 2**20 else 1
    nd = len(dims)
    bf16, f32 = jnp.bfloat16, jnp.float32
    axes = {"core": (nd, 2), "side": (nd + 1, nf)}
    line = [(nd - 1 - i, dims[i]) for i in range(nd)]
    orders = [
        [axes["core"], axes["side"]] + line,
        [axes["core"], line[0], axes["side"]] + line[1:],
    ]
    recvs = []
    for order in orders:
        left = list(lead) + [2, nf]
        for position, size in order:
            left[position] = None
            recvs.append(
                pltpu.VMEM((slots, size - 1) + tuple(x for x in left if x) + (tq, 2 * HS), bf16)
            )
    half = low.shape[1] // nf
    unit, deep = gup.shape[-2], dnp.shape[-2]
    plane = nctx // 2
    tails = [gup.shape[nd:], dnp.shape[nd:], (round_up(deep // 2, 16), round_up(half, 128))]
    for tail in tails:
        for stage in range(nd):
            left = list(lead)
            for i in range(stage + 1):
                left[nd - 1 - i] = None
            if stage == nd - 1:
                recvs.append(pltpu.VMEM((dims[stage] - 1,) + tail, bf16))
            else:
                recvs.append(pltpu.VMEM((dims[stage] - 1,) + tuple(x for x in left if x) + tail, bf16))
    chunks = dims[-1]
    stages = nd + 2
    most = max(dims + [2])
    pq = round_up(width_q // nctx, 16)
    pk = round_up(2 * (2 * parts * HS) // nctx, 16)
    model = w.shape[0]
    sr = round_up(2 * model // 128, 8)
    vmem = pl.BlockSpec(memory_space=pltpu.VMEM)
    smem = pl.BlockSpec(memory_space=pltpu.SMEM)
    hbm = pl.BlockSpec(memory_space=pl.ANY)
    return pl.pallas_call(
        functools.partial(backward_kernel, (nctx, nf, parts, heads, tq, slots)),
        out_shape=[
            jax.ShapeDtypeStruct((tq, model), f32),
            jax.ShapeDtypeStruct((n, pq, tq), bf16),
            jax.ShapeDtypeStruct((n, pk, tq), bf16),
            jax.ShapeDtypeStruct((n, sr, 128), f32),
            jax.ShapeDtypeStruct((half, 2 * unit), f32),
            jax.ShapeDtypeStruct((half, 2 * unit), f32),
            jax.ShapeDtypeStruct((2 * dnp.shape[-1], deep // 2), f32),
            jax.ShapeDtypeStruct((half, deep // 2), f32),
        ],
        in_specs=[smem, vmem, vmem, vmem, vmem, hbm] + [vmem] * 10 + [hbm] * 2,
        out_specs=[vmem] + [hbm] * 3 + [vmem] * 4,
        scratch_shapes=[
            pltpu.VMEM((slots, 2, n_tokens, 2 * HS) if slots == parts else (2, 2, 2 * nf * tq, 2 * HS), bf16),
            pltpu.VMEM((slots, 2) + lead + (2, nf, tq, 2 * HS), bf16),
            pltpu.VMEM((2, HS, heads * tq), f32),
            pltpu.VMEM((width_q, tq), bf16),
            pltpu.VMEM((model, tq), f32),
            pltpu.VMEM((nctx, pq, tq), bf16),
            pltpu.VMEM((nctx, pk, tq), bf16),
            pltpu.VMEM((sr, 128), f32),
            pltpu.SemaphoreType.DMA((max(slots, 2), 2)),
            pltpu.SemaphoreType.DMA((slots, 2, stages, most - 1)),
            pltpu.SemaphoreType.DMA((slots, 2, stages, most - 1)),
            pltpu.SemaphoreType.DMA((3, n)),
            pltpu.SemaphoreType.DMA((3, n)),
            pltpu.SemaphoreType.DMA((3,)),
            pltpu.SemaphoreType.REGULAR,
            pltpu.VMEM(lead[:-1] + tails[0], bf16),
            pltpu.VMEM(lead[:-1] + tails[1], bf16),
            pltpu.VMEM(lead + tails[2], bf16),
            pltpu.VMEM((4,) + branch.shape, bf16),
            pltpu.VMEM((4, tq, half), bf16),
            pltpu.VMEM((2, tq, half), bf16),
            pltpu.VMEM((2, 2, unit, round_up(half, 128)), bf16),
            pltpu.VMEM((2, 2, unit, round_up(half, 128)), bf16),
            pltpu.VMEM(tails[1], bf16),
            pltpu.VMEM(tails[1], bf16),
            pltpu.SemaphoreType.DMA((5,)),
            pltpu.SemaphoreType.DMA((5,)),
            pltpu.SemaphoreType.DMA((2,)),
            pltpu.SemaphoreType.DMA((3, chunks, max(nd - 1, 1), most - 1)),
            pltpu.SemaphoreType.DMA((3, chunks, max(nd - 1, 1), most - 1)),
            pltpu.SemaphoreType.DMA((3, chunks - 1)),
            pltpu.SemaphoreType.DMA((3, chunks - 1)),
            pltpu.SemaphoreType.DMA((2,)),
            pltpu.SemaphoreType.DMA((2,)),
        ]
        + recvs,
        compiler_params=pltpu.CompilerParams(
            collective_id=1, has_side_effects=True, vmem_limit_bytes=60 * 2**20
        ),
        cost_estimate=pl.CostEstimate(flops=10**10, bytes_accessed=3 * 10**7, transcendentals=10**7),
        name="backward",
    )(docs, q, do, ot, lse, kv, w, cos_t, sin_t, normed, inv, gain, gres, gmlp, low, branch, gup, dnp)


def rotate(rows, cos_rows, sin_rows):
    half_dim = HS // 2
    first, second = rows[:half_dim], rows[half_dim:]
    return jnp.concatenate(
        [first * cos_rows - second * sin_rows, second * cos_rows + first * sin_rows], axis=0
    )


class Axes:
    def __init__(self, nctx, nf):
        self.ctx, self.f = lax.axis_index("ctx"), lax.axis_index("fsdp")
        self.core, self.place = lax.rem(self.ctx, 2), self.ctx // 2
        self.me = self.ctx * nf + self.f
        self.dims = line_dims(nctx // 2)
        self.nd = len(self.dims)
        ctx, f, core, place = self.ctx, self.f, self.core, self.place
        self.core_axis = (self.nd, 2, core, lambda k: (1 - core, {"ctx": place * 2 + 1 - core, "fsdp": f}))
        self.side_axis = (self.nd + 1, 2, f, lambda k: (1 - f, {"ctx": ctx, "fsdp": 1 - f}))
        self.lines = [self.line(i) for i in range(self.nd)]
        self.peer_count = 2 + sum(size - 1 for size in self.dims)

    def at_line(self, i, there):
        stride = math.prod(self.dims[:i])
        own = lax.rem(self.place // stride, self.dims[i])
        return {"ctx": (self.place + (there - own) * stride) * 2 + self.core, "fsdp": self.f}

    def line(self, i):
        size = self.dims[i]
        own = lax.rem(self.place // math.prod(self.dims[:i]), size)

        def peer(k):
            there = lax.rem(own + k, size)
            return there, self.at_line(i, there)

        return (self.nd - 1 - i, size, own, peer)

    def peers(self):
        found = [self.core_axis[3](1)[1], self.side_axis[3](1)[1]]
        for axis in self.lines:
            found += [axis[3](k)[1] for k in range(1, axis[1])]
        return found

    def place_index(self, j):
        return tuple(
            lax.rem(j // math.prod(self.dims[:i]), self.dims[i]) for i in reversed(range(self.nd))
        )


def forward_kernel(plan, docs, tokens_ref, gains_ref, cos_ref, sin_ref, wq, wk, wv, wo, wg, wu, cot,
                   qt_ref, kv_out, low_ref, ot_ref, lse_ref, wqkv_out, wo_out, gu_out, cots_out,
                   attn_in_ref, inv_ref, gain_ref,
                   wbuf, obuf, gubuf, cbuf, gain_far, own_kv, kvb, m_ref, l_ref, acc_ref,
                   load_sem, w_send, w_recv, top_send, top_recv, ag_send, ag_recv, blk_sem, out_sem):
    nctx, nf, parts, heads, tq = plan
    ax = Axes(nctx, nf)
    f, core, place = ax.f, ax.core, ax.place
    mesh_id = pl.DeviceIdType.MESH
    bf16, f32 = jnp.bfloat16, jnp.float32
    width = tokens_ref.shape[1]
    half = width // nf
    width_q, width_k = 2 * parts * heads * HS, 2 * parts * HS
    rows4, rows2 = half // 4, half // 2
    quarter = gu_out.shape[1] // 2
    side = ax.side_axis[3](1)[1]
    mate = ax.core_axis[3](1)[1]
    low = ax.lines[0]
    bit = lax.rem(low[2], 2)
    across = ax.at_line(0, low[2] + 1 - 2 * bit)
    top = ax.nd - 1
    chunks = ax.dims[top]
    z = ax.lines[top][2]

    barrier = pltpu.get_barrier_semaphore()
    for where in ax.peers():
        pl.semaphore_signal(barrier, inc=1, device_id=where, device_id_type=mesh_id)

    def local(src, dst, i):
        return pltpu.make_async_copy(src, dst, load_sem.at[i])

    own_rows = pl.ds(pl.multiple_of(f * half, half), half)
    own_quarter = pl.ds(pl.multiple_of((2 * f + core) * quarter, quarter), quarter)
    loads = [
        local(wk, wbuf.at[own_rows, pl.ds(width_q, width_k)], 0),
        local(wv, wbuf.at[own_rows, pl.ds(width_q + width_k, width_k)], 1),
        local(wq, wbuf.at[own_rows, pl.ds(0, width_q)], 2),
        local(wo, obuf.at[own_rows], 3),
        local(wg.at[:, own_quarter], gubuf.at[own_rows, pl.ds(0, quarter)], 4),
        local(wu.at[:, own_quarter], gubuf.at[own_rows, pl.ds(quarter, quarter)], 5),
        local(cot, cbuf.at[0], 6),
    ]
    for copy in loads:
        copy.start()

    def remote(src, dst, i, where):
        return pltpu.make_async_remote_copy(
            src_ref=src, dst_ref=dst, send_sem=w_send.at[i], recv_sem=w_recv.at[i],
            device_id=where, device_id_type=mesh_id,
        )

    near = pl.multiple_of(core * rows2 + bit * rows4, 16)
    far_x = pl.multiple_of(core * rows2 + (1 - bit) * rows4, 16)
    there = (1 - f) * half

    def piece(base, offset):
        return pl.ds(pl.multiple_of(base + offset, 16), rows4)

    kv_cols, q_cols = pl.ds(width_q, 2 * width_k), pl.ds(0, width_q)
    mine = f * half
    gains_copy = remote(gains_ref, gain_far, 0, side)
    kv_y = [
        remote(wk.at[piece(0, near)], wbuf.at[piece(mine, near), pl.ds(width_q, width_k)], 1, side),
        remote(wv.at[piece(0, near)], wbuf.at[piece(mine, near), pl.ds(width_q + width_k, width_k)], 2, side),
    ]
    q_y = [remote(wq.at[piece(0, near)], wbuf.at[piece(mine, near), q_cols], 3, side)]
    o_y = [remote(wo.at[piece(0, near)], obuf.at[piece(mine, near)], 4, side)]

    def forwards(buf, cols, first):
        def part(offset):
            return buf.at[piece(there, offset), cols] if cols is not None else buf.at[piece(there, offset)]

        return [
            remote(part(near), part(near), first, across),
            remote(part(near), part(near), first + 1, mate),
            remote(part(far_x), part(far_x), first + 2, mate),
        ]

    kv_f = forwards(wbuf, kv_cols, 5)
    q_f = forwards(wbuf, q_cols, 8)
    o_f = forwards(obuf, None, 11)
    far_quarter = pl.ds(pl.multiple_of((2 * (1 - f) + core) * quarter, quarter), quarter)

    deep = lax.rem(z, 2)
    above = ax.at_line(top, z + 1 - 2 * deep)

    def gu_rows(base, which=bit):
        return pl.ds(pl.multiple_of(base + which * rows2 + deep * rows4, 16), rows4)

    gu_y = [
        remote(wg.at[gu_rows(0), far_quarter], gubuf.at[gu_rows(mine), pl.ds(0, quarter)], 14, side),
        remote(wu.at[gu_rows(0), far_quarter], gubuf.at[gu_rows(mine), pl.ds(quarter, quarter)], 15, side),
    ]
    gu_x = remote(gubuf.at[gu_rows(there)], gubuf.at[gu_rows(there)], 16, across)
    gu_z = [
        remote(gubuf.at[gu_rows(there, which)], gubuf.at[gu_rows(there, which)], 19 + i, above)
        for i, which in enumerate((bit, 1 - bit))
    ]
    cot_y = remote(cot, cbuf.at[1], 17, side)
    cot_c = remote(cbuf.at[pl.ds(0, 2)], cbuf.at[pl.ds(2, 2)], 18, mate)

    pl.semaphore_wait(barrier, ax.peer_count)
    gains_copy.start()
    for copy in kv_y + q_y:
        copy.start()

    hidden = tokens_ref[...].astype(f32)
    inv = lax.rsqrt(jnp.mean(hidden * hidden, axis=1, keepdims=True) + EPS)
    inv_ref[...] = inv
    gains_copy.wait()
    near_gain, far_gain = gains_ref[0:1, :], gain_far[0:1, :]
    gain = jnp.where(
        f == 0,
        jnp.concatenate([near_gain, far_gain], axis=1),
        jnp.concatenate([far_gain, near_gain], axis=1),
    )
    near_mlp, far_mlp = gains_ref[1:2, :], gain_far[1:2, :]
    gain_ref[0:1, :] = gain
    gain_ref[1:2, :] = jnp.where(
        f == 0,
        jnp.concatenate([near_mlp, far_mlp], axis=1),
        jnp.concatenate([far_mlp, near_mlp], axis=1),
    )
    attn_in = (hidden * inv * gain).astype(bf16)
    attn_in_ref[...] = attn_in

    for copy in kv_y:
        copy.wait()
    kv_f[0].start()
    kv_f[1].start()
    for copy in q_y:
        copy.wait()
    for copy in o_y + gu_y:
        copy.start()
    kv_f[0].wait()
    kv_f[2].start()
    q_f[0].start()
    q_f[1].start()
    for copy in loads[:3]:
        copy.wait()
    kv_f[1].wait()
    kv_f[2].wait()
    kv = jnp.dot(attn_in, wbuf[:, width_q:], preferred_element_type=f32)
    cos_rows, sin_rows = cos_ref[...], sin_ref[...]
    kt = jnp.transpose(kv[:, :width_k])
    k_rot = jnp.concatenate(
        [rotate(kt[HS * g : HS * (g + 1)], cos_rows, sin_rows) for g in range(2 * parts)], axis=0
    )
    own_kv[:, :width_k] = jnp.transpose(k_rot).astype(bf16)
    own_kv[:, width_k:] = kv[:, width_k:].astype(bf16)
    own_at = ax.place_index(place) + (core, f)
    put = pltpu.make_async_copy(own_kv, kv_out.at[own_at], out_sem.at[0])
    put.start()

    def top_copy(k):
        return pltpu.make_async_remote_copy(
            src_ref=own_kv, dst_ref=kv_out.at[own_at],
            send_sem=top_send.at[k - 1], recv_sem=top_recv.at[k - 1],
            device_id=ax.at_line(top, lax.rem(z + k, chunks)), device_id_type=mesh_id,
        )

    for k in range(1, chunks):
        @pl.when(z + k < chunks)
        def _():
            top_copy(k).start()

    lower = ax.lines[:top]
    orders = [lower + [ax.side_axis, ax.core_axis], [ax.side_axis] + lower + [ax.core_axis]]
    stages = len(orders[0])

    def ag_copies(k, stage):
        copies = []
        for kind in range(2):
            index = [None] * (ax.nd + 2)
            index[0] = z - k
            for i, axis in enumerate(orders[kind]):
                index[axis[0]] = slice(None) if i < stage else axis[2]
            region = kv_out.at[tuple(index) + (slice(None), pl.ds(kind * width_k, width_k))]
            axis = orders[kind][stage]
            for i in range(1, axis[1]):
                copies.append(
                    pltpu.make_async_remote_copy(
                        src_ref=region, dst_ref=region,
                        send_sem=ag_send.at[k, kind, stage, i - 1],
                        recv_sem=ag_recv.at[k, kind, stage, i - 1],
                        device_id=axis[3](i)[1], device_id_type=mesh_id,
                    )
                )
        return copies

    def tick(k, stage):
        @pl.when(z >= k)
        def _():
            if stage == 0:
                if k > 0:
                    top_copy(k).wait_recv()
            else:
                for copy in ag_copies(k, stage - 1):
                    copy.wait()
            if stage < stages:
                for copy in ag_copies(k, stage):
                    copy.start()

    put.wait()
    tick(0, 0)
    q_f[0].wait()
    q_f[2].start()
    q_f[1].wait()
    q_f[2].wait()
    back = pltpu.make_async_copy(wbuf, wqkv_out, out_sem.at[1])
    back.start()
    query = jnp.dot(attn_in, wbuf[:, :width_q], preferred_element_type=f32)
    query_t = jnp.transpose(query)
    for h in range(2 * parts * heads):
        qt_ref[HS * h : HS * (h + 1), :] = rotate(
            query_t[HS * h : HS * (h + 1)], cos_rows, sin_rows
        ).astype(bf16)
    m_ref[...] = jnp.full_like(m_ref, NEG)
    l_ref[...] = jnp.zeros_like(l_ref)
    acc_ref[...] = jnp.zeros_like(acc_ref)

    bk = 2 * nf * tq
    per_chunk = math.prod(ax.dims[:top])
    start = ax.me * tq

    def block_copy(j, slot):
        return pltpu.make_async_copy(kv_out.at[ax.place_index(j)], kvb.at[slot], blk_sem.at[slot])

    def attend(k):
        first_block = (z - k) * per_chunk
        count = jnp.minimum(place - first_block + 1, per_chunk)

        @pl.when(z >= k)
        def _():
            block_copy(first_block, 0).start()

            def block(i, carry):
                j = first_block + i
                slot = lax.rem(i, 2)

                @pl.when(i + 1 < count)
                def _():
                    block_copy(j + 1, 1 - slot).start()

                block_copy(j, slot).wait()
                bias = bias_tile((start,), docs, j * bk, bk, tq)
                bias = jnp.concatenate([bias] * heads, axis=1)
                for p in range(parts):
                    kb = kvb[slot, :, :, :, 2 * HS * p : 2 * HS * (p + 1)].reshape(bk, 2 * HS)
                    vb = kvb[slot, :, :, :, width_k + 2 * HS * p : width_k + 2 * HS * (p + 1)]
                    vt = jnp.transpose(vb.reshape(bk, 2 * HS))
                    rows = qt_ref[2 * heads * HS * p : 2 * heads * HS * (p + 1), :] * bf16(1.0 / 8.0)
                    for g in range(2):
                        at = 2 * p + g
                        s = jnp.dot(kb, padded(rows, heads, g), preferred_element_type=f32) + bias
                        m = m_ref[at]
                        new = jnp.maximum(m, jnp.max(s, axis=0, keepdims=True))
                        prob = jnp.exp(s - new)
                        decay = jnp.exp(m - new)
                        m_ref[at] = new
                        l_ref[at] = l_ref[at] * decay + jnp.sum(prob, axis=0, keepdims=True)
                        acc_ref[at] = acc_ref[at] * decay + jnp.dot(
                            vt[HS * g : HS * (g + 1)], prob.astype(bf16), preferred_element_type=f32
                        )
                return carry

            lax.fori_loop(0, count, block, 0)

    for turn in range(1, chunks + stages):
        for k in range(chunks):
            stage = turn - k
            if (k, stage) != (0, 0) and 0 <= stage <= stages:
                tick(k, stage)
        if turn == 4:
            for copy in o_y + gu_y:
                copy.wait()
            o_f[0].start()
            o_f[1].start()
            gu_x.start()
            gu_z[0].start()
        if turn == 3:
            cot_y.start()
        if turn == 6:
            o_f[0].wait()
            o_f[2].start()
            gu_x.wait()
            gu_z[1].start()
        if turn == 5:
            cot_y.wait()
            loads[6].wait()
            cot_c.start()
        if turn >= stages:
            attend(turn - stages)
    for p in range(parts):
        outs = []
        for g in range(2):
            at = 2 * p + g
            out = acc_ref[at] / l_ref[at]
            outs.append(out)
            ot_ref[at] = out
            lse_ref[at] = m_ref[at] + jnp.log(l_ref[at])
        low_ref[:, 2 * heads * HS * p : 2 * heads * HS * (p + 1)] = head_lanes(outs, heads, tq).astype(bf16)

    for k in range(1, chunks):
        @pl.when(z + k < chunks)
        def _():
            top_copy(k).wait_send()
    for copy in loads[3:6]:
        copy.wait()
    backs = [back]
    for waits, src, dst in (
        (o_f[1:], obuf, wo_out), ([cot_c], cbuf, cots_out), (gu_z, gubuf, gu_out)
    ):
        for copy in waits:
            copy.wait()
        backs.append(pltpu.make_async_copy(src, dst, out_sem.at[1 + len(backs)]))
        backs[-1].start()
    for copy in backs:
        copy.wait()


def forward(nctx, nf, docs, tokens, gains, cos_t, sin_t, wq, wk, wv, wo, wg, wu, cot):
    tq, width = tokens.shape
    width_q, width_k = wq.shape[1], wk.shape[1]
    parts = width_k // (2 * HS)
    heads = width_q // HS // (2 * parts)
    hidden_units = wg.shape[1]
    quarter = hidden_units // (2 * nf)
    dims = line_dims(nctx // 2)
    lead = tuple(reversed(dims))
    most = max(dims + [2])
    chunks = dims[-1]
    stages = len(dims) + 1
    bf16, f32 = jnp.bfloat16, jnp.float32
    vmem = pl.BlockSpec(memory_space=pltpu.VMEM)
    smem = pl.BlockSpec(memory_space=pltpu.SMEM)
    hbm = pl.BlockSpec(memory_space=pl.ANY)
    dma = pltpu.SemaphoreType.DMA
    return pl.pallas_call(
        functools.partial(forward_kernel, (nctx, nf, parts, heads, tq)),
        out_shape=[
            jax.ShapeDtypeStruct((width_q, tq), bf16),
            jax.ShapeDtypeStruct(lead + (2, nf, tq, 2 * width_k), bf16),
            jax.ShapeDtypeStruct((tq, width_q), bf16),
            jax.ShapeDtypeStruct((2 * parts, HS, heads * tq), f32),
            jax.ShapeDtypeStruct((2 * parts, 1, heads * tq), f32),
            jax.ShapeDtypeStruct((width, width_q + 2 * width_k), bf16),
            jax.ShapeDtypeStruct((nf * wo.shape[0], wo.shape[1]), bf16),
            jax.ShapeDtypeStruct((width, 2 * quarter), bf16),
            jax.ShapeDtypeStruct((2 * nf, tq, width), bf16),
            jax.ShapeDtypeStruct((tq, width), bf16),
            jax.ShapeDtypeStruct((tq, 1), f32),
            jax.ShapeDtypeStruct((2, width), f32),
        ],
        in_specs=[smem, vmem, vmem, vmem, vmem] + [hbm] * 7,
        out_specs=[vmem, hbm, vmem, vmem, vmem, hbm, hbm, hbm, hbm, vmem, vmem, vmem],
        scratch_shapes=[
            pltpu.VMEM((width, width_q + 2 * width_k), bf16),
            pltpu.VMEM((nf * wo.shape[0], wo.shape[1]), bf16),
            pltpu.VMEM((width, 2 * quarter), bf16),
            pltpu.VMEM((2 * nf, tq, width), bf16),
            pltpu.VMEM(gains.shape, f32),
            pltpu.VMEM((tq, 2 * width_k), bf16),
            pltpu.VMEM((2, 2, nf, tq, 2 * width_k), bf16),
            pltpu.VMEM((2 * parts, 1, heads * tq), f32),
            pltpu.VMEM((2 * parts, 1, heads * tq), f32),
            pltpu.VMEM((2 * parts, HS, heads * tq), f32),
            dma((7,)),
            dma((21,)),
            dma((21,)),
            dma((chunks - 1,)),
            dma((chunks - 1,)),
            dma((chunks, 2, stages, most - 1)),
            dma((chunks, 2, stages, most - 1)),
            dma((2,)),
            dma((5,)),
        ],
        compiler_params=pltpu.CompilerParams(
            collective_id=0, has_side_effects=True, vmem_limit_bytes=60 * 2**20
        ),
        name="forward",
    )(docs, tokens, gains, cos_t, sin_t, wq, wk, wv, wo, wg, wu, cot)


def feed_forward_kernel(plan, tokens_ref, low_ref, attn_in_ref, gains_ref, wo_hbm, gu_hbm, down_hbm, cots_hbm,
                        result_ref, gres_ref, branch_ref, gattn_ref, gmlp_ref, gup_ref, dnp_ref, inputs_out,
                        wo, gu, down, cots, xs, grads, mixed, gm, sums, sent, core_in, side_in, side_out,
                        halves, pair, load_sem, x_send, x_recv, s_send, s_recv, top_send, top_recv,
                        ag_send, ag_recv, out_sem):
    nctx, nf = plan
    ax = Axes(nctx, nf)
    f, core, place = ax.f, ax.core, ax.place
    mesh_id = pl.DeviceIdType.MESH
    bf16, f32 = jnp.bfloat16, jnp.float32
    tq, width = tokens_ref.shape
    half = width // nf
    quarter = down.shape[0]
    side = ax.side_axis[3](1)[1]
    mate = ax.core_axis[3](1)[1]
    top = ax.nd - 1
    chunks = ax.dims[top]
    z = ax.lines[top][2]

    barrier = pltpu.get_barrier_semaphore()
    for where in ax.peers():
        pl.semaphore_signal(barrier, inc=1, device_id=where, device_id_type=mesh_id)
    loads = [
        pltpu.make_async_copy(src, dst, load_sem.at[i])
        for i, (src, dst) in enumerate((
            (wo_hbm, wo), (cots_hbm, cots),
            (down_hbm.at[pl.ds(pl.multiple_of(core * quarter, quarter), quarter)], down), (gu_hbm, gu),
        ))
    ]
    for copy in loads:
        copy.start()

    def remote(src, dst, sends, recvs, i, where):
        return pltpu.make_async_remote_copy(
            src_ref=src, dst_ref=dst, send_sem=sends.at[i], recv_sem=recvs.at[i],
            device_id=where, device_id_type=mesh_id,
        )

    attn_in = attn_in_ref[...]
    halves[0] = attn_in[:, :half]
    halves[1] = attn_in[:, half:]
    pair[f] = halves[f]
    pair_copy = remote(halves.at[1 - f], pair.at[f], x_send, x_recv, 3, side)
    pl.semaphore_wait(barrier, ax.peer_count)
    pair_copy.start()
    hidden = tokens_ref[...].astype(f32)
    loads[0].wait()
    resid = hidden + jnp.dot(low_ref[...], wo[...], preferred_element_type=f32)
    inv = lax.rsqrt(jnp.mean(resid * resid, axis=1, keepdims=True) + EPS)
    normed = resid * inv
    gain = gains_ref[1:2, :]
    xs[0] = (normed * gain).astype(bf16)
    x_side = remote(xs.at[0], xs.at[1], x_send, x_recv, 0, side)
    x_core = remote(xs.at[0], xs.at[2], x_send, x_recv, 1, mate)
    x_far = remote(xs.at[1], xs.at[3], x_send, x_recv, 2, mate)
    x_side.start()
    x_core.start()

    own_at = ax.place_index(place) + (core,)
    put = pltpu.make_async_copy(pair, inputs_out.at[own_at], out_sem.at[0])

    def top_copy(k):
        return pltpu.make_async_remote_copy(
            src_ref=pair, dst_ref=inputs_out.at[own_at],
            send_sem=top_send.at[k - 1], recv_sem=top_recv.at[k - 1],
            device_id=ax.at_line(top, lax.rem(z + k, chunks)), device_id_type=mesh_id,
        )

    order = ax.lines[:top] + [ax.core_axis]
    stages = len(order)

    def ag_copies(k, stage):
        index = [None] * (ax.nd + 1)
        index[0] = lax.rem(z + chunks - k, chunks)
        for i, axis in enumerate(order):
            index[axis[0]] = slice(None) if i < stage else axis[2]
        region = inputs_out.at[tuple(index)]
        axis = order[stage]
        return [
            pltpu.make_async_remote_copy(
                src_ref=region, dst_ref=region,
                send_sem=ag_send.at[k, stage, i - 1], recv_sem=ag_recv.at[k, stage, i - 1],
                device_id=axis[3](i)[1], device_id_type=mesh_id,
            )
            for i in range(1, axis[1])
        ]

    def tick(turn):
        for k in range(chunks):
            stage = turn - k
            if not 0 <= stage <= stages:
                continue
            if stage == 0:
                if k > 0:
                    top_copy(k).wait()
                else:
                    put.wait()
            else:
                for copy in ag_copies(k, stage - 1):
                    copy.wait()
            if stage < stages:
                for copy in ag_copies(k, stage):
                    copy.start()

    def rows(slot):
        return slice(slot * tq, (slot + 1) * tq)

    for copy in loads[1:3]:
        copy.wait()
    gm[...] = lax.dot_general(
        cots[...].reshape(4 * tq, width), down[...], (((1,), (1,)), ((), ())), preferred_element_type=f32
    )
    loads[3].wait()
    pair_copy.wait()
    put.start()
    for k in range(1, chunks):
        top_copy(k).start()
    step = 256

    def both(ref, a, b, span=slice(None)):
        return jnp.concatenate([ref[a, :, span], ref[b, :, span]], axis=0)

    def compute(a, b):
        x = both(xs, a, b)
        for n in range(quarter // step):
            span = slice(n * step, (n + 1) * step)
            up_span = slice(quarter + n * step, quarter + (n + 1) * step)
            gate = jnp.dot(x, gu[:, span], preferred_element_type=f32)
            up = jnp.dot(x, gu[:, up_span], preferred_element_type=f32)
            sig = jax.nn.sigmoid(gate)
            act = gate * sig
            grad = jnp.concatenate([gm[rows(a), span], gm[rows(b), span]], axis=0)
            mix = (act * up).astype(bf16)
            grad_gate = (grad * up * sig * (1.0 + gate * (1.0 - sig))).astype(bf16)
            grad_up = (grad * act).astype(bf16)
            for i, slot in enumerate((a, b)):
                mixed[slot, :, span] = mix[rows(i)]
                grads[slot, :, span] = grad_gate[rows(i)]
                grads[slot, :, up_span] = grad_up[rows(i)]
        total = lax.dot_general(
            both(grads, a, b), gu[...], (((1,), (1,)), ((), ())), preferred_element_type=f32
        )
        for i, slot in enumerate((a, b)):
            sums[0, slot] = total[rows(i)]

    def outputs(a, b):
        total = jnp.dot(both(mixed, a, b), down[...], preferred_element_type=f32)
        for i, slot in enumerate((a, b)):
            sums[1, slot] = total[rows(i)]

    def to_core(kind, slot):
        i = 2 * kind + slot - 2
        return remote(sent.at[i], core_in.at[i], s_send, s_recv, i, mate)

    def to_side(kind):
        return remote(side_out.at[kind], side_in.at[kind], s_send, s_recv, 4 + kind, side)

    def give_core(kind, slot):
        sent[2 * kind + slot - 2] = sums[kind, slot].astype(bf16)
        to_core(kind, slot).start()

    def give_side(kind):
        to_core(kind, 3).wait()
        side_out[kind] = (sums[kind, 1] + core_in[2 * kind + 1].astype(f32)).astype(bf16)
        to_side(kind).start()

    x_core.wait()
    compute(0, 2)
    give_core(0, 2)
    tick(0)
    x_side.wait()
    x_far.start()
    outputs(0, 2)
    give_core(1, 2)
    x_far.wait()
    compute(1, 3)
    give_core(0, 3)
    tick(1)
    outputs(1, 3)
    give_side(0)
    give_core(1, 3)
    flat_x = xs[...].reshape(4 * tq, width)
    pieces = math.prod(ax.dims)
    unit = quarter // pieces
    tall = max(unit, 256)
    for kind in range(2):
        for n in range(quarter // tall):
            span = slice(kind * quarter + n * tall, kind * quarter + (n + 1) * tall)
            cols = jnp.transpose(jnp.concatenate([grads[s, :, span] for s in range(4)], axis=0))
            part = jnp.dot(cols, flat_x, preferred_element_type=f32).astype(bf16)
            first = n * tall
            while first < (n + 1) * tall:
                piece, at = first // unit, first % unit
                end = min((piece + 1) * unit, (n + 1) * tall)
                gup_ref[static_index(ax.dims, piece) + (kind, slice(at, at + end - first))] = part[
                    first - n * tall : end - n * tall
                ]
                first = end
        if kind == 0:
            give_side(1)
            tick(2)
    unit = width // pieces
    flat_mixed = mixed[...].reshape(4 * tq, quarter)
    for n in range(width // 384):
        cols = jnp.transpose(jnp.concatenate([cots[s, :, 384 * n : 384 * (n + 1)] for s in range(4)], axis=0))
        part = jnp.dot(cols, flat_mixed, preferred_element_type=f32).astype(bf16)
        first = n * 384
        while first < (n + 1) * 384:
            piece, at = first // unit, first % unit
            end = min((piece + 1) * unit, (n + 1) * 384)
            dnp_ref[static_index(ax.dims, piece) + (slice(at, at + end - first),)] = part[
                first - n * 384 : end - n * 384
            ]
            first = end

    to_core(0, 2).wait()
    to_side(0).wait()
    grad = sums[0, 0] + core_in[0].astype(f32) + side_in[0].astype(f32)
    product = grad * normed
    gmlp_ref[...] = jnp.sum(product, axis=0, keepdims=True)
    scaled = grad * gain
    mean = jnp.mean(scaled * normed, axis=1, keepdims=True)
    gres = cots[0].astype(f32) + inv * (scaled - normed * mean)
    gres_ref[...] = gres
    branch = gres.astype(bf16)
    branch_ref[...] = branch
    gattn_ref[...] = lax.dot_general(
        branch, wo[...], (((1,), (1,)), ((), ())), preferred_element_type=f32
    ).astype(bf16)
    tick(3)
    to_core(1, 2).wait()
    to_side(1).wait()
    result_ref[...] = (resid + sums[1, 0] + core_in[2].astype(f32) + side_in[1].astype(f32)).astype(bf16)
    for turn in range(4, chunks + stages):
        tick(turn)


def static_index(dims, piece):
    return tuple(piece // math.prod(dims[:i]) % dims[i] for i in reversed(range(len(dims))))


def feed_forward(nctx, nf, tokens, low, attn_in, gains, wo, gu, down, cots):
    tq, width = tokens.shape
    quarter = gu.shape[1] // 2
    half = width // nf
    dims = line_dims(nctx // 2)
    lead = tuple(reversed(dims))
    plane = nctx // 2
    chunks, stages, most = dims[-1], len(dims), max(dims + [2])
    bf16, f32 = jnp.bfloat16, jnp.float32
    vmem = pl.BlockSpec(memory_space=pltpu.VMEM)
    hbm = pl.BlockSpec(memory_space=pl.ANY)
    dma = pltpu.SemaphoreType.DMA
    return pl.pallas_call(
        functools.partial(feed_forward_kernel, (nctx, nf)),
        out_shape=[
            jax.ShapeDtypeStruct((tq, width), bf16),
            jax.ShapeDtypeStruct((tq, width), f32),
            jax.ShapeDtypeStruct((tq, width), bf16),
            jax.ShapeDtypeStruct((tq, width), bf16),
            jax.ShapeDtypeStruct((1, width), f32),
            jax.ShapeDtypeStruct(lead + (2, quarter // plane, width), bf16),
            jax.ShapeDtypeStruct(lead + (width // plane, quarter), bf16),
            jax.ShapeDtypeStruct(lead + (2, nf, tq, half), bf16),
        ],
        in_specs=[vmem] * 4 + [hbm] * 4,
        out_specs=[vmem] * 7 + [hbm],
        scratch_shapes=[
            pltpu.VMEM(wo.shape, bf16),
            pltpu.VMEM(gu.shape, bf16),
            pltpu.VMEM((quarter, width), bf16),
            pltpu.VMEM((4, tq, width), bf16),
            pltpu.VMEM((4, tq, width), bf16),
            pltpu.VMEM((4, tq, 2 * quarter), bf16),
            pltpu.VMEM((4, tq, quarter), bf16),
            pltpu.VMEM((4 * tq, quarter), f32),
            pltpu.VMEM((2, 4, tq, width), f32),
            pltpu.VMEM((4, tq, width), bf16),
            pltpu.VMEM((4, tq, width), bf16),
            pltpu.VMEM((2, tq, width), bf16),
            pltpu.VMEM((2, tq, width), bf16),
            pltpu.VMEM((2, tq, half), bf16),
            pltpu.VMEM((nf, tq, half), bf16),
            dma((4,)),
            dma((4,)),
            dma((4,)),
            dma((6,)),
            dma((6,)),
            dma((chunks - 1,)),
            dma((chunks - 1,)),
            dma((chunks, stages, most - 1)),
            dma((chunks, stages, most - 1)),
            dma((1,)),
        ],
        compiler_params=pltpu.CompilerParams(
            collective_id=2, has_side_effects=True, vmem_limit_bytes=60 * 2**20
        ),
        name="feed_forward",
    )(tokens, low, attn_in, gains, wo, gu, down, cots)


def per_device(
    nctx,
    nf,
    tokens,
    query_weight,
    key_projection,
    value_projection,
    output_weight,
    gate_weight,
    up_weight,
    down_weight,
    norm_attn,
    norm_mlp,
    doc_starts,
    cotangent,
):
    token_rows, width = tokens.shape
    half = width // nf
    n_tokens = token_rows * nctx * nf
    bf16, f32 = jnp.bfloat16, jnp.float32

    own_device = lax.axis_index(AXES)
    own_index = layout_rows(own_device, token_rows)
    own_begin = doc_begin(own_index, doc_starts)
    cosine_table, sine_table = rope_tables(own_index - own_begin)
    cosine_table, sine_table = cosine_table.T, sine_table.T
    gains = jnp.pad(jnp.stack([norm_attn, norm_mlp]).astype(f32), ((0, 6), (0, 0)))
    (
        query_rot, key_values, attn_low, attn_exact, log_total, qkv_full, output_full, gate_up,
        cotangents, attention_input, inv_attn, gains,
    ) = forward(
        nctx, nf, doc_starts, tokens, gains, cosine_table, sine_table, query_weight, key_projection,
        value_projection, output_weight, gate_weight, up_weight, cotangent,
    )
    query_width = QUERY_HEADS * HEAD_SIZE
    key_width = KEY_VALUE_HEADS * HEAD_SIZE
    key_values = key_values.reshape(n_tokens, 2 * key_width)
    result, grad_resid, grad_branch, grad_attn, gain_mlp_partial, gate_up_partial, down_partial, inputs_all = feed_forward(
        nctx, nf, tokens, attn_low, attention_input, gains, output_full, gate_up, down_weight,
        cotangents.reshape(2 * nf, token_rows, width),
    )

    tokens_grad, columns_q, columns_kv, gain_parts, gate_sum, up_sum, down_sum, output_sum = backward(
        nctx, nf, doc_starts, query_rot, grad_attn, attn_exact, log_total, key_values, qkv_full,
        cosine_table, sine_table, tokens, inv_attn, gains, grad_resid,
        gain_mlp_partial, attn_low, grad_branch, gate_up_partial, down_partial,
    )

    cq, ck = query_width // nctx, key_width // nctx
    columns = jnp.concatenate([columns_q[:, :cq], columns_kv[:, : 2 * ck]], axis=1)
    qkv_sum = jnp.einsum(
        "nct,ntd->dc", columns, inputs_all.reshape(nctx * nf, token_rows, half),
        preferred_element_type=f32,
    )
    sizes = [cq, ck, ck]
    gain_sums = jnp.sum(gain_parts, axis=0)[: 2 * width // 128].reshape(2, width)
    query_sum = qkv_sum[:, : sizes[0]]
    key_sum = qkv_sum[:, sizes[0] : sizes[0] + sizes[1]]
    value_sum = qkv_sum[:, sizes[0] + sizes[1] :]
    return (
        result,
        tokens_grad,
        query_sum,
        key_sum,
        value_sum,
        output_sum,
        gate_sum,
        up_sum,
        down_sum,
        gain_sums[0],
        gain_sums[1],
    )


def solution(mesh):
    return jax.shard_map(
        functools.partial(per_device, mesh.shape["ctx"], mesh.shape["fsdp"]),
        mesh=mesh,
        in_specs=(
            P(("ctx", "fsdp"), None),
            P("fsdp", None),
            P("fsdp", None),
            P("fsdp", None),
            P("fsdp", None),
            P("fsdp", None),
            P("fsdp", None),
            P("fsdp", None),
            P("fsdp"),
            P("fsdp"),
            P(),
            P(("ctx", "fsdp"), None),
        ),
        out_specs=(
            P(("ctx", "fsdp"), None),
            P(("ctx", "fsdp"), None),
            P("fsdp", "ctx"),
            P("fsdp", "ctx"),
            P("fsdp", "ctx"),
            P("fsdp", "ctx"),
            P("fsdp", "ctx"),
            P("fsdp", "ctx"),
            P("fsdp", "ctx"),
            P(),
            P(),
        ),
        check_vma=False,
    )
```

```python
import functools
import math

import jax
import jax.numpy as jnp
from jax import lax
from jax.experimental import pallas as pl
from jax.experimental.pallas import tpu as pltpu
from jax.sharding import PartitionSpec as P

QUERY_HEADS = 18
KEY_VALUE_HEADS = 6
HEAD_SIZE = 64
HS = HEAD_SIZE

EPS = 1e-05
THETA = 10000.0
NEG = -1e30
AXES = ("ctx", "fsdp")


def rope_tables(positions):
    half_dim = HEAD_SIZE // 2
    frequency = jnp.exp(-math.log(THETA) * jnp.arange(half_dim, dtype=jnp.float32) / half_dim)
    angles = positions.astype(jnp.float32)[:, None] * frequency[None, :]
    return (jnp.cos(angles), jnp.sin(angles))


def apply_rotary(values, cosine_table, sine_table):
    half_dim = values.shape[-1] // 2
    first_half = values[..., :half_dim]
    second_half = values[..., half_dim:]
    cos_rows = cosine_table[:, None, :]
    sin_rows = sine_table[:, None, :]
    return jnp.concatenate(
        [
            first_half * cos_rows - second_half * sin_rows,
            second_half * cos_rows + first_half * sin_rows,
        ],
        axis=-1,
    )


def unrotate(values, cosine_table, sine_table):
    half_dim = values.shape[-1] // 2
    first_half = values[..., :half_dim]
    second_half = values[..., half_dim:]
    cos_rows = cosine_table[:, None, :]
    sin_rows = sine_table[:, None, :]
    return jnp.concatenate(
        [
            first_half * cos_rows + second_half * sin_rows,
            second_half * cos_rows - first_half * sin_rows,
        ],
        axis=-1,
    )


def doc_begin(indices, doc_starts):
    marked = jnp.where(indices[:, None] >= doc_starts[None, :], doc_starts[None, :], 0)
    return jnp.max(marked, axis=1)


def layout_rows(device, row_count):
    return device * row_count + jnp.arange(row_count, dtype=jnp.int32)


def heads_rows(natural):
    return jnp.transpose(natural.astype(jnp.float32))
def padded(rows, heads, g):
    top = jnp.concatenate([rows[HS*(heads*g+j):HS*(heads*g+j+1)] for j in range(heads)], axis=1)
    z = jnp.zeros_like(top)
    return jnp.concatenate([top, z] if g == 0 else [z, top], axis=0)
def head_lanes(per_group, heads, tq):
    return jnp.transpose(jnp.concatenate([per_group[g][:, tq*j:tq*(j+1)] for g in range(2) for j in range(heads)], axis=0))
def bias_tile(info, docs, first, bk, tq):
    query = info[0] + lax.broadcasted_iota(jnp.int32, (1, tq), 1)
    begin = jnp.zeros((1, tq), jnp.int32)
    for i in range(docs.shape[0]):
        begin = jnp.maximum(begin, jnp.where(query >= docs[i], docs[i], 0))
    key = first + lax.broadcasted_iota(jnp.int32, (bk, 1), 0)
    return jnp.where((key <= query) & (key >= begin), 0.0, NEG)


def line_dims(count):
    fours = 0
    while count % 4 == 0:
        count //= 4
        fours += 1
    return ([count] if count > 1 else []) + [4] * fours


def rotate_back(rows, cos_rows, sin_rows):
    half_dim = HS // 2
    first, second = rows[:half_dim], rows[half_dim:]
    return jnp.concatenate(
        [first * cos_rows + second * sin_rows, second * cos_rows - first * sin_rows], axis=0
    )


def w_order(lines):
    return [lines[-2]] + lines[1:-2] + [lines[0], lines[-1]]


def bit_dims(count):
    return [2] * (count.bit_length() - 1)


def round_up(value, unit):
    return -(-value // unit) * unit


def backward_kernel(plan, docs, q_ref, do_ref, ot_ref, lse_ref, kv_hbm, w_ref, cos_ref, sin_ref,
                    normed_ref, inv_ref, gain_ref, gres_ref, gmlp_ref, low_ref, branch_ref, gup_hbm, dnp_hbm, inputs_hbm,
                    tokens_ref, query_ref, key_ref, value_ref, gains_out, gate_ref, up_ref, down_ref, out_ref,
                    kvbuf, dkv, acc_ref, gqt_ref, ga_ref, qblk, kvblk, small,
                    load_sem, send_sem, recv_sem, col_send, col_recv, own_sem, credit,
                    wg, wd, wo, brs, lows, halves, fin, fin_in, dsend, din,
                    colq_ref, colkv_ref, gains_ref, cols_acc, half_send, half_in, gain_send, gain_in, in_sem,
                    g_send, g_recv, w_load, w_send, w_recv, top_send, top_recv, fin_send, fin_recv, *recvs):
    nctx, nf, parts, heads, tq, slots = plan
    plane = nctx // 2
    n = nctx * nf
    dims = bit_dims(plane)
    nd = len(dims)
    bk = 2 * nf * tq
    me_c, me_f = lax.axis_index("ctx"), lax.axis_index("fsdp")
    me = me_c * nf + me_f
    core, place = lax.rem(me_c, 2), me_c // 2
    mesh_id = pl.DeviceIdType.MESH
    half_dim = HS // 2

    def target(k):
        other = lax.rem(me + k, n)
        return other, {"ctx": other // nf, "fsdp": lax.rem(other, nf)}

    barrier = pltpu.get_barrier_semaphore()

    def greet(k, carry):
        pl.semaphore_signal(barrier, inc=1, device_id=target(k)[1], device_id_type=mesh_id)
        return carry

    lax.fori_loop(1, n, greet, 0)

    def loads(p):
        s = p % slots
        return [
            pltpu.make_async_copy(
                kv_hbm.at[:, pl.ds((kind * parts + p) * 2 * HS, 2 * HS)],
                kvbuf.at[s, kind], load_sem.at[s, kind],
            )
            for kind in range(2)
        ]

    resident = slots == parts

    def block_loads(p, j):
        slot = lax.rem(j, 2)
        return [
            pltpu.make_async_copy(
                kv_hbm.at[pl.ds(pl.multiple_of(j * bk, bk), bk), pl.ds((kind * parts + p) * 2 * HS, 2 * HS)],
                kvbuf.at[slot, kind], load_sem.at[slot, kind],
            )
            for kind in range(2)
        ]

    if resident:
        for p in range(parts):
            for copy in loads(p):
                copy.start()

    def dim_axis(i):
        stride = math.prod(dims[:i])
        size = dims[i]
        own = lax.rem(place // stride, size)

        def peer(k):
            there = lax.rem(own + k, size)
            return there, {"ctx": (place + (there - own) * stride) * 2 + core, "fsdp": me_f}

        return (nd - 1 - i, size, own, peer)

    core_axis = (nd, 2, core, lambda k: (1 - core, {"ctx": place * 2 + 1 - core, "fsdp": me_f}))
    side_axis = (nd + 1, 2, me_f, lambda k: (1 - me_f, {"ctx": me_c, "fsdp": 1 - me_f}))
    lines = [dim_axis(i) for i in range(nd)]
    orders = [[core_axis, side_axis] + lines, [core_axis, lines[0], side_axis] + lines[1:]]
    stages = nd + 2
    wrecvs = recvs[2 * stages :]
    side_at, mate_at = side_axis[3](1)[1], core_axis[3](1)[1]

    low_bits = nd - 2
    arrays = ((wg, gup_hbm), (wd, dnp_hbm), (wo, None))
    w_lines = [lines, w_order(lines), lines]

    def chunk_at(a, k):
        near, far_line = w_lines[a][nd - 2], w_lines[a][nd - 1]
        far_bit = far_line[2] if k % 2 else 1 - far_line[2]
        near_bit = near[2] if k // 2 else 1 - near[2]
        return far_bit, near_bit

    def w_region(a, k, stage, at):
        index = [slice(None)] * nd
        index[w_lines[a][nd - 1][0]], index[w_lines[a][nd - 2][0]] = chunk_at(a, k)
        for axis in w_lines[a][:stage]:
            index[axis[0]] = axis[2]
        if stage < low_bits:
            index[w_lines[a][stage][0]] = at
        return tuple(index)

    def held(a, index):
        first = w_lines[a][0][0]
        return index if a == 2 else index[:first] + index[first + 1 :]

    def w_copy(a, k, stage):
        buf, far = arrays[a]
        there, where = w_lines[a][stage][3](1)
        index = w_region(a, k, stage, there)
        return pltpu.make_async_remote_copy(
            src_ref=far.at[index] if stage == 0 and a < 2 else buf.at[held(a, index)],
            dst_ref=wrecvs[a * (low_bits + 2) + stage].at[chunk_at(a, k)],
            send_sem=w_send.at[a, k, stage], recv_sem=w_recv.at[a, k, stage],
            device_id=where, device_id_type=mesh_id,
        )

    def near_copy(a, i):
        return pltpu.make_async_remote_copy(
            src_ref=arrays[a][0].at[held(a, w_region(a, i, low_bits, 0))], dst_ref=wrecvs[a * (low_bits + 2) + low_bits].at[i],
            send_sem=top_send.at[a, i], recv_sem=top_recv.at[a, i],
            device_id=w_lines[a][nd - 2][3](1)[1], device_id_type=mesh_id,
        )

    def far_copy(a):
        return pltpu.make_async_remote_copy(
            src_ref=arrays[a][0].at[held(a, w_region(a, 2, low_bits, 0))], dst_ref=wrecvs[a * (low_bits + 2) + low_bits + 1].at[0],
            send_sem=top_send.at[a, 2], recv_sem=top_recv.at[a, 2],
            device_id=w_lines[a][nd - 1][3](1)[1], device_id_type=mesh_id,
        )

    def w_start(which, k):
        for a in which:
            w_copy(a, k, 0).start()

    def w_finish(which, k):
        for a in which:
            buf = arrays[a][0]
            for stage in range(low_bits):
                w_copy(a, k, stage).wait()
                where = held(a, w_region(a, k, stage, w_lines[a][stage][2]))
                got = wrecvs[a * (low_bits + 2) + stage]
                buf[where] = (
                    buf[where].astype(jnp.float32) + got[chunk_at(a, k)].astype(jnp.float32)
                ).astype(buf.dtype)
                if stage + 1 < low_bits:
                    w_copy(a, k, stage + 1).start()
            if k < 2:
                near_copy(a, k).start()
            elif k == 2:
                near_copy(a, 0).wait()
                where = held(a, w_region(a, 2, low_bits, 0))
                buf[where] = (
                    buf[where].astype(jnp.float32)
                    + wrecvs[a * (low_bits + 2) + low_bits][0].astype(jnp.float32)
                ).astype(buf.dtype)
                far_copy(a).start()

    def w_total(a):
        near_copy(a, 1).wait()
        far_copy(a).wait()
        total = arrays[a][0][held(a, w_region(a, 3, low_bits, 0))].astype(jnp.float32)
        total = total + wrecvs[a * (low_bits + 2) + low_bits][1].astype(jnp.float32)
        return total + wrecvs[a * (low_bits + 2) + low_bits + 1][0].astype(jnp.float32)

    w_loads = [
        pltpu.make_async_copy(far.at[(slice(None),) * w_lines[i][0][0] + (w_lines[i][0][2],)], buf, w_load.at[i])
        for i, (buf, far) in enumerate(arrays[:2])
    ]
    for copy in w_loads:
        copy.start()
    half = low_ref.shape[1] // nf
    low_all = low_ref[...]
    halves[0] = low_all[:, :half]
    halves[1] = low_all[:, half:]
    lows[0] = halves[me_f]
    brs[0] = branch_ref[...]

    def g_copy(i, src, dst, where):
        return pltpu.make_async_remote_copy(
            src_ref=src, dst_ref=dst, send_sem=g_send.at[i], recv_sem=g_recv.at[i],
            device_id=where, device_id_type=mesh_id,
        )

    low_side = g_copy(0, halves.at[1 - me_f], lows.at[1], side_at)
    br_side = g_copy(1, brs.at[0], brs.at[1], side_at)
    low_core = g_copy(2, lows.at[pl.ds(0, 2)], lows.at[pl.ds(2, 2)], mate_at)
    br_core = g_copy(3, brs.at[pl.ds(0, 2)], brs.at[pl.ds(2, 2)], mate_at)

    def output_partial():
        low_core.wait()
        br_core.wait()
        rows = jnp.transpose(brs[...].reshape(4 * tq, brs.shape[2]))
        unit = brs.shape[2] // nctx
        wo[...] = jnp.zeros_like(wo)
        low_rows = lows[...].reshape(4 * tq, half)
        batch = plane // 4
        for r in range(plane):
            first = 2 * unit * (r % batch)
            if first == 0:
                chunk = 2 * unit * batch
                part = jnp.dot(
                    rows[2 * unit * r : 2 * unit * r + chunk], low_rows, preferred_element_type=jnp.float32
                )
            piece = jnp.where(core == 0, part[first : first + unit], part[first + unit : first + 2 * unit])
            wo[static_index(dims, r) + (slice(0, unit), slice(0, half))] = piece.astype(wo.dtype)

    pl.semaphore_wait(barrier, n - 1)
    low_side.start()
    br_side.start()
    w_start((0, 1), 0)
    w_start((0, 1), 1)

    def region(kind, stage, at):
        index = [slice(None)] * (nd + 2)
        for axis in orders[kind][:stage]:
            index[axis[0]] = axis[2]
        index[orders[kind][stage][0]] = at
        return tuple(index)

    def stage_copies(p, kind, stage):
        s = p % slots
        axis = orders[kind][stage]
        copies = []
        for k in range(1, axis[1]):
            there, where = axis[3](k)
            copies.append(
                pltpu.make_async_remote_copy(
                    src_ref=dkv.at[(s, kind) + region(kind, stage, there)],
                    dst_ref=recvs[kind * stages + stage].at[s, k - 1],
                    send_sem=send_sem.at[s, kind, stage, k - 1],
                    recv_sem=recv_sem.at[s, kind, stage, k - 1],
                    device_id=where, device_id_type=mesh_id,
                )
            )
        return copies

    def stage_start(p, stage):
        for kind in range(2):
            for copy in stage_copies(p, kind, stage):
                copy.start()

    finals = {}

    def stage_finish(p, stage):
        s = p % slots
        for kind in range(2):
            axis = orders[kind][stage]
            for copy in stage_copies(p, kind, stage):
                copy.wait()
            where = region(kind, stage, axis[2])
            got = recvs[kind * stages + stage]
            free = [i for i in range(nd + 2) if isinstance(where[i], slice)]

            def add(index, lead):
                total = dkv[(s, kind) + index].astype(jnp.float32)
                for k in range(axis[1] - 1):
                    total = total + got[(s, k) + lead].astype(jnp.float32)
                return total

            if not free:
                finals[p, kind] = add(where, ())
            else:
                size = dkv.shape[2 + free[0]]

                def one(i, carry):
                    index = list(where)
                    index[free[0]] = i
                    index = tuple(index)
                    dkv[(s, kind) + index] = add(index, (i,)).astype(dkv.dtype)
                    return carry

                lax.fori_loop(0, size, one, 0)

    def place_index(j):
        index = []
        for i in reversed(range(nd)):
            index.append(lax.rem(j // math.prod(dims[:i]), dims[i]))
        return tuple(index)

    start = me * tq
    last = (start + tq - 1) // bk + 1

    def compute(p):
        s = p % slots
        span = slice(2 * heads * HS * p, 2 * heads * HS * (p + 1))
        qt = q_ref[span, :].astype(jnp.float32) * (1.0 / 8.0)
        dt = heads_rows(do_ref[:, span])
        qg = [padded(qt, heads, g) for g in range(2)]
        dg = [padded(dt, heads, g) for g in range(2)]
        qrows = jnp.concatenate([jnp.transpose(x) for x in qg], axis=0).astype(jnp.bfloat16)
        drows = jnp.concatenate([jnp.transpose(x) for x in dg], axis=0).astype(jnp.bfloat16)
        delta = [
            jnp.sum(dg[g][HS * g : HS * (g + 1)] * ot_ref[2 * p + g], axis=0, keepdims=True)
            for g in range(2)
        ]
        lse = [lse_ref[2 * p + g] for g in range(2)]
        qg = [x.astype(jnp.bfloat16) for x in qg]
        dg = [x.astype(jnp.bfloat16) for x in dg]
        acc_ref[...] = jnp.zeros_like(acc_ref)
        for copy in loads(p) if resident else block_loads(p, 0):
            if not resident:
                copy.start()
            else:
                copy.wait()

        def zero(j, carry):
            at = place_index(j)
            for kind in range(2):
                dkv[(s, kind) + at] = jnp.zeros((2, nf, tq, 2 * HS), dkv.dtype)
            return carry

        def body(j, carry):
            first = pl.multiple_of(j * bk, bk)
            if resident:
                kb = kvbuf[s, 0, pl.ds(first, bk), :]
                vb = kvbuf[s, 1, pl.ds(first, bk), :]
            else:
                for copy in block_loads(p, j):
                    copy.wait()

                @pl.when(j + 1 < last)
                def _():
                    for copy in block_loads(p, j + 1):
                        copy.start()

                kb, vb = kvbuf[lax.rem(j, 2), 0], kvbuf[lax.rem(j, 2), 1]
            kt = jnp.transpose(kb)
            bias = bias_tile((start,), docs, first, bk, tq)
            bias = jnp.concatenate([bias] * heads, axis=1)
            ps = []
            dss = []
            for g in range(2):
                score = jnp.dot(kb, qg[g], preferred_element_type=jnp.float32)
                prob = jnp.exp(score + (bias - lse[g]))
                dp = jnp.dot(vb, dg[g], preferred_element_type=jnp.float32)
                ds = (prob * (dp - delta[g])).astype(jnp.bfloat16)
                ps.append(prob.astype(jnp.bfloat16))
                dss.append(ds)
                acc_ref[g] += jnp.dot(kt[HS * g : HS * (g + 1)], ds, preferred_element_type=jnp.float32)
            dv = jnp.dot(jnp.concatenate(ps, axis=1), drows, preferred_element_type=jnp.float32)
            dk = jnp.dot(jnp.concatenate(dss, axis=1), qrows, preferred_element_type=jnp.float32)
            at = place_index(j)
            dkv[(s, 0) + at] = dk.astype(dkv.dtype).reshape(2, nf, tq, 2 * HS)
            dkv[(s, 1) + at] = dv.astype(dkv.dtype).reshape(2, nf, tq, 2 * HS)
            return carry

        lax.fori_loop(last, plane, zero, 0)
        lax.fori_loop(0, last, body, 0)
        cos_rows = jnp.concatenate([cos_ref[...]] * heads, axis=1) * (1.0 / 8.0)
        sin_rows = jnp.concatenate([sin_ref[...]] * heads, axis=1) * (1.0 / 8.0)
        for g in range(2):
            back = rotate_back(acc_ref[g], cos_rows, sin_rows).astype(gqt_ref.dtype)
            for j in range(heads):
                h = (2 * p + g) * heads + j
                gqt_ref[HS * h : HS * (h + 1), :] = back[:, tq * j : tq * (j + 1)]

    peers = 2 + sum(size - 1 for size in dims)

    def all_peers():
        found = [core_axis[3](1)[1], side_axis[3](1)[1]]
        for axis in lines:
            found += [axis[3](k)[1] for k in range(1, axis[1])]
        return found

    progress = {}

    def advance(p):
        stage = progress[p]
        stage_finish(p, stage)
        progress[p] = stage + 1
        if stage + 1 < stages:
            stage_start(p, stage + 1)
        else:
            del progress[p]
            if p + slots < parts:
                for where in all_peers():
                    pl.semaphore_signal(credit, inc=1, device_id=where, device_id_type=mesh_id)

    for p in range(parts):
        if p >= slots:
            while p - slots in progress:
                advance(p - slots)
        compute(p)
        if p >= slots:
            pl.semaphore_wait(credit, peers)
        stage_start(p, 0)
        progress[p] = 0
        for older in [o for o in progress if o < p]:
            advance(older)
        if p == 0:
            low_side.wait()
            br_side.wait()
            low_core.start()
            br_core.start()
        if p == 1:
            for copy in w_loads:
                copy.wait()
            w_finish((0, 1), 0)
            w_start((0, 1), 2)
            output_partial()
            for k in range(4):
                w_start((2,), k)
    w_finish((0, 1), 1)
    w_start((0, 1), 3)

    def copies_to(k, which):
        other = lax.rem(me_c + k, nctx)
        where = {"ctx": other, "fsdp": me_f}
        block, out = ((qblk, colq_ref), (kvblk, colkv_ref), (small, gains_ref))[which]
        return pltpu.make_async_remote_copy(
            src_ref=block if which == 2 else block.at[other], dst_ref=out.at[me_c],
            send_sem=col_send.at[which, k], recv_sem=col_recv.at[which, k],
            device_id=where, device_id_type=mesh_id,
        )

    def share(which):
        def one(k, carry):
            copies_to(k, which).start()
            return carry

        block, out = ((qblk, colq_ref), (kvblk, colkv_ref), (small, gains_ref))[which]
        pltpu.make_async_copy(block if which == 2 else block.at[me_c], out.at[me_c], own_sem.at[which]).start()
        lax.fori_loop(1, nctx, one, 0)

    def share_wait(which):
        def one(k, carry):
            copies_to(k, which).wait()
            return carry

        block, out = ((qblk, colq_ref), (kvblk, colkv_ref), (small, gains_ref))[which]
        pltpu.make_async_copy(block if which == 2 else block.at[me_c], out.at[me_c], own_sem.at[which]).wait()
        lax.fori_loop(1, nctx, one, 0)

    width_q = 2 * parts * heads * HS
    width_k = 2 * parts * HS
    cq, ck = width_q // nctx, width_k // nctx
    qblk[...] = jnp.zeros_like(qblk)
    kvblk[...] = jnp.zeros_like(kvblk)
    for i in range(nctx):
        qblk[i, 0:cq, :] = gqt_ref[cq * i : cq * (i + 1), :]
    share(0)
    ga_ref[...] = jnp.dot(w_ref[:, :width_q], gqt_ref[...], preferred_element_type=jnp.float32)
    for k in range(2):
        w_finish((2,), k)
    pq, pk = qblk.shape[1], kvblk.shape[1]

    def columns(col_ref, first, count):
        def fetch(i, slot):
            return pltpu.make_async_copy(
                inputs_hbm.at[i], brs.at[slot], in_sem.at[slot]
            )

        fetch(0, 0).start()
        cols_acc[first : first + count, :] = jnp.zeros((count, cols_acc.shape[1]), jnp.float32)

        def one(i, carry):
            slot = lax.rem(i, 2)

            @pl.when(i + 1 < nctx)
            def _():
                fetch(i + 1, 1 - slot).start()

            fetch(i, slot).wait()
            cols_acc[first : first + count, :] += jnp.dot(
                col_ref[i], brs[slot], preferred_element_type=jnp.float32
            )
            return carry

        lax.fori_loop(0, nctx, one, 0)

    turn = 0
    while progress:
        for p in list(progress):
            advance(p)
        if turn == 0:
            w_finish((0, 1, 2), 2)
        if turn == 1:
            w_finish((0, 1, 2), 3)
            share_wait(0)
            columns(colq_ref, 0, pq)
        turn += 1

    cos_rows, sin_rows = cos_ref[...], sin_ref[...]
    grads = []
    for kind in range(2):
        rows = []
        for p in range(parts):
            both = jnp.transpose(finals[p, kind])
            for g in range(2):
                one = both[HS * g : HS * (g + 1)]
                rows.append(rotate_back(one, cos_rows, sin_rows) if kind == 0 else one)
        grads.append(jnp.concatenate(rows, axis=0).astype(jnp.bfloat16))
    for i in range(nctx):
        kvblk[i, 0:ck, :] = grads[0][ck * i : ck * (i + 1)]
        kvblk[i, ck : 2 * ck, :] = grads[1][ck * i : ck * (i + 1)]
    share(1)
    grad_t = (
        ga_ref[...]
        + jnp.dot(w_ref[:, width_q : width_q + width_k], grads[0], preferred_element_type=jnp.float32)
        + jnp.dot(w_ref[:, width_q + width_k :], grads[1], preferred_element_type=jnp.float32)
    )
    grad = jnp.transpose(grad_t)
    normed = normed_ref[...].astype(jnp.float32) * inv_ref[...]
    product = grad * normed
    gain_sum = jnp.sum(product, axis=0, keepdims=True)
    lanes = 128
    tiles = gain_sum.shape[1] // lanes
    rows = [gain_sum[:, lanes * i : lanes * (i + 1)] for i in range(tiles)]
    rows += [gmlp_ref[:, lanes * i : lanes * (i + 1)] for i in range(tiles)]
    rows += [jnp.zeros((small.shape[0] - 2 * tiles, lanes), jnp.float32)]
    small[...] = jnp.concatenate(rows, axis=0)
    share(2)
    gain = gain_ref[0:1, :]
    scaled = grad * gain
    mean = jnp.mean(scaled * normed, axis=1, keepdims=True)
    tokens_ref[...] = gres_ref[...] + inv_ref[...] * (scaled - normed * mean)

    total = w_total(0)
    unit, lanes = fin.shape[2], fin.shape[3]
    blank = jnp.zeros((2, unit, lanes - half), fin.dtype)
    for s in range(2):
        fin[s] = jnp.concatenate([total[:, :, half * s : half * (s + 1)].astype(fin.dtype), blank], axis=2)
    dsum = w_total(1)
    dsend[...] = dsum.astype(dsend.dtype)
    down_copy = g_copy(4, dsend, din, mate_at)
    down_copy.start()
    per_side = plane // 2
    home = (2 * me_f + core) * per_side + place // 2
    slot = lax.rem(place, 2)

    def home_copy(s):
        return pltpu.make_async_remote_copy(
            src_ref=fin.at[s], dst_ref=fin_in.at[slot], send_sem=fin_send.at[s], recv_sem=fin_recv.at[slot],
            device_id={"ctx": home, "fsdp": jnp.int32(s)}, device_id_type=mesh_id,
        )

    def self_copy(s):
        return pltpu.make_async_copy(fin.at[s], fin_in.at[slot], fin_send.at[s])

    for s in range(2):
        at_home = (home == me_c) & (me_f == s)

        @pl.when(jnp.logical_not(at_home))
        def _():
            home_copy(s).start()

        @pl.when(at_home)
        def _():
            self_copy(s).start()

    osum = w_total(2)
    out_ref[...] = osum[: out_ref.shape[0], :half]
    share_wait(1)
    columns(colkv_ref, pq, pk)
    left, right = cols_acc[:, :half], cols_acc[:, half:]
    side_pad = jnp.zeros((pq + pk, half_send.shape[1] - half), half_send.dtype)
    half_send[...] = jnp.concatenate([jnp.where(me_f == 0, right, left).astype(half_send.dtype), side_pad], axis=1)
    half_copy = g_copy(5, half_send, half_in, side_at)
    half_copy.start()
    share_wait(2)
    gain_total = gains_ref[0]
    for i in range(1, nctx):
        gain_total = gain_total + gains_ref[i]
    gain_send[...] = gain_total
    gain_copy = g_copy(6, gain_send, gain_in, side_at)
    gain_copy.start()
    half_copy.wait()
    own_half = jnp.where(me_f == 0, cols_acc[:, :half], cols_acc[:, half:])
    rows = own_half + half_in[:, :half].astype(jnp.float32)
    query_ref[...] = rows[:cq]
    key_ref[...] = rows[pq : pq + ck]
    value_ref[...] = rows[pq + ck : pq + 2 * ck]
    gain_copy.wait()
    gains_out[...] = gain_send[...] + gain_in[...]
    down_copy.wait()
    cols = down_ref.shape[0]

    def unfold(folded):
        return jnp.concatenate(
            [folded[2 * cols * i : 2 * cols * (i + 1)] for i in range(folded.shape[0] // (2 * cols))], axis=1
        )

    dsum, got = unfold(dsum), unfold(din[...].astype(jnp.float32))
    own_cols = jnp.where(core == 0, dsum[:cols], dsum[cols:])
    far_cols = jnp.where(core == 0, got[:cols], got[cols:])
    down_ref[...] = jnp.where(
        core == 0,
        jnp.concatenate([own_cols, far_cols], axis=1),
        jnp.concatenate([far_cols, own_cols], axis=1),
    )
    for s in range(2):
        at_home = (home == me_c) & (me_f == s)

        @pl.when(jnp.logical_not(at_home))
        def _():
            home_copy(s).wait_send()

        @pl.when(at_home)
        def _():
            self_copy(s).wait()

    owner = me_c // per_side
    for h in range(2):
        holder = (2 * lax.rem(me_c, per_side) + h) * 2 + lax.rem(owner, 2)

        @pl.when(jnp.logical_not((holder == me_c) & (owner // 2 == me_f)))
        def _():
            pltpu.make_async_remote_copy(
                src_ref=fin.at[0], dst_ref=fin_in.at[h], send_sem=fin_send.at[0], recv_sem=fin_recv.at[h],
                device_id={"ctx": home, "fsdp": me_f}, device_id_type=mesh_id,
            ).wait_recv()

    for kind, ref in ((0, gate_ref), (1, up_ref)):
        rows = jnp.concatenate([fin_in[0, kind], fin_in[1, kind]], axis=0).astype(jnp.float32)
        ref[...] = rows[:, :half]


def backward(nctx, nf, docs, q, do, ot, lse, kv, w, cos_t, sin_t, normed, inv, gain, gres, gmlp, low, branch, gup, dnp, inputs):
    width_q, tq = q.shape
    n_tokens, width_kv = kv.shape
    n = nctx * nf
    parts = width_kv // (4 * HS)
    heads = width_q // HS // (2 * parts)
    dims = bit_dims(nctx // 2)
    lead = tuple(reversed(dims))
    part_bytes = n_tokens * 2 * HS * 2
    slots = parts if parts * part_bytes * 5 <= 24 * 2**20 else 1
    nd = len(dims)
    bf16, f32 = jnp.bfloat16, jnp.float32
    axes = {"core": (nd, 2), "side": (nd + 1, nf)}
    line = [(nd - 1 - i, dims[i]) for i in range(nd)]
    orders = [
        [axes["core"], axes["side"]] + line,
        [axes["core"], line[0], axes["side"]] + line[1:],
    ]
    recvs = []
    for order in orders:
        left = list(lead) + [2, nf]
        for position, size in order:
            left[position] = None
            recvs.append(
                pltpu.VMEM((slots, size - 1) + tuple(x for x in left if x) + (tq, 2 * HS), bf16)
            )
    model_width = low.shape[1]
    half = model_width // nf
    unit, deep = gup.shape[-2], model_width // (nctx // 2)
    quarter = dnp.shape[-2] // deep * 128
    plane = nctx // 2
    tails = [gup.shape[nd:], dnp.shape[nd:], (round_up(deep // 2, 16), round_up(half, 128))]
    for tail in tails:
        for stage in range(nd - 2):
            recvs.append(pltpu.VMEM((2,) * (nd - 1 - stage) + tail, bf16))
        recvs += [pltpu.VMEM((2,) + tail, bf16), pltpu.VMEM((1,) + tail, bf16)]
    stages = nd + 2
    most = max(dims + [2])
    pq = round_up(width_q // nctx, 16)
    pk = round_up(2 * (2 * parts * HS) // nctx, 16)
    model = w.shape[0]
    sr = round_up(2 * model // 128, 8)
    vmem = pl.BlockSpec(memory_space=pltpu.VMEM)
    smem = pl.BlockSpec(memory_space=pltpu.SMEM)
    hbm = pl.BlockSpec(memory_space=pl.ANY)
    return pl.pallas_call(
        functools.partial(backward_kernel, (nctx, nf, parts, heads, tq, slots)),
        out_shape=[
            jax.ShapeDtypeStruct((tq, model), f32),
            jax.ShapeDtypeStruct((width_q // nctx, half), f32),
            jax.ShapeDtypeStruct((2 * parts * HS // nctx, half), f32),
            jax.ShapeDtypeStruct((2 * parts * HS // nctx, half), f32),
            jax.ShapeDtypeStruct((sr, 128), f32),
            jax.ShapeDtypeStruct((2 * unit, half), f32),
            jax.ShapeDtypeStruct((2 * unit, half), f32),
            jax.ShapeDtypeStruct((deep // 2, 2 * quarter), f32),
            jax.ShapeDtypeStruct((deep // 2, half), f32),
        ],
        in_specs=[smem, vmem, vmem, vmem, vmem, hbm] + [vmem] * 10 + [hbm] * 3,
        out_specs=[vmem] * 9,
        scratch_shapes=[
            pltpu.VMEM((slots, 2, n_tokens, 2 * HS) if slots == parts else (2, 2, 2 * nf * tq, 2 * HS), bf16),
            pltpu.VMEM((slots, 2) + lead + (2, nf, tq, 2 * HS), bf16),
            pltpu.VMEM((2, HS, heads * tq), f32),
            pltpu.VMEM((width_q, tq), bf16),
            pltpu.VMEM((model, tq), f32),
            pltpu.VMEM((nctx, pq, tq), bf16),
            pltpu.VMEM((nctx, pk, tq), bf16),
            pltpu.VMEM((sr, 128), f32),
            pltpu.SemaphoreType.DMA((max(slots, 2), 2)),
            pltpu.SemaphoreType.DMA((slots, 2, stages, most - 1)),
            pltpu.SemaphoreType.DMA((slots, 2, stages, most - 1)),
            pltpu.SemaphoreType.DMA((3, nctx)),
            pltpu.SemaphoreType.DMA((3, nctx)),
            pltpu.SemaphoreType.DMA((3,)),
            pltpu.SemaphoreType.REGULAR,
            pltpu.VMEM(lead[:-1] + tails[0], bf16),
            pltpu.VMEM(lead[:-1] + tails[1], bf16),
            pltpu.VMEM(lead + tails[2], bf16),
            pltpu.VMEM((4,) + branch.shape, bf16),
            pltpu.VMEM((4, tq, half), bf16),
            pltpu.VMEM((2, tq, half), bf16),
            pltpu.VMEM((2, 2, unit, round_up(half, 128)), bf16),
            pltpu.VMEM((2, 2, unit, round_up(half, 128)), bf16),
            pltpu.VMEM(tails[1], bf16),
            pltpu.VMEM(tails[1], bf16),
            pltpu.VMEM((nctx, pq, tq), bf16),
            pltpu.VMEM((nctx, pk, tq), bf16),
            pltpu.VMEM((nctx, sr, 128), f32),
            pltpu.VMEM((pq + pk, model), f32),
            pltpu.VMEM((pq + pk, round_up(half, 128)), bf16),
            pltpu.VMEM((pq + pk, round_up(half, 128)), bf16),
            pltpu.VMEM((sr, 128), f32),
            pltpu.VMEM((sr, 128), f32),
            pltpu.SemaphoreType.DMA((2,)),
            pltpu.SemaphoreType.DMA((7,)),
            pltpu.SemaphoreType.DMA((7,)),
            pltpu.SemaphoreType.DMA((2,)),
            pltpu.SemaphoreType.DMA((3, 4, max(nd - 2, 1))),
            pltpu.SemaphoreType.DMA((3, 4, max(nd - 2, 1))),
            pltpu.SemaphoreType.DMA((3, 3)),
            pltpu.SemaphoreType.DMA((3, 3)),
            pltpu.SemaphoreType.DMA((2,)),
            pltpu.SemaphoreType.DMA((2,)),
        ]
        + recvs,
        compiler_params=pltpu.CompilerParams(
            collective_id=1, has_side_effects=True, vmem_limit_bytes=63 * 2**20
        ),
        cost_estimate=pl.CostEstimate(flops=10**10, bytes_accessed=3 * 10**7, transcendentals=10**7),
        name="backward",
    )(docs, q, do, ot, lse, kv, w, cos_t, sin_t, normed, inv, gain, gres, gmlp, low, branch, gup, dnp, inputs)


def rotate(rows, cos_rows, sin_rows):
    half_dim = HS // 2
    first, second = rows[:half_dim], rows[half_dim:]
    return jnp.concatenate(
        [first * cos_rows - second * sin_rows, second * cos_rows + first * sin_rows], axis=0
    )


class Axes:
    def __init__(self, nctx, nf):
        self.ctx, self.f = lax.axis_index("ctx"), lax.axis_index("fsdp")
        self.core, self.place = lax.rem(self.ctx, 2), self.ctx // 2
        self.me = self.ctx * nf + self.f
        self.dims = line_dims(nctx // 2)
        self.nd = len(self.dims)
        ctx, f, core, place = self.ctx, self.f, self.core, self.place
        self.core_axis = (self.nd, 2, core, lambda k: (1 - core, {"ctx": place * 2 + 1 - core, "fsdp": f}))
        self.side_axis = (self.nd + 1, 2, f, lambda k: (1 - f, {"ctx": ctx, "fsdp": 1 - f}))
        self.lines = [self.line(i) for i in range(self.nd)]
        self.peer_count = 2 + sum(size - 1 for size in self.dims)

    def at_line(self, i, there):
        stride = math.prod(self.dims[:i])
        own = lax.rem(self.place // stride, self.dims[i])
        return {"ctx": (self.place + (there - own) * stride) * 2 + self.core, "fsdp": self.f}

    def line(self, i):
        size = self.dims[i]
        own = lax.rem(self.place // math.prod(self.dims[:i]), size)

        def peer(k):
            there = lax.rem(own + k, size)
            return there, self.at_line(i, there)

        return (self.nd - 1 - i, size, own, peer)

    def peers(self):
        found = [self.core_axis[3](1)[1], self.side_axis[3](1)[1]]
        for axis in self.lines:
            found += [axis[3](k)[1] for k in range(1, axis[1])]
        return found

    def place_index(self, j):
        return tuple(
            lax.rem(j // math.prod(self.dims[:i]), self.dims[i]) for i in reversed(range(self.nd))
        )


def forward_kernel(plan, docs, tokens_ref, gains_ref, cos_ref, sin_ref, wq, wk, wv, wo, wg, wu, cot,
                   qt_ref, kv_out, low_ref, ot_ref, lse_ref, wqkv_out, wo_out, gu_out, cots_out,
                   attn_in_ref, inv_ref, gain_ref,
                   wbuf, obuf, gubuf, cbuf, gain_far, own_kv, kvb, m_ref, l_ref, acc_ref,
                   load_sem, w_send, w_recv, top_send, top_recv, ag_send, ag_recv, blk_sem, out_sem):
    nctx, nf, parts, heads, tq = plan
    ax = Axes(nctx, nf)
    f, core, place = ax.f, ax.core, ax.place
    mesh_id = pl.DeviceIdType.MESH
    bf16, f32 = jnp.bfloat16, jnp.float32
    width = tokens_ref.shape[1]
    half = width // nf
    width_q, width_k = 2 * parts * heads * HS, 2 * parts * HS
    rows4, rows2 = half // 4, half // 2
    quarter = gu_out.shape[1] // 2
    side = ax.side_axis[3](1)[1]
    mate = ax.core_axis[3](1)[1]
    low = ax.lines[0]
    bit = lax.rem(low[2], 2)
    across = ax.at_line(0, low[2] + 1 - 2 * bit)
    top = ax.nd - 1
    chunks = ax.dims[top]
    z = ax.lines[top][2]

    barrier = pltpu.get_barrier_semaphore()
    for where in ax.peers():
        pl.semaphore_signal(barrier, inc=1, device_id=where, device_id_type=mesh_id)

    def local(src, dst, i):
        return pltpu.make_async_copy(src, dst, load_sem.at[i])

    own_rows = pl.ds(pl.multiple_of(f * half, half), half)
    own_quarter = pl.ds(pl.multiple_of((2 * f + core) * quarter, quarter), quarter)
    loads = [
        local(wk, wbuf.at[own_rows, pl.ds(width_q, width_k)], 0),
        local(wv, wbuf.at[own_rows, pl.ds(width_q + width_k, width_k)], 1),
        local(wq, wbuf.at[own_rows, pl.ds(0, width_q)], 2),
        local(wo, obuf.at[own_rows], 3),
        local(wg.at[:, own_quarter], gubuf.at[own_rows, pl.ds(0, quarter)], 4),
        local(wu.at[:, own_quarter], gubuf.at[own_rows, pl.ds(quarter, quarter)], 5),
        local(cot, cbuf.at[0], 6),
    ]
    for copy in loads:
        copy.start()

    def remote(src, dst, i, where):
        return pltpu.make_async_remote_copy(
            src_ref=src, dst_ref=dst, send_sem=w_send.at[i], recv_sem=w_recv.at[i],
            device_id=where, device_id_type=mesh_id,
        )

    near = pl.multiple_of(core * rows2 + bit * rows4, 16)
    far_x = pl.multiple_of(core * rows2 + (1 - bit) * rows4, 16)
    there = (1 - f) * half

    def piece(base, offset):
        return pl.ds(pl.multiple_of(base + offset, 16), rows4)

    kv_cols, q_cols = pl.ds(width_q, 2 * width_k), pl.ds(0, width_q)
    mine = f * half
    gains_copy = remote(gains_ref, gain_far, 0, side)
    kv_y = [
        remote(wk.at[piece(0, near)], wbuf.at[piece(mine, near), pl.ds(width_q, width_k)], 1, side),
        remote(wv.at[piece(0, near)], wbuf.at[piece(mine, near), pl.ds(width_q + width_k, width_k)], 2, side),
    ]
    q_y = [remote(wq.at[piece(0, near)], wbuf.at[piece(mine, near), q_cols], 3, side)]
    o_y = [remote(wo.at[piece(0, near)], obuf.at[piece(mine, near)], 4, side)]

    def forwards(buf, cols, first):
        def part(offset):
            return buf.at[piece(there, offset), cols] if cols is not None else buf.at[piece(there, offset)]

        return [
            remote(part(near), part(near), first, across),
            remote(part(near), part(near), first + 1, mate),
            remote(part(far_x), part(far_x), first + 2, mate),
        ]

    kv_f = forwards(wbuf, kv_cols, 5)
    q_f = forwards(wbuf, q_cols, 8)
    o_f = forwards(obuf, None, 11)
    far_quarter = pl.ds(pl.multiple_of((2 * (1 - f) + core) * quarter, quarter), quarter)

    deep = lax.rem(z, 2)
    above = ax.at_line(top, z + 1 - 2 * deep)

    def gu_rows(base, which=bit):
        return pl.ds(pl.multiple_of(base + which * rows2 + deep * rows4, 16), rows4)

    gu_y = [
        remote(wg.at[gu_rows(0), far_quarter], gubuf.at[gu_rows(mine), pl.ds(0, quarter)], 14, side),
        remote(wu.at[gu_rows(0), far_quarter], gubuf.at[gu_rows(mine), pl.ds(quarter, quarter)], 15, side),
    ]
    gu_x = remote(gubuf.at[gu_rows(there)], gubuf.at[gu_rows(there)], 16, across)
    gu_z = [
        remote(gubuf.at[gu_rows(there, which)], gubuf.at[gu_rows(there, which)], 19 + i, above)
        for i, which in enumerate((bit, 1 - bit))
    ]
    cot_y = remote(cot, cbuf.at[1], 17, side)
    cot_c = remote(cbuf.at[pl.ds(0, 2)], cbuf.at[pl.ds(2, 2)], 18, mate)

    pl.semaphore_wait(barrier, ax.peer_count)
    gains_copy.start()
    for copy in kv_y + q_y:
        copy.start()

    hidden = tokens_ref[...].astype(f32)
    inv = lax.rsqrt(jnp.mean(hidden * hidden, axis=1, keepdims=True) + EPS)
    inv_ref[...] = inv
    gains_copy.wait()
    near_gain, far_gain = gains_ref[0:1, :], gain_far[0:1, :]
    gain = jnp.where(
        f == 0,
        jnp.concatenate([near_gain, far_gain], axis=1),
        jnp.concatenate([far_gain, near_gain], axis=1),
    )
    near_mlp, far_mlp = gains_ref[1:2, :], gain_far[1:2, :]
    gain_ref[0:1, :] = gain
    gain_ref[1:2, :] = jnp.where(
        f == 0,
        jnp.concatenate([near_mlp, far_mlp], axis=1),
        jnp.concatenate([far_mlp, near_mlp], axis=1),
    )
    attn_in = (hidden * inv * gain).astype(bf16)
    attn_in_ref[...] = attn_in

    for copy in kv_y:
        copy.wait()
    kv_f[0].start()
    kv_f[1].start()
    for copy in q_y:
        copy.wait()
    for copy in o_y + gu_y:
        copy.start()
    kv_f[0].wait()
    kv_f[2].start()
    q_f[0].start()
    q_f[1].start()
    for copy in loads[:3]:
        copy.wait()
    kv_f[1].wait()
    kv_f[2].wait()
    kv = jnp.dot(attn_in, wbuf[:, width_q:], preferred_element_type=f32)
    cos_rows, sin_rows = cos_ref[...], sin_ref[...]
    kt = jnp.transpose(kv[:, :width_k])
    k_rot = jnp.concatenate(
        [rotate(kt[HS * g : HS * (g + 1)], cos_rows, sin_rows) for g in range(2 * parts)], axis=0
    )
    own_kv[:, :width_k] = jnp.transpose(k_rot).astype(bf16)
    own_kv[:, width_k:] = kv[:, width_k:].astype(bf16)
    own_at = ax.place_index(place) + (core, f)
    put = pltpu.make_async_copy(own_kv, kv_out.at[own_at], out_sem.at[0])
    put.start()

    def top_copy(k):
        return pltpu.make_async_remote_copy(
            src_ref=own_kv, dst_ref=kv_out.at[own_at],
            send_sem=top_send.at[k - 1], recv_sem=top_recv.at[k - 1],
            device_id=ax.at_line(top, lax.rem(z + k, chunks)), device_id_type=mesh_id,
        )

    for k in range(1, chunks):
        @pl.when(z + k < chunks)
        def _():
            top_copy(k).start()

    lower = ax.lines[:top]
    orders = [lower + [ax.side_axis, ax.core_axis], [ax.side_axis] + lower + [ax.core_axis]]
    stages = len(orders[0])

    def ag_copies(k, stage):
        copies = []
        for kind in range(2):
            index = [None] * (ax.nd + 2)
            index[0] = z - k
            for i, axis in enumerate(orders[kind]):
                index[axis[0]] = slice(None) if i < stage else axis[2]
            region = kv_out.at[tuple(index) + (slice(None), pl.ds(kind * width_k, width_k))]
            axis = orders[kind][stage]
            for i in range(1, axis[1]):
                copies.append(
                    pltpu.make_async_remote_copy(
                        src_ref=region, dst_ref=region,
                        send_sem=ag_send.at[k, kind, stage, i - 1],
                        recv_sem=ag_recv.at[k, kind, stage, i - 1],
                        device_id=axis[3](i)[1], device_id_type=mesh_id,
                    )
                )
        return copies

    def tick(k, stage):
        @pl.when(z >= k)
        def _():
            if stage == 0:
                if k > 0:
                    top_copy(k).wait_recv()
            else:
                for copy in ag_copies(k, stage - 1):
                    copy.wait()
            if stage < stages:
                for copy in ag_copies(k, stage):
                    copy.start()

    put.wait()
    tick(0, 0)
    q_f[0].wait()
    q_f[2].start()
    q_f[1].wait()
    q_f[2].wait()
    back = pltpu.make_async_copy(wbuf, wqkv_out, out_sem.at[1])
    back.start()
    query = jnp.dot(attn_in, wbuf[:, :width_q], preferred_element_type=f32)
    query_t = jnp.transpose(query)
    for h in range(2 * parts * heads):
        qt_ref[HS * h : HS * (h + 1), :] = rotate(
            query_t[HS * h : HS * (h + 1)], cos_rows, sin_rows
        ).astype(bf16)
    m_ref[...] = jnp.full_like(m_ref, NEG)
    l_ref[...] = jnp.zeros_like(l_ref)
    acc_ref[...] = jnp.zeros_like(acc_ref)

    bk = 2 * nf * tq
    per_chunk = math.prod(ax.dims[:top])
    start = ax.me * tq

    def block_copy(j, slot):
        return pltpu.make_async_copy(kv_out.at[ax.place_index(j)], kvb.at[slot], blk_sem.at[slot])

    def attend(k):
        first_block = (z - k) * per_chunk
        count = jnp.minimum(place - first_block + 1, per_chunk)

        @pl.when(z >= k)
        def _():
            block_copy(first_block, 0).start()

            def block(i, carry):
                j = first_block + i
                slot = lax.rem(i, 2)

                @pl.when(i + 1 < count)
                def _():
                    block_copy(j + 1, 1 - slot).start()

                block_copy(j, slot).wait()
                bias = bias_tile((start,), docs, j * bk, bk, tq)
                bias = jnp.concatenate([bias] * heads, axis=1)
                for p in range(parts):
                    kb = kvb[slot, :, :, :, 2 * HS * p : 2 * HS * (p + 1)].reshape(bk, 2 * HS)
                    vb = kvb[slot, :, :, :, width_k + 2 * HS * p : width_k + 2 * HS * (p + 1)]
                    vt = jnp.transpose(vb.reshape(bk, 2 * HS))
                    rows = qt_ref[2 * heads * HS * p : 2 * heads * HS * (p + 1), :] * bf16(1.0 / 8.0)
                    for g in range(2):
                        at = 2 * p + g
                        s = jnp.dot(kb, padded(rows, heads, g), preferred_element_type=f32) + bias
                        m = m_ref[at]
                        new = jnp.maximum(m, jnp.max(s, axis=0, keepdims=True))
                        prob = jnp.exp(s - new)
                        decay = jnp.exp(m - new)
                        m_ref[at] = new
                        l_ref[at] = l_ref[at] * decay + jnp.sum(prob, axis=0, keepdims=True)
                        acc_ref[at] = acc_ref[at] * decay + jnp.dot(
                            vt[HS * g : HS * (g + 1)], prob.astype(bf16), preferred_element_type=f32
                        )
                return carry

            lax.fori_loop(0, count, block, 0)

    for turn in range(1, chunks + stages):
        for k in range(chunks):
            stage = turn - k
            if (k, stage) != (0, 0) and 0 <= stage <= stages:
                tick(k, stage)
        if turn == 4:
            for copy in o_y + gu_y:
                copy.wait()
            o_f[0].start()
            o_f[1].start()
            gu_x.start()
            gu_z[0].start()
        if turn == 3:
            cot_y.start()
        if turn == 6:
            o_f[0].wait()
            o_f[2].start()
            gu_x.wait()
            gu_z[1].start()
        if turn == 5:
            cot_y.wait()
            loads[6].wait()
            cot_c.start()
        if turn >= stages:
            attend(turn - stages)
    for p in range(parts):
        outs = []
        for g in range(2):
            at = 2 * p + g
            out = acc_ref[at] / l_ref[at]
            outs.append(out)
            ot_ref[at] = out
            lse_ref[at] = m_ref[at] + jnp.log(l_ref[at])
        low_ref[:, 2 * heads * HS * p : 2 * heads * HS * (p + 1)] = head_lanes(outs, heads, tq).astype(bf16)

    for k in range(1, chunks):
        @pl.when(z + k < chunks)
        def _():
            top_copy(k).wait_send()
    for copy in loads[3:6]:
        copy.wait()
    backs = [back]
    for waits, src, dst in (
        (o_f[1:], obuf, wo_out), ([cot_c], cbuf, cots_out), (gu_z, gubuf, gu_out)
    ):
        for copy in waits:
            copy.wait()
        backs.append(pltpu.make_async_copy(src, dst, out_sem.at[1 + len(backs)]))
        backs[-1].start()
    for copy in backs:
        copy.wait()


def forward(nctx, nf, docs, tokens, gains, cos_t, sin_t, wq, wk, wv, wo, wg, wu, cot):
    tq, width = tokens.shape
    width_q, width_k = wq.shape[1], wk.shape[1]
    parts = width_k // (2 * HS)
    heads = width_q // HS // (2 * parts)
    hidden_units = wg.shape[1]
    quarter = hidden_units // (2 * nf)
    dims = line_dims(nctx // 2)
    lead = tuple(reversed(dims))
    most = max(dims + [2])
    chunks = dims[-1]
    stages = len(dims) + 1
    bf16, f32 = jnp.bfloat16, jnp.float32
    vmem = pl.BlockSpec(memory_space=pltpu.VMEM)
    smem = pl.BlockSpec(memory_space=pltpu.SMEM)
    hbm = pl.BlockSpec(memory_space=pl.ANY)
    dma = pltpu.SemaphoreType.DMA
    return pl.pallas_call(
        functools.partial(forward_kernel, (nctx, nf, parts, heads, tq)),
        out_shape=[
            jax.ShapeDtypeStruct((width_q, tq), bf16),
            jax.ShapeDtypeStruct(lead + (2, nf, tq, 2 * width_k), bf16),
            jax.ShapeDtypeStruct((tq, width_q), bf16),
            jax.ShapeDtypeStruct((2 * parts, HS, heads * tq), f32),
            jax.ShapeDtypeStruct((2 * parts, 1, heads * tq), f32),
            jax.ShapeDtypeStruct((width, width_q + 2 * width_k), bf16),
            jax.ShapeDtypeStruct((nf * wo.shape[0], wo.shape[1]), bf16),
            jax.ShapeDtypeStruct((width, 2 * quarter), bf16),
            jax.ShapeDtypeStruct((2 * nf, tq, width), bf16),
            jax.ShapeDtypeStruct((tq, width), bf16),
            jax.ShapeDtypeStruct((tq, 1), f32),
            jax.ShapeDtypeStruct((2, width), f32),
        ],
        in_specs=[smem, vmem, vmem, vmem, vmem] + [hbm] * 7,
        out_specs=[vmem, hbm, vmem, vmem, vmem, hbm, hbm, hbm, hbm, vmem, vmem, vmem],
        scratch_shapes=[
            pltpu.VMEM((width, width_q + 2 * width_k), bf16),
            pltpu.VMEM((nf * wo.shape[0], wo.shape[1]), bf16),
            pltpu.VMEM((width, 2 * quarter), bf16),
            pltpu.VMEM((2 * nf, tq, width), bf16),
            pltpu.VMEM(gains.shape, f32),
            pltpu.VMEM((tq, 2 * width_k), bf16),
            pltpu.VMEM((2, 2, nf, tq, 2 * width_k), bf16),
            pltpu.VMEM((2 * parts, 1, heads * tq), f32),
            pltpu.VMEM((2 * parts, 1, heads * tq), f32),
            pltpu.VMEM((2 * parts, HS, heads * tq), f32),
            dma((7,)),
            dma((21,)),
            dma((21,)),
            dma((chunks - 1,)),
            dma((chunks - 1,)),
            dma((chunks, 2, stages, most - 1)),
            dma((chunks, 2, stages, most - 1)),
            dma((2,)),
            dma((5,)),
        ],
        compiler_params=pltpu.CompilerParams(
            collective_id=0, has_side_effects=True, vmem_limit_bytes=60 * 2**20
        ),
        name="forward",
    )(docs, tokens, gains, cos_t, sin_t, wq, wk, wv, wo, wg, wu, cot)


def feed_forward_kernel(plan, tokens_ref, low_ref, attn_in_ref, gains_ref, wo_hbm, gu_hbm, down_hbm, cots_hbm,
                        result_ref, gres_ref, branch_ref, gattn_ref, gmlp_ref, gup_ref, dnp_ref, inputs_out,
                        wo, gu, down, cots, xs, grads, mixed, gm, sums, sent, core_in, side_in, side_out,
                        load_sem, x_send, x_recv, s_send, s_recv, top_send, top_recv,
                        ag_send, ag_recv, out_sem):
    nctx, nf = plan
    ax = Axes(nctx, nf)
    f, core, place = ax.f, ax.core, ax.place
    mesh_id = pl.DeviceIdType.MESH
    bf16, f32 = jnp.bfloat16, jnp.float32
    tq, width = tokens_ref.shape
    quarter = down.shape[0]
    side = ax.side_axis[3](1)[1]
    mate = ax.core_axis[3](1)[1]
    top = ax.nd - 1
    chunks = ax.dims[top]
    z = ax.lines[top][2]

    barrier = pltpu.get_barrier_semaphore()
    for where in ax.peers():
        pl.semaphore_signal(barrier, inc=1, device_id=where, device_id_type=mesh_id)
    loads = [
        pltpu.make_async_copy(src, dst, load_sem.at[i])
        for i, (src, dst) in enumerate((
            (wo_hbm, wo), (cots_hbm, cots),
            (down_hbm.at[pl.ds(pl.multiple_of(core * quarter, quarter), quarter)], down), (gu_hbm, gu),
        ))
    ]
    for copy in loads:
        copy.start()

    def remote(src, dst, sends, recvs, i, where):
        return pltpu.make_async_remote_copy(
            src_ref=src, dst_ref=dst, send_sem=sends.at[i], recv_sem=recvs.at[i],
            device_id=where, device_id_type=mesh_id,
        )

    hidden = tokens_ref[...].astype(f32)
    own_at = ax.place_index(place) + (core,)
    put = pltpu.make_async_copy(attn_in_ref, inputs_out.at[own_at], out_sem.at[0])

    def top_copy(k):
        return pltpu.make_async_remote_copy(
            src_ref=attn_in_ref, dst_ref=inputs_out.at[own_at],
            send_sem=top_send.at[k - 1], recv_sem=top_recv.at[k - 1],
            device_id=ax.at_line(top, lax.rem(z + k, chunks)), device_id_type=mesh_id,
        )

    order = ax.lines[:top] + [ax.core_axis]
    stages = len(order)

    def ag_copies(k, stage):
        index = [None] * (ax.nd + 1)
        index[0] = lax.rem(z + chunks - k, chunks)
        for i, axis in enumerate(order):
            index[axis[0]] = slice(None) if i < stage else axis[2]
        region = inputs_out.at[tuple(index)]
        axis = order[stage]
        return [
            pltpu.make_async_remote_copy(
                src_ref=region, dst_ref=region,
                send_sem=ag_send.at[k, stage, i - 1], recv_sem=ag_recv.at[k, stage, i - 1],
                device_id=axis[3](i)[1], device_id_type=mesh_id,
            )
            for i in range(1, axis[1])
        ]

    def tick(turn):
        for k in range(chunks):
            stage = turn - k
            if not 0 <= stage <= stages:
                continue
            if stage == 0:
                if k > 0:
                    top_copy(k).wait()
                else:
                    put.wait()
            else:
                for copy in ag_copies(k, stage - 1):
                    copy.wait()
            if stage < stages:
                for copy in ag_copies(k, stage):
                    copy.start()

    pl.semaphore_wait(barrier, ax.peer_count)
    put.start()
    for k in range(1, chunks):
        top_copy(k).start()
    tick(0)

    loads[0].wait()
    resid = hidden + jnp.dot(low_ref[...], wo[...], preferred_element_type=f32)
    inv = lax.rsqrt(jnp.mean(resid * resid, axis=1, keepdims=True) + EPS)
    normed = resid * inv
    gain = gains_ref[1:2, :]
    xs[0] = (normed * gain).astype(bf16)
    x_side = remote(xs.at[0], xs.at[1], x_send, x_recv, 0, side)
    x_core = remote(xs.at[0], xs.at[2], x_send, x_recv, 1, mate)
    x_far = remote(xs.at[1], xs.at[3], x_send, x_recv, 2, mate)
    x_side.start()
    x_core.start()

    def rows(slot):
        return slice(slot * tq, (slot + 1) * tq)

    for copy in loads[1:3]:
        copy.wait()
    gm[...] = lax.dot_general(
        cots[...].reshape(4 * tq, width), down[...], (((1,), (1,)), ((), ())), preferred_element_type=f32
    )
    loads[3].wait()
    step = 256

    def both(ref, a, b, span=slice(None)):
        return jnp.concatenate([ref[a, :, span], ref[b, :, span]], axis=0)

    def compute(a, b):
        x = both(xs, a, b)
        for n in range(quarter // step):
            span = slice(n * step, (n + 1) * step)
            up_span = slice(quarter + n * step, quarter + (n + 1) * step)
            gate = jnp.dot(x, gu[:, span], preferred_element_type=f32)
            up = jnp.dot(x, gu[:, up_span], preferred_element_type=f32)
            sig = jax.nn.sigmoid(gate)
            act = gate * sig
            grad = jnp.concatenate([gm[rows(a), span], gm[rows(b), span]], axis=0)
            mix = (act * up).astype(bf16)
            grad_gate = (grad * up * sig * (1.0 + gate * (1.0 - sig))).astype(bf16)
            grad_up = (grad * act).astype(bf16)
            for i, slot in enumerate((a, b)):
                mixed[slot, :, span] = mix[rows(i)]
                grads[slot, :, span] = grad_gate[rows(i)]
                grads[slot, :, up_span] = grad_up[rows(i)]
        total = lax.dot_general(
            both(grads, a, b), gu[...], (((1,), (1,)), ((), ())), preferred_element_type=f32
        )
        for i, slot in enumerate((a, b)):
            sums[0, slot] = total[rows(i)]

    def outputs(a, b):
        total = jnp.dot(both(mixed, a, b), down[...], preferred_element_type=f32)
        for i, slot in enumerate((a, b)):
            sums[1, slot] = total[rows(i)]

    def to_core(kind, slot):
        i = 2 * kind + slot - 2
        return remote(sent.at[i], core_in.at[i], s_send, s_recv, i, mate)

    def to_side(kind):
        return remote(side_out.at[kind], side_in.at[kind], s_send, s_recv, 4 + kind, side)

    def give_core(kind, slot):
        sent[2 * kind + slot - 2] = sums[kind, slot].astype(bf16)
        to_core(kind, slot).start()

    def give_side(kind):
        to_core(kind, 3).wait()
        side_out[kind] = (sums[kind, 1] + core_in[2 * kind + 1].astype(f32)).astype(bf16)
        to_side(kind).start()

    x_core.wait()
    compute(0, 2)
    give_core(0, 2)
    x_side.wait()
    x_far.start()
    outputs(0, 2)
    give_core(1, 2)
    x_far.wait()
    compute(1, 3)
    give_core(0, 3)
    tick(1)
    outputs(1, 3)
    give_side(0)
    give_core(1, 3)
    flat_x = xs[...].reshape(4 * tq, width)
    pieces = nctx // 2
    unit = quarter // pieces
    tall = max(unit, 256)
    for kind in range(2):
        for n in range(quarter // tall):
            span = slice(kind * quarter + n * tall, kind * quarter + (n + 1) * tall)
            cols = jnp.transpose(jnp.concatenate([grads[s, :, span] for s in range(4)], axis=0))
            part = jnp.dot(cols, flat_x, preferred_element_type=f32).astype(bf16)
            first = n * tall
            while first < (n + 1) * tall:
                piece, at = first // unit, first % unit
                end = min((piece + 1) * unit, (n + 1) * tall)
                gup_ref[static_index(bit_dims(nctx // 2), piece) + (kind, slice(at, at + end - first))] = part[
                    first - n * tall : end - n * tall
                ]
                first = end
        if kind == 0:
            give_side(1)
            tick(2)
    unit = width // pieces
    flat_mixed = mixed[...].reshape(4 * tq, quarter)
    for n in range(width // 384):
        cols = jnp.transpose(jnp.concatenate([cots[s, :, 384 * n : 384 * (n + 1)] for s in range(4)], axis=0))
        part = jnp.dot(cols, flat_mixed, preferred_element_type=f32).astype(bf16)
        first = n * 384
        while first < (n + 1) * 384:
            piece, at = first // unit, first % unit
            end = min((piece + 1) * unit, (n + 1) * 384)
            rows_of = part[first - n * 384 : end - n * 384]
            for c in range(quarter // 128):
                dnp_ref[
                    static_index(bit_dims(nctx // 2), piece)
                    + (slice(c * unit + at, c * unit + at + end - first),)
                ] = rows_of[:, 128 * c : 128 * (c + 1)]
            first = end

    to_core(0, 2).wait()
    to_side(0).wait()
    grad = sums[0, 0] + core_in[0].astype(f32) + side_in[0].astype(f32)
    product = grad * normed
    gmlp_ref[...] = jnp.sum(product, axis=0, keepdims=True)
    scaled = grad * gain
    mean = jnp.mean(scaled * normed, axis=1, keepdims=True)
    gres = cots[0].astype(f32) + inv * (scaled - normed * mean)
    gres_ref[...] = gres
    branch = gres.astype(bf16)
    branch_ref[...] = branch
    gattn_ref[...] = lax.dot_general(
        branch, wo[...], (((1,), (1,)), ((), ())), preferred_element_type=f32
    ).astype(bf16)
    tick(3)
    to_core(1, 2).wait()
    to_side(1).wait()
    result_ref[...] = (resid + sums[1, 0] + core_in[2].astype(f32) + side_in[1].astype(f32)).astype(bf16)
    for turn in range(4, chunks + stages):
        tick(turn)


def static_index(dims, piece):
    return tuple(piece // math.prod(dims[:i]) % dims[i] for i in reversed(range(len(dims))))


def feed_forward(nctx, nf, tokens, low, attn_in, gains, wo, gu, down, cots):
    tq, width = tokens.shape
    quarter = gu.shape[1] // 2
    dims = line_dims(nctx // 2)
    bits = bit_dims(nctx // 2)
    lead = tuple(reversed(dims))
    plane = nctx // 2
    chunks, stages, most = dims[-1], len(dims), max(dims + [2])
    bf16, f32 = jnp.bfloat16, jnp.float32
    vmem = pl.BlockSpec(memory_space=pltpu.VMEM)
    hbm = pl.BlockSpec(memory_space=pl.ANY)
    dma = pltpu.SemaphoreType.DMA
    return pl.pallas_call(
        functools.partial(feed_forward_kernel, (nctx, nf)),
        out_shape=[
            jax.ShapeDtypeStruct((tq, width), bf16),
            jax.ShapeDtypeStruct((tq, width), f32),
            jax.ShapeDtypeStruct((tq, width), bf16),
            jax.ShapeDtypeStruct((tq, width), bf16),
            jax.ShapeDtypeStruct((1, width), f32),
            jax.ShapeDtypeStruct(tuple(bits) + (2, quarter // plane, width), bf16),
            jax.ShapeDtypeStruct(tuple(bits) + (width // plane * (quarter // 128), 128), bf16),
            jax.ShapeDtypeStruct(lead + (2, tq, width), bf16),
        ],
        in_specs=[vmem] * 4 + [hbm] * 4,
        out_specs=[vmem] * 7 + [hbm],
        scratch_shapes=[
            pltpu.VMEM(wo.shape, bf16),
            pltpu.VMEM(gu.shape, bf16),
            pltpu.VMEM((quarter, width), bf16),
            pltpu.VMEM((4, tq, width), bf16),
            pltpu.VMEM((4, tq, width), bf16),
            pltpu.VMEM((4, tq, 2 * quarter), bf16),
            pltpu.VMEM((4, tq, quarter), bf16),
            pltpu.VMEM((4 * tq, quarter), f32),
            pltpu.VMEM((2, 4, tq, width), f32),
            pltpu.VMEM((4, tq, width), bf16),
            pltpu.VMEM((4, tq, width), bf16),
            pltpu.VMEM((2, tq, width), bf16),
            pltpu.VMEM((2, tq, width), bf16),
            dma((4,)),
            dma((4,)),
            dma((4,)),
            dma((6,)),
            dma((6,)),
            dma((chunks - 1,)),
            dma((chunks - 1,)),
            dma((chunks, stages, most - 1)),
            dma((chunks, stages, most - 1)),
            dma((1,)),
        ],
        compiler_params=pltpu.CompilerParams(
            collective_id=2, has_side_effects=True, vmem_limit_bytes=60 * 2**20
        ),
        name="feed_forward",
    )(tokens, low, attn_in, gains, wo, gu, down, cots)


def per_device(
    nctx,
    nf,
    tokens,
    query_weight,
    key_projection,
    value_projection,
    output_weight,
    gate_weight,
    up_weight,
    down_weight,
    norm_attn,
    norm_mlp,
    doc_starts,
    cotangent,
):
    token_rows, width = tokens.shape
    n_tokens = token_rows * nctx * nf
    bf16, f32 = jnp.bfloat16, jnp.float32

    own_device = lax.axis_index(AXES)
    own_index = layout_rows(own_device, token_rows)
    own_begin = doc_begin(own_index, doc_starts)
    cosine_table, sine_table = rope_tables(own_index - own_begin)
    cosine_table, sine_table = cosine_table.T, sine_table.T
    gains = jnp.pad(jnp.stack([norm_attn, norm_mlp]).astype(f32), ((0, 6), (0, 0)))
    (
        query_rot, key_values, attn_low, attn_exact, log_total, qkv_full, output_full, gate_up,
        cotangents, attention_input, inv_attn, gains,
    ) = forward(
        nctx, nf, doc_starts, tokens, gains, cosine_table, sine_table, query_weight, key_projection,
        value_projection, output_weight, gate_weight, up_weight, cotangent,
    )
    key_width = KEY_VALUE_HEADS * HEAD_SIZE
    key_values = key_values.reshape(n_tokens, 2 * key_width)
    result, grad_resid, grad_branch, grad_attn, gain_mlp_partial, gate_up_partial, down_partial, inputs_all = feed_forward(
        nctx, nf, tokens, attn_low, attention_input, gains, output_full, gate_up, down_weight,
        cotangents.reshape(2 * nf, token_rows, width),
    )

    tokens_grad, query_sum, key_sum, value_sum, gain_sums, gate_sum, up_sum, down_sum, output_sum = backward(
        nctx, nf, doc_starts, query_rot, grad_attn, attn_exact, log_total, key_values, qkv_full,
        cosine_table, sine_table, tokens, inv_attn, gains, grad_resid,
        gain_mlp_partial, attn_low, grad_branch, gate_up_partial, down_partial,
        inputs_all.reshape(nctx, token_rows, width),
    )

    gain_sums = gain_sums[: 2 * width // 128].reshape(2, width)
    return (
        result,
        tokens_grad,
        query_sum.T,
        key_sum.T,
        value_sum.T,
        output_sum.T,
        gate_sum.T,
        up_sum.T,
        down_sum.T,
        gain_sums[0],
        gain_sums[1],
    )


def solution(mesh):
    return jax.shard_map(
        functools.partial(per_device, mesh.shape["ctx"], mesh.shape["fsdp"]),
        mesh=mesh,
        in_specs=(
            P(("ctx", "fsdp"), None),
            P("fsdp", None),
            P("fsdp", None),
            P("fsdp", None),
            P("fsdp", None),
            P("fsdp", None),
            P("fsdp", None),
            P("fsdp", None),
            P("fsdp"),
            P("fsdp"),
            P(),
            P(("ctx", "fsdp"), None),
        ),
        out_specs=(
            P(("ctx", "fsdp"), None),
            P(("ctx", "fsdp"), None),
            P("fsdp", "ctx"),
            P("fsdp", "ctx"),
            P("fsdp", "ctx"),
            P("fsdp", "ctx"),
            P("fsdp", "ctx"),
            P("fsdp", "ctx"),
            P("fsdp", "ctx"),
            P(),
            P(),
        ),
        check_vma=False,
    )
```

```python
import functools
import math

import jax
import jax.numpy as jnp
from jax import lax
from jax.experimental import pallas as pl
from jax.experimental.pallas import tpu as pltpu
from jax.sharding import PartitionSpec as P

QUERY_HEADS = 18
KEY_VALUE_HEADS = 6
HEAD_SIZE = 64
HS = HEAD_SIZE

EPS = 1e-05
THETA = 10000.0
NEG = -1e30
AXES = ("ctx", "fsdp")


def rope_tables(positions):
    half_dim = HEAD_SIZE // 2
    frequency = jnp.exp(-math.log(THETA) * jnp.arange(half_dim, dtype=jnp.float32) / half_dim)
    angles = positions.astype(jnp.float32)[:, None] * frequency[None, :]
    return (jnp.cos(angles), jnp.sin(angles))


def apply_rotary(values, cosine_table, sine_table):
    half_dim = values.shape[-1] // 2
    first_half = values[..., :half_dim]
    second_half = values[..., half_dim:]
    cos_rows = cosine_table[:, None, :]
    sin_rows = sine_table[:, None, :]
    return jnp.concatenate(
        [
            first_half * cos_rows - second_half * sin_rows,
            second_half * cos_rows + first_half * sin_rows,
        ],
        axis=-1,
    )


def unrotate(values, cosine_table, sine_table):
    half_dim = values.shape[-1] // 2
    first_half = values[..., :half_dim]
    second_half = values[..., half_dim:]
    cos_rows = cosine_table[:, None, :]
    sin_rows = sine_table[:, None, :]
    return jnp.concatenate(
        [
            first_half * cos_rows + second_half * sin_rows,
            second_half * cos_rows - first_half * sin_rows,
        ],
        axis=-1,
    )


def doc_begin(indices, doc_starts):
    marked = jnp.where(indices[:, None] >= doc_starts[None, :], doc_starts[None, :], 0)
    return jnp.max(marked, axis=1)


def layout_rows(device, row_count):
    return device * row_count + jnp.arange(row_count, dtype=jnp.int32)


def heads_rows(natural):
    return jnp.transpose(natural.astype(jnp.float32))
def padded(rows, heads, g):
    top = jnp.concatenate([rows[HS*(heads*g+j):HS*(heads*g+j+1)] for j in range(heads)], axis=1)
    z = jnp.zeros_like(top)
    return jnp.concatenate([top, z] if g == 0 else [z, top], axis=0)
def head_lanes(per_group, heads, tq):
    return jnp.transpose(jnp.concatenate([per_group[g][:, tq*j:tq*(j+1)] for g in range(2) for j in range(heads)], axis=0))
def bias_tile(info, docs, first, bk, tq):
    query = info[0] + lax.broadcasted_iota(jnp.int32, (1, tq), 1)
    begin = jnp.zeros((1, tq), jnp.int32)
    for i in range(docs.shape[0]):
        begin = jnp.maximum(begin, jnp.where(query >= docs[i], docs[i], 0))
    key = first + lax.broadcasted_iota(jnp.int32, (bk, 1), 0)
    return jnp.where((key <= query) & (key >= begin), 0.0, NEG)


def line_dims(count):
    fours = 0
    while count % 4 == 0:
        count //= 4
        fours += 1
    return ([count] if count > 1 else []) + [4] * fours


def rotate_back(rows, cos_rows, sin_rows):
    half_dim = HS // 2
    first, second = rows[:half_dim], rows[half_dim:]
    return jnp.concatenate(
        [first * cos_rows + second * sin_rows, second * cos_rows - first * sin_rows], axis=0
    )


def w_order(lines):
    return [lines[-2]] + lines[1:-2] + [lines[0], lines[-1]]


def bit_dims(count):
    return [2] * (count.bit_length() - 1)


def round_up(value, unit):
    return -(-value // unit) * unit


def backward_kernel(plan, docs, q_ref, do_ref, ot_ref, lse_ref, kv_hbm, w_ref, cos_ref, sin_ref,
                    normed_ref, inv_ref, gain_ref, gres_ref, gmlp_ref, low_ref, branch_ref, gup_hbm, dnp_hbm, inputs_hbm,
                    tokens_ref, query_ref, key_ref, value_ref, gains_out, gate_ref, up_ref, down_ref, out_ref,
                    kvbuf, dkv, acc_ref, gqt_ref, ga_ref, qblk, kvblk, small,
                    load_sem, send_sem, recv_sem, col_send, col_recv, own_sem, credit,
                    wg, wd, wo, brs, lows, halves, fin, fin_in, dsend, din,
                    colq_ref, colkv_ref, gains_ref, cols_acc, half_send, half_in, gain_send, gain_in, in_sem,
                    g_send, g_recv, w_load, w_send, w_recv, top_send, top_recv, fin_send, fin_recv, *recvs):
    nctx, nf, parts, heads, tq, slots = plan
    plane = nctx // 2
    n = nctx * nf
    dims = bit_dims(plane)
    nd = len(dims)
    bk = 2 * nf * tq
    me_c, me_f = lax.axis_index("ctx"), lax.axis_index("fsdp")
    me = me_c * nf + me_f
    core, place = lax.rem(me_c, 2), me_c // 2
    mesh_id = pl.DeviceIdType.MESH
    half_dim = HS // 2

    def target(k):
        other = lax.rem(me + k, n)
        return other, {"ctx": other // nf, "fsdp": lax.rem(other, nf)}

    barrier = pltpu.get_barrier_semaphore()

    def greet(k, carry):
        pl.semaphore_signal(barrier, inc=1, device_id=target(k)[1], device_id_type=mesh_id)
        return carry

    lax.fori_loop(1, n, greet, 0)

    def loads(p):
        s = p % slots
        return [
            pltpu.make_async_copy(
                kv_hbm.at[:, pl.ds((kind * parts + p) * 2 * HS, 2 * HS)],
                kvbuf.at[s, kind], load_sem.at[s, kind],
            )
            for kind in range(2)
        ]

    resident = slots == parts

    def block_loads(p, j):
        slot = lax.rem(j, 2)
        return [
            pltpu.make_async_copy(
                kv_hbm.at[pl.ds(pl.multiple_of(j * bk, bk), bk), pl.ds((kind * parts + p) * 2 * HS, 2 * HS)],
                kvbuf.at[slot, kind], load_sem.at[slot, kind],
            )
            for kind in range(2)
        ]

    if resident:
        for p in range(parts):
            for copy in loads(p):
                copy.start()

    def dim_axis(i):
        stride = math.prod(dims[:i])
        size = dims[i]
        own = lax.rem(place // stride, size)

        def peer(k):
            there = lax.rem(own + k, size)
            return there, {"ctx": (place + (there - own) * stride) * 2 + core, "fsdp": me_f}

        return (nd - 1 - i, size, own, peer)

    core_axis = (nd, 2, core, lambda k: (1 - core, {"ctx": place * 2 + 1 - core, "fsdp": me_f}))
    side_axis = (nd + 1, 2, me_f, lambda k: (1 - me_f, {"ctx": me_c, "fsdp": 1 - me_f}))
    lines = [dim_axis(i) for i in range(nd)]
    orders = [[core_axis, side_axis] + lines, [core_axis, side_axis] + w_order(lines)]
    stages = nd + 2
    wrecvs = recvs[2 * stages :]
    side_at, mate_at = side_axis[3](1)[1], core_axis[3](1)[1]

    low_bits = nd - 2
    arrays = ((wg, gup_hbm, (0,)), (wd, dnp_hbm, ()), (wo, None, ()), (wg, gup_hbm, (1,)))
    w_lines = [lines, w_order(lines), w_order(lines), lines]

    def chunk_at(a, k):
        near, far_line = w_lines[a][nd - 2], w_lines[a][nd - 1]
        far_bit = far_line[2] if k % 2 else 1 - far_line[2]
        near_bit = near[2] if k // 2 else 1 - near[2]
        return far_bit, near_bit

    def w_region(a, k, stage, at):
        index = [slice(None)] * nd
        index[w_lines[a][nd - 1][0]], index[w_lines[a][nd - 2][0]] = chunk_at(a, k)
        for axis in w_lines[a][:stage]:
            index[axis[0]] = axis[2]
        if stage < low_bits:
            index[w_lines[a][stage][0]] = at
        return tuple(index)

    def held(a, index):
        first = w_lines[a][0][0]
        return index if a == 2 else index[:first] + index[first + 1 :] + arrays[a][2]

    def w_copy(a, k, stage):
        buf, far, sub = arrays[a]
        there, where = w_lines[a][stage][3](1)
        index = w_region(a, k, stage, there)
        return pltpu.make_async_remote_copy(
            src_ref=far.at[index + sub] if stage == 0 and a != 2 else buf.at[held(a, index)],
            dst_ref=wrecvs[a * (low_bits + 2) + stage].at[chunk_at(a, k)],
            send_sem=w_send.at[a, k, stage], recv_sem=w_recv.at[a, k, stage],
            device_id=where, device_id_type=mesh_id,
        )

    def near_copy(a, i):
        return pltpu.make_async_remote_copy(
            src_ref=arrays[a][0].at[held(a, w_region(a, i, low_bits, 0))], dst_ref=wrecvs[a * (low_bits + 2) + low_bits].at[i],
            send_sem=top_send.at[a, i], recv_sem=top_recv.at[a, i],
            device_id=w_lines[a][nd - 2][3](1)[1], device_id_type=mesh_id,
        )

    def far_copy(a):
        return pltpu.make_async_remote_copy(
            src_ref=arrays[a][0].at[held(a, w_region(a, 2, low_bits, 0))], dst_ref=wrecvs[a * (low_bits + 2) + low_bits + 1].at[0],
            send_sem=top_send.at[a, 2], recv_sem=top_recv.at[a, 2],
            device_id=w_lines[a][nd - 1][3](1)[1], device_id_type=mesh_id,
        )

    def w_start(which, k):
        for a in which:
            w_copy(a, k, 0).start()

    def w_finish(which, k):
        for a in which:
            buf = arrays[a][0]
            for stage in range(low_bits):
                w_copy(a, k, stage).wait()
                where = held(a, w_region(a, k, stage, w_lines[a][stage][2]))
                got = wrecvs[a * (low_bits + 2) + stage]
                buf[where] = (
                    buf[where].astype(jnp.float32) + got[chunk_at(a, k)].astype(jnp.float32)
                ).astype(buf.dtype)
                if stage + 1 < low_bits:
                    w_copy(a, k, stage + 1).start()
            if k < 2:
                near_copy(a, k).start()
            elif k == 2:
                near_copy(a, 0).wait()
                where = held(a, w_region(a, 2, low_bits, 0))
                buf[where] = (
                    buf[where].astype(jnp.float32)
                    + wrecvs[a * (low_bits + 2) + low_bits][0].astype(jnp.float32)
                ).astype(buf.dtype)
                far_copy(a).start()

    def w_total(a):
        near_copy(a, 1).wait()
        far_copy(a).wait()
        total = arrays[a][0][held(a, w_region(a, 3, low_bits, 0))].astype(jnp.float32)
        total = total + wrecvs[a * (low_bits + 2) + low_bits][1].astype(jnp.float32)
        return total + wrecvs[a * (low_bits + 2) + low_bits + 1][0].astype(jnp.float32)

    w_loads = [
        pltpu.make_async_copy(far.at[(slice(None),) * w_lines[i][0][0] + (w_lines[i][0][2],)], buf, w_load.at[i])
        for i, (buf, far, _) in enumerate(arrays[:2])
    ]
    for copy in w_loads:
        copy.start()
    half = low_ref.shape[1] // nf
    low_all = low_ref[...]
    halves[0] = low_all[:, :half]
    halves[1] = low_all[:, half:]
    lows[0] = halves[me_f]
    brs[0] = branch_ref[...]

    def g_copy(i, src, dst, where):
        return pltpu.make_async_remote_copy(
            src_ref=src, dst_ref=dst, send_sem=g_send.at[i], recv_sem=g_recv.at[i],
            device_id=where, device_id_type=mesh_id,
        )

    low_side = g_copy(0, halves.at[1 - me_f], lows.at[1], side_at)
    br_side = g_copy(1, brs.at[0], brs.at[1], side_at)
    low_core = g_copy(2, lows.at[pl.ds(0, 2)], lows.at[pl.ds(2, 2)], mate_at)
    br_core = g_copy(3, brs.at[pl.ds(0, 2)], brs.at[pl.ds(2, 2)], mate_at)

    def output_partial():
        low_core.wait()
        br_core.wait()
        rows = jnp.transpose(brs[...].reshape(4 * tq, brs.shape[2]))
        unit = brs.shape[2] // nctx
        wo[...] = jnp.zeros_like(wo)
        low_rows = lows[...].reshape(4 * tq, half)
        batch = plane // 4
        for r in range(plane):
            first = 2 * unit * (r % batch)
            if first == 0:
                chunk = 2 * unit * batch
                part = jnp.dot(
                    rows[2 * unit * r : 2 * unit * r + chunk], low_rows, preferred_element_type=jnp.float32
                )
            piece = jnp.where(core == 0, part[first : first + unit], part[first + unit : first + 2 * unit])
            wo[static_index(dims, r) + (slice(0, unit), slice(0, half))] = piece.astype(wo.dtype)

    pl.semaphore_wait(barrier, n - 1)
    low_side.start()
    br_side.start()
    for k in range(4):
        w_start((0, 3, 1) if k < 2 else (1,), k)

    def region(kind, stage, at):
        index = [slice(None)] * (nd + 2)
        for axis in orders[kind][:stage]:
            index[axis[0]] = axis[2]
        index[orders[kind][stage][0]] = at
        return tuple(index)

    def stage_copies(p, kind, stage):
        s = p % slots
        axis = orders[kind][stage]
        copies = []
        for k in range(1, axis[1]):
            there, where = axis[3](k)
            copies.append(
                pltpu.make_async_remote_copy(
                    src_ref=dkv.at[(s, kind) + region(kind, stage, there)],
                    dst_ref=recvs[kind * stages + stage].at[s, k - 1],
                    send_sem=send_sem.at[s, kind, stage, k - 1],
                    recv_sem=recv_sem.at[s, kind, stage, k - 1],
                    device_id=where, device_id_type=mesh_id,
                )
            )
        return copies

    def stage_start(p, stage):
        for kind in range(2):
            for copy in stage_copies(p, kind, stage):
                copy.start()

    finals = {}

    def stage_finish(p, stage):
        s = p % slots
        for kind in range(2):
            axis = orders[kind][stage]
            for copy in stage_copies(p, kind, stage):
                copy.wait()
            where = region(kind, stage, axis[2])
            got = recvs[kind * stages + stage]
            free = [i for i in range(nd + 2) if isinstance(where[i], slice)]

            def add(index, lead):
                total = dkv[(s, kind) + index].astype(jnp.float32)
                for k in range(axis[1] - 1):
                    total = total + got[(s, k) + lead].astype(jnp.float32)
                return total

            if not free:
                finals[p, kind] = add(where, ())
            else:
                size = dkv.shape[2 + free[0]]

                def one(i, carry):
                    index = list(where)
                    index[free[0]] = i
                    index = tuple(index)
                    dkv[(s, kind) + index] = add(index, (i,)).astype(dkv.dtype)
                    return carry

                lax.fori_loop(0, size, one, 0)

    def place_index(j):
        index = []
        for i in reversed(range(nd)):
            index.append(lax.rem(j // math.prod(dims[:i]), dims[i]))
        return tuple(index)

    start = me * tq
    last = (start + tq - 1) // bk + 1

    def compute(p):
        s = p % slots
        span = slice(2 * heads * HS * p, 2 * heads * HS * (p + 1))
        qt = q_ref[span, :].astype(jnp.float32) * (1.0 / 8.0)
        dt = heads_rows(do_ref[:, span])
        qg = [padded(qt, heads, g) for g in range(2)]
        dg = [padded(dt, heads, g) for g in range(2)]
        qrows = jnp.concatenate([jnp.transpose(x) for x in qg], axis=0).astype(jnp.bfloat16)
        drows = jnp.concatenate([jnp.transpose(x) for x in dg], axis=0).astype(jnp.bfloat16)
        delta = [
            jnp.sum(dg[g][HS * g : HS * (g + 1)] * ot_ref[2 * p + g], axis=0, keepdims=True)
            for g in range(2)
        ]
        lse = [lse_ref[2 * p + g] for g in range(2)]
        qg = [x.astype(jnp.bfloat16) for x in qg]
        dg = [x.astype(jnp.bfloat16) for x in dg]
        acc_ref[...] = jnp.zeros_like(acc_ref)
        for copy in loads(p) if resident else block_loads(p, 0):
            if not resident:
                copy.start()
            else:
                copy.wait()

        def zero(j, carry):
            at = place_index(j)
            for kind in range(2):
                dkv[(s, kind) + at] = jnp.zeros((2, nf, tq, 2 * HS), dkv.dtype)
            return carry

        def body(j, carry):
            first = pl.multiple_of(j * bk, bk)
            if resident:
                kb = kvbuf[s, 0, pl.ds(first, bk), :]
                vb = kvbuf[s, 1, pl.ds(first, bk), :]
            else:
                for copy in block_loads(p, j):
                    copy.wait()

                @pl.when(j + 1 < last)
                def _():
                    for copy in block_loads(p, j + 1):
                        copy.start()

                kb, vb = kvbuf[lax.rem(j, 2), 0], kvbuf[lax.rem(j, 2), 1]
            kt = jnp.transpose(kb)
            bias = bias_tile((start,), docs, first, bk, tq)
            bias = jnp.concatenate([bias] * heads, axis=1)
            ps = []
            dss = []
            for g in range(2):
                score = jnp.dot(kb, qg[g], preferred_element_type=jnp.float32)
                prob = jnp.exp(score + (bias - lse[g]))
                dp = jnp.dot(vb, dg[g], preferred_element_type=jnp.float32)
                ds = (prob * (dp - delta[g])).astype(jnp.bfloat16)
                ps.append(prob.astype(jnp.bfloat16))
                dss.append(ds)
                acc_ref[g] += jnp.dot(kt[HS * g : HS * (g + 1)], ds, preferred_element_type=jnp.float32)
            dv = jnp.dot(jnp.concatenate(ps, axis=1), drows, preferred_element_type=jnp.float32)
            dk = jnp.dot(jnp.concatenate(dss, axis=1), qrows, preferred_element_type=jnp.float32)
            at = place_index(j)
            dkv[(s, 0) + at] = dk.astype(dkv.dtype).reshape(2, nf, tq, 2 * HS)
            dkv[(s, 1) + at] = dv.astype(dkv.dtype).reshape(2, nf, tq, 2 * HS)
            return carry

        lax.fori_loop(last, plane, zero, 0)
        lax.fori_loop(0, last, body, 0)
        cos_rows = jnp.concatenate([cos_ref[...]] * heads, axis=1) * (1.0 / 8.0)
        sin_rows = jnp.concatenate([sin_ref[...]] * heads, axis=1) * (1.0 / 8.0)
        for g in range(2):
            back = rotate_back(acc_ref[g], cos_rows, sin_rows).astype(gqt_ref.dtype)
            for j in range(heads):
                h = (2 * p + g) * heads + j
                gqt_ref[HS * h : HS * (h + 1), :] = back[:, tq * j : tq * (j + 1)]

    peers = 2 + sum(size - 1 for size in dims)

    def all_peers():
        found = [core_axis[3](1)[1], side_axis[3](1)[1]]
        for axis in lines:
            found += [axis[3](k)[1] for k in range(1, axis[1])]
        return found

    progress = {}

    def advance(p):
        stage = progress[p]
        stage_finish(p, stage)
        progress[p] = stage + 1
        if stage + 1 < stages:
            stage_start(p, stage + 1)
        else:
            del progress[p]
            if p + slots < parts:
                for where in all_peers():
                    pl.semaphore_signal(credit, inc=1, device_id=where, device_id_type=mesh_id)

    for p in range(parts):
        if p >= slots:
            while p - slots in progress:
                advance(p - slots)
        compute(p)
        if p >= slots:
            pl.semaphore_wait(credit, peers)
        stage_start(p, 0)
        progress[p] = 0
        for older in [o for o in progress if o < p]:
            advance(older)
        if p == 0:
            low_side.wait()
            br_side.wait()
            low_core.start()
            br_core.start()
        if p == 1:
            for copy in w_loads:
                copy.wait()
            for k in range(2):
                w_finish((0, 3), k)
                w_start((0, 3), k + 2)
    for k in range(2):
        w_finish((1,), k)
    output_partial()

    def copies_to(k, which):
        other = lax.rem(me_c + k, nctx)
        where = {"ctx": other, "fsdp": me_f}
        block, out = ((qblk, colq_ref), (kvblk, colkv_ref), (small, gains_ref))[which]
        return pltpu.make_async_remote_copy(
            src_ref=block if which == 2 else block.at[other], dst_ref=out.at[me_c],
            send_sem=col_send.at[which, k], recv_sem=col_recv.at[which, k],
            device_id=where, device_id_type=mesh_id,
        )

    def share(which):
        def one(k, carry):
            copies_to(k, which).start()
            return carry

        block, out = ((qblk, colq_ref), (kvblk, colkv_ref), (small, gains_ref))[which]
        pltpu.make_async_copy(block if which == 2 else block.at[me_c], out.at[me_c], own_sem.at[which]).start()
        lax.fori_loop(1, nctx, one, 0)

    def share_wait(which):
        def one(k, carry):
            copies_to(k, which).wait()
            return carry

        block, out = ((qblk, colq_ref), (kvblk, colkv_ref), (small, gains_ref))[which]
        pltpu.make_async_copy(block if which == 2 else block.at[me_c], out.at[me_c], own_sem.at[which]).wait()
        lax.fori_loop(1, nctx, one, 0)

    width_q = 2 * parts * heads * HS
    width_k = 2 * parts * HS
    cq, ck = width_q // nctx, width_k // nctx
    qblk[...] = jnp.zeros_like(qblk)
    kvblk[...] = jnp.zeros_like(kvblk)
    for i in range(nctx):
        qblk[i, 0:cq, :] = gqt_ref[cq * i : cq * (i + 1), :]
    share(0)
    ga_ref[...] = jnp.dot(w_ref[:, :width_q], gqt_ref[...], preferred_element_type=jnp.float32)
    for k in range(4):
        w_start((2,), k)
    pq, pk = qblk.shape[1], kvblk.shape[1]

    def columns(col_ref, first, count):
        def fetch(i, slot):
            return pltpu.make_async_copy(
                inputs_hbm.at[i], brs.at[slot], in_sem.at[slot]
            )

        fetch(0, 0).start()
        cols_acc[first : first + count, :] = jnp.zeros((count, cols_acc.shape[1]), jnp.float32)

        def one(i, carry):
            slot = lax.rem(i, 2)

            @pl.when(i + 1 < nctx)
            def _():
                fetch(i + 1, 1 - slot).start()

            fetch(i, slot).wait()
            cols_acc[first : first + count, :] += jnp.dot(
                col_ref[i], brs[slot], preferred_element_type=jnp.float32
            )
            return carry

        lax.fori_loop(0, nctx, one, 0)

    per_side = plane // 2
    home = (2 * me_f + core) * per_side + place // 2
    slot = lax.rem(place, 2)

    def home_copy(kind, s):
        return pltpu.make_async_remote_copy(
            src_ref=fin.at[kind, s], dst_ref=fin_in.at[kind, slot],
            send_sem=fin_send.at[kind, s], recv_sem=fin_recv.at[kind, slot],
            device_id={"ctx": home, "fsdp": jnp.int32(s)}, device_id_type=mesh_id,
        )

    def self_copy(kind, s):
        return pltpu.make_async_copy(fin.at[kind, s], fin_in.at[kind, slot], fin_send.at[kind, s])

    def to_homes(kind, a):
        total = w_total(a)
        unit, lanes = fin.shape[2], fin.shape[3]
        blank = jnp.zeros((unit, lanes - half), fin.dtype)
        for s in range(2):
            fin[kind, s] = jnp.concatenate([total[:, half * s : half * (s + 1)].astype(fin.dtype), blank], axis=1)
            at_home = (home == me_c) & (me_f == s)

            @pl.when(jnp.logical_not(at_home))
            def _():
                home_copy(kind, s).start()

            @pl.when(at_home)
            def _():
                self_copy(kind, s).start()

    turn = 0
    while progress:
        for p in list(progress):
            advance(p)
        if turn == 0:
            for k in range(2, 4):
                w_finish((0, 3, 1), k)
        if turn == 1:
            for k in range(2):
                w_finish((2,), k)
        if turn == 2:
            for k in range(2, 4):
                w_finish((2,), k)
        turn += 1

    cos_rows, sin_rows = cos_ref[...], sin_ref[...]
    grads = []
    for kind in range(2):
        rows = []
        for p in range(parts):
            both = jnp.transpose(finals[p, kind])
            for g in range(2):
                one = both[HS * g : HS * (g + 1)]
                rows.append(rotate_back(one, cos_rows, sin_rows) if kind == 0 else one)
        grads.append(jnp.concatenate(rows, axis=0).astype(jnp.bfloat16))
    for i in range(nctx):
        kvblk[i, 0:ck, :] = grads[0][ck * i : ck * (i + 1)]
        kvblk[i, ck : 2 * ck, :] = grads[1][ck * i : ck * (i + 1)]
    share(1)
    grad_t = (
        ga_ref[...]
        + jnp.dot(w_ref[:, width_q : width_q + width_k], grads[0], preferred_element_type=jnp.float32)
        + jnp.dot(w_ref[:, width_q + width_k :], grads[1], preferred_element_type=jnp.float32)
    )
    grad = jnp.transpose(grad_t)
    normed = normed_ref[...].astype(jnp.float32) * inv_ref[...]
    product = grad * normed
    gain_sum = jnp.sum(product, axis=0, keepdims=True)
    lanes = 128
    tiles = gain_sum.shape[1] // lanes
    rows = [gain_sum[:, lanes * i : lanes * (i + 1)] for i in range(tiles)]
    rows += [gmlp_ref[:, lanes * i : lanes * (i + 1)] for i in range(tiles)]
    rows += [jnp.zeros((small.shape[0] - 2 * tiles, lanes), jnp.float32)]
    small[...] = jnp.concatenate(rows, axis=0)
    share(2)
    gain = gain_ref[0:1, :]
    scaled = grad * gain
    mean = jnp.mean(scaled * normed, axis=1, keepdims=True)
    tokens_ref[...] = gres_ref[...] + inv_ref[...] * (scaled - normed * mean)

    to_homes(0, 0)
    share_wait(0)
    columns(colq_ref, 0, pq)
    to_homes(1, 3)
    dsum = w_total(1)
    dsend[...] = dsum.astype(dsend.dtype)
    down_copy = g_copy(4, dsend, din, mate_at)
    down_copy.start()
    osum = w_total(2)
    out_ref[...] = osum[: out_ref.shape[0], :half]
    share_wait(1)
    columns(colkv_ref, pq, pk)
    left, right = cols_acc[:, :half], cols_acc[:, half:]
    side_pad = jnp.zeros((pq + pk, half_send.shape[1] - half), half_send.dtype)
    half_send[...] = jnp.concatenate([jnp.where(me_f == 0, right, left).astype(half_send.dtype), side_pad], axis=1)
    half_copy = g_copy(5, half_send, half_in, side_at)
    half_copy.start()
    share_wait(2)
    gain_total = gains_ref[0]
    for i in range(1, nctx):
        gain_total = gain_total + gains_ref[i]
    gain_send[...] = gain_total
    gain_copy = g_copy(6, gain_send, gain_in, side_at)
    gain_copy.start()
    half_copy.wait()
    own_half = jnp.where(me_f == 0, cols_acc[:, :half], cols_acc[:, half:])
    rows = own_half + half_in[:, :half].astype(jnp.float32)
    query_ref[...] = rows[:cq]
    key_ref[...] = rows[pq : pq + ck]
    value_ref[...] = rows[pq + ck : pq + 2 * ck]
    gain_copy.wait()
    gains_out[...] = gain_send[...] + gain_in[...]
    down_copy.wait()
    cols = down_ref.shape[0]

    def unfold(folded):
        return jnp.concatenate(
            [folded[2 * cols * i : 2 * cols * (i + 1)] for i in range(folded.shape[0] // (2 * cols))], axis=1
        )

    dsum, got = unfold(dsum), unfold(din[...].astype(jnp.float32))
    own_cols = jnp.where(core == 0, dsum[:cols], dsum[cols:])
    far_cols = jnp.where(core == 0, got[:cols], got[cols:])
    down_ref[...] = jnp.where(
        core == 0,
        jnp.concatenate([own_cols, far_cols], axis=1),
        jnp.concatenate([far_cols, own_cols], axis=1),
    )
    owner = me_c // per_side
    for kind in range(2):
        for s in range(2):
            at_home = (home == me_c) & (me_f == s)

            @pl.when(jnp.logical_not(at_home))
            def _():
                home_copy(kind, s).wait_send()

            @pl.when(at_home)
            def _():
                self_copy(kind, s).wait()

        for h in range(2):
            holder = (2 * lax.rem(me_c, per_side) + h) * 2 + lax.rem(owner, 2)

            @pl.when(jnp.logical_not((holder == me_c) & (owner // 2 == me_f)))
            def _():
                pltpu.make_async_remote_copy(
                    src_ref=fin.at[0, 0], dst_ref=fin_in.at[kind, h],
                    send_sem=fin_send.at[0, 0], recv_sem=fin_recv.at[kind, h],
                    device_id={"ctx": home, "fsdp": me_f}, device_id_type=mesh_id,
                ).wait_recv()

    for kind, ref in ((0, gate_ref), (1, up_ref)):
        rows = jnp.concatenate([fin_in[kind, 0], fin_in[kind, 1]], axis=0).astype(jnp.float32)
        ref[...] = rows[:, :half]


def backward(nctx, nf, docs, q, do, ot, lse, kv, w, cos_t, sin_t, normed, inv, gain, gres, gmlp, low, branch, gup, dnp, inputs):
    width_q, tq = q.shape
    n_tokens, width_kv = kv.shape
    n = nctx * nf
    parts = width_kv // (4 * HS)
    heads = width_q // HS // (2 * parts)
    dims = bit_dims(nctx // 2)
    lead = tuple(reversed(dims))
    part_bytes = n_tokens * 2 * HS * 2
    slots = parts if parts * part_bytes * 5 <= 24 * 2**20 else 1
    nd = len(dims)
    bf16, f32 = jnp.bfloat16, jnp.float32
    axes = {"core": (nd, 2), "side": (nd + 1, nf)}
    line = [(nd - 1 - i, dims[i]) for i in range(nd)]
    orders = [
        [axes["core"], axes["side"]] + line,
        [axes["core"], axes["side"]] + w_order(line),
    ]
    recvs = []
    for order in orders:
        left = list(lead) + [2, nf]
        for position, size in order:
            left[position] = None
            recvs.append(
                pltpu.VMEM((slots, size - 1) + tuple(x for x in left if x) + (tq, 2 * HS), bf16)
            )
    model_width = low.shape[1]
    half = model_width // nf
    unit, deep = gup.shape[-2], model_width // (nctx // 2)
    quarter = dnp.shape[-2] // deep * 128
    plane = nctx // 2
    tails = [gup.shape[nd:], dnp.shape[nd:], (round_up(deep // 2, 16), round_up(half, 128))]
    for tail in (tails[0][1:], tails[1], tails[2], tails[0][1:]):
        for stage in range(nd - 2):
            recvs.append(pltpu.VMEM((2,) * (nd - 1 - stage) + tail, bf16))
        recvs += [pltpu.VMEM((2,) + tail, bf16), pltpu.VMEM((1,) + tail, bf16)]
    stages = nd + 2
    most = max(dims + [2])
    pq = round_up(width_q // nctx, 16)
    pk = round_up(2 * (2 * parts * HS) // nctx, 16)
    model = w.shape[0]
    sr = round_up(2 * model // 128, 8)
    vmem = pl.BlockSpec(memory_space=pltpu.VMEM)
    smem = pl.BlockSpec(memory_space=pltpu.SMEM)
    hbm = pl.BlockSpec(memory_space=pl.ANY)
    return pl.pallas_call(
        functools.partial(backward_kernel, (nctx, nf, parts, heads, tq, slots)),
        out_shape=[
            jax.ShapeDtypeStruct((tq, model), f32),
            jax.ShapeDtypeStruct((width_q // nctx, half), f32),
            jax.ShapeDtypeStruct((2 * parts * HS // nctx, half), f32),
            jax.ShapeDtypeStruct((2 * parts * HS // nctx, half), f32),
            jax.ShapeDtypeStruct((sr, 128), f32),
            jax.ShapeDtypeStruct((2 * unit, half), f32),
            jax.ShapeDtypeStruct((2 * unit, half), f32),
            jax.ShapeDtypeStruct((deep // 2, 2 * quarter), f32),
            jax.ShapeDtypeStruct((deep // 2, half), f32),
        ],
        in_specs=[smem, vmem, vmem, vmem, vmem, hbm] + [vmem] * 10 + [hbm] * 3,
        out_specs=[vmem] * 9,
        scratch_shapes=[
            pltpu.VMEM((slots, 2, n_tokens, 2 * HS) if slots == parts else (2, 2, 2 * nf * tq, 2 * HS), bf16),
            pltpu.VMEM((slots, 2) + lead + (2, nf, tq, 2 * HS), bf16),
            pltpu.VMEM((2, HS, heads * tq), f32),
            pltpu.VMEM((width_q, tq), bf16),
            pltpu.VMEM((model, tq), f32),
            pltpu.VMEM((nctx, pq, tq), bf16),
            pltpu.VMEM((nctx, pk, tq), bf16),
            pltpu.VMEM((sr, 128), f32),
            pltpu.SemaphoreType.DMA((max(slots, 2), 2)),
            pltpu.SemaphoreType.DMA((slots, 2, stages, most - 1)),
            pltpu.SemaphoreType.DMA((slots, 2, stages, most - 1)),
            pltpu.SemaphoreType.DMA((3, nctx)),
            pltpu.SemaphoreType.DMA((3, nctx)),
            pltpu.SemaphoreType.DMA((3,)),
            pltpu.SemaphoreType.REGULAR,
            pltpu.VMEM(lead[:-1] + tails[0], bf16),
            pltpu.VMEM(lead[:-1] + tails[1], bf16),
            pltpu.VMEM(lead + tails[2], bf16),
            pltpu.VMEM((4,) + branch.shape, bf16),
            pltpu.VMEM((4, tq, half), bf16),
            pltpu.VMEM((2, tq, half), bf16),
            pltpu.VMEM((2, 2, unit, round_up(half, 128)), bf16),
            pltpu.VMEM((2, 2, unit, round_up(half, 128)), bf16),
            pltpu.VMEM(tails[1], bf16),
            pltpu.VMEM(tails[1], bf16),
            pltpu.VMEM((nctx, pq, tq), bf16),
            pltpu.VMEM((nctx, pk, tq), bf16),
            pltpu.VMEM((nctx, sr, 128), f32),
            pltpu.VMEM((pq + pk, model), f32),
            pltpu.VMEM((pq + pk, round_up(half, 128)), bf16),
            pltpu.VMEM((pq + pk, round_up(half, 128)), bf16),
            pltpu.VMEM((sr, 128), f32),
            pltpu.VMEM((sr, 128), f32),
            pltpu.SemaphoreType.DMA((2,)),
            pltpu.SemaphoreType.DMA((7,)),
            pltpu.SemaphoreType.DMA((7,)),
            pltpu.SemaphoreType.DMA((2,)),
            pltpu.SemaphoreType.DMA((4, 4, max(nd - 2, 1))),
            pltpu.SemaphoreType.DMA((4, 4, max(nd - 2, 1))),
            pltpu.SemaphoreType.DMA((4, 3)),
            pltpu.SemaphoreType.DMA((4, 3)),
            pltpu.SemaphoreType.DMA((2, 2)),
            pltpu.SemaphoreType.DMA((2, 2)),
        ]
        + recvs,
        compiler_params=pltpu.CompilerParams(
            collective_id=1, has_side_effects=True, vmem_limit_bytes=63 * 2**20
        ),
        cost_estimate=pl.CostEstimate(flops=10**10, bytes_accessed=3 * 10**7, transcendentals=10**7),
        name="backward",
    )(docs, q, do, ot, lse, kv, w, cos_t, sin_t, normed, inv, gain, gres, gmlp, low, branch, gup, dnp, inputs)


def rotate(rows, cos_rows, sin_rows):
    half_dim = HS // 2
    first, second = rows[:half_dim], rows[half_dim:]
    return jnp.concatenate(
        [first * cos_rows - second * sin_rows, second * cos_rows + first * sin_rows], axis=0
    )


class Axes:
    def __init__(self, nctx, nf):
        self.ctx, self.f = lax.axis_index("ctx"), lax.axis_index("fsdp")
        self.core, self.place = lax.rem(self.ctx, 2), self.ctx // 2
        self.me = self.ctx * nf + self.f
        self.dims = line_dims(nctx // 2)
        self.nd = len(self.dims)
        ctx, f, core, place = self.ctx, self.f, self.core, self.place
        self.core_axis = (self.nd, 2, core, lambda k: (1 - core, {"ctx": place * 2 + 1 - core, "fsdp": f}))
        self.side_axis = (self.nd + 1, 2, f, lambda k: (1 - f, {"ctx": ctx, "fsdp": 1 - f}))
        self.lines = [self.line(i) for i in range(self.nd)]
        self.peer_count = 2 + sum(size - 1 for size in self.dims)

    def at_line(self, i, there):
        stride = math.prod(self.dims[:i])
        own = lax.rem(self.place // stride, self.dims[i])
        return {"ctx": (self.place + (there - own) * stride) * 2 + self.core, "fsdp": self.f}

    def line(self, i):
        size = self.dims[i]
        own = lax.rem(self.place // math.prod(self.dims[:i]), size)

        def peer(k):
            there = lax.rem(own + k, size)
            return there, self.at_line(i, there)

        return (self.nd - 1 - i, size, own, peer)

    def peers(self):
        found = [self.core_axis[3](1)[1], self.side_axis[3](1)[1]]
        for axis in self.lines:
            found += [axis[3](k)[1] for k in range(1, axis[1])]
        return found

    def place_index(self, j):
        return tuple(
            lax.rem(j // math.prod(self.dims[:i]), self.dims[i]) for i in reversed(range(self.nd))
        )


def forward_kernel(plan, docs, tokens_ref, gains_ref, cos_ref, sin_ref, wq, wk, wv, wo, wg, wu, cot,
                   qt_ref, kv_out, low_ref, ot_ref, lse_ref, wqkv_out, wo_out, gu_out, cots_out,
                   attn_in_ref, inv_ref, gain_ref,
                   wbuf, obuf, gubuf, cbuf, gain_far, own_kv, kvb, m_ref, l_ref, acc_ref,
                   load_sem, w_send, w_recv, top_send, top_recv, ag_send, ag_recv, blk_sem, out_sem):
    nctx, nf, parts, heads, tq = plan
    ax = Axes(nctx, nf)
    f, core, place = ax.f, ax.core, ax.place
    mesh_id = pl.DeviceIdType.MESH
    bf16, f32 = jnp.bfloat16, jnp.float32
    width = tokens_ref.shape[1]
    half = width // nf
    width_q, width_k = 2 * parts * heads * HS, 2 * parts * HS
    rows4, rows2 = half // 4, half // 2
    quarter = gu_out.shape[1] // 2
    side = ax.side_axis[3](1)[1]
    mate = ax.core_axis[3](1)[1]
    low = ax.lines[0]
    bit = lax.rem(low[2], 2)
    across = ax.at_line(0, low[2] + 1 - 2 * bit)
    top = ax.nd - 1
    chunks = ax.dims[top]
    z = ax.lines[top][2]

    barrier = pltpu.get_barrier_semaphore()
    for where in ax.peers():
        pl.semaphore_signal(barrier, inc=1, device_id=where, device_id_type=mesh_id)

    def local(src, dst, i):
        return pltpu.make_async_copy(src, dst, load_sem.at[i])

    own_rows = pl.ds(pl.multiple_of(f * half, half), half)
    own_quarter = pl.ds(pl.multiple_of((2 * f + core) * quarter, quarter), quarter)
    loads = [
        local(wk, wbuf.at[own_rows, pl.ds(width_q, width_k)], 0),
        local(wv, wbuf.at[own_rows, pl.ds(width_q + width_k, width_k)], 1),
        local(wq, wbuf.at[own_rows, pl.ds(0, width_q)], 2),
        local(wo, obuf.at[own_rows], 3),
        local(wg.at[:, own_quarter], gubuf.at[own_rows, pl.ds(0, quarter)], 4),
        local(wu.at[:, own_quarter], gubuf.at[own_rows, pl.ds(quarter, quarter)], 5),
        local(cot, cbuf.at[0], 6),
    ]
    for copy in loads:
        copy.start()

    def remote(src, dst, i, where):
        return pltpu.make_async_remote_copy(
            src_ref=src, dst_ref=dst, send_sem=w_send.at[i], recv_sem=w_recv.at[i],
            device_id=where, device_id_type=mesh_id,
        )

    near = pl.multiple_of(core * rows2 + bit * rows4, 16)
    far_x = pl.multiple_of(core * rows2 + (1 - bit) * rows4, 16)
    there = (1 - f) * half

    def piece(base, offset):
        return pl.ds(pl.multiple_of(base + offset, 16), rows4)

    kv_cols, q_cols = pl.ds(width_q, 2 * width_k), pl.ds(0, width_q)
    mine = f * half
    gains_copy = remote(gains_ref, gain_far, 0, side)
    kv_y = [
        remote(wk.at[piece(0, near)], wbuf.at[piece(mine, near), pl.ds(width_q, width_k)], 1, side),
        remote(wv.at[piece(0, near)], wbuf.at[piece(mine, near), pl.ds(width_q + width_k, width_k)], 2, side),
    ]
    q_y = [remote(wq.at[piece(0, near)], wbuf.at[piece(mine, near), q_cols], 3, side)]
    o_y = [remote(wo.at[piece(0, near)], obuf.at[piece(mine, near)], 4, side)]

    def forwards(buf, cols, first):
        def part(offset):
            return buf.at[piece(there, offset), cols] if cols is not None else buf.at[piece(there, offset)]

        return [
            remote(part(near), part(near), first, across),
            remote(part(near), part(near), first + 1, mate),
            remote(part(far_x), part(far_x), first + 2, mate),
        ]

    kv_f = forwards(wbuf, kv_cols, 5)
    q_f = forwards(wbuf, q_cols, 8)
    o_f = forwards(obuf, None, 11)
    far_quarter = pl.ds(pl.multiple_of((2 * (1 - f) + core) * quarter, quarter), quarter)

    deep = lax.rem(z, 2)
    above = ax.at_line(top, z + 1 - 2 * deep)

    def gu_rows(base, which=bit):
        return pl.ds(pl.multiple_of(base + which * rows2 + deep * rows4, 16), rows4)

    gu_y = [
        remote(wg.at[gu_rows(0), far_quarter], gubuf.at[gu_rows(mine), pl.ds(0, quarter)], 14, side),
        remote(wu.at[gu_rows(0), far_quarter], gubuf.at[gu_rows(mine), pl.ds(quarter, quarter)], 15, side),
    ]
    gu_x = remote(gubuf.at[gu_rows(there)], gubuf.at[gu_rows(there)], 16, across)
    gu_z = [
        remote(gubuf.at[gu_rows(there, which)], gubuf.at[gu_rows(there, which)], 19 + i, above)
        for i, which in enumerate((bit, 1 - bit))
    ]
    cot_y = remote(cot, cbuf.at[1], 17, side)
    cot_c = remote(cbuf.at[pl.ds(0, 2)], cbuf.at[pl.ds(2, 2)], 18, mate)

    pl.semaphore_wait(barrier, ax.peer_count)
    gains_copy.start()
    for copy in kv_y + q_y:
        copy.start()

    hidden = tokens_ref[...].astype(f32)
    inv = lax.rsqrt(jnp.mean(hidden * hidden, axis=1, keepdims=True) + EPS)
    inv_ref[...] = inv
    gains_copy.wait()
    near_gain, far_gain = gains_ref[0:1, :], gain_far[0:1, :]
    gain = jnp.where(
        f == 0,
        jnp.concatenate([near_gain, far_gain], axis=1),
        jnp.concatenate([far_gain, near_gain], axis=1),
    )
    near_mlp, far_mlp = gains_ref[1:2, :], gain_far[1:2, :]
    gain_ref[0:1, :] = gain
    gain_ref[1:2, :] = jnp.where(
        f == 0,
        jnp.concatenate([near_mlp, far_mlp], axis=1),
        jnp.concatenate([far_mlp, near_mlp], axis=1),
    )
    attn_in = (hidden * inv * gain).astype(bf16)
    attn_in_ref[...] = attn_in

    for copy in kv_y:
        copy.wait()
    kv_f[0].start()
    kv_f[1].start()
    for copy in q_y:
        copy.wait()
    for copy in o_y + gu_y:
        copy.start()
    kv_f[0].wait()
    kv_f[2].start()
    q_f[0].start()
    q_f[1].start()
    for copy in loads[:3]:
        copy.wait()
    kv_f[1].wait()
    kv_f[2].wait()
    kv = jnp.dot(attn_in, wbuf[:, width_q:], preferred_element_type=f32)
    cos_rows, sin_rows = cos_ref[...], sin_ref[...]
    kt = jnp.transpose(kv[:, :width_k])
    k_rot = jnp.concatenate(
        [rotate(kt[HS * g : HS * (g + 1)], cos_rows, sin_rows) for g in range(2 * parts)], axis=0
    )
    own_kv[:, :width_k] = jnp.transpose(k_rot).astype(bf16)
    own_kv[:, width_k:] = kv[:, width_k:].astype(bf16)
    own_at = ax.place_index(place) + (core, f)
    put = pltpu.make_async_copy(own_kv, kv_out.at[own_at], out_sem.at[0])
    put.start()

    def top_copy(k):
        return pltpu.make_async_remote_copy(
            src_ref=own_kv, dst_ref=kv_out.at[own_at],
            send_sem=top_send.at[k - 1], recv_sem=top_recv.at[k - 1],
            device_id=ax.at_line(top, lax.rem(z + k, chunks)), device_id_type=mesh_id,
        )

    for k in range(1, chunks):
        @pl.when(z + k < chunks)
        def _():
            top_copy(k).start()

    lower = ax.lines[:top]
    orders = [lower + [ax.side_axis, ax.core_axis], [ax.side_axis] + lower + [ax.core_axis]]
    stages = len(orders[0])

    def ag_copies(k, stage):
        copies = []
        for kind in range(2):
            index = [None] * (ax.nd + 2)
            index[0] = z - k
            for i, axis in enumerate(orders[kind]):
                index[axis[0]] = slice(None) if i < stage else axis[2]
            region = kv_out.at[tuple(index) + (slice(None), pl.ds(kind * width_k, width_k))]
            axis = orders[kind][stage]
            for i in range(1, axis[1]):
                copies.append(
                    pltpu.make_async_remote_copy(
                        src_ref=region, dst_ref=region,
                        send_sem=ag_send.at[k, kind, stage, i - 1],
                        recv_sem=ag_recv.at[k, kind, stage, i - 1],
                        device_id=axis[3](i)[1], device_id_type=mesh_id,
                    )
                )
        return copies

    def tick(k, stage):
        @pl.when(z >= k)
        def _():
            if stage == 0:
                if k > 0:
                    top_copy(k).wait_recv()
            else:
                for copy in ag_copies(k, stage - 1):
                    copy.wait()
            if stage < stages:
                for copy in ag_copies(k, stage):
                    copy.start()

    put.wait()
    tick(0, 0)
    q_f[0].wait()
    q_f[2].start()
    q_f[1].wait()
    q_f[2].wait()
    back = pltpu.make_async_copy(wbuf, wqkv_out, out_sem.at[1])
    back.start()
    query = jnp.dot(attn_in, wbuf[:, :width_q], preferred_element_type=f32)
    query_t = jnp.transpose(query)
    for h in range(2 * parts * heads):
        qt_ref[HS * h : HS * (h + 1), :] = rotate(
            query_t[HS * h : HS * (h + 1)], cos_rows, sin_rows
        ).astype(bf16)
    m_ref[...] = jnp.full_like(m_ref, NEG)
    l_ref[...] = jnp.zeros_like(l_ref)
    acc_ref[...] = jnp.zeros_like(acc_ref)

    bk = 2 * nf * tq
    per_chunk = math.prod(ax.dims[:top])
    start = ax.me * tq

    def block_copy(j, slot):
        return pltpu.make_async_copy(kv_out.at[ax.place_index(j)], kvb.at[slot], blk_sem.at[slot])

    def attend(k):
        first_block = (z - k) * per_chunk
        count = jnp.minimum(place - first_block + 1, per_chunk)

        @pl.when(z >= k)
        def _():
            block_copy(first_block, 0).start()

            def block(i, carry):
                j = first_block + i
                slot = lax.rem(i, 2)

                @pl.when(i + 1 < count)
                def _():
                    block_copy(j + 1, 1 - slot).start()

                block_copy(j, slot).wait()
                bias = bias_tile((start,), docs, j * bk, bk, tq)
                bias = jnp.concatenate([bias] * heads, axis=1)
                for p in range(parts):
                    kb = kvb[slot, :, :, :, 2 * HS * p : 2 * HS * (p + 1)].reshape(bk, 2 * HS)
                    vb = kvb[slot, :, :, :, width_k + 2 * HS * p : width_k + 2 * HS * (p + 1)]
                    vt = jnp.transpose(vb.reshape(bk, 2 * HS))
                    rows = qt_ref[2 * heads * HS * p : 2 * heads * HS * (p + 1), :] * bf16(1.0 / 8.0)
                    for g in range(2):
                        at = 2 * p + g
                        s = jnp.dot(kb, padded(rows, heads, g), preferred_element_type=f32) + bias
                        m = m_ref[at]
                        new = jnp.maximum(m, jnp.max(s, axis=0, keepdims=True))
                        prob = jnp.exp(s - new)
                        decay = jnp.exp(m - new)
                        m_ref[at] = new
                        l_ref[at] = l_ref[at] * decay + jnp.sum(prob, axis=0, keepdims=True)
                        acc_ref[at] = acc_ref[at] * decay + jnp.dot(
                            vt[HS * g : HS * (g + 1)], prob.astype(bf16), preferred_element_type=f32
                        )
                return carry

            lax.fori_loop(0, count, block, 0)

    for turn in range(1, chunks + stages):
        for k in range(chunks):
            stage = turn - k
            if (k, stage) != (0, 0) and 0 <= stage <= stages:
                tick(k, stage)
        if turn == 4:
            for copy in o_y + gu_y:
                copy.wait()
            o_f[0].start()
            o_f[1].start()
            gu_x.start()
            gu_z[0].start()
        if turn == 3:
            cot_y.start()
        if turn == 6:
            o_f[0].wait()
            o_f[2].start()
            gu_x.wait()
            gu_z[1].start()
        if turn == 5:
            cot_y.wait()
            loads[6].wait()
            cot_c.start()
        if turn >= stages:
            attend(turn - stages)
    for p in range(parts):
        outs = []
        for g in range(2):
            at = 2 * p + g
            out = acc_ref[at] / l_ref[at]
            outs.append(out)
            ot_ref[at] = out
            lse_ref[at] = m_ref[at] + jnp.log(l_ref[at])
        low_ref[:, 2 * heads * HS * p : 2 * heads * HS * (p + 1)] = head_lanes(outs, heads, tq).astype(bf16)

    for k in range(1, chunks):
        @pl.when(z + k < chunks)
        def _():
            top_copy(k).wait_send()
    for copy in loads[3:6]:
        copy.wait()
    backs = [back]
    for waits, src, dst in (
        (o_f[1:], obuf, wo_out), ([cot_c], cbuf, cots_out), (gu_z, gubuf, gu_out)
    ):
        for copy in waits:
            copy.wait()
        backs.append(pltpu.make_async_copy(src, dst, out_sem.at[1 + len(backs)]))
        backs[-1].start()
    for copy in backs:
        copy.wait()


def forward(nctx, nf, docs, tokens, gains, cos_t, sin_t, wq, wk, wv, wo, wg, wu, cot):
    tq, width = tokens.shape
    width_q, width_k = wq.shape[1], wk.shape[1]
    parts = width_k // (2 * HS)
    heads = width_q // HS // (2 * parts)
    hidden_units = wg.shape[1]
    quarter = hidden_units // (2 * nf)
    dims = line_dims(nctx // 2)
    lead = tuple(reversed(dims))
    most = max(dims + [2])
    chunks = dims[-1]
    stages = len(dims) + 1
    bf16, f32 = jnp.bfloat16, jnp.float32
    vmem = pl.BlockSpec(memory_space=pltpu.VMEM)
    smem = pl.BlockSpec(memory_space=pltpu.SMEM)
    hbm = pl.BlockSpec(memory_space=pl.ANY)
    dma = pltpu.SemaphoreType.DMA
    return pl.pallas_call(
        functools.partial(forward_kernel, (nctx, nf, parts, heads, tq)),
        out_shape=[
            jax.ShapeDtypeStruct((width_q, tq), bf16),
            jax.ShapeDtypeStruct(lead + (2, nf, tq, 2 * width_k), bf16),
            jax.ShapeDtypeStruct((tq, width_q), bf16),
            jax.ShapeDtypeStruct((2 * parts, HS, heads * tq), f32),
            jax.ShapeDtypeStruct((2 * parts, 1, heads * tq), f32),
            jax.ShapeDtypeStruct((width, width_q + 2 * width_k), bf16),
            jax.ShapeDtypeStruct((nf * wo.shape[0], wo.shape[1]), bf16),
            jax.ShapeDtypeStruct((width, 2 * quarter), bf16),
            jax.ShapeDtypeStruct((2 * nf, tq, width), bf16),
            jax.ShapeDtypeStruct((tq, width), bf16),
            jax.ShapeDtypeStruct((tq, 1), f32),
            jax.ShapeDtypeStruct((2, width), f32),
        ],
        in_specs=[smem, vmem, vmem, vmem, vmem] + [hbm] * 7,
        out_specs=[vmem, hbm, vmem, vmem, vmem, hbm, hbm, hbm, hbm, vmem, vmem, vmem],
        scratch_shapes=[
            pltpu.VMEM((width, width_q + 2 * width_k), bf16),
            pltpu.VMEM((nf * wo.shape[0], wo.shape[1]), bf16),
            pltpu.VMEM((width, 2 * quarter), bf16),
            pltpu.VMEM((2 * nf, tq, width), bf16),
            pltpu.VMEM(gains.shape, f32),
            pltpu.VMEM((tq, 2 * width_k), bf16),
            pltpu.VMEM((2, 2, nf, tq, 2 * width_k), bf16),
            pltpu.VMEM((2 * parts, 1, heads * tq), f32),
            pltpu.VMEM((2 * parts, 1, heads * tq), f32),
            pltpu.VMEM((2 * parts, HS, heads * tq), f32),
            dma((7,)),
            dma((21,)),
            dma((21,)),
            dma((chunks - 1,)),
            dma((chunks - 1,)),
            dma((chunks, 2, stages, most - 1)),
            dma((chunks, 2, stages, most - 1)),
            dma((2,)),
            dma((5,)),
        ],
        compiler_params=pltpu.CompilerParams(
            collective_id=0, has_side_effects=True, vmem_limit_bytes=60 * 2**20
        ),
        name="forward",
    )(docs, tokens, gains, cos_t, sin_t, wq, wk, wv, wo, wg, wu, cot)


def feed_forward_kernel(plan, tokens_ref, low_ref, attn_in_ref, gains_ref, wo_hbm, gu_hbm, down_hbm, cots_hbm,
                        result_ref, gres_ref, branch_ref, gattn_ref, gmlp_ref, gup_ref, dnp_ref, inputs_out,
                        wo, gu, down, cots, xs, grads, mixed, gm, sums, sent, core_in, side_in, side_out,
                        load_sem, x_send, x_recv, s_send, s_recv, top_send, top_recv,
                        ag_send, ag_recv, out_sem):
    nctx, nf = plan
    ax = Axes(nctx, nf)
    f, core, place = ax.f, ax.core, ax.place
    mesh_id = pl.DeviceIdType.MESH
    bf16, f32 = jnp.bfloat16, jnp.float32
    tq, width = tokens_ref.shape
    quarter = down.shape[0]
    side = ax.side_axis[3](1)[1]
    mate = ax.core_axis[3](1)[1]
    top = ax.nd - 1
    chunks = ax.dims[top]
    z = ax.lines[top][2]

    barrier = pltpu.get_barrier_semaphore()
    for where in ax.peers():
        pl.semaphore_signal(barrier, inc=1, device_id=where, device_id_type=mesh_id)
    loads = [
        pltpu.make_async_copy(src, dst, load_sem.at[i])
        for i, (src, dst) in enumerate((
            (wo_hbm, wo), (cots_hbm, cots),
            (down_hbm.at[pl.ds(pl.multiple_of(core * quarter, quarter), quarter)], down), (gu_hbm, gu),
        ))
    ]
    for copy in loads:
        copy.start()

    def remote(src, dst, sends, recvs, i, where):
        return pltpu.make_async_remote_copy(
            src_ref=src, dst_ref=dst, send_sem=sends.at[i], recv_sem=recvs.at[i],
            device_id=where, device_id_type=mesh_id,
        )

    hidden = tokens_ref[...].astype(f32)
    own_at = ax.place_index(place) + (core,)
    put = pltpu.make_async_copy(attn_in_ref, inputs_out.at[own_at], out_sem.at[0])

    def top_copy(k):
        return pltpu.make_async_remote_copy(
            src_ref=attn_in_ref, dst_ref=inputs_out.at[own_at],
            send_sem=top_send.at[k - 1], recv_sem=top_recv.at[k - 1],
            device_id=ax.at_line(top, lax.rem(z + k, chunks)), device_id_type=mesh_id,
        )

    order = ax.lines[:top] + [ax.core_axis]
    stages = len(order)

    def ag_copies(k, stage):
        index = [None] * (ax.nd + 1)
        index[0] = lax.rem(z + chunks - k, chunks)
        for i, axis in enumerate(order):
            index[axis[0]] = slice(None) if i < stage else axis[2]
        region = inputs_out.at[tuple(index)]
        axis = order[stage]
        return [
            pltpu.make_async_remote_copy(
                src_ref=region, dst_ref=region,
                send_sem=ag_send.at[k, stage, i - 1], recv_sem=ag_recv.at[k, stage, i - 1],
                device_id=axis[3](i)[1], device_id_type=mesh_id,
            )
            for i in range(1, axis[1])
        ]

    def tick(turn):
        for k in range(chunks):
            stage = turn - k
            if not 0 <= stage <= stages:
                continue
            if stage == 0:
                if k > 0:
                    top_copy(k).wait()
                else:
                    put.wait()
            else:
                for copy in ag_copies(k, stage - 1):
                    copy.wait()
            if stage < stages:
                for copy in ag_copies(k, stage):
                    copy.start()

    pl.semaphore_wait(barrier, ax.peer_count)
    put.start()
    for k in range(1, chunks):
        top_copy(k).start()
    tick(0)

    loads[0].wait()
    resid = hidden + jnp.dot(low_ref[...], wo[...], preferred_element_type=f32)
    inv = lax.rsqrt(jnp.mean(resid * resid, axis=1, keepdims=True) + EPS)
    normed = resid * inv
    gain = gains_ref[1:2, :]
    xs[0] = (normed * gain).astype(bf16)
    x_side = remote(xs.at[0], xs.at[1], x_send, x_recv, 0, side)
    x_core = remote(xs.at[0], xs.at[2], x_send, x_recv, 1, mate)
    x_far = remote(xs.at[1], xs.at[3], x_send, x_recv, 2, mate)
    x_side.start()
    x_core.start()

    def rows(slot):
        return slice(slot * tq, (slot + 1) * tq)

    for copy in loads[1:3]:
        copy.wait()
    gm[...] = lax.dot_general(
        cots[...].reshape(4 * tq, width), down[...], (((1,), (1,)), ((), ())), preferred_element_type=f32
    )
    loads[3].wait()
    step = 256

    def both(ref, a, b, span=slice(None)):
        return jnp.concatenate([ref[a, :, span], ref[b, :, span]], axis=0)

    def compute(a, b):
        x = both(xs, a, b)
        for n in range(quarter // step):
            span = slice(n * step, (n + 1) * step)
            up_span = slice(quarter + n * step, quarter + (n + 1) * step)
            gate = jnp.dot(x, gu[:, span], preferred_element_type=f32)
            up = jnp.dot(x, gu[:, up_span], preferred_element_type=f32)
            sig = jax.nn.sigmoid(gate)
            act = gate * sig
            grad = jnp.concatenate([gm[rows(a), span], gm[rows(b), span]], axis=0)
            mix = (act * up).astype(bf16)
            grad_gate = (grad * up * sig * (1.0 + gate * (1.0 - sig))).astype(bf16)
            grad_up = (grad * act).astype(bf16)
            for i, slot in enumerate((a, b)):
                mixed[slot, :, span] = mix[rows(i)]
                grads[slot, :, span] = grad_gate[rows(i)]
                grads[slot, :, up_span] = grad_up[rows(i)]
        total = lax.dot_general(
            both(grads, a, b), gu[...], (((1,), (1,)), ((), ())), preferred_element_type=f32
        )
        for i, slot in enumerate((a, b)):
            sums[0, slot] = total[rows(i)]

    def outputs(a, b):
        total = jnp.dot(both(mixed, a, b), down[...], preferred_element_type=f32)
        for i, slot in enumerate((a, b)):
            sums[1, slot] = total[rows(i)]

    def to_core(kind, slot):
        i = 2 * kind + slot - 2
        return remote(sent.at[i], core_in.at[i], s_send, s_recv, i, mate)

    def to_side(kind):
        return remote(side_out.at[kind], side_in.at[kind], s_send, s_recv, 4 + kind, side)

    def give_core(kind, slot):
        sent[2 * kind + slot - 2] = sums[kind, slot].astype(bf16)
        to_core(kind, slot).start()

    def give_side(kind):
        to_core(kind, 3).wait()
        side_out[kind] = (sums[kind, 1] + core_in[2 * kind + 1].astype(f32)).astype(bf16)
        to_side(kind).start()

    x_core.wait()
    compute(0, 2)
    give_core(0, 2)
    x_side.wait()
    x_far.start()
    outputs(0, 2)
    give_core(1, 2)
    x_far.wait()
    compute(1, 3)
    give_core(0, 3)
    tick(1)
    outputs(1, 3)
    give_side(0)
    give_core(1, 3)
    flat_x = xs[...].reshape(4 * tq, width)
    pieces = nctx // 2
    unit = quarter // pieces
    tall = max(unit, 256)
    for kind in range(2):
        for n in range(quarter // tall):
            span = slice(kind * quarter + n * tall, kind * quarter + (n + 1) * tall)
            cols = jnp.transpose(jnp.concatenate([grads[s, :, span] for s in range(4)], axis=0))
            part = jnp.dot(cols, flat_x, preferred_element_type=f32).astype(bf16)
            first = n * tall
            while first < (n + 1) * tall:
                piece, at = first // unit, first % unit
                end = min((piece + 1) * unit, (n + 1) * tall)
                gup_ref[static_index(bit_dims(nctx // 2), piece) + (kind, slice(at, at + end - first))] = part[
                    first - n * tall : end - n * tall
                ]
                first = end
        if kind == 0:
            give_side(1)
            tick(2)
    unit = width // pieces
    flat_mixed = mixed[...].reshape(4 * tq, quarter)
    for n in range(width // 384):
        cols = jnp.transpose(jnp.concatenate([cots[s, :, 384 * n : 384 * (n + 1)] for s in range(4)], axis=0))
        part = jnp.dot(cols, flat_mixed, preferred_element_type=f32).astype(bf16)
        first = n * 384
        while first < (n + 1) * 384:
            piece, at = first // unit, first % unit
            end = min((piece + 1) * unit, (n + 1) * 384)
            rows_of = part[first - n * 384 : end - n * 384]
            for c in range(quarter // 128):
                dnp_ref[
                    static_index(bit_dims(nctx // 2), piece)
                    + (slice(c * unit + at, c * unit + at + end - first),)
                ] = rows_of[:, 128 * c : 128 * (c + 1)]
            first = end

    to_core(0, 2).wait()
    to_side(0).wait()
    grad = sums[0, 0] + core_in[0].astype(f32) + side_in[0].astype(f32)
    product = grad * normed
    gmlp_ref[...] = jnp.sum(product, axis=0, keepdims=True)
    scaled = grad * gain
    mean = jnp.mean(scaled * normed, axis=1, keepdims=True)
    gres = cots[0].astype(f32) + inv * (scaled - normed * mean)
    gres_ref[...] = gres
    branch = gres.astype(bf16)
    branch_ref[...] = branch
    gattn_ref[...] = lax.dot_general(
        branch, wo[...], (((1,), (1,)), ((), ())), preferred_element_type=f32
    ).astype(bf16)
    tick(3)
    to_core(1, 2).wait()
    to_side(1).wait()
    result_ref[...] = (resid + sums[1, 0] + core_in[2].astype(f32) + side_in[1].astype(f32)).astype(bf16)
    for turn in range(4, chunks + stages):
        tick(turn)


def static_index(dims, piece):
    return tuple(piece // math.prod(dims[:i]) % dims[i] for i in reversed(range(len(dims))))


def feed_forward(nctx, nf, tokens, low, attn_in, gains, wo, gu, down, cots):
    tq, width = tokens.shape
    quarter = gu.shape[1] // 2
    dims = line_dims(nctx // 2)
    bits = bit_dims(nctx // 2)
    lead = tuple(reversed(dims))
    plane = nctx // 2
    chunks, stages, most = dims[-1], len(dims), max(dims + [2])
    bf16, f32 = jnp.bfloat16, jnp.float32
    vmem = pl.BlockSpec(memory_space=pltpu.VMEM)
    hbm = pl.BlockSpec(memory_space=pl.ANY)
    dma = pltpu.SemaphoreType.DMA
    return pl.pallas_call(
        functools.partial(feed_forward_kernel, (nctx, nf)),
        out_shape=[
            jax.ShapeDtypeStruct((tq, width), bf16),
            jax.ShapeDtypeStruct((tq, width), f32),
            jax.ShapeDtypeStruct((tq, width), bf16),
            jax.ShapeDtypeStruct((tq, width), bf16),
            jax.ShapeDtypeStruct((1, width), f32),
            jax.ShapeDtypeStruct(tuple(bits) + (2, quarter // plane, width), bf16),
            jax.ShapeDtypeStruct(tuple(bits) + (width // plane * (quarter // 128), 128), bf16),
            jax.ShapeDtypeStruct(lead + (2, tq, width), bf16),
        ],
        in_specs=[vmem] * 4 + [hbm] * 4,
        out_specs=[vmem] * 7 + [hbm],
        scratch_shapes=[
            pltpu.VMEM(wo.shape, bf16),
            pltpu.VMEM(gu.shape, bf16),
            pltpu.VMEM((quarter, width), bf16),
            pltpu.VMEM((4, tq, width), bf16),
            pltpu.VMEM((4, tq, width), bf16),
            pltpu.VMEM((4, tq, 2 * quarter), bf16),
            pltpu.VMEM((4, tq, quarter), bf16),
            pltpu.VMEM((4 * tq, quarter), f32),
            pltpu.VMEM((2, 4, tq, width), f32),
            pltpu.VMEM((4, tq, width), bf16),
            pltpu.VMEM((4, tq, width), bf16),
            pltpu.VMEM((2, tq, width), bf16),
            pltpu.VMEM((2, tq, width), bf16),
            dma((4,)),
            dma((4,)),
            dma((4,)),
            dma((6,)),
            dma((6,)),
            dma((chunks - 1,)),
            dma((chunks - 1,)),
            dma((chunks, stages, most - 1)),
            dma((chunks, stages, most - 1)),
            dma((1,)),
        ],
        compiler_params=pltpu.CompilerParams(
            collective_id=2, has_side_effects=True, vmem_limit_bytes=60 * 2**20
        ),
        name="feed_forward",
    )(tokens, low, attn_in, gains, wo, gu, down, cots)


def finish_kernel(result, tokens, q, k, v, o, gate, up, down, gains, *outs):
    outs[0][...] = result[...]
    outs[1][...] = tokens[...]
    for src, dst in zip((q, k, v, o, gate, up, down), outs[2:9]):
        dst[...] = jnp.transpose(src[...])
    tiles = outs[9].shape[1] // 128
    for i in range(2):
        outs[9 + i][...] = jnp.concatenate(
            [gains[tiles * i + j : tiles * i + j + 1, :] for j in range(tiles)], axis=1
        )


def finish(nf, width, result, tokens, *sums):
    weights, gains = sums[:-1], sums[-1]
    f32 = jnp.float32
    vmem = pl.BlockSpec(memory_space=pltpu.VMEM)
    outs = pl.pallas_call(
        finish_kernel,
        out_shape=[
            jax.ShapeDtypeStruct(result.shape, result.dtype),
            jax.ShapeDtypeStruct(tokens.shape, f32),
        ]
        + [jax.ShapeDtypeStruct(w.shape[::-1], f32) for w in weights]
        + [jax.ShapeDtypeStruct((1, width), f32)] * 2,
        in_specs=[vmem] * 10,
        out_specs=[vmem] * 11,
        compiler_params=pltpu.CompilerParams(vmem_limit_bytes=32 * 2**20),
        name="finish",
    )(result, tokens, *weights, gains)
    return tuple(outs[:9]) + (outs[9].reshape(width), outs[10].reshape(width))


def per_device(
    nctx,
    nf,
    tokens,
    query_weight,
    key_projection,
    value_projection,
    output_weight,
    gate_weight,
    up_weight,
    down_weight,
    norm_attn,
    norm_mlp,
    doc_starts,
    cotangent,
):
    token_rows, width = tokens.shape
    n_tokens = token_rows * nctx * nf
    bf16, f32 = jnp.bfloat16, jnp.float32

    own_device = lax.axis_index(AXES)
    own_index = layout_rows(own_device, token_rows)
    own_begin = doc_begin(own_index, doc_starts)
    cosine_table, sine_table = rope_tables(own_index - own_begin)
    cosine_table, sine_table = cosine_table.T, sine_table.T
    gains = jnp.pad(jnp.stack([norm_attn, norm_mlp]).astype(f32), ((0, 6), (0, 0)))
    (
        query_rot, key_values, attn_low, attn_exact, log_total, qkv_full, output_full, gate_up,
        cotangents, attention_input, inv_attn, gains,
    ) = forward(
        nctx, nf, doc_starts, tokens, gains, cosine_table, sine_table, query_weight, key_projection,
        value_projection, output_weight, gate_weight, up_weight, cotangent,
    )
    key_width = KEY_VALUE_HEADS * HEAD_SIZE
    key_values = key_values.reshape(n_tokens, 2 * key_width)
    result, grad_resid, grad_branch, grad_attn, gain_mlp_partial, gate_up_partial, down_partial, inputs_all = feed_forward(
        nctx, nf, tokens, attn_low, attention_input, gains, output_full, gate_up, down_weight,
        cotangents.reshape(2 * nf, token_rows, width),
    )

    tokens_grad, query_sum, key_sum, value_sum, gain_sums, gate_sum, up_sum, down_sum, output_sum = backward(
        nctx, nf, doc_starts, query_rot, grad_attn, attn_exact, log_total, key_values, qkv_full,
        cosine_table, sine_table, tokens, inv_attn, gains, grad_resid,
        gain_mlp_partial, attn_low, grad_branch, gate_up_partial, down_partial,
        inputs_all.reshape(nctx, token_rows, width),
    )

    return finish(
        nf, width, result, tokens_grad, query_sum, key_sum, value_sum, output_sum, gate_sum, up_sum,
        down_sum, gain_sums,
    )


def solution(mesh):
    return jax.shard_map(
        functools.partial(per_device, mesh.shape["ctx"], mesh.shape["fsdp"]),
        mesh=mesh,
        in_specs=(
            P(("ctx", "fsdp"), None),
            P("fsdp", None),
            P("fsdp", None),
            P("fsdp", None),
            P("fsdp", None),
            P("fsdp", None),
            P("fsdp", None),
            P("fsdp", None),
            P("fsdp"),
            P("fsdp"),
            P(),
            P(("ctx", "fsdp"), None),
        ),
        out_specs=(
            P(("ctx", "fsdp"), None),
            P(("ctx", "fsdp"), None),
            P("fsdp", "ctx"),
            P("fsdp", "ctx"),
            P("fsdp", "ctx"),
            P("fsdp", "ctx"),
            P("fsdp", "ctx"),
            P("fsdp", "ctx"),
            P("fsdp", "ctx"),
            P(),
            P(),
        ),
        check_vma=False,
    )
```

```python
import functools
import math

import jax
import jax.numpy as jnp
from jax import lax
from jax.experimental import pallas as pl
from jax.experimental.pallas import tpu as pltpu
from jax.sharding import PartitionSpec as P

QUERY_HEADS = 18
KEY_VALUE_HEADS = 6
HEAD_SIZE = 64
HS = HEAD_SIZE

EPS = 1e-05
THETA = 10000.0
NEG = -1e30
AXES = ("ctx", "fsdp")


def rope_tables(positions):
    half_dim = HEAD_SIZE // 2
    frequency = jnp.exp(-math.log(THETA) * jnp.arange(half_dim, dtype=jnp.float32) / half_dim)
    angles = positions.astype(jnp.float32)[:, None] * frequency[None, :]
    return (jnp.cos(angles), jnp.sin(angles))


def apply_rotary(values, cosine_table, sine_table):
    half_dim = values.shape[-1] // 2
    first_half = values[..., :half_dim]
    second_half = values[..., half_dim:]
    cos_rows = cosine_table[:, None, :]
    sin_rows = sine_table[:, None, :]
    return jnp.concatenate(
        [
            first_half * cos_rows - second_half * sin_rows,
            second_half * cos_rows + first_half * sin_rows,
        ],
        axis=-1,
    )


def unrotate(values, cosine_table, sine_table):
    half_dim = values.shape[-1] // 2
    first_half = values[..., :half_dim]
    second_half = values[..., half_dim:]
    cos_rows = cosine_table[:, None, :]
    sin_rows = sine_table[:, None, :]
    return jnp.concatenate(
        [
            first_half * cos_rows + second_half * sin_rows,
            second_half * cos_rows - first_half * sin_rows,
        ],
        axis=-1,
    )


def doc_begin(indices, doc_starts):
    marked = jnp.where(indices[:, None] >= doc_starts[None, :], doc_starts[None, :], 0)
    return jnp.max(marked, axis=1)


def layout_rows(device, row_count):
    return device * row_count + jnp.arange(row_count, dtype=jnp.int32)


def heads_rows(natural):
    return jnp.transpose(natural.astype(jnp.float32))
def padded(rows, heads, g):
    top = jnp.concatenate([rows[HS*(heads*g+j):HS*(heads*g+j+1)] for j in range(heads)], axis=1)
    z = jnp.zeros_like(top)
    return jnp.concatenate([top, z] if g == 0 else [z, top], axis=0)
def head_lanes(per_group, heads, tq):
    return jnp.transpose(jnp.concatenate([per_group[g][:, tq*j:tq*(j+1)] for g in range(2) for j in range(heads)], axis=0))
def bias_tile(info, docs, first, bk, tq):
    query = info[0] + lax.broadcasted_iota(jnp.int32, (1, tq), 1)
    begin = jnp.zeros((1, tq), jnp.int32)
    for i in range(docs.shape[0]):
        begin = jnp.maximum(begin, jnp.where(query >= docs[i], docs[i], 0))
    key = first + lax.broadcasted_iota(jnp.int32, (bk, 1), 0)
    return jnp.where((key <= query) & (key >= begin), 0.0, NEG)


def line_dims(count):
    fours = 0
    while count % 4 == 0:
        count //= 4
        fours += 1
    return ([count] if count > 1 else []) + [4] * fours


def rotate_back(rows, cos_rows, sin_rows):
    half_dim = HS // 2
    first, second = rows[:half_dim], rows[half_dim:]
    return jnp.concatenate(
        [first * cos_rows + second * sin_rows, second * cos_rows - first * sin_rows], axis=0
    )


def w_order(lines):
    return [lines[-2]] + lines[1:-2] + [lines[0], lines[-1]]


def bit_dims(count):
    return [2] * (count.bit_length() - 1)


def round_up(value, unit):
    return -(-value // unit) * unit


def backward_kernel(plan, docs, q_ref, do_ref, ot_ref, lse_ref, kv_hbm, w_ref, cos_ref, sin_ref,
                    normed_ref, inv_ref, gain_ref, gres_ref, gmlp_ref, low_ref, branch_ref, gup_hbm, dnp_hbm, inputs_hbm,
                    tokens_ref, query_ref, key_ref, value_ref, gains_out, gate_ref, up_ref, down_ref, out_ref,
                    kvbuf, dkv, acc_ref, gqt_ref, ga_ref, qblk, kvblk, small,
                    load_sem, send_sem, recv_sem, col_send, col_recv, own_sem, credit,
                    wg, wd, wo, brs, lows, halves, fin, fin_in, dsend, din,
                    colq_ref, colkv_ref, gains_ref, cols_acc, half_send, half_in, gain_send, gain_in, in_sem,
                    g_send, g_recv, w_load, w_send, w_recv, top_send, top_recv, fin_send, fin_recv, *recvs):
    nctx, nf, parts, heads, tq, slots = plan
    plane = nctx // 2
    n = nctx * nf
    dims = bit_dims(plane)
    nd = len(dims)
    bk = 2 * nf * tq
    me_c, me_f = lax.axis_index("ctx"), lax.axis_index("fsdp")
    me = me_c * nf + me_f
    core, place = lax.rem(me_c, 2), me_c // 2
    mesh_id = pl.DeviceIdType.MESH
    half_dim = HS // 2

    def target(k):
        other = lax.rem(me + k, n)
        return other, {"ctx": other // nf, "fsdp": lax.rem(other, nf)}

    barrier = pltpu.get_barrier_semaphore()

    def greet(k, carry):
        pl.semaphore_signal(barrier, inc=1, device_id=target(k)[1], device_id_type=mesh_id)
        return carry

    lax.fori_loop(1, n, greet, 0)

    def loads(p):
        s = p % slots
        return [
            pltpu.make_async_copy(
                kv_hbm.at[:, pl.ds((kind * parts + p) * 2 * HS, 2 * HS)],
                kvbuf.at[s, kind], load_sem.at[s, kind],
            )
            for kind in range(2)
        ]

    resident = slots == parts

    def block_loads(p, j):
        slot = lax.rem(j, 2)
        return [
            pltpu.make_async_copy(
                kv_hbm.at[pl.ds(pl.multiple_of(j * bk, bk), bk), pl.ds((kind * parts + p) * 2 * HS, 2 * HS)],
                kvbuf.at[slot, kind], load_sem.at[slot, kind],
            )
            for kind in range(2)
        ]

    if resident:
        for p in range(parts):
            for copy in loads(p):
                copy.start()

    def dim_axis(i):
        stride = math.prod(dims[:i])
        size = dims[i]
        own = lax.rem(place // stride, size)

        def peer(k):
            there = lax.rem(own + k, size)
            return there, {"ctx": (place + (there - own) * stride) * 2 + core, "fsdp": me_f}

        return (nd - 1 - i, size, own, peer)

    core_axis = (nd, 2, core, lambda k: (1 - core, {"ctx": place * 2 + 1 - core, "fsdp": me_f}))
    side_axis = (nd + 1, 2, me_f, lambda k: (1 - me_f, {"ctx": me_c, "fsdp": 1 - me_f}))
    lines = [dim_axis(i) for i in range(nd)]
    orders = [[core_axis, side_axis] + lines, [core_axis, side_axis] + w_order(lines)]
    stages = nd + 2
    wrecvs = recvs[2 * stages :]
    side_at, mate_at = side_axis[3](1)[1], core_axis[3](1)[1]

    low_bits = nd - 2
    arrays = ((wg, gup_hbm, (0,)), (wd, dnp_hbm, ()), (wo, None, ()), (wg, gup_hbm, (1,)))
    w_lines = [lines, w_order(lines), w_order(lines), lines]

    def chunk_at(a, k):
        near, far_line = w_lines[a][nd - 2], w_lines[a][nd - 1]
        far_bit = far_line[2] if k % 2 else 1 - far_line[2]
        near_bit = near[2] if k // 2 else 1 - near[2]
        return far_bit, near_bit

    def w_region(a, k, stage, at):
        index = [slice(None)] * nd
        index[w_lines[a][nd - 1][0]], index[w_lines[a][nd - 2][0]] = chunk_at(a, k)
        for axis in w_lines[a][:stage]:
            index[axis[0]] = axis[2]
        if stage < low_bits:
            index[w_lines[a][stage][0]] = at
        return tuple(index)

    def held(a, index):
        first = w_lines[a][0][0]
        return index if a == 2 else index[:first] + index[first + 1 :] + arrays[a][2]

    def w_copy(a, k, stage):
        buf, far, sub = arrays[a]
        there, where = w_lines[a][stage][3](1)
        index = w_region(a, k, stage, there)
        return pltpu.make_async_remote_copy(
            src_ref=far.at[index + sub] if stage == 0 and a != 2 else buf.at[held(a, index)],
            dst_ref=wrecvs[a * (low_bits + 2) + stage].at[chunk_at(a, k)],
            send_sem=w_send.at[a, k, stage], recv_sem=w_recv.at[a, k, stage],
            device_id=where, device_id_type=mesh_id,
        )

    def near_copy(a, i):
        return pltpu.make_async_remote_copy(
            src_ref=arrays[a][0].at[held(a, w_region(a, i, low_bits, 0))], dst_ref=wrecvs[a * (low_bits + 2) + low_bits].at[i],
            send_sem=top_send.at[a, i], recv_sem=top_recv.at[a, i],
            device_id=w_lines[a][nd - 2][3](1)[1], device_id_type=mesh_id,
        )

    def far_copy(a):
        return pltpu.make_async_remote_copy(
            src_ref=arrays[a][0].at[held(a, w_region(a, 2, low_bits, 0))], dst_ref=wrecvs[a * (low_bits + 2) + low_bits + 1].at[0],
            send_sem=top_send.at[a, 2], recv_sem=top_recv.at[a, 2],
            device_id=w_lines[a][nd - 1][3](1)[1], device_id_type=mesh_id,
        )

    def w_start(which, k):
        for a in which:
            w_copy(a, k, 0).start()

    def w_finish(which, k):
        for a in which:
            buf = arrays[a][0]
            for stage in range(low_bits):
                w_copy(a, k, stage).wait()
                where = held(a, w_region(a, k, stage, w_lines[a][stage][2]))
                got = wrecvs[a * (low_bits + 2) + stage]
                buf[where] = (
                    buf[where].astype(jnp.float32) + got[chunk_at(a, k)].astype(jnp.float32)
                ).astype(buf.dtype)
                if stage + 1 < low_bits:
                    w_copy(a, k, stage + 1).start()
            if k < 2:
                near_copy(a, k).start()
            elif k == 2:
                near_copy(a, 0).wait()
                where = held(a, w_region(a, 2, low_bits, 0))
                buf[where] = (
                    buf[where].astype(jnp.float32)
                    + wrecvs[a * (low_bits + 2) + low_bits][0].astype(jnp.float32)
                ).astype(buf.dtype)
                far_copy(a).start()

    def w_total(a):
        near_copy(a, 1).wait()
        far_copy(a).wait()
        total = arrays[a][0][held(a, w_region(a, 3, low_bits, 0))].astype(jnp.float32)
        total = total + wrecvs[a * (low_bits + 2) + low_bits][1].astype(jnp.float32)
        return total + wrecvs[a * (low_bits + 2) + low_bits + 1][0].astype(jnp.float32)

    w_loads = [
        pltpu.make_async_copy(far.at[(slice(None),) * w_lines[i][0][0] + (w_lines[i][0][2],)], buf, w_load.at[i])
        for i, (buf, far, _) in enumerate(arrays[:2])
    ]
    for copy in w_loads:
        copy.start()
    half = low_ref.shape[1] // nf
    low_all = low_ref[...]
    halves[0] = low_all[:, :half]
    halves[1] = low_all[:, half:]
    lows[0] = halves[me_f]
    brs[0] = branch_ref[...]

    def g_copy(i, src, dst, where):
        return pltpu.make_async_remote_copy(
            src_ref=src, dst_ref=dst, send_sem=g_send.at[i], recv_sem=g_recv.at[i],
            device_id=where, device_id_type=mesh_id,
        )

    low_side = g_copy(0, halves.at[1 - me_f], lows.at[1], side_at)
    br_side = g_copy(1, brs.at[0], brs.at[1], side_at)
    low_core = g_copy(2, lows.at[pl.ds(0, 2)], lows.at[pl.ds(2, 2)], mate_at)
    br_core = g_copy(3, brs.at[pl.ds(0, 2)], brs.at[pl.ds(2, 2)], mate_at)

    def output_partial():
        low_core.wait()
        br_core.wait()
        rows = jnp.transpose(brs[...].reshape(4 * tq, brs.shape[2]))
        unit = brs.shape[2] // nctx
        wo[...] = jnp.zeros_like(wo)
        low_rows = lows[...].reshape(4 * tq, half)
        batch = plane // 4
        for r in range(plane):
            first = 2 * unit * (r % batch)
            if first == 0:
                chunk = 2 * unit * batch
                part = jnp.dot(
                    rows[2 * unit * r : 2 * unit * r + chunk], low_rows, preferred_element_type=jnp.float32
                )
            piece = jnp.where(core == 0, part[first : first + unit], part[first + unit : first + 2 * unit])
            wo[static_index(dims, r) + (slice(0, unit), slice(0, half))] = piece.astype(wo.dtype)

    pl.semaphore_wait(barrier, n - 1)
    low_side.start()
    br_side.start()
    for k in range(4):
        w_start((0, 3, 1) if k < 2 else (1,), k)

    def region(kind, stage, at):
        index = [slice(None)] * (nd + 2)
        for axis in orders[kind][:stage]:
            index[axis[0]] = axis[2]
        index[orders[kind][stage][0]] = at
        return tuple(index)

    def stage_copies(p, kind, stage):
        s = p % slots
        axis = orders[kind][stage]
        copies = []
        for k in range(1, axis[1]):
            there, where = axis[3](k)
            copies.append(
                pltpu.make_async_remote_copy(
                    src_ref=dkv.at[(s, kind) + region(kind, stage, there)],
                    dst_ref=recvs[kind * stages + stage].at[s, k - 1],
                    send_sem=send_sem.at[s, kind, stage, k - 1],
                    recv_sem=recv_sem.at[s, kind, stage, k - 1],
                    device_id=where, device_id_type=mesh_id,
                )
            )
        return copies

    def stage_start(p, stage):
        for kind in range(2):
            for copy in stage_copies(p, kind, stage):
                copy.start()

    finals = {}

    def stage_finish(p, stage):
        s = p % slots
        for kind in range(2):
            axis = orders[kind][stage]
            for copy in stage_copies(p, kind, stage):
                copy.wait()
            where = region(kind, stage, axis[2])
            got = recvs[kind * stages + stage]
            free = [i for i in range(nd + 2) if isinstance(where[i], slice)]

            def add(index, lead):
                total = dkv[(s, kind) + index].astype(jnp.float32)
                for k in range(axis[1] - 1):
                    total = total + got[(s, k) + lead].astype(jnp.float32)
                return total

            if not free:
                finals[p, kind] = add(where, ())
            else:
                size = dkv.shape[2 + free[0]]

                def one(i, carry):
                    index = list(where)
                    index[free[0]] = i
                    index = tuple(index)
                    dkv[(s, kind) + index] = add(index, (i,)).astype(dkv.dtype)
                    return carry

                lax.fori_loop(0, size, one, 0)

    def place_index(j):
        index = []
        for i in reversed(range(nd)):
            index.append(lax.rem(j // math.prod(dims[:i]), dims[i]))
        return tuple(index)

    start = me * tq
    last = (start + tq - 1) // bk + 1

    def compute(p):
        s = p % slots
        span = slice(2 * heads * HS * p, 2 * heads * HS * (p + 1))
        qt = q_ref[span, :].astype(jnp.float32) * (1.0 / 8.0)
        dt = heads_rows(do_ref[:, span])
        qg = [padded(qt, heads, g) for g in range(2)]
        dg = [padded(dt, heads, g) for g in range(2)]
        qrows = jnp.concatenate([jnp.transpose(x) for x in qg], axis=0).astype(jnp.bfloat16)
        drows = jnp.concatenate([jnp.transpose(x) for x in dg], axis=0).astype(jnp.bfloat16)
        delta = [
            jnp.sum(dg[g][HS * g : HS * (g + 1)] * ot_ref[2 * p + g], axis=0, keepdims=True)
            for g in range(2)
        ]
        lse = [lse_ref[2 * p + g] for g in range(2)]
        qg = [x.astype(jnp.bfloat16) for x in qg]
        dg = [x.astype(jnp.bfloat16) for x in dg]
        acc_ref[...] = jnp.zeros_like(acc_ref)
        for copy in loads(p) if resident else block_loads(p, 0):
            if not resident:
                copy.start()
            else:
                copy.wait()

        def zero(j, carry):
            at = place_index(j)
            for kind in range(2):
                dkv[(s, kind) + at] = jnp.zeros((2, nf, tq, 2 * HS), dkv.dtype)
            return carry

        def body(j, carry):
            first = pl.multiple_of(j * bk, bk)
            if resident:
                kb = kvbuf[s, 0, pl.ds(first, bk), :]
                vb = kvbuf[s, 1, pl.ds(first, bk), :]
            else:
                for copy in block_loads(p, j):
                    copy.wait()

                @pl.when(j + 1 < last)
                def _():
                    for copy in block_loads(p, j + 1):
                        copy.start()

                kb, vb = kvbuf[lax.rem(j, 2), 0], kvbuf[lax.rem(j, 2), 1]
            kt = jnp.transpose(kb)
            bias = bias_tile((start,), docs, first, bk, tq)
            bias = jnp.concatenate([bias] * heads, axis=1)
            ps = []
            dss = []
            for g in range(2):
                score = jnp.dot(kb, qg[g], preferred_element_type=jnp.float32)
                prob = jnp.exp(score + (bias - lse[g]))
                dp = jnp.dot(vb, dg[g], preferred_element_type=jnp.float32)
                ds = (prob * (dp - delta[g])).astype(jnp.bfloat16)
                ps.append(prob.astype(jnp.bfloat16))
                dss.append(ds)
                acc_ref[g] += jnp.dot(kt[HS * g : HS * (g + 1)], ds, preferred_element_type=jnp.float32)
            dv = jnp.dot(jnp.concatenate(ps, axis=1), drows, preferred_element_type=jnp.float32)
            dk = jnp.dot(jnp.concatenate(dss, axis=1), qrows, preferred_element_type=jnp.float32)
            at = place_index(j)
            dkv[(s, 0) + at] = dk.astype(dkv.dtype).reshape(2, nf, tq, 2 * HS)
            dkv[(s, 1) + at] = dv.astype(dkv.dtype).reshape(2, nf, tq, 2 * HS)
            return carry

        lax.fori_loop(last, plane, zero, 0)
        lax.fori_loop(0, last, body, 0)
        cos_rows = jnp.concatenate([cos_ref[...]] * heads, axis=1) * (1.0 / 8.0)
        sin_rows = jnp.concatenate([sin_ref[...]] * heads, axis=1) * (1.0 / 8.0)
        for g in range(2):
            back = rotate_back(acc_ref[g], cos_rows, sin_rows).astype(gqt_ref.dtype)
            for j in range(heads):
                h = (2 * p + g) * heads + j
                gqt_ref[HS * h : HS * (h + 1), :] = back[:, tq * j : tq * (j + 1)]

    peers = 2 + sum(size - 1 for size in dims)

    def all_peers():
        found = [core_axis[3](1)[1], side_axis[3](1)[1]]
        for axis in lines:
            found += [axis[3](k)[1] for k in range(1, axis[1])]
        return found

    progress = {}

    def advance(p):
        stage = progress[p]
        stage_finish(p, stage)
        progress[p] = stage + 1
        if stage + 1 < stages:
            stage_start(p, stage + 1)
        else:
            del progress[p]
            if p + slots < parts:
                for where in all_peers():
                    pl.semaphore_signal(credit, inc=1, device_id=where, device_id_type=mesh_id)

    for p in range(parts):
        if p >= slots:
            while p - slots in progress:
                advance(p - slots)
        compute(p)
        if p >= slots:
            pl.semaphore_wait(credit, peers)
        stage_start(p, 0)
        progress[p] = 0
        for older in [o for o in progress if o < p]:
            advance(older)
        if p == 0:
            low_side.wait()
            br_side.wait()
            low_core.start()
            br_core.start()
        if p == 1:
            for copy in w_loads:
                copy.wait()
            for k in range(2):
                w_finish((0, 3), k)
                w_start((0, 3), k + 2)
    for k in range(2):
        w_finish((1,), k)
    output_partial()

    def copies_to(k, which):
        other = lax.rem(me_c + k, nctx)
        where = {"ctx": other, "fsdp": me_f}
        block, out = ((qblk, colq_ref), (kvblk, colkv_ref), (small, gains_ref))[which]
        return pltpu.make_async_remote_copy(
            src_ref=block if which == 2 else block.at[other], dst_ref=out.at[me_c],
            send_sem=col_send.at[which, k], recv_sem=col_recv.at[which, k],
            device_id=where, device_id_type=mesh_id,
        )

    def share(which):
        def one(k, carry):
            copies_to(k, which).start()
            return carry

        block, out = ((qblk, colq_ref), (kvblk, colkv_ref), (small, gains_ref))[which]
        pltpu.make_async_copy(block if which == 2 else block.at[me_c], out.at[me_c], own_sem.at[which]).start()
        lax.fori_loop(1, nctx, one, 0)

    def share_wait(which):
        def one(k, carry):
            copies_to(k, which).wait()
            return carry

        block, out = ((qblk, colq_ref), (kvblk, colkv_ref), (small, gains_ref))[which]
        pltpu.make_async_copy(block if which == 2 else block.at[me_c], out.at[me_c], own_sem.at[which]).wait()
        lax.fori_loop(1, nctx, one, 0)

    width_q = 2 * parts * heads * HS
    width_k = 2 * parts * HS
    cq, ck = width_q // nctx, width_k // nctx
    qblk[...] = jnp.zeros_like(qblk)
    kvblk[...] = jnp.zeros_like(kvblk)
    for i in range(nctx):
        qblk[i, 0:cq, :] = gqt_ref[cq * i : cq * (i + 1), :]
    share(0)
    ga_ref[...] = jnp.dot(w_ref[:, :width_q], gqt_ref[...], preferred_element_type=jnp.float32)
    for k in range(4):
        w_start((2,), k)
    pq, pk = qblk.shape[1], kvblk.shape[1]

    def columns(col_ref, first, count):
        def fetch(i, slot):
            return pltpu.make_async_copy(
                inputs_hbm.at[i], brs.at[slot], in_sem.at[slot]
            )

        fetch(0, 0).start()
        cols_acc[first : first + count, :] = jnp.zeros((count, cols_acc.shape[1]), jnp.float32)

        def one(i, carry):
            slot = lax.rem(i, 2)

            @pl.when(i + 1 < nctx)
            def _():
                fetch(i + 1, 1 - slot).start()

            fetch(i, slot).wait()
            cols_acc[first : first + count, :] += jnp.dot(
                col_ref[i], brs[slot], preferred_element_type=jnp.float32
            )
            return carry

        lax.fori_loop(0, nctx, one, 0)

    per_side = plane // 2
    home = (2 * me_f + core) * per_side + place // 2
    slot = lax.rem(place, 2)

    def home_copy(kind, s):
        return pltpu.make_async_remote_copy(
            src_ref=fin.at[kind, s], dst_ref=fin_in.at[kind, slot],
            send_sem=fin_send.at[kind, s], recv_sem=fin_recv.at[kind, slot],
            device_id={"ctx": home, "fsdp": jnp.int32(s)}, device_id_type=mesh_id,
        )

    def self_copy(kind, s):
        return pltpu.make_async_copy(fin.at[kind, s], fin_in.at[kind, slot], fin_send.at[kind, s])

    def to_homes(kind, a):
        total = w_total(a)
        unit, lanes = fin.shape[2], fin.shape[3]
        blank = jnp.zeros((unit, lanes - half), fin.dtype)
        for s in range(2):
            fin[kind, s] = jnp.concatenate([total[:, half * s : half * (s + 1)].astype(fin.dtype), blank], axis=1)
            at_home = (home == me_c) & (me_f == s)

            @pl.when(jnp.logical_not(at_home))
            def _():
                home_copy(kind, s).start()

            @pl.when(at_home)
            def _():
                self_copy(kind, s).start()

    turn = 0
    while progress:
        for p in list(progress):
            advance(p)
        if turn == 0:
            for k in range(2, 4):
                w_finish((0, 3, 1), k)
        if turn == 1:
            for k in range(2):
                w_finish((2,), k)
        if turn == 2:
            for k in range(2, 4):
                w_finish((2,), k)
        turn += 1

    cos_rows, sin_rows = cos_ref[...], sin_ref[...]
    grads = []
    for kind in range(2):
        rows = []
        for p in range(parts):
            both = jnp.transpose(finals[p, kind])
            for g in range(2):
                one = both[HS * g : HS * (g + 1)]
                rows.append(rotate_back(one, cos_rows, sin_rows) if kind == 0 else one)
        grads.append(jnp.concatenate(rows, axis=0).astype(jnp.bfloat16))
    for i in range(nctx):
        kvblk[i, 0:ck, :] = grads[0][ck * i : ck * (i + 1)]
        kvblk[i, ck : 2 * ck, :] = grads[1][ck * i : ck * (i + 1)]
    share(1)
    grad_t = (
        ga_ref[...]
        + jnp.dot(w_ref[:, width_q : width_q + width_k], grads[0], preferred_element_type=jnp.float32)
        + jnp.dot(w_ref[:, width_q + width_k :], grads[1], preferred_element_type=jnp.float32)
    )
    grad = jnp.transpose(grad_t)
    normed = normed_ref[...].astype(jnp.float32) * inv_ref[...]
    product = grad * normed
    gain_sum = jnp.sum(product, axis=0, keepdims=True)
    lanes = 128
    tiles = gain_sum.shape[1] // lanes
    rows = [gain_sum[:, lanes * i : lanes * (i + 1)] for i in range(tiles)]
    rows += [gmlp_ref[:, lanes * i : lanes * (i + 1)] for i in range(tiles)]
    rows += [jnp.zeros((small.shape[0] - 2 * tiles, lanes), jnp.float32)]
    small[...] = jnp.concatenate(rows, axis=0)
    share(2)
    gain = gain_ref[0:1, :]
    scaled = grad * gain
    mean = jnp.mean(scaled * normed, axis=1, keepdims=True)
    tokens_ref[...] = gres_ref[...] + inv_ref[...] * (scaled - normed * mean)

    to_homes(0, 0)
    share_wait(0)
    columns(colq_ref, 0, pq)
    to_homes(1, 3)
    dsum = w_total(1)
    dsend[...] = dsum.astype(dsend.dtype)
    down_copy = g_copy(4, dsend, din, mate_at)
    down_copy.start()
    osum = w_total(2)
    out_ref[...] = osum[: out_ref.shape[0], :half]
    share_wait(1)
    columns(colkv_ref, pq, pk)
    left, right = cols_acc[:, :half], cols_acc[:, half:]
    side_pad = jnp.zeros((pq + pk, half_send.shape[1] - half), half_send.dtype)
    half_send[...] = jnp.concatenate([jnp.where(me_f == 0, right, left).astype(half_send.dtype), side_pad], axis=1)
    half_copy = g_copy(5, half_send, half_in, side_at)
    half_copy.start()
    share_wait(2)
    gain_total = gains_ref[0]
    for i in range(1, nctx):
        gain_total = gain_total + gains_ref[i]
    gain_send[...] = gain_total
    gain_copy = g_copy(6, gain_send, gain_in, side_at)
    gain_copy.start()
    half_copy.wait()
    own_half = jnp.where(me_f == 0, cols_acc[:, :half], cols_acc[:, half:])
    rows = own_half + half_in[:, :half].astype(jnp.float32)
    query_ref[...] = rows[:cq]
    key_ref[...] = rows[pq : pq + ck]
    value_ref[...] = rows[pq + ck : pq + 2 * ck]
    gain_copy.wait()
    gains_out[...] = gain_send[...] + gain_in[...]
    down_copy.wait()
    cols = down_ref.shape[0]

    def unfold(folded):
        return jnp.concatenate(
            [folded[2 * cols * i : 2 * cols * (i + 1)] for i in range(folded.shape[0] // (2 * cols))], axis=1
        )

    dsum, got = unfold(dsum), unfold(din[...].astype(jnp.float32))
    own_cols = jnp.where(core == 0, dsum[:cols], dsum[cols:])
    far_cols = jnp.where(core == 0, got[:cols], got[cols:])
    down_ref[...] = jnp.where(
        core == 0,
        jnp.concatenate([own_cols, far_cols], axis=1),
        jnp.concatenate([far_cols, own_cols], axis=1),
    )
    owner = me_c // per_side
    for kind in range(2):
        for s in range(2):
            at_home = (home == me_c) & (me_f == s)

            @pl.when(jnp.logical_not(at_home))
            def _():
                home_copy(kind, s).wait_send()

            @pl.when(at_home)
            def _():
                self_copy(kind, s).wait()

        for h in range(2):
            holder = (2 * lax.rem(me_c, per_side) + h) * 2 + lax.rem(owner, 2)

            @pl.when(jnp.logical_not((holder == me_c) & (owner // 2 == me_f)))
            def _():
                pltpu.make_async_remote_copy(
                    src_ref=fin.at[0, 0], dst_ref=fin_in.at[kind, h],
                    send_sem=fin_send.at[0, 0], recv_sem=fin_recv.at[kind, h],
                    device_id={"ctx": home, "fsdp": me_f}, device_id_type=mesh_id,
                ).wait_recv()

    for kind, ref in ((0, gate_ref), (1, up_ref)):
        rows = jnp.concatenate([fin_in[kind, 0], fin_in[kind, 1]], axis=0).astype(jnp.float32)
        ref[...] = rows[:, :half]


def backward(nctx, nf, docs, q, do, ot, lse, kv, w, cos_t, sin_t, normed, inv, gain, gres, gmlp, low, branch, gup, dnp, inputs):
    width_q, tq = q.shape
    n_tokens, width_kv = kv.shape
    n = nctx * nf
    parts = width_kv // (4 * HS)
    heads = width_q // HS // (2 * parts)
    dims = bit_dims(nctx // 2)
    lead = tuple(reversed(dims))
    part_bytes = n_tokens * 2 * HS * 2
    slots = parts if parts * part_bytes * 5 <= 24 * 2**20 else 1
    nd = len(dims)
    bf16, f32 = jnp.bfloat16, jnp.float32
    axes = {"core": (nd, 2), "side": (nd + 1, nf)}
    line = [(nd - 1 - i, dims[i]) for i in range(nd)]
    orders = [
        [axes["core"], axes["side"]] + line,
        [axes["core"], axes["side"]] + w_order(line),
    ]
    recvs = []
    for order in orders:
        left = list(lead) + [2, nf]
        for position, size in order:
            left[position] = None
            recvs.append(
                pltpu.VMEM((slots, size - 1) + tuple(x for x in left if x) + (tq, 2 * HS), bf16)
            )
    model_width = low.shape[1]
    half = model_width // nf
    unit, deep = gup.shape[-2], model_width // (nctx // 2)
    quarter = dnp.shape[-2] // deep * 128
    plane = nctx // 2
    tails = [gup.shape[nd:], dnp.shape[nd:], (round_up(deep // 2, 16), round_up(half, 128))]
    for tail in (tails[0][1:], tails[1], tails[2], tails[0][1:]):
        for stage in range(nd - 2):
            recvs.append(pltpu.VMEM((2,) * (nd - 1 - stage) + tail, bf16))
        recvs += [pltpu.VMEM((2,) + tail, bf16), pltpu.VMEM((1,) + tail, bf16)]
    stages = nd + 2
    most = max(dims + [2])
    pq = round_up(width_q // nctx, 16)
    pk = round_up(2 * (2 * parts * HS) // nctx, 16)
    model = w.shape[0]
    sr = round_up(2 * model // 128, 8)
    vmem = pl.BlockSpec(memory_space=pltpu.VMEM)
    smem = pl.BlockSpec(memory_space=pltpu.SMEM)
    hbm = pl.BlockSpec(memory_space=pl.ANY)
    return pl.pallas_call(
        functools.partial(backward_kernel, (nctx, nf, parts, heads, tq, slots)),
        out_shape=[
            jax.ShapeDtypeStruct((tq, model), f32),
            jax.ShapeDtypeStruct((width_q // nctx, half), f32),
            jax.ShapeDtypeStruct((2 * parts * HS // nctx, half), f32),
            jax.ShapeDtypeStruct((2 * parts * HS // nctx, half), f32),
            jax.ShapeDtypeStruct((sr, 128), f32),
            jax.ShapeDtypeStruct((2 * unit, half), f32),
            jax.ShapeDtypeStruct((2 * unit, half), f32),
            jax.ShapeDtypeStruct((deep // 2, 2 * quarter), f32),
            jax.ShapeDtypeStruct((deep // 2, half), f32),
        ],
        in_specs=[smem, vmem, vmem, vmem, vmem, hbm] + [vmem] * 10 + [hbm] * 3,
        out_specs=[vmem] * 9,
        scratch_shapes=[
            pltpu.VMEM((slots, 2, n_tokens, 2 * HS) if slots == parts else (2, 2, 2 * nf * tq, 2 * HS), bf16),
            pltpu.VMEM((slots, 2) + lead + (2, nf, tq, 2 * HS), bf16),
            pltpu.VMEM((2, HS, heads * tq), f32),
            pltpu.VMEM((width_q, tq), bf16),
            pltpu.VMEM((model, tq), f32),
            pltpu.VMEM((nctx, pq, tq), bf16),
            pltpu.VMEM((nctx, pk, tq), bf16),
            pltpu.VMEM((sr, 128), f32),
            pltpu.SemaphoreType.DMA((max(slots, 2), 2)),
            pltpu.SemaphoreType.DMA((slots, 2, stages, most - 1)),
            pltpu.SemaphoreType.DMA((slots, 2, stages, most - 1)),
            pltpu.SemaphoreType.DMA((3, nctx)),
            pltpu.SemaphoreType.DMA((3, nctx)),
            pltpu.SemaphoreType.DMA((3,)),
            pltpu.SemaphoreType.REGULAR,
            pltpu.VMEM(lead[:-1] + tails[0], bf16),
            pltpu.VMEM(lead[:-1] + tails[1], bf16),
            pltpu.VMEM(lead + tails[2], bf16),
            pltpu.VMEM((4,) + branch.shape, bf16),
            pltpu.VMEM((4, tq, half), bf16),
            pltpu.VMEM((2, tq, half), bf16),
            pltpu.VMEM((2, 2, unit, round_up(half, 128)), bf16),
            pltpu.VMEM((2, 2, unit, round_up(half, 128)), bf16),
            pltpu.VMEM(tails[1], bf16),
            pltpu.VMEM(tails[1], bf16),
            pltpu.VMEM((nctx, pq, tq), bf16),
            pltpu.VMEM((nctx, pk, tq), bf16),
            pltpu.VMEM((nctx, sr, 128), f32),
            pltpu.VMEM((pq + pk, model), f32),
            pltpu.VMEM((pq + pk, round_up(half, 128)), bf16),
            pltpu.VMEM((pq + pk, round_up(half, 128)), bf16),
            pltpu.VMEM((sr, 128), f32),
            pltpu.VMEM((sr, 128), f32),
            pltpu.SemaphoreType.DMA((2,)),
            pltpu.SemaphoreType.DMA((7,)),
            pltpu.SemaphoreType.DMA((7,)),
            pltpu.SemaphoreType.DMA((2,)),
            pltpu.SemaphoreType.DMA((4, 4, max(nd - 2, 1))),
            pltpu.SemaphoreType.DMA((4, 4, max(nd - 2, 1))),
            pltpu.SemaphoreType.DMA((4, 3)),
            pltpu.SemaphoreType.DMA((4, 3)),
            pltpu.SemaphoreType.DMA((2, 2)),
            pltpu.SemaphoreType.DMA((2, 2)),
        ]
        + recvs,
        compiler_params=pltpu.CompilerParams(
            collective_id=1, has_side_effects=True, vmem_limit_bytes=63 * 2**20
        ),
        cost_estimate=pl.CostEstimate(flops=10**10, bytes_accessed=3 * 10**7, transcendentals=10**7),
        name="backward",
    )(docs, q, do, ot, lse, kv, w, cos_t, sin_t, normed, inv, gain, gres, gmlp, low, branch, gup, dnp, inputs)


def rotate(rows, cos_rows, sin_rows):
    half_dim = HS // 2
    first, second = rows[:half_dim], rows[half_dim:]
    return jnp.concatenate(
        [first * cos_rows - second * sin_rows, second * cos_rows + first * sin_rows], axis=0
    )


class Axes:
    def __init__(self, nctx, nf):
        self.ctx, self.f = lax.axis_index("ctx"), lax.axis_index("fsdp")
        self.core, self.place = lax.rem(self.ctx, 2), self.ctx // 2
        self.me = self.ctx * nf + self.f
        self.dims = line_dims(nctx // 2)
        self.nd = len(self.dims)
        ctx, f, core, place = self.ctx, self.f, self.core, self.place
        self.core_axis = (self.nd, 2, core, lambda k: (1 - core, {"ctx": place * 2 + 1 - core, "fsdp": f}))
        self.side_axis = (self.nd + 1, 2, f, lambda k: (1 - f, {"ctx": ctx, "fsdp": 1 - f}))
        self.lines = [self.line(i) for i in range(self.nd)]
        self.peer_count = 2 + sum(size - 1 for size in self.dims)

    def at_line(self, i, there):
        stride = math.prod(self.dims[:i])
        own = lax.rem(self.place // stride, self.dims[i])
        return {"ctx": (self.place + (there - own) * stride) * 2 + self.core, "fsdp": self.f}

    def line(self, i):
        size = self.dims[i]
        own = lax.rem(self.place // math.prod(self.dims[:i]), size)

        def peer(k):
            there = lax.rem(own + k, size)
            return there, self.at_line(i, there)

        return (self.nd - 1 - i, size, own, peer)

    def peers(self):
        found = [self.core_axis[3](1)[1], self.side_axis[3](1)[1]]
        for axis in self.lines:
            found += [axis[3](k)[1] for k in range(1, axis[1])]
        return found

    def place_index(self, j):
        return tuple(
            lax.rem(j // math.prod(self.dims[:i]), self.dims[i]) for i in reversed(range(self.nd))
        )


def forward_kernel(plan, docs, tokens_ref, gains_ref, cos_ref, sin_ref, wq, wk, wv, wo, wg, wu, cot,
                   qt_ref, kv_out, low_ref, ot_ref, lse_ref, wqkv_out, wo_out, gu_out, cots_out,
                   attn_in_ref, inv_ref, gain_ref,
                   wbuf, obuf, gubuf, cbuf, gain_far, own_kv, kvb, m_ref, l_ref, acc_ref,
                   load_sem, w_send, w_recv, top_send, top_recv, ag_send, ag_recv, blk_sem, out_sem):
    nctx, nf, parts, heads, tq = plan
    ax = Axes(nctx, nf)
    f, core, place = ax.f, ax.core, ax.place
    mesh_id = pl.DeviceIdType.MESH
    bf16, f32 = jnp.bfloat16, jnp.float32
    width = tokens_ref.shape[1]
    half = width // nf
    width_q, width_k = 2 * parts * heads * HS, 2 * parts * HS
    rows4, rows2 = half // 4, half // 2
    quarter = gu_out.shape[1] // 2
    side = ax.side_axis[3](1)[1]
    mate = ax.core_axis[3](1)[1]
    low = ax.lines[0]
    bit = lax.rem(low[2], 2)
    across = ax.at_line(0, low[2] + 1 - 2 * bit)
    top = ax.nd - 1
    chunks = ax.dims[top]
    z = ax.lines[top][2]

    barrier = pltpu.get_barrier_semaphore()
    for where in ax.peers():
        pl.semaphore_signal(barrier, inc=1, device_id=where, device_id_type=mesh_id)

    def local(src, dst, i):
        return pltpu.make_async_copy(src, dst, load_sem.at[i])

    own_rows = pl.ds(pl.multiple_of(f * half, half), half)
    own_quarter = pl.ds(pl.multiple_of((2 * f + core) * quarter, quarter), quarter)
    loads = [
        local(wk, wbuf.at[own_rows, pl.ds(width_q, width_k)], 0),
        local(wv, wbuf.at[own_rows, pl.ds(width_q + width_k, width_k)], 1),
        local(wq, wbuf.at[own_rows, pl.ds(0, width_q)], 2),
        local(wo, obuf.at[own_rows], 3),
        local(wg.at[:, own_quarter], gubuf.at[own_rows, pl.ds(0, quarter)], 4),
        local(wu.at[:, own_quarter], gubuf.at[own_rows, pl.ds(quarter, quarter)], 5),
        local(cot, cbuf.at[0], 6),
    ]
    for copy in loads:
        copy.start()

    def remote(src, dst, i, where):
        return pltpu.make_async_remote_copy(
            src_ref=src, dst_ref=dst, send_sem=w_send.at[i], recv_sem=w_recv.at[i],
            device_id=where, device_id_type=mesh_id,
        )

    near = pl.multiple_of(core * rows2 + bit * rows4, 16)
    far_x = pl.multiple_of(core * rows2 + (1 - bit) * rows4, 16)
    there = (1 - f) * half

    def piece(base, offset):
        return pl.ds(pl.multiple_of(base + offset, 16), rows4)

    kv_cols, q_cols = pl.ds(width_q, 2 * width_k), pl.ds(0, width_q)
    mine = f * half
    gains_copy = remote(gains_ref, gain_far, 0, side)
    kv_y = [
        remote(wk.at[piece(0, near)], wbuf.at[piece(mine, near), pl.ds(width_q, width_k)], 1, side),
        remote(wv.at[piece(0, near)], wbuf.at[piece(mine, near), pl.ds(width_q + width_k, width_k)], 2, side),
    ]
    q_y = [remote(wq.at[piece(0, near)], wbuf.at[piece(mine, near), q_cols], 3, side)]
    o_y = [remote(wo.at[piece(0, near)], obuf.at[piece(mine, near)], 4, side)]

    def forwards(buf, cols, first):
        def part(offset):
            return buf.at[piece(there, offset), cols] if cols is not None else buf.at[piece(there, offset)]

        return [
            remote(part(near), part(near), first, across),
            remote(part(near), part(near), first + 1, mate),
            remote(part(far_x), part(far_x), first + 2, mate),
        ]

    kv_f = forwards(wbuf, kv_cols, 5)
    q_f = forwards(wbuf, q_cols, 8)
    o_f = forwards(obuf, None, 11)
    far_quarter = pl.ds(pl.multiple_of((2 * (1 - f) + core) * quarter, quarter), quarter)

    deep = lax.rem(z, 2)
    above = ax.at_line(top, z + 1 - 2 * deep)

    def gu_rows(base, which=bit):
        return pl.ds(pl.multiple_of(base + which * rows2 + deep * rows4, 16), rows4)

    gu_y = [
        remote(wg.at[gu_rows(0), far_quarter], gubuf.at[gu_rows(mine), pl.ds(0, quarter)], 14, side),
        remote(wu.at[gu_rows(0), far_quarter], gubuf.at[gu_rows(mine), pl.ds(quarter, quarter)], 15, side),
    ]
    gu_x = remote(gubuf.at[gu_rows(there)], gubuf.at[gu_rows(there)], 16, across)
    gu_z = [
        remote(gubuf.at[gu_rows(there, which)], gubuf.at[gu_rows(there, which)], 19 + i, above)
        for i, which in enumerate((bit, 1 - bit))
    ]
    cot_y = remote(cot, cbuf.at[1], 17, side)
    cot_c = remote(cbuf.at[pl.ds(0, 2)], cbuf.at[pl.ds(2, 2)], 18, mate)

    pl.semaphore_wait(barrier, ax.peer_count)
    gains_copy.start()
    for copy in kv_y + q_y:
        copy.start()

    hidden = tokens_ref[...].astype(f32)
    inv = lax.rsqrt(jnp.mean(hidden * hidden, axis=1, keepdims=True) + EPS)
    inv_ref[...] = inv
    gains_copy.wait()
    near_gain, far_gain = gains_ref[0:1, :], gain_far[0:1, :]
    gain = jnp.where(
        f == 0,
        jnp.concatenate([near_gain, far_gain], axis=1),
        jnp.concatenate([far_gain, near_gain], axis=1),
    )
    near_mlp, far_mlp = gains_ref[1:2, :], gain_far[1:2, :]
    gain_ref[0:1, :] = gain
    gain_ref[1:2, :] = jnp.where(
        f == 0,
        jnp.concatenate([near_mlp, far_mlp], axis=1),
        jnp.concatenate([far_mlp, near_mlp], axis=1),
    )
    attn_in = (hidden * inv * gain).astype(bf16)
    attn_in_ref[...] = attn_in

    for copy in kv_y:
        copy.wait()
    kv_f[0].start()
    kv_f[1].start()
    for copy in q_y:
        copy.wait()
    for copy in o_y + gu_y:
        copy.start()
    kv_f[0].wait()
    kv_f[2].start()
    q_f[0].start()
    q_f[1].start()
    for copy in loads[:3]:
        copy.wait()
    kv_f[1].wait()
    kv_f[2].wait()
    kv = jnp.dot(attn_in, wbuf[:, width_q:], preferred_element_type=f32)
    cos_rows, sin_rows = cos_ref[...], sin_ref[...]
    kt = jnp.transpose(kv[:, :width_k])
    k_rot = jnp.concatenate(
        [rotate(kt[HS * g : HS * (g + 1)], cos_rows, sin_rows) for g in range(2 * parts)], axis=0
    )
    own_kv[:, :width_k] = jnp.transpose(k_rot).astype(bf16)
    own_kv[:, width_k:] = kv[:, width_k:].astype(bf16)
    own_at = ax.place_index(place) + (core, f)
    put = pltpu.make_async_copy(own_kv, kv_out.at[own_at], out_sem.at[0])
    put.start()

    def top_copy(k):
        return pltpu.make_async_remote_copy(
            src_ref=own_kv, dst_ref=kv_out.at[own_at],
            send_sem=top_send.at[k - 1], recv_sem=top_recv.at[k - 1],
            device_id=ax.at_line(top, lax.rem(z + k, chunks)), device_id_type=mesh_id,
        )

    for k in range(1, chunks):
        @pl.when(z + k < chunks)
        def _():
            top_copy(k).start()

    lower = ax.lines[:top]
    orders = [lower + [ax.side_axis, ax.core_axis], [ax.side_axis] + lower + [ax.core_axis]]
    stages = len(orders[0])

    def ag_copies(k, stage):
        copies = []
        for kind in range(2):
            index = [None] * (ax.nd + 2)
            index[0] = z - k
            for i, axis in enumerate(orders[kind]):
                index[axis[0]] = slice(None) if i < stage else axis[2]
            region = kv_out.at[tuple(index) + (slice(None), pl.ds(kind * width_k, width_k))]
            axis = orders[kind][stage]
            for i in range(1, axis[1]):
                copies.append(
                    pltpu.make_async_remote_copy(
                        src_ref=region, dst_ref=region,
                        send_sem=ag_send.at[k, kind, stage, i - 1],
                        recv_sem=ag_recv.at[k, kind, stage, i - 1],
                        device_id=axis[3](i)[1], device_id_type=mesh_id,
                    )
                )
        return copies

    def tick(k, stage):
        @pl.when(z >= k)
        def _():
            if stage == 0:
                if k > 0:
                    top_copy(k).wait_recv()
            else:
                for copy in ag_copies(k, stage - 1):
                    copy.wait()
            if stage < stages:
                for copy in ag_copies(k, stage):
                    copy.start()

    put.wait()
    tick(0, 0)
    q_f[0].wait()
    q_f[2].start()
    q_f[1].wait()
    q_f[2].wait()
    back = pltpu.make_async_copy(wbuf, wqkv_out, out_sem.at[1])
    back.start()
    query = jnp.dot(attn_in, wbuf[:, :width_q], preferred_element_type=f32)
    query_t = jnp.transpose(query)
    for h in range(2 * parts * heads):
        qt_ref[HS * h : HS * (h + 1), :] = rotate(
            query_t[HS * h : HS * (h + 1)], cos_rows, sin_rows
        ).astype(bf16)
    m_ref[...] = jnp.full_like(m_ref, NEG)
    l_ref[...] = jnp.zeros_like(l_ref)
    acc_ref[...] = jnp.zeros_like(acc_ref)

    bk = 2 * nf * tq
    per_chunk = math.prod(ax.dims[:top])
    start = ax.me * tq

    def block_copy(j, slot):
        return pltpu.make_async_copy(kv_out.at[ax.place_index(j)], kvb.at[slot], blk_sem.at[slot])

    def attend(k):
        first_block = (z - k) * per_chunk
        count = jnp.minimum(place - first_block + 1, per_chunk)

        @pl.when(z >= k)
        def _():
            block_copy(first_block, 0).start()

            def block(i, carry):
                j = first_block + i
                slot = lax.rem(i, 2)

                @pl.when(i + 1 < count)
                def _():
                    block_copy(j + 1, 1 - slot).start()

                block_copy(j, slot).wait()
                bias = bias_tile((start,), docs, j * bk, bk, tq)
                bias = jnp.concatenate([bias] * heads, axis=1)
                for p in range(parts):
                    kb = kvb[slot, :, :, :, 2 * HS * p : 2 * HS * (p + 1)].reshape(bk, 2 * HS)
                    vb = kvb[slot, :, :, :, width_k + 2 * HS * p : width_k + 2 * HS * (p + 1)]
                    vt = jnp.transpose(vb.reshape(bk, 2 * HS))
                    rows = qt_ref[2 * heads * HS * p : 2 * heads * HS * (p + 1), :] * bf16(1.0 / 8.0)
                    for g in range(2):
                        at = 2 * p + g
                        s = jnp.dot(kb, padded(rows, heads, g), preferred_element_type=f32) + bias
                        m = m_ref[at]
                        new = jnp.maximum(m, jnp.max(s, axis=0, keepdims=True))
                        prob = jnp.exp(s - new)
                        decay = jnp.exp(m - new)
                        m_ref[at] = new
                        l_ref[at] = l_ref[at] * decay + jnp.sum(prob, axis=0, keepdims=True)
                        acc_ref[at] = acc_ref[at] * decay + jnp.dot(
                            vt[HS * g : HS * (g + 1)], prob.astype(bf16), preferred_element_type=f32
                        )
                return carry

            lax.fori_loop(0, count, block, 0)

    for turn in range(1, chunks + stages):
        for k in range(chunks):
            stage = turn - k
            if (k, stage) != (0, 0) and 0 <= stage <= stages:
                tick(k, stage)
        if turn == 4:
            for copy in o_y + gu_y:
                copy.wait()
            o_f[0].start()
            o_f[1].start()
            gu_x.start()
            gu_z[0].start()
        if turn == 3:
            cot_y.start()
        if turn == 6:
            o_f[0].wait()
            o_f[2].start()
            gu_x.wait()
            gu_z[1].start()
        if turn == 5:
            cot_y.wait()
            loads[6].wait()
            cot_c.start()
        if turn >= stages:
            attend(turn - stages)
    for p in range(parts):
        outs = []
        for g in range(2):
            at = 2 * p + g
            out = acc_ref[at] / l_ref[at]
            outs.append(out)
            ot_ref[at] = out
            lse_ref[at] = m_ref[at] + jnp.log(l_ref[at])
        low_ref[:, 2 * heads * HS * p : 2 * heads * HS * (p + 1)] = head_lanes(outs, heads, tq).astype(bf16)

    for k in range(1, chunks):
        @pl.when(z + k < chunks)
        def _():
            top_copy(k).wait_send()
    for copy in loads[3:6]:
        copy.wait()
    backs = [back]
    for waits, src, dst in (
        (o_f[1:], obuf, wo_out), ([cot_c], cbuf, cots_out), (gu_z, gubuf, gu_out)
    ):
        for copy in waits:
            copy.wait()
        backs.append(pltpu.make_async_copy(src, dst, out_sem.at[1 + len(backs)]))
        backs[-1].start()
    for copy in backs:
        copy.wait()


def forward(nctx, nf, docs, tokens, gains, cos_t, sin_t, wq, wk, wv, wo, wg, wu, cot):
    tq, width = tokens.shape
    width_q, width_k = wq.shape[1], wk.shape[1]
    parts = width_k // (2 * HS)
    heads = width_q // HS // (2 * parts)
    hidden_units = wg.shape[1]
    quarter = hidden_units // (2 * nf)
    dims = line_dims(nctx // 2)
    lead = tuple(reversed(dims))
    most = max(dims + [2])
    chunks = dims[-1]
    stages = len(dims) + 1
    bf16, f32 = jnp.bfloat16, jnp.float32
    vmem = pl.BlockSpec(memory_space=pltpu.VMEM)
    smem = pl.BlockSpec(memory_space=pltpu.SMEM)
    hbm = pl.BlockSpec(memory_space=pl.ANY)
    dma = pltpu.SemaphoreType.DMA
    return pl.pallas_call(
        functools.partial(forward_kernel, (nctx, nf, parts, heads, tq)),
        out_shape=[
            jax.ShapeDtypeStruct((width_q, tq), bf16),
            jax.ShapeDtypeStruct(lead + (2, nf, tq, 2 * width_k), bf16),
            jax.ShapeDtypeStruct((tq, width_q), bf16),
            jax.ShapeDtypeStruct((2 * parts, HS, heads * tq), f32),
            jax.ShapeDtypeStruct((2 * parts, 1, heads * tq), f32),
            jax.ShapeDtypeStruct((width, width_q + 2 * width_k), bf16),
            jax.ShapeDtypeStruct((nf * wo.shape[0], wo.shape[1]), bf16),
            jax.ShapeDtypeStruct((width, 2 * quarter), bf16),
            jax.ShapeDtypeStruct((2 * nf, tq, width), bf16),
            jax.ShapeDtypeStruct((tq, width), bf16),
            jax.ShapeDtypeStruct((tq, 1), f32),
            jax.ShapeDtypeStruct((2, width), f32),
        ],
        in_specs=[smem, vmem, vmem, vmem, vmem] + [hbm] * 7,
        out_specs=[vmem, hbm, vmem, vmem, vmem, hbm, hbm, hbm, hbm, vmem, vmem, vmem],
        scratch_shapes=[
            pltpu.VMEM((width, width_q + 2 * width_k), bf16),
            pltpu.VMEM((nf * wo.shape[0], wo.shape[1]), bf16),
            pltpu.VMEM((width, 2 * quarter), bf16),
            pltpu.VMEM((2 * nf, tq, width), bf16),
            pltpu.VMEM(gains.shape, f32),
            pltpu.VMEM((tq, 2 * width_k), bf16),
            pltpu.VMEM((2, 2, nf, tq, 2 * width_k), bf16),
            pltpu.VMEM((2 * parts, 1, heads * tq), f32),
            pltpu.VMEM((2 * parts, 1, heads * tq), f32),
            pltpu.VMEM((2 * parts, HS, heads * tq), f32),
            dma((7,)),
            dma((21,)),
            dma((21,)),
            dma((chunks - 1,)),
            dma((chunks - 1,)),
            dma((chunks, 2, stages, most - 1)),
            dma((chunks, 2, stages, most - 1)),
            dma((2,)),
            dma((5,)),
        ],
        compiler_params=pltpu.CompilerParams(
            collective_id=0, has_side_effects=True, vmem_limit_bytes=60 * 2**20
        ),
        name="forward",
    )(docs, tokens, gains, cos_t, sin_t, wq, wk, wv, wo, wg, wu, cot)


def feed_forward_kernel(plan, tokens_ref, low_ref, attn_in_ref, gains_ref, wo_hbm, gu_hbm, down_hbm, cots_hbm,
                        result_ref, gres_ref, branch_ref, gattn_ref, gmlp_ref, gup_ref, dnp_ref, inputs_out,
                        wo, gu, down, cots, xs, grads, mixed, gm, sums, sent, core_in, side_in, side_out,
                        load_sem, x_send, x_recv, s_send, s_recv, top_send, top_recv,
                        ag_send, ag_recv, out_sem):
    nctx, nf = plan
    ax = Axes(nctx, nf)
    f, core, place = ax.f, ax.core, ax.place
    mesh_id = pl.DeviceIdType.MESH
    bf16, f32 = jnp.bfloat16, jnp.float32
    tq, width = tokens_ref.shape
    quarter = down.shape[0]
    side = ax.side_axis[3](1)[1]
    mate = ax.core_axis[3](1)[1]
    top = ax.nd - 1
    chunks = ax.dims[top]
    z = ax.lines[top][2]

    barrier = pltpu.get_barrier_semaphore()
    for where in ax.peers():
        pl.semaphore_signal(barrier, inc=1, device_id=where, device_id_type=mesh_id)
    loads = [
        pltpu.make_async_copy(src, dst, load_sem.at[i])
        for i, (src, dst) in enumerate((
            (wo_hbm, wo), (cots_hbm, cots),
            (down_hbm.at[pl.ds(pl.multiple_of(core * quarter, quarter), quarter)], down), (gu_hbm, gu),
        ))
    ]
    for copy in loads:
        copy.start()

    def remote(src, dst, sends, recvs, i, where):
        return pltpu.make_async_remote_copy(
            src_ref=src, dst_ref=dst, send_sem=sends.at[i], recv_sem=recvs.at[i],
            device_id=where, device_id_type=mesh_id,
        )

    hidden = tokens_ref[...].astype(f32)
    own_at = ax.place_index(place) + (core,)
    put = pltpu.make_async_copy(attn_in_ref, inputs_out.at[own_at], out_sem.at[0])

    def top_copy(k):
        return pltpu.make_async_remote_copy(
            src_ref=attn_in_ref, dst_ref=inputs_out.at[own_at],
            send_sem=top_send.at[k - 1], recv_sem=top_recv.at[k - 1],
            device_id=ax.at_line(top, lax.rem(z + k, chunks)), device_id_type=mesh_id,
        )

    order = ax.lines[:top] + [ax.core_axis]
    stages = len(order)

    def ag_copies(k, stage):
        index = [None] * (ax.nd + 1)
        index[0] = lax.rem(z + chunks - k, chunks)
        for i, axis in enumerate(order):
            index[axis[0]] = slice(None) if i < stage else axis[2]
        region = inputs_out.at[tuple(index)]
        axis = order[stage]
        return [
            pltpu.make_async_remote_copy(
                src_ref=region, dst_ref=region,
                send_sem=ag_send.at[k, stage, i - 1], recv_sem=ag_recv.at[k, stage, i - 1],
                device_id=axis[3](i)[1], device_id_type=mesh_id,
            )
            for i in range(1, axis[1])
        ]

    def tick(turn):
        for k in range(chunks):
            stage = turn - k
            if not 0 <= stage <= stages:
                continue
            if stage == 0:
                if k > 0:
                    top_copy(k).wait()
                else:
                    put.wait()
            else:
                for copy in ag_copies(k, stage - 1):
                    copy.wait()
            if stage < stages:
                for copy in ag_copies(k, stage):
                    copy.start()

    pl.semaphore_wait(barrier, ax.peer_count)
    put.start()
    top_copy(1).start()
    tick(0)

    loads[0].wait()
    resid = hidden + jnp.dot(low_ref[...], wo[...], preferred_element_type=f32)
    inv = lax.rsqrt(jnp.mean(resid * resid, axis=1, keepdims=True) + EPS)
    normed = resid * inv
    gain = gains_ref[1:2, :]
    xs[0] = (normed * gain).astype(bf16)
    x_side = remote(xs.at[0], xs.at[1], x_send, x_recv, 0, side)
    x_core = remote(xs.at[0], xs.at[2], x_send, x_recv, 1, mate)
    x_far = remote(xs.at[1], xs.at[3], x_send, x_recv, 2, mate)
    x_side.start()
    x_core.start()

    def rows(slot):
        return slice(slot * tq, (slot + 1) * tq)

    for copy in loads[1:3]:
        copy.wait()
    gm[...] = lax.dot_general(
        cots[...].reshape(4 * tq, width), down[...], (((1,), (1,)), ((), ())), preferred_element_type=f32
    )
    loads[3].wait()
    top_copy(2).start()
    step = 256

    def both(ref, a, b, span=slice(None)):
        return jnp.concatenate([ref[a, :, span], ref[b, :, span]], axis=0)

    def compute(a, b):
        x = both(xs, a, b)
        for n in range(quarter // step):
            span = slice(n * step, (n + 1) * step)
            up_span = slice(quarter + n * step, quarter + (n + 1) * step)
            gate = jnp.dot(x, gu[:, span], preferred_element_type=f32)
            up = jnp.dot(x, gu[:, up_span], preferred_element_type=f32)
            sig = jax.nn.sigmoid(gate)
            act = gate * sig
            grad = jnp.concatenate([gm[rows(a), span], gm[rows(b), span]], axis=0)
            mix = (act * up).astype(bf16)
            grad_gate = (grad * up * sig * (1.0 + gate * (1.0 - sig))).astype(bf16)
            grad_up = (grad * act).astype(bf16)
            for i, slot in enumerate((a, b)):
                mixed[slot, :, span] = mix[rows(i)]
                grads[slot, :, span] = grad_gate[rows(i)]
                grads[slot, :, up_span] = grad_up[rows(i)]
        total = lax.dot_general(
            both(grads, a, b), gu[...], (((1,), (1,)), ((), ())), preferred_element_type=f32
        )
        for i, slot in enumerate((a, b)):
            sums[0, slot] = total[rows(i)]

    def outputs(a, b):
        total = jnp.dot(both(mixed, a, b), down[...], preferred_element_type=f32)
        for i, slot in enumerate((a, b)):
            sums[1, slot] = total[rows(i)]

    def to_core(kind, slot):
        i = 2 * kind + slot - 2
        return remote(sent.at[i], core_in.at[i], s_send, s_recv, i, mate)

    def to_side(kind):
        return remote(side_out.at[kind], side_in.at[kind], s_send, s_recv, 4 + kind, side)

    def give_core(kind, slot):
        sent[2 * kind + slot - 2] = sums[kind, slot].astype(bf16)
        to_core(kind, slot).start()

    def give_side(kind):
        to_core(kind, 3).wait()
        side_out[kind] = (sums[kind, 1] + core_in[2 * kind + 1].astype(f32)).astype(bf16)
        to_side(kind).start()

    x_core.wait()
    compute(0, 2)
    give_core(0, 2)
    top_copy(3).start()
    x_side.wait()
    x_far.start()
    tick(1)
    outputs(0, 2)
    give_core(1, 2)
    x_far.wait()
    compute(1, 3)
    give_core(0, 3)
    tick(2)
    outputs(1, 3)
    give_side(0)
    give_core(1, 3)
    flat_x = xs[...].reshape(4 * tq, width)
    pieces = nctx // 2
    unit = quarter // pieces
    tall = max(unit, 256)
    for kind in range(2):
        for n in range(quarter // tall):
            span = slice(kind * quarter + n * tall, kind * quarter + (n + 1) * tall)
            cols = jnp.transpose(jnp.concatenate([grads[s, :, span] for s in range(4)], axis=0))
            part = jnp.dot(cols, flat_x, preferred_element_type=f32).astype(bf16)
            first = n * tall
            while first < (n + 1) * tall:
                piece, at = first // unit, first % unit
                end = min((piece + 1) * unit, (n + 1) * tall)
                gup_ref[static_index(bit_dims(nctx // 2), piece) + (kind, slice(at, at + end - first))] = part[
                    first - n * tall : end - n * tall
                ]
                first = end
        if kind == 0:
            give_side(1)
            tick(3)
    unit = width // pieces
    flat_mixed = mixed[...].reshape(4 * tq, quarter)
    for n in range(width // 384):
        cols = jnp.transpose(jnp.concatenate([cots[s, :, 384 * n : 384 * (n + 1)] for s in range(4)], axis=0))
        part = jnp.dot(cols, flat_mixed, preferred_element_type=f32).astype(bf16)
        first = n * 384
        while first < (n + 1) * 384:
            piece, at = first // unit, first % unit
            end = min((piece + 1) * unit, (n + 1) * 384)
            rows_of = part[first - n * 384 : end - n * 384]
            for c in range(quarter // 128):
                dnp_ref[
                    static_index(bit_dims(nctx // 2), piece)
                    + (slice(c * unit + at, c * unit + at + end - first),)
                ] = rows_of[:, 128 * c : 128 * (c + 1)]
            first = end

    tick(4)
    to_core(0, 2).wait()
    to_side(0).wait()
    grad = sums[0, 0] + core_in[0].astype(f32) + side_in[0].astype(f32)
    product = grad * normed
    gmlp_ref[...] = jnp.sum(product, axis=0, keepdims=True)
    scaled = grad * gain
    mean = jnp.mean(scaled * normed, axis=1, keepdims=True)
    gres = cots[0].astype(f32) + inv * (scaled - normed * mean)
    gres_ref[...] = gres
    branch = gres.astype(bf16)
    branch_ref[...] = branch
    gattn_ref[...] = lax.dot_general(
        branch, wo[...], (((1,), (1,)), ((), ())), preferred_element_type=f32
    ).astype(bf16)
    to_core(1, 2).wait()
    to_side(1).wait()
    result_ref[...] = (resid + sums[1, 0] + core_in[2].astype(f32) + side_in[1].astype(f32)).astype(bf16)
    for turn in range(5, chunks + stages):
        tick(turn)


def static_index(dims, piece):
    return tuple(piece // math.prod(dims[:i]) % dims[i] for i in reversed(range(len(dims))))


def feed_forward(nctx, nf, tokens, low, attn_in, gains, wo, gu, down, cots):
    tq, width = tokens.shape
    quarter = gu.shape[1] // 2
    dims = line_dims(nctx // 2)
    bits = bit_dims(nctx // 2)
    lead = tuple(reversed(dims))
    plane = nctx // 2
    chunks, stages, most = dims[-1], len(dims), max(dims + [2])
    bf16, f32 = jnp.bfloat16, jnp.float32
    vmem = pl.BlockSpec(memory_space=pltpu.VMEM)
    hbm = pl.BlockSpec(memory_space=pl.ANY)
    dma = pltpu.SemaphoreType.DMA
    return pl.pallas_call(
        functools.partial(feed_forward_kernel, (nctx, nf)),
        out_shape=[
            jax.ShapeDtypeStruct((tq, width), bf16),
            jax.ShapeDtypeStruct((tq, width), f32),
            jax.ShapeDtypeStruct((tq, width), bf16),
            jax.ShapeDtypeStruct((tq, width), bf16),
            jax.ShapeDtypeStruct((1, width), f32),
            jax.ShapeDtypeStruct(tuple(bits) + (2, quarter // plane, width), bf16),
            jax.ShapeDtypeStruct(tuple(bits) + (width // plane * (quarter // 128), 128), bf16),
            jax.ShapeDtypeStruct(lead + (2, tq, width), bf16),
        ],
        in_specs=[vmem] * 4 + [hbm] * 4,
        out_specs=[vmem] * 7 + [hbm],
        scratch_shapes=[
            pltpu.VMEM(wo.shape, bf16),
            pltpu.VMEM(gu.shape, bf16),
            pltpu.VMEM((quarter, width), bf16),
            pltpu.VMEM((4, tq, width), bf16),
            pltpu.VMEM((4, tq, width), bf16),
            pltpu.VMEM((4, tq, 2 * quarter), bf16),
            pltpu.VMEM((4, tq, quarter), bf16),
            pltpu.VMEM((4 * tq, quarter), f32),
            pltpu.VMEM((2, 4, tq, width), f32),
            pltpu.VMEM((4, tq, width), bf16),
            pltpu.VMEM((4, tq, width), bf16),
            pltpu.VMEM((2, tq, width), bf16),
            pltpu.VMEM((2, tq, width), bf16),
            dma((4,)),
            dma((4,)),
            dma((4,)),
            dma((6,)),
            dma((6,)),
            dma((chunks - 1,)),
            dma((chunks - 1,)),
            dma((chunks, stages, most - 1)),
            dma((chunks, stages, most - 1)),
            dma((1,)),
        ],
        compiler_params=pltpu.CompilerParams(
            collective_id=2, has_side_effects=True, vmem_limit_bytes=60 * 2**20
        ),
        name="feed_forward",
    )(tokens, low, attn_in, gains, wo, gu, down, cots)


def finish_kernel(result, tokens, q, k, v, o, gate, up, down, gains, *outs):
    outs[0][...] = result[...]
    outs[1][...] = tokens[...]
    for src, dst in zip((q, k, v, o, gate, up, down), outs[2:9]):
        dst[...] = jnp.transpose(src[...])
    tiles = outs[9].shape[1] // 128
    for i in range(2):
        outs[9 + i][...] = jnp.concatenate(
            [gains[tiles * i + j : tiles * i + j + 1, :] for j in range(tiles)], axis=1
        )


def finish(width, result, tokens, *sums):
    weights, gains = sums[:-1], sums[-1]
    f32 = jnp.float32

    def whole(x):
        return pl.BlockSpec(x.shape, lambda i: (0,) * len(x.shape))

    shapes = (
        [jax.ShapeDtypeStruct(result.shape, result.dtype), jax.ShapeDtypeStruct(tokens.shape, f32)]
        + [jax.ShapeDtypeStruct(w.shape[::-1], f32) for w in weights]
        + [jax.ShapeDtypeStruct((1, width), f32)] * 2
    )
    outs = pl.pallas_call(
        finish_kernel,
        grid=(1,),
        out_shape=shapes,
        in_specs=[whole(x) for x in (result, tokens) + sums],
        out_specs=[whole(x) for x in shapes],
        compiler_params=pltpu.CompilerParams(vmem_limit_bytes=60 * 2**20),
        name="finish",
    )(result, tokens, *weights, gains)
    return tuple(outs[:9]) + (outs[9].reshape(width), outs[10].reshape(width))


def per_device(
    nctx,
    nf,
    tokens,
    query_weight,
    key_projection,
    value_projection,
    output_weight,
    gate_weight,
    up_weight,
    down_weight,
    norm_attn,
    norm_mlp,
    doc_starts,
    cotangent,
):
    token_rows, width = tokens.shape
    n_tokens = token_rows * nctx * nf
    bf16, f32 = jnp.bfloat16, jnp.float32

    own_device = lax.axis_index(AXES)
    own_index = layout_rows(own_device, token_rows)
    own_begin = doc_begin(own_index, doc_starts)
    cosine_table, sine_table = rope_tables(own_index - own_begin)
    cosine_table, sine_table = cosine_table.T, sine_table.T
    gains = jnp.pad(jnp.stack([norm_attn, norm_mlp]).astype(f32), ((0, 6), (0, 0)))
    (
        query_rot, key_values, attn_low, attn_exact, log_total, qkv_full, output_full, gate_up,
        cotangents, attention_input, inv_attn, gains,
    ) = forward(
        nctx, nf, doc_starts, tokens, gains, cosine_table, sine_table, query_weight, key_projection,
        value_projection, output_weight, gate_weight, up_weight, cotangent,
    )
    key_width = KEY_VALUE_HEADS * HEAD_SIZE
    key_values = key_values.reshape(n_tokens, 2 * key_width)
    result, grad_resid, grad_branch, grad_attn, gain_mlp_partial, gate_up_partial, down_partial, inputs_all = feed_forward(
        nctx, nf, tokens, attn_low, attention_input, gains, output_full, gate_up, down_weight,
        cotangents.reshape(2 * nf, token_rows, width),
    )

    tokens_grad, query_sum, key_sum, value_sum, gain_sums, gate_sum, up_sum, down_sum, output_sum = backward(
        nctx, nf, doc_starts, query_rot, grad_attn, attn_exact, log_total, key_values, qkv_full,
        cosine_table, sine_table, tokens, inv_attn, gains, grad_resid,
        gain_mlp_partial, attn_low, grad_branch, gate_up_partial, down_partial,
        inputs_all.reshape(nctx, token_rows, width),
    )

    return finish(
        width, result, tokens_grad, query_sum, key_sum, value_sum, output_sum, gate_sum, up_sum,
        down_sum, gain_sums,
    )


def solution(mesh):
    return jax.shard_map(
        functools.partial(per_device, mesh.shape["ctx"], mesh.shape["fsdp"]),
        mesh=mesh,
        in_specs=(
            P(("ctx", "fsdp"), None),
            P("fsdp", None),
            P("fsdp", None),
            P("fsdp", None),
            P("fsdp", None),
            P("fsdp", None),
            P("fsdp", None),
            P("fsdp", None),
            P("fsdp"),
            P("fsdp"),
            P(),
            P(("ctx", "fsdp"), None),
        ),
        out_specs=(
            P(("ctx", "fsdp"), None),
            P(("ctx", "fsdp"), None),
            P("fsdp", "ctx"),
            P("fsdp", "ctx"),
            P("fsdp", "ctx"),
            P("fsdp", "ctx"),
            P("fsdp", "ctx"),
            P("fsdp", "ctx"),
            P("fsdp", "ctx"),
            P(),
            P(),
        ),
        check_vma=False,
    )
```

```python
import functools
import math

import jax
import jax.numpy as jnp
from jax import lax
from jax.experimental import pallas as pl
from jax.experimental.pallas import tpu as pltpu
from jax.sharding import PartitionSpec as P

QUERY_HEADS = 18
KEY_VALUE_HEADS = 6
HEAD_SIZE = 64
HS = HEAD_SIZE

EPS = 1e-05
THETA = 10000.0
NEG = -1e30
AXES = ("ctx", "fsdp")


def rope_tables(positions):
    half_dim = HEAD_SIZE // 2
    frequency = jnp.exp(-math.log(THETA) * jnp.arange(half_dim, dtype=jnp.float32) / half_dim)
    angles = positions.astype(jnp.float32)[:, None] * frequency[None, :]
    return (jnp.cos(angles), jnp.sin(angles))


def apply_rotary(values, cosine_table, sine_table):
    half_dim = values.shape[-1] // 2
    first_half = values[..., :half_dim]
    second_half = values[..., half_dim:]
    cos_rows = cosine_table[:, None, :]
    sin_rows = sine_table[:, None, :]
    return jnp.concatenate(
        [
            first_half * cos_rows - second_half * sin_rows,
            second_half * cos_rows + first_half * sin_rows,
        ],
        axis=-1,
    )


def unrotate(values, cosine_table, sine_table):
    half_dim = values.shape[-1] // 2
    first_half = values[..., :half_dim]
    second_half = values[..., half_dim:]
    cos_rows = cosine_table[:, None, :]
    sin_rows = sine_table[:, None, :]
    return jnp.concatenate(
        [
            first_half * cos_rows + second_half * sin_rows,
            second_half * cos_rows - first_half * sin_rows,
        ],
        axis=-1,
    )


def doc_begin(indices, doc_starts):
    marked = jnp.where(indices[:, None] >= doc_starts[None, :], doc_starts[None, :], 0)
    return jnp.max(marked, axis=1)


def layout_rows(device, row_count):
    return device * row_count + jnp.arange(row_count, dtype=jnp.int32)


def heads_rows(natural):
    return jnp.transpose(natural.astype(jnp.float32))
def padded(rows, heads, g):
    top = jnp.concatenate([rows[HS*(heads*g+j):HS*(heads*g+j+1)] for j in range(heads)], axis=1)
    z = jnp.zeros_like(top)
    return jnp.concatenate([top, z] if g == 0 else [z, top], axis=0)
def head_lanes(per_group, heads, tq):
    return jnp.transpose(jnp.concatenate([per_group[g][:, tq*j:tq*(j+1)] for g in range(2) for j in range(heads)], axis=0))
def bias_tile(info, docs, first, bk, tq):
    query = info[0] + lax.broadcasted_iota(jnp.int32, (1, tq), 1)
    begin = jnp.zeros((1, tq), jnp.int32)
    for i in range(docs.shape[0]):
        begin = jnp.maximum(begin, jnp.where(query >= docs[i], docs[i], 0))
    key = first + lax.broadcasted_iota(jnp.int32, (bk, 1), 0)
    return jnp.where((key <= query) & (key >= begin), 0.0, NEG)


def line_dims(count):
    fours = 0
    while count % 4 == 0:
        count //= 4
        fours += 1
    return ([count] if count > 1 else []) + [4] * fours


def rotate_back(rows, cos_rows, sin_rows):
    half_dim = HS // 2
    first, second = rows[:half_dim], rows[half_dim:]
    return jnp.concatenate(
        [first * cos_rows + second * sin_rows, second * cos_rows - first * sin_rows], axis=0
    )


def w_order(lines):
    return [lines[-2]] + lines[1:-2] + [lines[0], lines[-1]]


def bit_dims(count):
    return [2] * (count.bit_length() - 1)


def round_up(value, unit):
    return -(-value // unit) * unit


def backward_kernel(plan, docs, q_ref, do_ref, ot_ref, lse_ref, kv_hbm, w_ref, cos_ref, sin_ref,
                    normed_ref, inv_ref, gain_ref, gres_ref, gmlp_ref, low_ref, branch_ref, gup_hbm, dnp_hbm, inputs_hbm,
                    tokens_ref, query_ref, key_ref, value_ref, gains_out, gate_ref, up_ref, down_ref, out_ref,
                    kvbuf, dkv, acc_ref, gqt_ref, ga_ref, qblk, kvblk, small,
                    load_sem, send_sem, recv_sem, col_send, col_recv, own_sem, credit,
                    wg, wd, wo, brs, lows, halves, fin, fin_in, dsend, din,
                    colq_ref, colkv_ref, gains_ref, cols_acc, half_send, half_in, gain_send, gain_in, in_sem,
                    g_send, g_recv, w_load, w_send, w_recv, top_send, top_recv, fin_send, fin_recv, *recvs):
    nctx, nf, parts, heads, tq, slots = plan
    plane = nctx // 2
    n = nctx * nf
    dims = bit_dims(plane)
    nd = len(dims)
    bk = 2 * nf * tq
    me_c, me_f = lax.axis_index("ctx"), lax.axis_index("fsdp")
    me = me_c * nf + me_f
    core, place = lax.rem(me_c, 2), me_c // 2
    mesh_id = pl.DeviceIdType.MESH
    half_dim = HS // 2

    def target(k):
        other = lax.rem(me + k, n)
        return other, {"ctx": other // nf, "fsdp": lax.rem(other, nf)}

    barrier = pltpu.get_barrier_semaphore()

    def greet(k, carry):
        pl.semaphore_signal(barrier, inc=1, device_id=target(k)[1], device_id_type=mesh_id)
        return carry

    lax.fori_loop(1, n, greet, 0)

    def loads(p):
        s = p % slots
        return [
            pltpu.make_async_copy(
                kv_hbm.at[:, pl.ds((kind * parts + p) * 2 * HS, 2 * HS)],
                kvbuf.at[s, kind], load_sem.at[s, kind],
            )
            for kind in range(2)
        ]

    resident = slots == parts

    def block_loads(p, j):
        slot = lax.rem(j, 2)
        return [
            pltpu.make_async_copy(
                kv_hbm.at[pl.ds(pl.multiple_of(j * bk, bk), bk), pl.ds((kind * parts + p) * 2 * HS, 2 * HS)],
                kvbuf.at[slot, kind], load_sem.at[slot, kind],
            )
            for kind in range(2)
        ]

    if resident:
        for p in range(parts):
            for copy in loads(p):
                copy.start()

    def dim_axis(i):
        stride = math.prod(dims[:i])
        size = dims[i]
        own = lax.rem(place // stride, size)

        def peer(k):
            there = lax.rem(own + k, size)
            return there, {"ctx": (place + (there - own) * stride) * 2 + core, "fsdp": me_f}

        return (nd - 1 - i, size, own, peer)

    core_axis = (nd, 2, core, lambda k: (1 - core, {"ctx": place * 2 + 1 - core, "fsdp": me_f}))
    side_axis = (nd + 1, 2, me_f, lambda k: (1 - me_f, {"ctx": me_c, "fsdp": 1 - me_f}))
    lines = [dim_axis(i) for i in range(nd)]
    orders = [[core_axis, side_axis] + lines, [core_axis, side_axis] + w_order(lines)]
    stages = nd + 2
    wrecvs = recvs[2 * stages :]
    side_at, mate_at = side_axis[3](1)[1], core_axis[3](1)[1]

    low_bits = nd - 2
    arrays = ((wg, gup_hbm, (0,)), (wd, dnp_hbm, ()), (wo, None, ()), (wg, gup_hbm, (1,)))
    w_lines = [lines, w_order(lines), w_order(lines), lines]

    def chunk_at(a, k):
        near, far_line = w_lines[a][nd - 2], w_lines[a][nd - 1]
        far_bit = far_line[2] if k % 2 else 1 - far_line[2]
        near_bit = near[2] if k // 2 else 1 - near[2]
        return far_bit, near_bit

    def w_region(a, k, stage, at):
        index = [slice(None)] * nd
        index[w_lines[a][nd - 1][0]], index[w_lines[a][nd - 2][0]] = chunk_at(a, k)
        for axis in w_lines[a][:stage]:
            index[axis[0]] = axis[2]
        if stage < low_bits:
            index[w_lines[a][stage][0]] = at
        return tuple(index)

    def held(a, index):
        first = w_lines[a][0][0]
        return index if a == 2 else index[:first] + index[first + 1 :] + arrays[a][2]

    def w_copy(a, k, stage):
        buf, far, sub = arrays[a]
        there, where = w_lines[a][stage][3](1)
        index = w_region(a, k, stage, there)
        return pltpu.make_async_remote_copy(
            src_ref=far.at[index + sub] if stage == 0 and a != 2 else buf.at[held(a, index)],
            dst_ref=wrecvs[a * (low_bits + 2) + stage].at[chunk_at(a, k)],
            send_sem=w_send.at[a, k, stage], recv_sem=w_recv.at[a, k, stage],
            device_id=where, device_id_type=mesh_id,
        )

    def near_copy(a, i):
        return pltpu.make_async_remote_copy(
            src_ref=arrays[a][0].at[held(a, w_region(a, i, low_bits, 0))], dst_ref=wrecvs[a * (low_bits + 2) + low_bits].at[i],
            send_sem=top_send.at[a, i], recv_sem=top_recv.at[a, i],
            device_id=w_lines[a][nd - 2][3](1)[1], device_id_type=mesh_id,
        )

    def far_copy(a):
        return pltpu.make_async_remote_copy(
            src_ref=arrays[a][0].at[held(a, w_region(a, 2, low_bits, 0))], dst_ref=wrecvs[a * (low_bits + 2) + low_bits + 1].at[0],
            send_sem=top_send.at[a, 2], recv_sem=top_recv.at[a, 2],
            device_id=w_lines[a][nd - 1][3](1)[1], device_id_type=mesh_id,
        )

    def w_start(which, k):
        for a in which:
            w_copy(a, k, 0).start()

    def w_finish(which, k):
        for a in which:
            buf = arrays[a][0]
            for stage in range(low_bits):
                w_copy(a, k, stage).wait()
                where = held(a, w_region(a, k, stage, w_lines[a][stage][2]))
                got = wrecvs[a * (low_bits + 2) + stage]
                buf[where] = (
                    buf[where].astype(jnp.float32) + got[chunk_at(a, k)].astype(jnp.float32)
                ).astype(buf.dtype)
                if stage + 1 < low_bits:
                    w_copy(a, k, stage + 1).start()
            if k < 2:
                near_copy(a, k).start()
            elif k == 2:
                near_copy(a, 0).wait()
                where = held(a, w_region(a, 2, low_bits, 0))
                buf[where] = (
                    buf[where].astype(jnp.float32)
                    + wrecvs[a * (low_bits + 2) + low_bits][0].astype(jnp.float32)
                ).astype(buf.dtype)
                far_copy(a).start()

    def w_total(a):
        near_copy(a, 1).wait()
        far_copy(a).wait()
        total = arrays[a][0][held(a, w_region(a, 3, low_bits, 0))].astype(jnp.float32)
        total = total + wrecvs[a * (low_bits + 2) + low_bits][1].astype(jnp.float32)
        return total + wrecvs[a * (low_bits + 2) + low_bits + 1][0].astype(jnp.float32)

    w_loads = [
        pltpu.make_async_copy(far.at[(slice(None),) * w_lines[i][0][0] + (w_lines[i][0][2],)], buf, w_load.at[i])
        for i, (buf, far, _) in enumerate(arrays[:2])
    ]
    for copy in w_loads:
        copy.start()
    half = low_ref.shape[1] // nf
    low_all = low_ref[...]
    halves[0] = low_all[:, :half]
    halves[1] = low_all[:, half:]
    lows[0] = halves[me_f]
    brs[0] = branch_ref[...]

    def g_copy(i, src, dst, where):
        return pltpu.make_async_remote_copy(
            src_ref=src, dst_ref=dst, send_sem=g_send.at[i], recv_sem=g_recv.at[i],
            device_id=where, device_id_type=mesh_id,
        )

    low_side = g_copy(0, halves.at[1 - me_f], lows.at[1], side_at)
    br_side = g_copy(1, brs.at[0], brs.at[1], side_at)
    low_core = g_copy(2, lows.at[pl.ds(0, 2)], lows.at[pl.ds(2, 2)], mate_at)
    br_core = g_copy(3, brs.at[pl.ds(0, 2)], brs.at[pl.ds(2, 2)], mate_at)

    def output_partial():
        low_core.wait()
        br_core.wait()
        rows = jnp.transpose(brs[...].reshape(4 * tq, brs.shape[2]))
        unit = brs.shape[2] // nctx
        wo[...] = jnp.zeros_like(wo)
        low_rows = lows[...].reshape(4 * tq, half)
        batch = plane // 4
        for r in range(plane):
            first = 2 * unit * (r % batch)
            if first == 0:
                chunk = 2 * unit * batch
                part = jnp.dot(
                    rows[2 * unit * r : 2 * unit * r + chunk], low_rows, preferred_element_type=jnp.float32
                )
            piece = jnp.where(core == 0, part[first : first + unit], part[first + unit : first + 2 * unit])
            wo[static_index(dims, r) + (slice(0, unit), slice(0, half))] = piece.astype(wo.dtype)

    pl.semaphore_wait(barrier, n - 1)
    low_side.start()
    br_side.start()
    for k in range(4):
        w_start((0, 3, 1) if k < 2 else (1,), k)

    def region(kind, stage, at):
        index = [slice(None)] * (nd + 2)
        for axis in orders[kind][:stage]:
            index[axis[0]] = axis[2]
        index[orders[kind][stage][0]] = at
        return tuple(index)

    def stage_copies(p, kind, stage):
        s = p % slots
        axis = orders[kind][stage]
        copies = []
        for k in range(1, axis[1]):
            there, where = axis[3](k)
            copies.append(
                pltpu.make_async_remote_copy(
                    src_ref=dkv.at[(s, kind) + region(kind, stage, there)],
                    dst_ref=recvs[kind * stages + stage].at[s, k - 1],
                    send_sem=send_sem.at[s, kind, stage, k - 1],
                    recv_sem=recv_sem.at[s, kind, stage, k - 1],
                    device_id=where, device_id_type=mesh_id,
                )
            )
        return copies

    def stage_start(p, stage):
        for kind in range(2):
            for copy in stage_copies(p, kind, stage):
                copy.start()

    finals = {}

    def stage_finish(p, stage):
        s = p % slots
        for kind in range(2):
            axis = orders[kind][stage]
            for copy in stage_copies(p, kind, stage):
                copy.wait()
            where = region(kind, stage, axis[2])
            got = recvs[kind * stages + stage]
            free = [i for i in range(nd + 2) if isinstance(where[i], slice)]

            def add(index, lead):
                total = dkv[(s, kind) + index].astype(jnp.float32)
                for k in range(axis[1] - 1):
                    total = total + got[(s, k) + lead].astype(jnp.float32)
                return total

            if not free:
                finals[p, kind] = add(where, ())
            else:
                size = dkv.shape[2 + free[0]]

                def one(i, carry):
                    index = list(where)
                    index[free[0]] = i
                    index = tuple(index)
                    dkv[(s, kind) + index] = add(index, (i,)).astype(dkv.dtype)
                    return carry

                lax.fori_loop(0, size, one, 0)

    def place_index(j):
        index = []
        for i in reversed(range(nd)):
            index.append(lax.rem(j // math.prod(dims[:i]), dims[i]))
        return tuple(index)

    start = me * tq
    last = (start + tq - 1) // bk + 1

    def compute(p):
        s = p % slots
        span = slice(2 * heads * HS * p, 2 * heads * HS * (p + 1))
        qt = q_ref[span, :].astype(jnp.float32) * (1.0 / 8.0)
        dt = heads_rows(do_ref[:, span])
        qg = [padded(qt, heads, g) for g in range(2)]
        dg = [padded(dt, heads, g) for g in range(2)]
        qrows = jnp.concatenate([jnp.transpose(x) for x in qg], axis=0).astype(jnp.bfloat16)
        drows = jnp.concatenate([jnp.transpose(x) for x in dg], axis=0).astype(jnp.bfloat16)
        delta = [
            jnp.sum(dg[g][HS * g : HS * (g + 1)] * ot_ref[2 * p + g], axis=0, keepdims=True)
            for g in range(2)
        ]
        lse = [lse_ref[2 * p + g] for g in range(2)]
        qg = [x.astype(jnp.bfloat16) for x in qg]
        dg = [x.astype(jnp.bfloat16) for x in dg]
        acc_ref[...] = jnp.zeros_like(acc_ref)
        for copy in loads(p) if resident else block_loads(p, 0):
            if not resident:
                copy.start()
            else:
                copy.wait()

        def zero(j, carry):
            at = place_index(j)
            for kind in range(2):
                dkv[(s, kind) + at] = jnp.zeros((2, nf, tq, 2 * HS), dkv.dtype)
            return carry

        def body(j, carry):
            first = pl.multiple_of(j * bk, bk)
            if resident:
                kb = kvbuf[s, 0, pl.ds(first, bk), :]
                vb = kvbuf[s, 1, pl.ds(first, bk), :]
            else:
                for copy in block_loads(p, j):
                    copy.wait()

                @pl.when(j + 1 < last)
                def _():
                    for copy in block_loads(p, j + 1):
                        copy.start()

                kb, vb = kvbuf[lax.rem(j, 2), 0], kvbuf[lax.rem(j, 2), 1]
            kt = jnp.transpose(kb)
            bias = bias_tile((start,), docs, first, bk, tq)
            bias = jnp.concatenate([bias] * heads, axis=1)
            ps = []
            dss = []
            for g in range(2):
                score = jnp.dot(kb, qg[g], preferred_element_type=jnp.float32)
                prob = jnp.exp(score + (bias - lse[g]))
                dp = jnp.dot(vb, dg[g], preferred_element_type=jnp.float32)
                ds = (prob * (dp - delta[g])).astype(jnp.bfloat16)
                ps.append(prob.astype(jnp.bfloat16))
                dss.append(ds)
                acc_ref[g] += jnp.dot(kt[HS * g : HS * (g + 1)], ds, preferred_element_type=jnp.float32)
            dv = jnp.dot(jnp.concatenate(ps, axis=1), drows, preferred_element_type=jnp.float32)
            dk = jnp.dot(jnp.concatenate(dss, axis=1), qrows, preferred_element_type=jnp.float32)
            at = place_index(j)
            dkv[(s, 0) + at] = dk.astype(dkv.dtype).reshape(2, nf, tq, 2 * HS)
            dkv[(s, 1) + at] = dv.astype(dkv.dtype).reshape(2, nf, tq, 2 * HS)
            return carry

        lax.fori_loop(last, plane, zero, 0)
        lax.fori_loop(0, last, body, 0)
        cos_rows = jnp.concatenate([cos_ref[...]] * heads, axis=1) * (1.0 / 8.0)
        sin_rows = jnp.concatenate([sin_ref[...]] * heads, axis=1) * (1.0 / 8.0)
        for g in range(2):
            back = rotate_back(acc_ref[g], cos_rows, sin_rows).astype(gqt_ref.dtype)
            for j in range(heads):
                h = (2 * p + g) * heads + j
                gqt_ref[HS * h : HS * (h + 1), :] = back[:, tq * j : tq * (j + 1)]

    peers = 2 + sum(size - 1 for size in dims)

    def all_peers():
        found = [core_axis[3](1)[1], side_axis[3](1)[1]]
        for axis in lines:
            found += [axis[3](k)[1] for k in range(1, axis[1])]
        return found

    progress = {}

    def advance(p):
        stage = progress[p]
        stage_finish(p, stage)
        progress[p] = stage + 1
        if stage + 1 < stages:
            stage_start(p, stage + 1)
        else:
            del progress[p]
            if p + slots < parts:
                for where in all_peers():
                    pl.semaphore_signal(credit, inc=1, device_id=where, device_id_type=mesh_id)

    for p in range(parts):
        if p >= slots:
            while p - slots in progress:
                advance(p - slots)
        compute(p)
        if p >= slots:
            pl.semaphore_wait(credit, peers)
        stage_start(p, 0)
        progress[p] = 0
        for older in [o for o in progress if o < p]:
            advance(older)
        if p == 0:
            low_side.wait()
            br_side.wait()
            low_core.start()
            br_core.start()
        if p == 1:
            for copy in w_loads:
                copy.wait()
            for k in range(2):
                w_finish((0, 3), k)
                w_start((0, 3), k + 2)
    for k in range(2):
        w_finish((1,), k)
    output_partial()

    def copies_to(k, which):
        other = lax.rem(me_c + k, nctx)
        where = {"ctx": other, "fsdp": me_f}
        block, out = ((qblk, colq_ref), (kvblk, colkv_ref), (small, gains_ref))[which]
        return pltpu.make_async_remote_copy(
            src_ref=block if which == 2 else block.at[other], dst_ref=out.at[me_c],
            send_sem=col_send.at[which, k], recv_sem=col_recv.at[which, k],
            device_id=where, device_id_type=mesh_id,
        )

    def share(which):
        def one(k, carry):
            copies_to(k, which).start()
            return carry

        block, out = ((qblk, colq_ref), (kvblk, colkv_ref), (small, gains_ref))[which]
        pltpu.make_async_copy(block if which == 2 else block.at[me_c], out.at[me_c], own_sem.at[which]).start()
        lax.fori_loop(1, nctx, one, 0)

    def share_wait(which):
        def one(k, carry):
            copies_to(k, which).wait()
            return carry

        block, out = ((qblk, colq_ref), (kvblk, colkv_ref), (small, gains_ref))[which]
        pltpu.make_async_copy(block if which == 2 else block.at[me_c], out.at[me_c], own_sem.at[which]).wait()
        lax.fori_loop(1, nctx, one, 0)

    width_q = 2 * parts * heads * HS
    width_k = 2 * parts * HS
    cq, ck = width_q // nctx, width_k // nctx
    qblk[...] = jnp.zeros_like(qblk)
    kvblk[...] = jnp.zeros_like(kvblk)
    for i in range(nctx):
        qblk[i, 0:cq, :] = gqt_ref[cq * i : cq * (i + 1), :]
    share(0)
    ga_ref[...] = jnp.dot(w_ref[:, :width_q], gqt_ref[...], preferred_element_type=jnp.float32)
    for k in range(4):
        w_start((2,), k)
    pq, pk = qblk.shape[1], kvblk.shape[1]

    def columns(col_ref, first, count):
        def fetch(i, slot):
            return pltpu.make_async_copy(
                inputs_hbm.at[i], brs.at[slot], in_sem.at[slot]
            )

        fetch(0, 0).start()
        cols_acc[first : first + count, :] = jnp.zeros((count, cols_acc.shape[1]), jnp.float32)

        def one(i, carry):
            slot = lax.rem(i, 2)

            @pl.when(i + 1 < nctx)
            def _():
                fetch(i + 1, 1 - slot).start()

            fetch(i, slot).wait()
            cols_acc[first : first + count, :] += jnp.dot(
                col_ref[i], brs[slot], preferred_element_type=jnp.float32
            )
            return carry

        lax.fori_loop(0, nctx, one, 0)

    per_side = plane // 2
    home = (2 * me_f + core) * per_side + place // 2
    slot = lax.rem(place, 2)

    def home_copy(kind, s):
        return pltpu.make_async_remote_copy(
            src_ref=fin.at[kind, s], dst_ref=fin_in.at[kind, slot],
            send_sem=fin_send.at[kind, s], recv_sem=fin_recv.at[kind, slot],
            device_id={"ctx": home, "fsdp": jnp.int32(s)}, device_id_type=mesh_id,
        )

    def self_copy(kind, s):
        return pltpu.make_async_copy(fin.at[kind, s], fin_in.at[kind, slot], fin_send.at[kind, s])

    def to_homes(kind, a):
        total = w_total(a)
        unit, lanes = fin.shape[2], fin.shape[3]
        blank = jnp.zeros((unit, lanes - half), fin.dtype)
        for s in range(2):
            fin[kind, s] = jnp.concatenate([total[:, half * s : half * (s + 1)].astype(fin.dtype), blank], axis=1)
            at_home = (home == me_c) & (me_f == s)

            @pl.when(jnp.logical_not(at_home))
            def _():
                home_copy(kind, s).start()

            @pl.when(at_home)
            def _():
                self_copy(kind, s).start()

    turn = 0
    while progress:
        for p in list(progress):
            advance(p)
        if turn == 0:
            for k in range(2, 4):
                w_finish((0, 3, 1), k)
        if turn == 1:
            for k in range(2):
                w_finish((2,), k)
        if turn == 2:
            for k in range(2, 4):
                w_finish((2,), k)
        turn += 1

    cos_rows, sin_rows = cos_ref[...], sin_ref[...]
    grads = []
    for kind in range(2):
        rows = []
        for p in range(parts):
            both = jnp.transpose(finals[p, kind])
            for g in range(2):
                one = both[HS * g : HS * (g + 1)]
                rows.append(rotate_back(one, cos_rows, sin_rows) if kind == 0 else one)
        grads.append(jnp.concatenate(rows, axis=0).astype(jnp.bfloat16))
    for i in range(nctx):
        kvblk[i, 0:ck, :] = grads[0][ck * i : ck * (i + 1)]
        kvblk[i, ck : 2 * ck, :] = grads[1][ck * i : ck * (i + 1)]
    share(1)
    grad_t = (
        ga_ref[...]
        + jnp.dot(w_ref[:, width_q : width_q + width_k], grads[0], preferred_element_type=jnp.float32)
        + jnp.dot(w_ref[:, width_q + width_k :], grads[1], preferred_element_type=jnp.float32)
    )
    grad = jnp.transpose(grad_t)
    normed = normed_ref[...].astype(jnp.float32) * inv_ref[...]
    product = grad * normed
    gain_sum = jnp.sum(product, axis=0, keepdims=True)
    lanes = 128
    tiles = gain_sum.shape[1] // lanes
    rows = [gain_sum[:, lanes * i : lanes * (i + 1)] for i in range(tiles)]
    rows += [gmlp_ref[:, lanes * i : lanes * (i + 1)] for i in range(tiles)]
    rows += [jnp.zeros((small.shape[0] - 2 * tiles, lanes), jnp.float32)]
    small[...] = jnp.concatenate(rows, axis=0)
    share(2)
    gain = gain_ref[0:1, :]
    scaled = grad * gain
    mean = jnp.mean(scaled * normed, axis=1, keepdims=True)
    tokens_ref[...] = gres_ref[...] + inv_ref[...] * (scaled - normed * mean)

    to_homes(0, 0)
    share_wait(0)
    columns(colq_ref, 0, pq)
    to_homes(1, 3)
    dsum = w_total(1)
    dsend[...] = dsum.astype(dsend.dtype)
    down_copy = g_copy(4, dsend, din, mate_at)
    down_copy.start()
    osum = w_total(2)
    out_ref[...] = osum[: out_ref.shape[0], :half]
    share_wait(1)
    columns(colkv_ref, pq, pk)
    left, right = cols_acc[:, :half], cols_acc[:, half:]
    side_pad = jnp.zeros((pq + pk, half_send.shape[1] - half), half_send.dtype)
    half_send[...] = jnp.concatenate([jnp.where(me_f == 0, right, left).astype(half_send.dtype), side_pad], axis=1)
    half_copy = g_copy(5, half_send, half_in, side_at)
    half_copy.start()
    share_wait(2)
    gain_total = gains_ref[0]
    for i in range(1, nctx):
        gain_total = gain_total + gains_ref[i]
    gain_send[...] = gain_total
    gain_copy = g_copy(6, gain_send, gain_in, side_at)
    gain_copy.start()
    half_copy.wait()
    own_half = jnp.where(me_f == 0, cols_acc[:, :half], cols_acc[:, half:])
    rows = own_half + half_in[:, :half].astype(jnp.float32)
    query_ref[...] = rows[:cq]
    key_ref[...] = rows[pq : pq + ck]
    value_ref[...] = rows[pq + ck : pq + 2 * ck]
    gain_copy.wait()
    gains_out[...] = gain_send[...] + gain_in[...]
    down_copy.wait()
    cols = down_ref.shape[0]

    def unfold(folded):
        return jnp.concatenate(
            [folded[2 * cols * i : 2 * cols * (i + 1)] for i in range(folded.shape[0] // (2 * cols))], axis=1
        )

    dsum, got = unfold(dsum), unfold(din[...].astype(jnp.float32))
    own_cols = jnp.where(core == 0, dsum[:cols], dsum[cols:])
    far_cols = jnp.where(core == 0, got[:cols], got[cols:])
    down_ref[...] = jnp.where(
        core == 0,
        jnp.concatenate([own_cols, far_cols], axis=1),
        jnp.concatenate([far_cols, own_cols], axis=1),
    )
    owner = me_c // per_side
    for kind in range(2):
        for s in range(2):
            at_home = (home == me_c) & (me_f == s)

            @pl.when(jnp.logical_not(at_home))
            def _():
                home_copy(kind, s).wait_send()

            @pl.when(at_home)
            def _():
                self_copy(kind, s).wait()

        for h in range(2):
            holder = (2 * lax.rem(me_c, per_side) + h) * 2 + lax.rem(owner, 2)

            @pl.when(jnp.logical_not((holder == me_c) & (owner // 2 == me_f)))
            def _():
                pltpu.make_async_remote_copy(
                    src_ref=fin.at[0, 0], dst_ref=fin_in.at[kind, h],
                    send_sem=fin_send.at[0, 0], recv_sem=fin_recv.at[kind, h],
                    device_id={"ctx": home, "fsdp": me_f}, device_id_type=mesh_id,
                ).wait_recv()

    for kind, ref in ((0, gate_ref), (1, up_ref)):
        rows = jnp.concatenate([fin_in[kind, 0], fin_in[kind, 1]], axis=0).astype(jnp.float32)
        ref[...] = rows[:, :half]


def backward(nctx, nf, docs, q, do, ot, lse, kv, w, cos_t, sin_t, normed, inv, gain, gres, gmlp, low, branch, gup, dnp, inputs):
    width_q, tq = q.shape
    n_tokens, width_kv = kv.shape
    n = nctx * nf
    parts = width_kv // (4 * HS)
    heads = width_q // HS // (2 * parts)
    dims = bit_dims(nctx // 2)
    lead = tuple(reversed(dims))
    part_bytes = n_tokens * 2 * HS * 2
    slots = parts if parts * part_bytes * 5 <= 24 * 2**20 else 1
    nd = len(dims)
    bf16, f32 = jnp.bfloat16, jnp.float32
    axes = {"core": (nd, 2), "side": (nd + 1, nf)}
    line = [(nd - 1 - i, dims[i]) for i in range(nd)]
    orders = [
        [axes["core"], axes["side"]] + line,
        [axes["core"], axes["side"]] + w_order(line),
    ]
    recvs = []
    for order in orders:
        left = list(lead) + [2, nf]
        for position, size in order:
            left[position] = None
            recvs.append(
                pltpu.VMEM((slots, size - 1) + tuple(x for x in left if x) + (tq, 2 * HS), bf16)
            )
    model_width = low.shape[1]
    half = model_width // nf
    unit, deep = gup.shape[-2], model_width // (nctx // 2)
    quarter = dnp.shape[-2] // deep * 128
    plane = nctx // 2
    tails = [gup.shape[nd:], dnp.shape[nd:], (round_up(deep // 2, 16), round_up(half, 128))]
    for tail in (tails[0][1:], tails[1], tails[2], tails[0][1:]):
        for stage in range(nd - 2):
            recvs.append(pltpu.VMEM((2,) * (nd - 1 - stage) + tail, bf16))
        recvs += [pltpu.VMEM((2,) + tail, bf16), pltpu.VMEM((1,) + tail, bf16)]
    stages = nd + 2
    most = max(dims + [2])
    pq = round_up(width_q // nctx, 16)
    pk = round_up(2 * (2 * parts * HS) // nctx, 16)
    model = w.shape[0]
    sr = round_up(2 * model // 128, 8)
    vmem = pl.BlockSpec(memory_space=pltpu.VMEM)
    smem = pl.BlockSpec(memory_space=pltpu.SMEM)
    hbm = pl.BlockSpec(memory_space=pl.ANY)
    return pl.pallas_call(
        functools.partial(backward_kernel, (nctx, nf, parts, heads, tq, slots)),
        out_shape=[
            jax.ShapeDtypeStruct((tq, model), f32),
            jax.ShapeDtypeStruct((width_q // nctx, half), f32),
            jax.ShapeDtypeStruct((2 * parts * HS // nctx, half), f32),
            jax.ShapeDtypeStruct((2 * parts * HS // nctx, half), f32),
            jax.ShapeDtypeStruct((sr, 128), f32),
            jax.ShapeDtypeStruct((2 * unit, half), f32),
            jax.ShapeDtypeStruct((2 * unit, half), f32),
            jax.ShapeDtypeStruct((deep // 2, 2 * quarter), f32),
            jax.ShapeDtypeStruct((deep // 2, half), f32),
        ],
        in_specs=[smem, vmem, vmem, vmem, vmem, hbm] + [vmem] * 10 + [hbm] * 3,
        out_specs=[vmem] * 9,
        scratch_shapes=[
            pltpu.VMEM((slots, 2, n_tokens, 2 * HS) if slots == parts else (2, 2, 2 * nf * tq, 2 * HS), bf16),
            pltpu.VMEM((slots, 2) + lead + (2, nf, tq, 2 * HS), bf16),
            pltpu.VMEM((2, HS, heads * tq), f32),
            pltpu.VMEM((width_q, tq), bf16),
            pltpu.VMEM((model, tq), f32),
            pltpu.VMEM((nctx, pq, tq), bf16),
            pltpu.VMEM((nctx, pk, tq), bf16),
            pltpu.VMEM((sr, 128), f32),
            pltpu.SemaphoreType.DMA((max(slots, 2), 2)),
            pltpu.SemaphoreType.DMA((slots, 2, stages, most - 1)),
            pltpu.SemaphoreType.DMA((slots, 2, stages, most - 1)),
            pltpu.SemaphoreType.DMA((3, nctx)),
            pltpu.SemaphoreType.DMA((3, nctx)),
            pltpu.SemaphoreType.DMA((3,)),
            pltpu.SemaphoreType.REGULAR,
            pltpu.VMEM(lead[:-1] + tails[0], bf16),
            pltpu.VMEM(lead[:-1] + tails[1], bf16),
            pltpu.VMEM(lead + tails[2], bf16),
            pltpu.VMEM((4,) + branch.shape, bf16),
            pltpu.VMEM((4, tq, half), bf16),
            pltpu.VMEM((2, tq, half), bf16),
            pltpu.VMEM((2, 2, unit, round_up(half, 128)), bf16),
            pltpu.VMEM((2, 2, unit, round_up(half, 128)), bf16),
            pltpu.VMEM(tails[1], bf16),
            pltpu.VMEM(tails[1], bf16),
            pltpu.VMEM((nctx, pq, tq), bf16),
            pltpu.VMEM((nctx, pk, tq), bf16),
            pltpu.VMEM((nctx, sr, 128), f32),
            pltpu.VMEM((pq + pk, model), f32),
            pltpu.VMEM((pq + pk, round_up(half, 128)), bf16),
            pltpu.VMEM((pq + pk, round_up(half, 128)), bf16),
            pltpu.VMEM((sr, 128), f32),
            pltpu.VMEM((sr, 128), f32),
            pltpu.SemaphoreType.DMA((2,)),
            pltpu.SemaphoreType.DMA((7,)),
            pltpu.SemaphoreType.DMA((7,)),
            pltpu.SemaphoreType.DMA((2,)),
            pltpu.SemaphoreType.DMA((4, 4, max(nd - 2, 1))),
            pltpu.SemaphoreType.DMA((4, 4, max(nd - 2, 1))),
            pltpu.SemaphoreType.DMA((4, 3)),
            pltpu.SemaphoreType.DMA((4, 3)),
            pltpu.SemaphoreType.DMA((2, 2)),
            pltpu.SemaphoreType.DMA((2, 2)),
        ]
        + recvs,
        compiler_params=pltpu.CompilerParams(
            collective_id=1, has_side_effects=True, vmem_limit_bytes=63 * 2**20
        ),
        cost_estimate=pl.CostEstimate(flops=10**10, bytes_accessed=3 * 10**7, transcendentals=10**7),
        name="backward",
    )(docs, q, do, ot, lse, kv, w, cos_t, sin_t, normed, inv, gain, gres, gmlp, low, branch, gup, dnp, inputs)


def rotate(rows, cos_rows, sin_rows):
    half_dim = HS // 2
    first, second = rows[:half_dim], rows[half_dim:]
    return jnp.concatenate(
        [first * cos_rows - second * sin_rows, second * cos_rows + first * sin_rows], axis=0
    )


class Axes:
    def __init__(self, nctx, nf):
        self.ctx, self.f = lax.axis_index("ctx"), lax.axis_index("fsdp")
        self.core, self.place = lax.rem(self.ctx, 2), self.ctx // 2
        self.me = self.ctx * nf + self.f
        self.dims = line_dims(nctx // 2)
        self.nd = len(self.dims)
        ctx, f, core, place = self.ctx, self.f, self.core, self.place
        self.core_axis = (self.nd, 2, core, lambda k: (1 - core, {"ctx": place * 2 + 1 - core, "fsdp": f}))
        self.side_axis = (self.nd + 1, 2, f, lambda k: (1 - f, {"ctx": ctx, "fsdp": 1 - f}))
        self.lines = [self.line(i) for i in range(self.nd)]
        self.peer_count = 2 + sum(size - 1 for size in self.dims)

    def at_line(self, i, there):
        stride = math.prod(self.dims[:i])
        own = lax.rem(self.place // stride, self.dims[i])
        return {"ctx": (self.place + (there - own) * stride) * 2 + self.core, "fsdp": self.f}

    def line(self, i):
        size = self.dims[i]
        own = lax.rem(self.place // math.prod(self.dims[:i]), size)

        def peer(k):
            there = lax.rem(own + k, size)
            return there, self.at_line(i, there)

        return (self.nd - 1 - i, size, own, peer)

    def peers(self):
        found = [self.core_axis[3](1)[1], self.side_axis[3](1)[1]]
        for axis in self.lines:
            found += [axis[3](k)[1] for k in range(1, axis[1])]
        return found

    def place_index(self, j):
        return tuple(
            lax.rem(j // math.prod(self.dims[:i]), self.dims[i]) for i in reversed(range(self.nd))
        )


def forward_kernel(plan, docs, tokens_ref, gains_ref, cos_ref, sin_ref, wq, wk, wv, wo, wg, wu, cot,
                   qt_ref, kv_out, low_ref, ot_ref, lse_ref, wqkv_out, wo_out, gu_out, cots_out,
                   attn_in_ref, inv_ref, gain_ref,
                   wbuf, obuf, gubuf, cbuf, gain_far, own_kv, kvb, m_ref, l_ref, acc_ref,
                   load_sem, w_send, w_recv, top_send, top_recv, ag_send, ag_recv, blk_sem, out_sem):
    nctx, nf, parts, heads, tq = plan
    ax = Axes(nctx, nf)
    f, core, place = ax.f, ax.core, ax.place
    mesh_id = pl.DeviceIdType.MESH
    bf16, f32 = jnp.bfloat16, jnp.float32
    width = tokens_ref.shape[1]
    half = width // nf
    width_q, width_k = 2 * parts * heads * HS, 2 * parts * HS
    rows4, rows2 = half // 4, half // 2
    quarter = gu_out.shape[1] // 2
    side = ax.side_axis[3](1)[1]
    mate = ax.core_axis[3](1)[1]
    low = ax.lines[0]
    bit = lax.rem(low[2], 2)
    across = ax.at_line(0, low[2] + 1 - 2 * bit)
    top = ax.nd - 1
    chunks = ax.dims[top]
    z = ax.lines[top][2]

    barrier = pltpu.get_barrier_semaphore()
    for where in ax.peers():
        pl.semaphore_signal(barrier, inc=1, device_id=where, device_id_type=mesh_id)

    def local(src, dst, i):
        return pltpu.make_async_copy(src, dst, load_sem.at[i])

    own_rows = pl.ds(pl.multiple_of(f * half, half), half)
    own_quarter = pl.ds(pl.multiple_of((2 * f + core) * quarter, quarter), quarter)
    loads = [
        local(wk, wbuf.at[own_rows, pl.ds(width_q, width_k)], 0),
        local(wv, wbuf.at[own_rows, pl.ds(width_q + width_k, width_k)], 1),
        local(wq, wbuf.at[own_rows, pl.ds(0, width_q)], 2),
        local(wo, obuf.at[own_rows], 3),
        local(wg.at[:, own_quarter], gubuf.at[own_rows, pl.ds(0, quarter)], 4),
        local(wu.at[:, own_quarter], gubuf.at[own_rows, pl.ds(quarter, quarter)], 5),
        local(cot, cbuf.at[0], 6),
    ]
    for copy in loads:
        copy.start()

    def remote(src, dst, i, where):
        return pltpu.make_async_remote_copy(
            src_ref=src, dst_ref=dst, send_sem=w_send.at[i], recv_sem=w_recv.at[i],
            device_id=where, device_id_type=mesh_id,
        )

    near = pl.multiple_of(core * rows2 + bit * rows4, 16)
    far_x = pl.multiple_of(core * rows2 + (1 - bit) * rows4, 16)
    there = (1 - f) * half

    def piece(base, offset):
        return pl.ds(pl.multiple_of(base + offset, 16), rows4)

    kv_cols, q_cols = pl.ds(width_q, 2 * width_k), pl.ds(0, width_q)
    mine = f * half
    gains_copy = remote(gains_ref, gain_far, 0, side)
    kv_y = [
        remote(wk.at[piece(0, near)], wbuf.at[piece(mine, near), pl.ds(width_q, width_k)], 1, side),
        remote(wv.at[piece(0, near)], wbuf.at[piece(mine, near), pl.ds(width_q + width_k, width_k)], 2, side),
    ]
    q_y = [remote(wq.at[piece(0, near)], wbuf.at[piece(mine, near), q_cols], 3, side)]
    o_y = [remote(wo.at[piece(0, near)], obuf.at[piece(mine, near)], 4, side)]

    def forwards(buf, cols, first):
        def part(offset):
            return buf.at[piece(there, offset), cols] if cols is not None else buf.at[piece(there, offset)]

        return [
            remote(part(near), part(near), first, across),
            remote(part(near), part(near), first + 1, mate),
            remote(part(far_x), part(far_x), first + 2, mate),
        ]

    kv_f = forwards(wbuf, kv_cols, 5)
    q_f = forwards(wbuf, q_cols, 8)
    o_f = forwards(obuf, None, 11)
    far_quarter = pl.ds(pl.multiple_of((2 * (1 - f) + core) * quarter, quarter), quarter)

    deep = lax.rem(z, 2)
    above = ax.at_line(top, z + 1 - 2 * deep)

    def gu_rows(base, which=bit):
        return pl.ds(pl.multiple_of(base + which * rows2 + deep * rows4, 16), rows4)

    gu_y = [
        remote(wg.at[gu_rows(0), far_quarter], gubuf.at[gu_rows(mine), pl.ds(0, quarter)], 14, side),
        remote(wu.at[gu_rows(0), far_quarter], gubuf.at[gu_rows(mine), pl.ds(quarter, quarter)], 15, side),
    ]
    gu_x = remote(gubuf.at[gu_rows(there)], gubuf.at[gu_rows(there)], 16, across)
    gu_z = [
        remote(gubuf.at[gu_rows(there, which)], gubuf.at[gu_rows(there, which)], 19 + i, above)
        for i, which in enumerate((bit, 1 - bit))
    ]
    cot_y = remote(cot, cbuf.at[1], 17, side)
    cot_c = remote(cbuf.at[pl.ds(0, 2)], cbuf.at[pl.ds(2, 2)], 18, mate)

    pl.semaphore_wait(barrier, ax.peer_count)
    gains_copy.start()
    for copy in kv_y + q_y:
        copy.start()

    hidden = tokens_ref[...].astype(f32)
    inv = lax.rsqrt(jnp.mean(hidden * hidden, axis=1, keepdims=True) + EPS)
    inv_ref[...] = inv
    gains_copy.wait()
    near_gain, far_gain = gains_ref[0:1, :], gain_far[0:1, :]
    gain = jnp.where(
        f == 0,
        jnp.concatenate([near_gain, far_gain], axis=1),
        jnp.concatenate([far_gain, near_gain], axis=1),
    )
    near_mlp, far_mlp = gains_ref[1:2, :], gain_far[1:2, :]
    gain_ref[0:1, :] = gain
    gain_ref[1:2, :] = jnp.where(
        f == 0,
        jnp.concatenate([near_mlp, far_mlp], axis=1),
        jnp.concatenate([far_mlp, near_mlp], axis=1),
    )
    attn_in = (hidden * inv * gain).astype(bf16)
    attn_in_ref[...] = attn_in

    for copy in kv_y:
        copy.wait()
    kv_f[0].start()
    kv_f[1].start()
    for copy in q_y:
        copy.wait()
    for copy in o_y + gu_y:
        copy.start()
    kv_f[0].wait()
    kv_f[2].start()
    q_f[0].start()
    q_f[1].start()
    for copy in loads[:3]:
        copy.wait()
    kv_f[1].wait()
    kv_f[2].wait()
    kv = jnp.dot(attn_in, wbuf[:, width_q:], preferred_element_type=f32)
    cos_rows, sin_rows = cos_ref[...], sin_ref[...]
    kt = jnp.transpose(kv[:, :width_k])
    k_rot = jnp.concatenate(
        [rotate(kt[HS * g : HS * (g + 1)], cos_rows, sin_rows) for g in range(2 * parts)], axis=0
    )
    own_kv[:, :width_k] = jnp.transpose(k_rot).astype(bf16)
    own_kv[:, width_k:] = kv[:, width_k:].astype(bf16)
    own_at = ax.place_index(place) + (core, f)
    put = pltpu.make_async_copy(own_kv, kv_out.at[own_at], out_sem.at[0])
    put.start()

    def top_copy(k):
        return pltpu.make_async_remote_copy(
            src_ref=own_kv, dst_ref=kv_out.at[own_at],
            send_sem=top_send.at[k - 1], recv_sem=top_recv.at[k - 1],
            device_id=ax.at_line(top, lax.rem(z + k, chunks)), device_id_type=mesh_id,
        )

    for k in range(1, chunks):
        @pl.when(z + k < chunks)
        def _():
            top_copy(k).start()

    lower = ax.lines[:top]
    orders = [lower + [ax.side_axis, ax.core_axis], [ax.side_axis] + lower + [ax.core_axis]]
    stages = len(orders[0])

    def ag_copies(k, stage):
        copies = []
        for kind in range(2):
            index = [None] * (ax.nd + 2)
            index[0] = z - k
            for i, axis in enumerate(orders[kind]):
                index[axis[0]] = slice(None) if i < stage else axis[2]
            region = kv_out.at[tuple(index) + (slice(None), pl.ds(kind * width_k, width_k))]
            axis = orders[kind][stage]
            for i in range(1, axis[1]):
                copies.append(
                    pltpu.make_async_remote_copy(
                        src_ref=region, dst_ref=region,
                        send_sem=ag_send.at[k, kind, stage, i - 1],
                        recv_sem=ag_recv.at[k, kind, stage, i - 1],
                        device_id=axis[3](i)[1], device_id_type=mesh_id,
                    )
                )
        return copies

    def tick(k, stage):
        @pl.when(z >= k)
        def _():
            if stage == 0:
                if k > 0:
                    top_copy(k).wait_recv()
            else:
                for copy in ag_copies(k, stage - 1):
                    copy.wait()
            if stage < stages:
                for copy in ag_copies(k, stage):
                    copy.start()

    put.wait()
    tick(0, 0)
    q_f[0].wait()
    q_f[2].start()
    q_f[1].wait()
    q_f[2].wait()
    back = pltpu.make_async_copy(wbuf, wqkv_out, out_sem.at[1])
    back.start()
    query = jnp.dot(attn_in, wbuf[:, :width_q], preferred_element_type=f32)
    query_t = jnp.transpose(query)
    for h in range(2 * parts * heads):
        qt_ref[HS * h : HS * (h + 1), :] = rotate(
            query_t[HS * h : HS * (h + 1)], cos_rows, sin_rows
        ).astype(bf16)
    m_ref[...] = jnp.full_like(m_ref, NEG)
    l_ref[...] = jnp.zeros_like(l_ref)
    acc_ref[...] = jnp.zeros_like(acc_ref)

    bk = 2 * nf * tq
    per_chunk = math.prod(ax.dims[:top])
    start = ax.me * tq

    def block_copy(j, slot):
        return pltpu.make_async_copy(kv_out.at[ax.place_index(j)], kvb.at[slot], blk_sem.at[slot])

    def attend(k):
        first_block = (z - k) * per_chunk
        count = jnp.minimum(place - first_block + 1, per_chunk)

        @pl.when(z >= k)
        def _():
            block_copy(first_block, 0).start()

            def block(i, carry):
                j = first_block + i
                slot = lax.rem(i, 2)

                @pl.when(i + 1 < count)
                def _():
                    block_copy(j + 1, 1 - slot).start()

                block_copy(j, slot).wait()
                bias = bias_tile((start,), docs, j * bk, bk, tq)
                bias = jnp.concatenate([bias] * heads, axis=1)
                for p in range(parts):
                    kb = kvb[slot, :, :, :, 2 * HS * p : 2 * HS * (p + 1)].reshape(bk, 2 * HS)
                    vb = kvb[slot, :, :, :, width_k + 2 * HS * p : width_k + 2 * HS * (p + 1)]
                    vt = jnp.transpose(vb.reshape(bk, 2 * HS))
                    rows = qt_ref[2 * heads * HS * p : 2 * heads * HS * (p + 1), :] * bf16(1.0 / 8.0)
                    for g in range(2):
                        at = 2 * p + g
                        s = jnp.dot(kb, padded(rows, heads, g), preferred_element_type=f32) + bias
                        m = m_ref[at]
                        new = jnp.maximum(m, jnp.max(s, axis=0, keepdims=True))
                        prob = jnp.exp(s - new)
                        decay = jnp.exp(m - new)
                        m_ref[at] = new
                        l_ref[at] = l_ref[at] * decay + jnp.sum(prob, axis=0, keepdims=True)
                        acc_ref[at] = acc_ref[at] * decay + jnp.dot(
                            vt[HS * g : HS * (g + 1)], prob.astype(bf16), preferred_element_type=f32
                        )
                return carry

            lax.fori_loop(0, count, block, 0)

    for turn in range(1, chunks + stages):
        for k in range(chunks):
            stage = turn - k
            if (k, stage) != (0, 0) and 0 <= stage <= stages:
                tick(k, stage)
        if turn == 4:
            for copy in o_y + gu_y:
                copy.wait()
            o_f[0].start()
            o_f[1].start()
            gu_x.start()
            gu_z[0].start()
        if turn == 3:
            cot_y.start()
        if turn == 6:
            o_f[0].wait()
            o_f[2].start()
            gu_x.wait()
            gu_z[1].start()
        if turn == 5:
            cot_y.wait()
            loads[6].wait()
            cot_c.start()
        if turn >= stages:
            attend(turn - stages)
    for p in range(parts):
        outs = []
        for g in range(2):
            at = 2 * p + g
            out = acc_ref[at] / l_ref[at]
            outs.append(out)
            ot_ref[at] = out
            lse_ref[at] = m_ref[at] + jnp.log(l_ref[at])
        low_ref[:, 2 * heads * HS * p : 2 * heads * HS * (p + 1)] = head_lanes(outs, heads, tq).astype(bf16)

    for k in range(1, chunks):
        @pl.when(z + k < chunks)
        def _():
            top_copy(k).wait_send()
    for copy in loads[3:6]:
        copy.wait()
    backs = [back]
    for waits, src, dst in (
        (o_f[1:], obuf, wo_out), ([cot_c], cbuf, cots_out), (gu_z, gubuf, gu_out)
    ):
        for copy in waits:
            copy.wait()
        backs.append(pltpu.make_async_copy(src, dst, out_sem.at[1 + len(backs)]))
        backs[-1].start()
    for copy in backs:
        copy.wait()


def forward(nctx, nf, docs, tokens, gains, cos_t, sin_t, wq, wk, wv, wo, wg, wu, cot):
    tq, width = tokens.shape
    width_q, width_k = wq.shape[1], wk.shape[1]
    parts = width_k // (2 * HS)
    heads = width_q // HS // (2 * parts)
    hidden_units = wg.shape[1]
    quarter = hidden_units // (2 * nf)
    dims = line_dims(nctx // 2)
    lead = tuple(reversed(dims))
    most = max(dims + [2])
    chunks = dims[-1]
    stages = len(dims) + 1
    bf16, f32 = jnp.bfloat16, jnp.float32
    vmem = pl.BlockSpec(memory_space=pltpu.VMEM)
    smem = pl.BlockSpec(memory_space=pltpu.SMEM)
    hbm = pl.BlockSpec(memory_space=pl.ANY)
    dma = pltpu.SemaphoreType.DMA
    return pl.pallas_call(
        functools.partial(forward_kernel, (nctx, nf, parts, heads, tq)),
        out_shape=[
            jax.ShapeDtypeStruct((width_q, tq), bf16),
            jax.ShapeDtypeStruct(lead + (2, nf, tq, 2 * width_k), bf16),
            jax.ShapeDtypeStruct((tq, width_q), bf16),
            jax.ShapeDtypeStruct((2 * parts, HS, heads * tq), f32),
            jax.ShapeDtypeStruct((2 * parts, 1, heads * tq), f32),
            jax.ShapeDtypeStruct((width, width_q + 2 * width_k), bf16),
            jax.ShapeDtypeStruct((nf * wo.shape[0], wo.shape[1]), bf16),
            jax.ShapeDtypeStruct((width, 2 * quarter), bf16),
            jax.ShapeDtypeStruct((2 * nf, tq, width), bf16),
            jax.ShapeDtypeStruct((tq, width), bf16),
            jax.ShapeDtypeStruct((tq, 1), f32),
            jax.ShapeDtypeStruct((2, width), f32),
        ],
        in_specs=[smem, vmem, vmem, vmem, vmem] + [hbm] * 7,
        out_specs=[vmem, hbm, vmem, vmem, vmem, hbm, hbm, hbm, hbm, vmem, vmem, vmem],
        scratch_shapes=[
            pltpu.VMEM((width, width_q + 2 * width_k), bf16),
            pltpu.VMEM((nf * wo.shape[0], wo.shape[1]), bf16),
            pltpu.VMEM((width, 2 * quarter), bf16),
            pltpu.VMEM((2 * nf, tq, width), bf16),
            pltpu.VMEM(gains.shape, f32),
            pltpu.VMEM((tq, 2 * width_k), bf16),
            pltpu.VMEM((2, 2, nf, tq, 2 * width_k), bf16),
            pltpu.VMEM((2 * parts, 1, heads * tq), f32),
            pltpu.VMEM((2 * parts, 1, heads * tq), f32),
            pltpu.VMEM((2 * parts, HS, heads * tq), f32),
            dma((7,)),
            dma((21,)),
            dma((21,)),
            dma((chunks - 1,)),
            dma((chunks - 1,)),
            dma((chunks, 2, stages, most - 1)),
            dma((chunks, 2, stages, most - 1)),
            dma((2,)),
            dma((5,)),
        ],
        compiler_params=pltpu.CompilerParams(
            collective_id=0, has_side_effects=True, vmem_limit_bytes=60 * 2**20
        ),
        name="forward",
    )(docs, tokens, gains, cos_t, sin_t, wq, wk, wv, wo, wg, wu, cot)


def feed_forward_kernel(plan, tokens_ref, low_ref, attn_in_ref, gains_ref, wo_hbm, gu_hbm, down_hbm, cots_hbm,
                        result_ref, gres_ref, branch_ref, gattn_ref, gmlp_ref, gup_ref, dnp_ref, inputs_out,
                        wo, gu, down, cots, xs, grads, mixed, gm, sums, sent, core_in, side_in, side_out,
                        load_sem, x_send, x_recv, s_send, s_recv, top_send, top_recv,
                        ag_send, ag_recv, out_sem):
    nctx, nf = plan
    ax = Axes(nctx, nf)
    f, core, place = ax.f, ax.core, ax.place
    mesh_id = pl.DeviceIdType.MESH
    bf16, f32 = jnp.bfloat16, jnp.float32
    tq, width = tokens_ref.shape
    quarter = down.shape[0]
    side = ax.side_axis[3](1)[1]
    mate = ax.core_axis[3](1)[1]
    top = ax.nd - 1
    chunks = ax.dims[top]
    z = ax.lines[top][2]

    barrier = pltpu.get_barrier_semaphore()
    for where in ax.peers():
        pl.semaphore_signal(barrier, inc=1, device_id=where, device_id_type=mesh_id)
    loads = [
        pltpu.make_async_copy(src, dst, load_sem.at[i])
        for i, (src, dst) in enumerate((
            (wo_hbm, wo), (cots_hbm, cots),
            (down_hbm.at[pl.ds(pl.multiple_of(core * quarter, quarter), quarter)], down), (gu_hbm, gu),
        ))
    ]
    for copy in loads:
        copy.start()

    def remote(src, dst, sends, recvs, i, where):
        return pltpu.make_async_remote_copy(
            src_ref=src, dst_ref=dst, send_sem=sends.at[i], recv_sem=recvs.at[i],
            device_id=where, device_id_type=mesh_id,
        )

    hidden = tokens_ref[...].astype(f32)
    own_at = ax.place_index(place) + (core,)
    put = pltpu.make_async_copy(attn_in_ref, inputs_out.at[own_at], out_sem.at[0])

    def top_copy(k):
        return pltpu.make_async_remote_copy(
            src_ref=attn_in_ref, dst_ref=inputs_out.at[own_at],
            send_sem=top_send.at[k - 1], recv_sem=top_recv.at[k - 1],
            device_id=ax.at_line(top, lax.rem(z + k, chunks)), device_id_type=mesh_id,
        )

    order = ax.lines[:top] + [ax.core_axis]
    stages = len(order)

    def ag_copies(k, stage):
        index = [None] * (ax.nd + 1)
        index[0] = lax.rem(z + chunks - k, chunks)
        for i, axis in enumerate(order):
            index[axis[0]] = slice(None) if i < stage else axis[2]
        region = inputs_out.at[tuple(index)]
        axis = order[stage]
        return [
            pltpu.make_async_remote_copy(
                src_ref=region, dst_ref=region,
                send_sem=ag_send.at[k, stage, i - 1], recv_sem=ag_recv.at[k, stage, i - 1],
                device_id=axis[3](i)[1], device_id_type=mesh_id,
            )
            for i in range(1, axis[1])
        ]

    def tick(turn):
        for k in range(chunks):
            stage = turn - k
            if not 0 <= stage <= stages:
                continue
            if stage == 0:
                if k > 0:
                    top_copy(k).wait()
                else:
                    put.wait()
            else:
                for copy in ag_copies(k, stage - 1):
                    copy.wait()
            if stage < stages:
                for copy in ag_copies(k, stage):
                    copy.start()

    pl.semaphore_wait(barrier, ax.peer_count)
    put.start()
    top_copy(1).start()
    tick(0)

    loads[0].wait()
    resid = hidden + jnp.dot(low_ref[...], wo[...], preferred_element_type=f32)
    inv = lax.rsqrt(jnp.mean(resid * resid, axis=1, keepdims=True) + EPS)
    normed = resid * inv
    gain = gains_ref[1:2, :]
    xs[0] = (normed * gain).astype(bf16)
    x_side = remote(xs.at[0], xs.at[1], x_send, x_recv, 0, side)
    x_core = remote(xs.at[0], xs.at[2], x_send, x_recv, 1, mate)
    x_far = remote(xs.at[1], xs.at[3], x_send, x_recv, 2, mate)
    x_side.start()
    x_core.start()

    def rows(slot):
        return slice(slot * tq, (slot + 1) * tq)

    for copy in loads[1:3]:
        copy.wait()
    gm[...] = lax.dot_general(
        cots[...].reshape(4 * tq, width), down[...], (((1,), (1,)), ((), ())), preferred_element_type=f32
    )
    loads[3].wait()
    top_copy(2).start()
    step = 256

    def both(ref, a, b, span=slice(None)):
        return jnp.concatenate([ref[a, :, span], ref[b, :, span]], axis=0)

    def compute(a, b):
        x = both(xs, a, b)
        for n in range(quarter // step):
            span = slice(n * step, (n + 1) * step)
            up_span = slice(quarter + n * step, quarter + (n + 1) * step)
            gate = jnp.dot(x, gu[:, span], preferred_element_type=f32)
            up = jnp.dot(x, gu[:, up_span], preferred_element_type=f32)
            sig = jax.nn.sigmoid(gate)
            act = gate * sig
            grad = jnp.concatenate([gm[rows(a), span], gm[rows(b), span]], axis=0)
            mix = (act * up).astype(bf16)
            grad_gate = (grad * up * sig * (1.0 + gate * (1.0 - sig))).astype(bf16)
            grad_up = (grad * act).astype(bf16)
            for i, slot in enumerate((a, b)):
                mixed[slot, :, span] = mix[rows(i)]
                grads[slot, :, span] = grad_gate[rows(i)]
                grads[slot, :, up_span] = grad_up[rows(i)]
        total = lax.dot_general(
            both(grads, a, b), gu[...], (((1,), (1,)), ((), ())), preferred_element_type=f32
        )
        for i, slot in enumerate((a, b)):
            sums[0, slot] = total[rows(i)]

    def outputs(a, b):
        total = jnp.dot(both(mixed, a, b), down[...], preferred_element_type=f32)
        for i, slot in enumerate((a, b)):
            sums[1, slot] = total[rows(i)]

    def to_core(kind, slot):
        i = 2 * kind + slot - 2
        return remote(sent.at[i], core_in.at[i], s_send, s_recv, i, mate)

    def to_side(kind):
        return remote(side_out.at[kind], side_in.at[kind], s_send, s_recv, 4 + kind, side)

    def give_core(kind, slot):
        sent[2 * kind + slot - 2] = sums[kind, slot].astype(bf16)
        to_core(kind, slot).start()

    def give_side(kind):
        to_core(kind, 3).wait()
        side_out[kind] = (sums[kind, 1] + core_in[2 * kind + 1].astype(f32)).astype(bf16)
        to_side(kind).start()

    x_core.wait()
    compute(0, 2)
    give_core(0, 2)
    top_copy(3).start()
    x_side.wait()
    x_far.start()
    tick(1)
    outputs(0, 2)
    give_core(1, 2)
    x_far.wait()
    compute(1, 3)
    give_core(0, 3)
    tick(2)
    outputs(1, 3)
    give_side(0)
    give_core(1, 3)
    flat_x = xs[...].reshape(4 * tq, width)
    pieces = nctx // 2
    unit = quarter // pieces
    tall = max(unit, 256)
    for kind in range(2):
        for n in range(quarter // tall):
            span = slice(kind * quarter + n * tall, kind * quarter + (n + 1) * tall)
            cols = jnp.transpose(jnp.concatenate([grads[s, :, span] for s in range(4)], axis=0))
            part = jnp.dot(cols, flat_x, preferred_element_type=f32).astype(bf16)
            first = n * tall
            while first < (n + 1) * tall:
                piece, at = first // unit, first % unit
                end = min((piece + 1) * unit, (n + 1) * tall)
                gup_ref[static_index(bit_dims(nctx // 2), piece) + (kind, slice(at, at + end - first))] = part[
                    first - n * tall : end - n * tall
                ]
                first = end
        if kind == 0:
            give_side(1)
            tick(3)
    unit = width // pieces
    flat_mixed = mixed[...].reshape(4 * tq, quarter)
    for n in range(width // 384):
        cols = jnp.transpose(jnp.concatenate([cots[s, :, 384 * n : 384 * (n + 1)] for s in range(4)], axis=0))
        part = jnp.dot(cols, flat_mixed, preferred_element_type=f32).astype(bf16)
        first = n * 384
        while first < (n + 1) * 384:
            piece, at = first // unit, first % unit
            end = min((piece + 1) * unit, (n + 1) * 384)
            rows_of = part[first - n * 384 : end - n * 384]
            for c in range(quarter // 128):
                dnp_ref[
                    static_index(bit_dims(nctx // 2), piece)
                    + (slice(c * unit + at, c * unit + at + end - first),)
                ] = rows_of[:, 128 * c : 128 * (c + 1)]
            first = end

    tick(4)
    to_core(0, 2).wait()
    to_side(0).wait()
    grad = sums[0, 0] + core_in[0].astype(f32) + side_in[0].astype(f32)
    product = grad * normed
    gmlp_ref[...] = jnp.sum(product, axis=0, keepdims=True)
    scaled = grad * gain
    mean = jnp.mean(scaled * normed, axis=1, keepdims=True)
    gres = cots[0].astype(f32) + inv * (scaled - normed * mean)
    gres_ref[...] = gres
    branch = gres.astype(bf16)
    branch_ref[...] = branch
    gattn_ref[...] = lax.dot_general(
        branch, wo[...], (((1,), (1,)), ((), ())), preferred_element_type=f32
    ).astype(bf16)
    to_core(1, 2).wait()
    to_side(1).wait()
    result_ref[...] = (resid + sums[1, 0] + core_in[2].astype(f32) + side_in[1].astype(f32)).astype(bf16)
    for turn in range(5, chunks + stages):
        tick(turn)


def static_index(dims, piece):
    return tuple(piece // math.prod(dims[:i]) % dims[i] for i in reversed(range(len(dims))))


def feed_forward(nctx, nf, tokens, low, attn_in, gains, wo, gu, down, cots):
    tq, width = tokens.shape
    quarter = gu.shape[1] // 2
    dims = line_dims(nctx // 2)
    bits = bit_dims(nctx // 2)
    lead = tuple(reversed(dims))
    plane = nctx // 2
    chunks, stages, most = dims[-1], len(dims), max(dims + [2])
    bf16, f32 = jnp.bfloat16, jnp.float32
    vmem = pl.BlockSpec(memory_space=pltpu.VMEM)
    hbm = pl.BlockSpec(memory_space=pl.ANY)
    dma = pltpu.SemaphoreType.DMA
    return pl.pallas_call(
        functools.partial(feed_forward_kernel, (nctx, nf)),
        out_shape=[
            jax.ShapeDtypeStruct((tq, width), bf16),
            jax.ShapeDtypeStruct((tq, width), f32),
            jax.ShapeDtypeStruct((tq, width), bf16),
            jax.ShapeDtypeStruct((tq, width), bf16),
            jax.ShapeDtypeStruct((1, width), f32),
            jax.ShapeDtypeStruct(tuple(bits) + (2, quarter // plane, width), bf16),
            jax.ShapeDtypeStruct(tuple(bits) + (width // plane * (quarter // 128), 128), bf16),
            jax.ShapeDtypeStruct(lead + (2, tq, width), bf16),
        ],
        in_specs=[vmem] * 4 + [hbm] * 4,
        out_specs=[vmem] * 7 + [hbm],
        scratch_shapes=[
            pltpu.VMEM(wo.shape, bf16),
            pltpu.VMEM(gu.shape, bf16),
            pltpu.VMEM((quarter, width), bf16),
            pltpu.VMEM((4, tq, width), bf16),
            pltpu.VMEM((4, tq, width), bf16),
            pltpu.VMEM((4, tq, 2 * quarter), bf16),
            pltpu.VMEM((4, tq, quarter), bf16),
            pltpu.VMEM((4 * tq, quarter), f32),
            pltpu.VMEM((2, 4, tq, width), f32),
            pltpu.VMEM((4, tq, width), bf16),
            pltpu.VMEM((4, tq, width), bf16),
            pltpu.VMEM((2, tq, width), bf16),
            pltpu.VMEM((2, tq, width), bf16),
            dma((4,)),
            dma((4,)),
            dma((4,)),
            dma((6,)),
            dma((6,)),
            dma((chunks - 1,)),
            dma((chunks - 1,)),
            dma((chunks, stages, most - 1)),
            dma((chunks, stages, most - 1)),
            dma((1,)),
        ],
        compiler_params=pltpu.CompilerParams(
            collective_id=2, has_side_effects=True, vmem_limit_bytes=60 * 2**20
        ),
        name="feed_forward",
    )(tokens, low, attn_in, gains, wo, gu, down, cots)


def finish_kernel(*refs):
    count = len(refs) // 2
    for src, dst in zip(refs[:count], refs[count:]):
        dst[...] = src[...]


def finish(*values):
    def whole(x):
        return pl.BlockSpec(x.shape, lambda i: (0,) * len(x.shape))

    return pl.pallas_call(
        finish_kernel,
        grid=(1,),
        out_shape=[jax.ShapeDtypeStruct(x.shape, x.dtype) for x in values],
        in_specs=[whole(x) for x in values],
        out_specs=[whole(x) for x in values],
        compiler_params=pltpu.CompilerParams(vmem_limit_bytes=60 * 2**20),
        name="finish",
    )(*values)


def per_device(
    nctx,
    nf,
    tokens,
    query_weight,
    key_projection,
    value_projection,
    output_weight,
    gate_weight,
    up_weight,
    down_weight,
    norm_attn,
    norm_mlp,
    doc_starts,
    cotangent,
):
    token_rows, width = tokens.shape
    n_tokens = token_rows * nctx * nf
    bf16, f32 = jnp.bfloat16, jnp.float32

    own_device = lax.axis_index(AXES)
    own_index = layout_rows(own_device, token_rows)
    own_begin = doc_begin(own_index, doc_starts)
    cosine_table, sine_table = rope_tables(own_index - own_begin)
    cosine_table, sine_table = cosine_table.T, sine_table.T
    gains = jnp.pad(jnp.stack([norm_attn, norm_mlp]).astype(f32), ((0, 6), (0, 0)))
    (
        query_rot, key_values, attn_low, attn_exact, log_total, qkv_full, output_full, gate_up,
        cotangents, attention_input, inv_attn, gains,
    ) = forward(
        nctx, nf, doc_starts, tokens, gains, cosine_table, sine_table, query_weight, key_projection,
        value_projection, output_weight, gate_weight, up_weight, cotangent,
    )
    key_width = KEY_VALUE_HEADS * HEAD_SIZE
    key_values = key_values.reshape(n_tokens, 2 * key_width)
    result, grad_resid, grad_branch, grad_attn, gain_mlp_partial, gate_up_partial, down_partial, inputs_all = feed_forward(
        nctx, nf, tokens, attn_low, attention_input, gains, output_full, gate_up, down_weight,
        cotangents.reshape(2 * nf, token_rows, width),
    )

    tokens_grad, query_sum, key_sum, value_sum, gain_sums, gate_sum, up_sum, down_sum, output_sum = backward(
        nctx, nf, doc_starts, query_rot, grad_attn, attn_exact, log_total, key_values, qkv_full,
        cosine_table, sine_table, tokens, inv_attn, gains, grad_resid,
        gain_mlp_partial, attn_low, grad_branch, gate_up_partial, down_partial,
        inputs_all.reshape(nctx, token_rows, width),
    )

    gain_sums = gain_sums[: 2 * width // 128].reshape(2, width)
    result, tokens_grad, *sums = finish(
        result, tokens_grad, query_sum, key_sum, value_sum, output_sum, gate_sum, up_sum, down_sum
    )
    return (result, tokens_grad, *(weight.T for weight in sums), gain_sums[0], gain_sums[1])


def solution(mesh):
    return jax.shard_map(
        functools.partial(per_device, mesh.shape["ctx"], mesh.shape["fsdp"]),
        mesh=mesh,
        in_specs=(
            P(("ctx", "fsdp"), None),
            P("fsdp", None),
            P("fsdp", None),
            P("fsdp", None),
            P("fsdp", None),
            P("fsdp", None),
            P("fsdp", None),
            P("fsdp", None),
            P("fsdp"),
            P("fsdp"),
            P(),
            P(("ctx", "fsdp"), None),
        ),
        out_specs=(
            P(("ctx", "fsdp"), None),
            P(("ctx", "fsdp"), None),
            P("fsdp", "ctx"),
            P("fsdp", "ctx"),
            P("fsdp", "ctx"),
            P("fsdp", "ctx"),
            P("fsdp", "ctx"),
            P("fsdp", "ctx"),
            P("fsdp", "ctx"),
            P(),
            P(),
        ),
        check_vma=False,
    )
```

```python
import functools
import math

import jax
import jax.numpy as jnp
from jax import lax
from jax.experimental import pallas as pl
from jax.experimental.pallas import tpu as pltpu
from jax.sharding import PartitionSpec as P

QUERY_HEADS = 18
KEY_VALUE_HEADS = 6
HEAD_SIZE = 64
HS = HEAD_SIZE

EPS = 1e-05
THETA = 10000.0
NEG = -1e30
AXES = ("ctx", "fsdp")


def rope_tables(positions):
    half_dim = HEAD_SIZE // 2
    frequency = jnp.exp(-math.log(THETA) * jnp.arange(half_dim, dtype=jnp.float32) / half_dim)
    angles = positions.astype(jnp.float32)[:, None] * frequency[None, :]
    return (jnp.cos(angles), jnp.sin(angles))


def apply_rotary(values, cosine_table, sine_table):
    half_dim = values.shape[-1] // 2
    first_half = values[..., :half_dim]
    second_half = values[..., half_dim:]
    cos_rows = cosine_table[:, None, :]
    sin_rows = sine_table[:, None, :]
    return jnp.concatenate(
        [
            first_half * cos_rows - second_half * sin_rows,
            second_half * cos_rows + first_half * sin_rows,
        ],
        axis=-1,
    )


def unrotate(values, cosine_table, sine_table):
    half_dim = values.shape[-1] // 2
    first_half = values[..., :half_dim]
    second_half = values[..., half_dim:]
    cos_rows = cosine_table[:, None, :]
    sin_rows = sine_table[:, None, :]
    return jnp.concatenate(
        [
            first_half * cos_rows + second_half * sin_rows,
            second_half * cos_rows - first_half * sin_rows,
        ],
        axis=-1,
    )


def doc_begin(indices, doc_starts):
    marked = jnp.where(indices[:, None] >= doc_starts[None, :], doc_starts[None, :], 0)
    return jnp.max(marked, axis=1)


def layout_rows(device, row_count):
    return device * row_count + jnp.arange(row_count, dtype=jnp.int32)


def heads_rows(natural):
    return jnp.transpose(natural.astype(jnp.float32))
def padded(rows, heads, g):
    top = jnp.concatenate([rows[HS*(heads*g+j):HS*(heads*g+j+1)] for j in range(heads)], axis=1)
    z = jnp.zeros_like(top)
    return jnp.concatenate([top, z] if g == 0 else [z, top], axis=0)
def head_lanes(per_group, heads, tq):
    return jnp.transpose(jnp.concatenate([per_group[g][:, tq*j:tq*(j+1)] for g in range(2) for j in range(heads)], axis=0))
def bias_tile(info, docs, first, bk, tq):
    query = info[0] + lax.broadcasted_iota(jnp.int32, (1, tq), 1)
    begin = jnp.zeros((1, tq), jnp.int32)
    for i in range(docs.shape[0]):
        begin = jnp.maximum(begin, jnp.where(query >= docs[i], docs[i], 0))
    key = first + lax.broadcasted_iota(jnp.int32, (bk, 1), 0)
    return jnp.where((key <= query) & (key >= begin), 0.0, NEG)


def line_dims(count):
    fours = 0
    while count % 4 == 0:
        count //= 4
        fours += 1
    return ([count] if count > 1 else []) + [4] * fours


def rotate_back(rows, cos_rows, sin_rows):
    half_dim = HS // 2
    first, second = rows[:half_dim], rows[half_dim:]
    return jnp.concatenate(
        [first * cos_rows + second * sin_rows, second * cos_rows - first * sin_rows], axis=0
    )


def w_order(lines):
    return [lines[-2]] + lines[1:-2] + [lines[0], lines[-1]]


def bit_dims(count):
    return [2] * (count.bit_length() - 1)


def round_up(value, unit):
    return -(-value // unit) * unit


def backward_kernel(plan, docs, q_ref, do_ref, ot_ref, lse_ref, kv_hbm, w_ref, cos_ref, sin_ref,
                    normed_ref, inv_ref, gain_ref, gres_ref, gmlp_ref, low_ref, branch_ref, gup_hbm, dnp_hbm, inputs_hbm,
                    tokens_ref, query_ref, key_ref, value_ref, gains_out, gate_ref, up_ref, down_ref, out_ref,
                    kvbuf, dkv, acc_ref, gqt_ref, ga_ref, qblk, kvblk, small,
                    load_sem, send_sem, recv_sem, col_send, col_recv, own_sem, credit,
                    wg, wd, wo, brs, lows, halves, fin, fin_in, dsend, din,
                    colq_ref, colkv_ref, gains_ref, cols_acc, half_send, half_in, gain_send, gain_in, in_sem,
                    g_send, g_recv, w_load, w_send, w_recv, top_send, top_recv, fin_send, fin_recv, *recvs):
    nctx, nf, parts, heads, tq, slots = plan
    plane = nctx // 2
    n = nctx * nf
    dims = bit_dims(plane)
    nd = len(dims)
    bk = 2 * nf * tq
    me_c, me_f = lax.axis_index("ctx"), lax.axis_index("fsdp")
    me = me_c * nf + me_f
    core, place = lax.rem(me_c, 2), me_c // 2
    mesh_id = pl.DeviceIdType.MESH
    half_dim = HS // 2

    def target(k):
        other = lax.rem(me + k, n)
        return other, {"ctx": other // nf, "fsdp": lax.rem(other, nf)}

    barrier = pltpu.get_barrier_semaphore()

    def greet(k, carry):
        pl.semaphore_signal(barrier, inc=1, device_id=target(k)[1], device_id_type=mesh_id)
        return carry

    lax.fori_loop(1, n, greet, 0)

    def loads(p):
        s = p % slots
        return [
            pltpu.make_async_copy(
                kv_hbm.at[:, pl.ds((kind * parts + p) * 2 * HS, 2 * HS)],
                kvbuf.at[s, kind], load_sem.at[s, kind],
            )
            for kind in range(2)
        ]

    resident = slots == parts

    def block_loads(p, j):
        slot = lax.rem(j, 2)
        return [
            pltpu.make_async_copy(
                kv_hbm.at[pl.ds(pl.multiple_of(j * bk, bk), bk), pl.ds((kind * parts + p) * 2 * HS, 2 * HS)],
                kvbuf.at[slot, kind], load_sem.at[slot, kind],
            )
            for kind in range(2)
        ]

    if resident:
        for p in range(parts):
            for copy in loads(p):
                copy.start()

    def dim_axis(i):
        stride = math.prod(dims[:i])
        size = dims[i]
        own = lax.rem(place // stride, size)

        def peer(k):
            there = lax.rem(own + k, size)
            return there, {"ctx": (place + (there - own) * stride) * 2 + core, "fsdp": me_f}

        return (nd - 1 - i, size, own, peer)

    core_axis = (nd, 2, core, lambda k: (1 - core, {"ctx": place * 2 + 1 - core, "fsdp": me_f}))
    side_axis = (nd + 1, 2, me_f, lambda k: (1 - me_f, {"ctx": me_c, "fsdp": 1 - me_f}))
    lines = [dim_axis(i) for i in range(nd)]
    orders = [[core_axis, side_axis] + lines, [core_axis, side_axis] + w_order(lines)]
    stages = nd + 2
    wrecvs = recvs[2 * stages :]
    side_at, mate_at = side_axis[3](1)[1], core_axis[3](1)[1]

    low_bits = nd - 2
    arrays = ((wg, gup_hbm, (0,)), (wd, dnp_hbm, ()), (wo, None, ()), (wg, gup_hbm, (1,)))
    w_lines = [lines, w_order(lines), w_order(lines), lines]

    def chunk_at(a, k):
        near, far_line = w_lines[a][nd - 2], w_lines[a][nd - 1]
        far_bit = far_line[2] if k % 2 else 1 - far_line[2]
        near_bit = near[2] if k // 2 else 1 - near[2]
        return far_bit, near_bit

    def w_region(a, k, stage, at):
        index = [slice(None)] * nd
        index[w_lines[a][nd - 1][0]], index[w_lines[a][nd - 2][0]] = chunk_at(a, k)
        for axis in w_lines[a][:stage]:
            index[axis[0]] = axis[2]
        if stage < low_bits:
            index[w_lines[a][stage][0]] = at
        return tuple(index)

    def held(a, index):
        first = w_lines[a][0][0]
        return index if a == 2 else index[:first] + index[first + 1 :] + arrays[a][2]

    def w_copy(a, k, stage):
        buf, far, sub = arrays[a]
        there, where = w_lines[a][stage][3](1)
        index = w_region(a, k, stage, there)
        return pltpu.make_async_remote_copy(
            src_ref=far.at[index + sub] if stage == 0 and a != 2 else buf.at[held(a, index)],
            dst_ref=wrecvs[a * (low_bits + 2) + stage].at[chunk_at(a, k)],
            send_sem=w_send.at[a, k, stage], recv_sem=w_recv.at[a, k, stage],
            device_id=where, device_id_type=mesh_id,
        )

    def near_copy(a, i):
        return pltpu.make_async_remote_copy(
            src_ref=arrays[a][0].at[held(a, w_region(a, i, low_bits, 0))], dst_ref=wrecvs[a * (low_bits + 2) + low_bits].at[i],
            send_sem=top_send.at[a, i], recv_sem=top_recv.at[a, i],
            device_id=w_lines[a][nd - 2][3](1)[1], device_id_type=mesh_id,
        )

    def far_copy(a):
        return pltpu.make_async_remote_copy(
            src_ref=arrays[a][0].at[held(a, w_region(a, 2, low_bits, 0))], dst_ref=wrecvs[a * (low_bits + 2) + low_bits + 1].at[0],
            send_sem=top_send.at[a, 2], recv_sem=top_recv.at[a, 2],
            device_id=w_lines[a][nd - 1][3](1)[1], device_id_type=mesh_id,
        )

    def w_start(which, k):
        for a in which:
            w_copy(a, k, 0).start()

    def w_finish(which, k):
        for a in which:
            buf = arrays[a][0]
            for stage in range(low_bits):
                w_copy(a, k, stage).wait()
                where = held(a, w_region(a, k, stage, w_lines[a][stage][2]))
                got = wrecvs[a * (low_bits + 2) + stage]
                buf[where] = (
                    buf[where].astype(jnp.float32) + got[chunk_at(a, k)].astype(jnp.float32)
                ).astype(buf.dtype)
                if stage + 1 < low_bits:
                    w_copy(a, k, stage + 1).start()
            if k < 2:
                near_copy(a, k).start()
            elif k == 2:
                near_copy(a, 0).wait()
                where = held(a, w_region(a, 2, low_bits, 0))
                buf[where] = (
                    buf[where].astype(jnp.float32)
                    + wrecvs[a * (low_bits + 2) + low_bits][0].astype(jnp.float32)
                ).astype(buf.dtype)
                far_copy(a).start()

    def w_total(a):
        near_copy(a, 1).wait()
        far_copy(a).wait()
        total = arrays[a][0][held(a, w_region(a, 3, low_bits, 0))].astype(jnp.float32)
        total = total + wrecvs[a * (low_bits + 2) + low_bits][1].astype(jnp.float32)
        return total + wrecvs[a * (low_bits + 2) + low_bits + 1][0].astype(jnp.float32)

    w_loads = [
        pltpu.make_async_copy(far.at[(slice(None),) * w_lines[i][0][0] + (w_lines[i][0][2],)], buf, w_load.at[i])
        for i, (buf, far, _) in enumerate(arrays[:2])
    ]
    for copy in w_loads:
        copy.start()
    half = low_ref.shape[1] // nf
    low_all = low_ref[...]
    halves[0] = low_all[:, :half]
    halves[1] = low_all[:, half:]
    lows[0] = halves[me_f]
    brs[0] = branch_ref[...]

    def g_copy(i, src, dst, where):
        return pltpu.make_async_remote_copy(
            src_ref=src, dst_ref=dst, send_sem=g_send.at[i], recv_sem=g_recv.at[i],
            device_id=where, device_id_type=mesh_id,
        )

    low_side = g_copy(0, halves.at[1 - me_f], lows.at[1], side_at)
    br_side = g_copy(1, brs.at[0], brs.at[1], side_at)
    low_core = g_copy(2, lows.at[pl.ds(0, 2)], lows.at[pl.ds(2, 2)], mate_at)
    br_core = g_copy(3, brs.at[pl.ds(0, 2)], brs.at[pl.ds(2, 2)], mate_at)

    def output_partial():
        low_core.wait()
        br_core.wait()
        rows = jnp.transpose(brs[...].reshape(4 * tq, brs.shape[2]))
        unit = brs.shape[2] // nctx
        wo[...] = jnp.zeros_like(wo)
        low_rows = lows[...].reshape(4 * tq, half)
        batch = plane // 4
        for r in range(plane):
            first = 2 * unit * (r % batch)
            if first == 0:
                chunk = 2 * unit * batch
                part = jnp.dot(
                    rows[2 * unit * r : 2 * unit * r + chunk], low_rows, preferred_element_type=jnp.float32
                )
            piece = jnp.where(core == 0, part[first : first + unit], part[first + unit : first + 2 * unit])
            wo[static_index(dims, r) + (slice(0, unit), slice(0, half))] = piece.astype(wo.dtype)

    pl.semaphore_wait(barrier, n - 1)
    low_side.start()
    br_side.start()
    for k in range(4):
        w_start((0, 3, 1) if k < 2 else (1,), k)

    def region(kind, stage, at):
        index = [slice(None)] * (nd + 2)
        for axis in orders[kind][:stage]:
            index[axis[0]] = axis[2]
        index[orders[kind][stage][0]] = at
        return tuple(index)

    def stage_copies(p, kind, stage):
        s = p % slots
        axis = orders[kind][stage]
        copies = []
        for k in range(1, axis[1]):
            there, where = axis[3](k)
            copies.append(
                pltpu.make_async_remote_copy(
                    src_ref=dkv.at[(s, kind) + region(kind, stage, there)],
                    dst_ref=recvs[kind * stages + stage].at[s, k - 1],
                    send_sem=send_sem.at[s, kind, stage, k - 1],
                    recv_sem=recv_sem.at[s, kind, stage, k - 1],
                    device_id=where, device_id_type=mesh_id,
                )
            )
        return copies

    def stage_start(p, stage):
        for kind in range(2):
            for copy in stage_copies(p, kind, stage):
                copy.start()

    finals = {}

    def stage_finish(p, stage):
        s = p % slots
        for kind in range(2):
            axis = orders[kind][stage]
            for copy in stage_copies(p, kind, stage):
                copy.wait()
            where = region(kind, stage, axis[2])
            got = recvs[kind * stages + stage]
            free = [i for i in range(nd + 2) if isinstance(where[i], slice)]

            def add(index, lead):
                total = dkv[(s, kind) + index].astype(jnp.float32)
                for k in range(axis[1] - 1):
                    total = total + got[(s, k) + lead].astype(jnp.float32)
                return total

            if not free:
                finals[p, kind] = add(where, ())
            else:
                size = dkv.shape[2 + free[0]]

                def one(i, carry):
                    index = list(where)
                    index[free[0]] = i
                    index = tuple(index)
                    dkv[(s, kind) + index] = add(index, (i,)).astype(dkv.dtype)
                    return carry

                lax.fori_loop(0, size, one, 0)

    def place_index(j):
        index = []
        for i in reversed(range(nd)):
            index.append(lax.rem(j // math.prod(dims[:i]), dims[i]))
        return tuple(index)

    start = me * tq
    last = (start + tq - 1) // bk + 1

    def compute(p):
        s = p % slots
        span = slice(2 * heads * HS * p, 2 * heads * HS * (p + 1))
        qt = q_ref[span, :].astype(jnp.float32) * (1.0 / 8.0)
        dt = heads_rows(do_ref[:, span])
        qg = [padded(qt, heads, g) for g in range(2)]
        dg = [padded(dt, heads, g) for g in range(2)]
        qrows = jnp.concatenate([jnp.transpose(x) for x in qg], axis=0).astype(jnp.bfloat16)
        drows = jnp.concatenate([jnp.transpose(x) for x in dg], axis=0).astype(jnp.bfloat16)
        delta = [
            jnp.sum(dg[g][HS * g : HS * (g + 1)] * ot_ref[2 * p + g], axis=0, keepdims=True)
            for g in range(2)
        ]
        lse = [lse_ref[2 * p + g] for g in range(2)]
        qg = [x.astype(jnp.bfloat16) for x in qg]
        dg = [x.astype(jnp.bfloat16) for x in dg]
        acc_ref[...] = jnp.zeros_like(acc_ref)
        for copy in loads(p) if resident else block_loads(p, 0):
            if not resident:
                copy.start()
            else:
                copy.wait()

        def zero(j, carry):
            at = place_index(j)
            for kind in range(2):
                dkv[(s, kind) + at] = jnp.zeros((2, nf, tq, 2 * HS), dkv.dtype)
            return carry

        def body(j, carry):
            first = pl.multiple_of(j * bk, bk)
            if resident:
                kb = kvbuf[s, 0, pl.ds(first, bk), :]
                vb = kvbuf[s, 1, pl.ds(first, bk), :]
            else:
                for copy in block_loads(p, j):
                    copy.wait()

                @pl.when(j + 1 < last)
                def _():
                    for copy in block_loads(p, j + 1):
                        copy.start()

                kb, vb = kvbuf[lax.rem(j, 2), 0], kvbuf[lax.rem(j, 2), 1]
            kt = jnp.transpose(kb)
            bias = bias_tile((start,), docs, first, bk, tq)
            bias = jnp.concatenate([bias] * heads, axis=1)
            ps = []
            dss = []
            for g in range(2):
                score = jnp.dot(kb, qg[g], preferred_element_type=jnp.float32)
                prob = jnp.exp(score + (bias - lse[g]))
                dp = jnp.dot(vb, dg[g], preferred_element_type=jnp.float32)
                ds = (prob * (dp - delta[g])).astype(jnp.bfloat16)
                ps.append(prob.astype(jnp.bfloat16))
                dss.append(ds)
                acc_ref[g] += jnp.dot(kt[HS * g : HS * (g + 1)], ds, preferred_element_type=jnp.float32)
            dv = jnp.dot(jnp.concatenate(ps, axis=1), drows, preferred_element_type=jnp.float32)
            dk = jnp.dot(jnp.concatenate(dss, axis=1), qrows, preferred_element_type=jnp.float32)
            at = place_index(j)
            dkv[(s, 0) + at] = dk.astype(dkv.dtype).reshape(2, nf, tq, 2 * HS)
            dkv[(s, 1) + at] = dv.astype(dkv.dtype).reshape(2, nf, tq, 2 * HS)
            return carry

        lax.fori_loop(last, plane, zero, 0)
        lax.fori_loop(0, last, body, 0)
        cos_rows = jnp.concatenate([cos_ref[...]] * heads, axis=1) * (1.0 / 8.0)
        sin_rows = jnp.concatenate([sin_ref[...]] * heads, axis=1) * (1.0 / 8.0)
        for g in range(2):
            back = rotate_back(acc_ref[g], cos_rows, sin_rows).astype(gqt_ref.dtype)
            for j in range(heads):
                h = (2 * p + g) * heads + j
                gqt_ref[HS * h : HS * (h + 1), :] = back[:, tq * j : tq * (j + 1)]

    peers = 2 + sum(size - 1 for size in dims)

    def all_peers():
        found = [core_axis[3](1)[1], side_axis[3](1)[1]]
        for axis in lines:
            found += [axis[3](k)[1] for k in range(1, axis[1])]
        return found

    progress = {}

    def advance(p):
        stage = progress[p]
        stage_finish(p, stage)
        progress[p] = stage + 1
        if stage + 1 < stages:
            stage_start(p, stage + 1)
        else:
            del progress[p]
            if p + slots < parts:
                for where in all_peers():
                    pl.semaphore_signal(credit, inc=1, device_id=where, device_id_type=mesh_id)

    for p in range(parts):
        if p >= slots:
            while p - slots in progress:
                advance(p - slots)
        compute(p)
        if p >= slots:
            pl.semaphore_wait(credit, peers)
        stage_start(p, 0)
        progress[p] = 0
        for older in [o for o in progress if o < p]:
            advance(older)
        if p == 0:
            low_side.wait()
            br_side.wait()
            low_core.start()
            br_core.start()
        if p == 1:
            for copy in w_loads:
                copy.wait()
            for k in range(2):
                w_finish((0, 3), k)
                w_start((0, 3), k + 2)
    for k in range(2):
        w_finish((1,), k)
    output_partial()

    def copies_to(k, which):
        other = lax.rem(me_c + k, nctx)
        where = {"ctx": other, "fsdp": me_f}
        block, out = ((qblk, colq_ref), (kvblk, colkv_ref), (small, gains_ref))[which]
        return pltpu.make_async_remote_copy(
            src_ref=block if which == 2 else block.at[other], dst_ref=out.at[me_c],
            send_sem=col_send.at[which, k], recv_sem=col_recv.at[which, k],
            device_id=where, device_id_type=mesh_id,
        )

    def share(which):
        def one(k, carry):
            copies_to(k, which).start()
            return carry

        block, out = ((qblk, colq_ref), (kvblk, colkv_ref), (small, gains_ref))[which]
        pltpu.make_async_copy(block if which == 2 else block.at[me_c], out.at[me_c], own_sem.at[which]).start()
        lax.fori_loop(1, nctx, one, 0)

    def share_wait(which):
        def one(k, carry):
            copies_to(k, which).wait()
            return carry

        block, out = ((qblk, colq_ref), (kvblk, colkv_ref), (small, gains_ref))[which]
        pltpu.make_async_copy(block if which == 2 else block.at[me_c], out.at[me_c], own_sem.at[which]).wait()
        lax.fori_loop(1, nctx, one, 0)

    width_q = 2 * parts * heads * HS
    width_k = 2 * parts * HS
    cq, ck = width_q // nctx, width_k // nctx
    qblk[...] = jnp.zeros_like(qblk)
    kvblk[...] = jnp.zeros_like(kvblk)
    for i in range(nctx):
        qblk[i, 0:cq, :] = gqt_ref[cq * i : cq * (i + 1), :]
    share(0)
    ga_ref[...] = jnp.dot(w_ref[:, :width_q], gqt_ref[...], preferred_element_type=jnp.float32)
    for k in range(4):
        w_start((2,), k)
    pq, pk = qblk.shape[1], kvblk.shape[1]

    def columns(col_ref, first, count):
        def fetch(i, slot):
            return pltpu.make_async_copy(
                inputs_hbm.at[i], brs.at[slot], in_sem.at[slot]
            )

        fetch(0, 0).start()
        cols_acc[first : first + count, :] = jnp.zeros((count, cols_acc.shape[1]), jnp.float32)

        def one(i, carry):
            slot = lax.rem(i, 2)

            @pl.when(i + 1 < nctx)
            def _():
                fetch(i + 1, 1 - slot).start()

            fetch(i, slot).wait()
            cols_acc[first : first + count, :] += jnp.dot(
                col_ref[i], brs[slot], preferred_element_type=jnp.float32
            )
            return carry

        lax.fori_loop(0, nctx, one, 0)

    per_side = plane // 2
    home = (2 * me_f + core) * per_side + place // 2
    slot = lax.rem(place, 2)

    def home_copy(kind, s):
        return pltpu.make_async_remote_copy(
            src_ref=fin.at[kind, s], dst_ref=fin_in.at[kind, slot],
            send_sem=fin_send.at[kind, s], recv_sem=fin_recv.at[kind, slot],
            device_id={"ctx": home, "fsdp": jnp.int32(s)}, device_id_type=mesh_id,
        )

    def self_copy(kind, s):
        return pltpu.make_async_copy(fin.at[kind, s], fin_in.at[kind, slot], fin_send.at[kind, s])

    def to_homes(kind, a):
        total = w_total(a)
        unit, lanes = fin.shape[2], fin.shape[3]
        blank = jnp.zeros((unit, lanes - half), fin.dtype)
        for s in range(2):
            fin[kind, s] = jnp.concatenate([total[:, half * s : half * (s + 1)].astype(fin.dtype), blank], axis=1)
            at_home = (home == me_c) & (me_f == s)

            @pl.when(jnp.logical_not(at_home))
            def _():
                home_copy(kind, s).start()

            @pl.when(at_home)
            def _():
                self_copy(kind, s).start()

    turn = 0
    while progress:
        for p in list(progress):
            advance(p)
        if turn == 0:
            for k in range(2, 4):
                w_finish((0, 3, 1), k)
        if turn == 1:
            for k in range(2):
                w_finish((2,), k)
        if turn == 2:
            for k in range(2, 4):
                w_finish((2,), k)
        turn += 1

    cos_rows, sin_rows = cos_ref[...], sin_ref[...]
    grads = []
    for kind in range(2):
        rows = []
        for p in range(parts):
            both = jnp.transpose(finals[p, kind])
            for g in range(2):
                one = both[HS * g : HS * (g + 1)]
                rows.append(rotate_back(one, cos_rows, sin_rows) if kind == 0 else one)
        grads.append(jnp.concatenate(rows, axis=0).astype(jnp.bfloat16))
    for i in range(nctx):
        kvblk[i, 0:ck, :] = grads[0][ck * i : ck * (i + 1)]
        kvblk[i, ck : 2 * ck, :] = grads[1][ck * i : ck * (i + 1)]
    share(1)
    grad_t = (
        ga_ref[...]
        + jnp.dot(w_ref[:, width_q : width_q + width_k], grads[0], preferred_element_type=jnp.float32)
        + jnp.dot(w_ref[:, width_q + width_k :], grads[1], preferred_element_type=jnp.float32)
    )
    grad = jnp.transpose(grad_t)
    normed = normed_ref[...].astype(jnp.float32) * inv_ref[...]
    product = grad * normed
    gain_sum = jnp.sum(product, axis=0, keepdims=True)
    lanes = 128
    tiles = gain_sum.shape[1] // lanes
    rows = [gain_sum[:, lanes * i : lanes * (i + 1)] for i in range(tiles)]
    rows += [gmlp_ref[:, lanes * i : lanes * (i + 1)] for i in range(tiles)]
    rows += [jnp.zeros((small.shape[0] - 2 * tiles, lanes), jnp.float32)]
    small[...] = jnp.concatenate(rows, axis=0)
    share(2)
    gain = gain_ref[0:1, :]
    scaled = grad * gain
    mean = jnp.mean(scaled * normed, axis=1, keepdims=True)
    tokens_ref[...] = gres_ref[...] + inv_ref[...] * (scaled - normed * mean)

    to_homes(0, 0)
    share_wait(0)
    columns(colq_ref, 0, pq)

    def give_half(first, count, i):
        rows = slice(first, first + count)
        theirs = jnp.where(me_f == 0, cols_acc[rows, half:], cols_acc[rows, :half]).astype(half_send.dtype)
        side_pad = jnp.zeros((count, half_send.shape[1] - half), half_send.dtype)
        half_send[rows, :] = jnp.concatenate([theirs, side_pad], axis=1)
        span = pl.ds(first, count)
        copy = g_copy(i, half_send.at[span], half_in.at[span], side_at)
        copy.start()
        return copy

    half_q = give_half(0, pq, 5)
    to_homes(1, 3)
    dsum = w_total(1)
    dsend[...] = dsum.astype(dsend.dtype)
    down_copy = g_copy(4, dsend, din, mate_at)
    down_copy.start()
    osum = w_total(2)
    out_ref[...] = osum[: out_ref.shape[0], :half]
    share_wait(1)
    columns(colkv_ref, pq, pk)
    half_kv = give_half(pq, pk, 7)
    share_wait(2)
    gain_total = gains_ref[0]
    for i in range(1, nctx):
        gain_total = gain_total + gains_ref[i]
    gain_send[...] = gain_total
    gain_copy = g_copy(6, gain_send, gain_in, side_at)
    gain_copy.start()
    half_q.wait()
    half_kv.wait()
    own_half = jnp.where(me_f == 0, cols_acc[:, :half], cols_acc[:, half:])
    rows = own_half + half_in[:, :half].astype(jnp.float32)
    query_ref[...] = rows[:cq]
    key_ref[...] = rows[pq : pq + ck]
    value_ref[...] = rows[pq + ck : pq + 2 * ck]
    gain_copy.wait()
    gains_out[...] = gain_send[...] + gain_in[...]
    down_copy.wait()
    cols = down_ref.shape[0]

    def unfold(folded):
        return jnp.concatenate(
            [folded[2 * cols * i : 2 * cols * (i + 1)] for i in range(folded.shape[0] // (2 * cols))], axis=1
        )

    dsum, got = unfold(dsum), unfold(din[...].astype(jnp.float32))
    own_cols = jnp.where(core == 0, dsum[:cols], dsum[cols:])
    far_cols = jnp.where(core == 0, got[:cols], got[cols:])
    down_ref[...] = jnp.where(
        core == 0,
        jnp.concatenate([own_cols, far_cols], axis=1),
        jnp.concatenate([far_cols, own_cols], axis=1),
    )
    owner = me_c // per_side
    for kind in range(2):
        for s in range(2):
            at_home = (home == me_c) & (me_f == s)

            @pl.when(jnp.logical_not(at_home))
            def _():
                home_copy(kind, s).wait_send()

            @pl.when(at_home)
            def _():
                self_copy(kind, s).wait()

        for h in range(2):
            holder = (2 * lax.rem(me_c, per_side) + h) * 2 + lax.rem(owner, 2)

            @pl.when(jnp.logical_not((holder == me_c) & (owner // 2 == me_f)))
            def _():
                pltpu.make_async_remote_copy(
                    src_ref=fin.at[0, 0], dst_ref=fin_in.at[kind, h],
                    send_sem=fin_send.at[0, 0], recv_sem=fin_recv.at[kind, h],
                    device_id={"ctx": home, "fsdp": me_f}, device_id_type=mesh_id,
                ).wait_recv()

    for kind, ref in ((0, gate_ref), (1, up_ref)):
        rows = jnp.concatenate([fin_in[kind, 0], fin_in[kind, 1]], axis=0).astype(jnp.float32)
        ref[...] = rows[:, :half]


def backward(nctx, nf, docs, q, do, ot, lse, kv, w, cos_t, sin_t, normed, inv, gain, gres, gmlp, low, branch, gup, dnp, inputs):
    width_q, tq = q.shape
    n_tokens, width_kv = kv.shape
    n = nctx * nf
    parts = width_kv // (4 * HS)
    heads = width_q // HS // (2 * parts)
    dims = bit_dims(nctx // 2)
    lead = tuple(reversed(dims))
    part_bytes = n_tokens * 2 * HS * 2
    slots = parts if parts * part_bytes * 5 <= 24 * 2**20 else 1
    nd = len(dims)
    bf16, f32 = jnp.bfloat16, jnp.float32
    axes = {"core": (nd, 2), "side": (nd + 1, nf)}
    line = [(nd - 1 - i, dims[i]) for i in range(nd)]
    orders = [
        [axes["core"], axes["side"]] + line,
        [axes["core"], axes["side"]] + w_order(line),
    ]
    recvs = []
    for order in orders:
        left = list(lead) + [2, nf]
        for position, size in order:
            left[position] = None
            recvs.append(
                pltpu.VMEM((slots, size - 1) + tuple(x for x in left if x) + (tq, 2 * HS), bf16)
            )
    model_width = low.shape[1]
    half = model_width // nf
    unit, deep = gup.shape[-2], model_width // (nctx // 2)
    quarter = dnp.shape[-2] // deep * 128
    plane = nctx // 2
    tails = [gup.shape[nd:], dnp.shape[nd:], (round_up(deep // 2, 16), round_up(half, 128))]
    for tail in (tails[0][1:], tails[1], tails[2], tails[0][1:]):
        for stage in range(nd - 2):
            recvs.append(pltpu.VMEM((2,) * (nd - 1 - stage) + tail, bf16))
        recvs += [pltpu.VMEM((2,) + tail, bf16), pltpu.VMEM((1,) + tail, bf16)]
    stages = nd + 2
    most = max(dims + [2])
    pq = round_up(width_q // nctx, 16)
    pk = round_up(2 * (2 * parts * HS) // nctx, 16)
    model = w.shape[0]
    sr = round_up(2 * model // 128, 8)
    vmem = pl.BlockSpec(memory_space=pltpu.VMEM)
    smem = pl.BlockSpec(memory_space=pltpu.SMEM)
    hbm = pl.BlockSpec(memory_space=pl.ANY)
    return pl.pallas_call(
        functools.partial(backward_kernel, (nctx, nf, parts, heads, tq, slots)),
        out_shape=[
            jax.ShapeDtypeStruct((tq, model), f32),
            jax.ShapeDtypeStruct((width_q // nctx, half), f32),
            jax.ShapeDtypeStruct((2 * parts * HS // nctx, half), f32),
            jax.ShapeDtypeStruct((2 * parts * HS // nctx, half), f32),
            jax.ShapeDtypeStruct((sr, 128), f32),
            jax.ShapeDtypeStruct((2 * unit, half), f32),
            jax.ShapeDtypeStruct((2 * unit, half), f32),
            jax.ShapeDtypeStruct((deep // 2, 2 * quarter), f32),
            jax.ShapeDtypeStruct((deep // 2, half), f32),
        ],
        in_specs=[smem, vmem, vmem, vmem, vmem, hbm] + [vmem] * 10 + [hbm] * 3,
        out_specs=[vmem] * 9,
        scratch_shapes=[
            pltpu.VMEM((slots, 2, n_tokens, 2 * HS) if slots == parts else (2, 2, 2 * nf * tq, 2 * HS), bf16),
            pltpu.VMEM((slots, 2) + lead + (2, nf, tq, 2 * HS), bf16),
            pltpu.VMEM((2, HS, heads * tq), f32),
            pltpu.VMEM((width_q, tq), bf16),
            pltpu.VMEM((model, tq), f32),
            pltpu.VMEM((nctx, pq, tq), bf16),
            pltpu.VMEM((nctx, pk, tq), bf16),
            pltpu.VMEM((sr, 128), f32),
            pltpu.SemaphoreType.DMA((max(slots, 2), 2)),
            pltpu.SemaphoreType.DMA((slots, 2, stages, most - 1)),
            pltpu.SemaphoreType.DMA((slots, 2, stages, most - 1)),
            pltpu.SemaphoreType.DMA((3, nctx)),
            pltpu.SemaphoreType.DMA((3, nctx)),
            pltpu.SemaphoreType.DMA((3,)),
            pltpu.SemaphoreType.REGULAR,
            pltpu.VMEM(lead[:-1] + tails[0], bf16),
            pltpu.VMEM(lead[:-1] + tails[1], bf16),
            pltpu.VMEM(lead + tails[2], bf16),
            pltpu.VMEM((4,) + branch.shape, bf16),
            pltpu.VMEM((4, tq, half), bf16),
            pltpu.VMEM((2, tq, half), bf16),
            pltpu.VMEM((2, 2, unit, round_up(half, 128)), bf16),
            pltpu.VMEM((2, 2, unit, round_up(half, 128)), bf16),
            pltpu.VMEM(tails[1], bf16),
            pltpu.VMEM(tails[1], bf16),
            pltpu.VMEM((nctx, pq, tq), bf16),
            pltpu.VMEM((nctx, pk, tq), bf16),
            pltpu.VMEM((nctx, sr, 128), f32),
            pltpu.VMEM((pq + pk, model), f32),
            pltpu.VMEM((pq + pk, round_up(half, 128)), bf16),
            pltpu.VMEM((pq + pk, round_up(half, 128)), bf16),
            pltpu.VMEM((sr, 128), f32),
            pltpu.VMEM((sr, 128), f32),
            pltpu.SemaphoreType.DMA((2,)),
            pltpu.SemaphoreType.DMA((8,)),
            pltpu.SemaphoreType.DMA((8,)),
            pltpu.SemaphoreType.DMA((2,)),
            pltpu.SemaphoreType.DMA((4, 4, max(nd - 2, 1))),
            pltpu.SemaphoreType.DMA((4, 4, max(nd - 2, 1))),
            pltpu.SemaphoreType.DMA((4, 3)),
            pltpu.SemaphoreType.DMA((4, 3)),
            pltpu.SemaphoreType.DMA((2, 2)),
            pltpu.SemaphoreType.DMA((2, 2)),
        ]
        + recvs,
        compiler_params=pltpu.CompilerParams(
            collective_id=1, has_side_effects=True, vmem_limit_bytes=63 * 2**20
        ),
        cost_estimate=pl.CostEstimate(flops=10**10, bytes_accessed=3 * 10**7, transcendentals=10**7),
        name="backward",
    )(docs, q, do, ot, lse, kv, w, cos_t, sin_t, normed, inv, gain, gres, gmlp, low, branch, gup, dnp, inputs)


def rotate(rows, cos_rows, sin_rows):
    half_dim = HS // 2
    first, second = rows[:half_dim], rows[half_dim:]
    return jnp.concatenate(
        [first * cos_rows - second * sin_rows, second * cos_rows + first * sin_rows], axis=0
    )


class Axes:
    def __init__(self, nctx, nf):
        self.ctx, self.f = lax.axis_index("ctx"), lax.axis_index("fsdp")
        self.core, self.place = lax.rem(self.ctx, 2), self.ctx // 2
        self.me = self.ctx * nf + self.f
        self.dims = line_dims(nctx // 2)
        self.nd = len(self.dims)
        ctx, f, core, place = self.ctx, self.f, self.core, self.place
        self.core_axis = (self.nd, 2, core, lambda k: (1 - core, {"ctx": place * 2 + 1 - core, "fsdp": f}))
        self.side_axis = (self.nd + 1, 2, f, lambda k: (1 - f, {"ctx": ctx, "fsdp": 1 - f}))
        self.lines = [self.line(i) for i in range(self.nd)]
        self.peer_count = 2 + sum(size - 1 for size in self.dims)

    def at_line(self, i, there):
        stride = math.prod(self.dims[:i])
        own = lax.rem(self.place // stride, self.dims[i])
        return {"ctx": (self.place + (there - own) * stride) * 2 + self.core, "fsdp": self.f}

    def line(self, i):
        size = self.dims[i]
        own = lax.rem(self.place // math.prod(self.dims[:i]), size)

        def peer(k):
            there = lax.rem(own + k, size)
            return there, self.at_line(i, there)

        return (self.nd - 1 - i, size, own, peer)

    def peers(self):
        found = [self.core_axis[3](1)[1], self.side_axis[3](1)[1]]
        for axis in self.lines:
            found += [axis[3](k)[1] for k in range(1, axis[1])]
        return found

    def place_index(self, j):
        return tuple(
            lax.rem(j // math.prod(self.dims[:i]), self.dims[i]) for i in reversed(range(self.nd))
        )


def forward_kernel(plan, docs, tokens_ref, gains_ref, cos_ref, sin_ref, wq, wk, wv, wo, wg, wu, cot,
                   qt_ref, kv_out, low_ref, ot_ref, lse_ref, wqkv_out, wo_out, gu_out, cots_out,
                   attn_in_ref, inv_ref, gain_ref,
                   wbuf, obuf, gubuf, cbuf, gain_far, own_kv, kvb, m_ref, l_ref, acc_ref,
                   load_sem, w_send, w_recv, top_send, top_recv, ag_send, ag_recv, blk_sem, out_sem):
    nctx, nf, parts, heads, tq = plan
    ax = Axes(nctx, nf)
    f, core, place = ax.f, ax.core, ax.place
    mesh_id = pl.DeviceIdType.MESH
    bf16, f32 = jnp.bfloat16, jnp.float32
    width = tokens_ref.shape[1]
    half = width // nf
    width_q, width_k = 2 * parts * heads * HS, 2 * parts * HS
    rows4, rows2 = half // 4, half // 2
    quarter = gu_out.shape[1] // 2
    side = ax.side_axis[3](1)[1]
    mate = ax.core_axis[3](1)[1]
    low = ax.lines[0]
    bit = lax.rem(low[2], 2)
    across = ax.at_line(0, low[2] + 1 - 2 * bit)
    top = ax.nd - 1
    chunks = ax.dims[top]
    z = ax.lines[top][2]

    barrier = pltpu.get_barrier_semaphore()
    for where in ax.peers():
        pl.semaphore_signal(barrier, inc=1, device_id=where, device_id_type=mesh_id)

    def local(src, dst, i):
        return pltpu.make_async_copy(src, dst, load_sem.at[i])

    own_rows = pl.ds(pl.multiple_of(f * half, half), half)
    own_quarter = pl.ds(pl.multiple_of((2 * f + core) * quarter, quarter), quarter)
    loads = [
        local(wk, wbuf.at[own_rows, pl.ds(width_q, width_k)], 0),
        local(wv, wbuf.at[own_rows, pl.ds(width_q + width_k, width_k)], 1),
        local(wq, wbuf.at[own_rows, pl.ds(0, width_q)], 2),
        local(wo, obuf.at[own_rows], 3),
        local(wg.at[:, own_quarter], gubuf.at[own_rows, pl.ds(0, quarter)], 4),
        local(wu.at[:, own_quarter], gubuf.at[own_rows, pl.ds(quarter, quarter)], 5),
        local(cot, cbuf.at[0], 6),
    ]
    for copy in loads:
        copy.start()

    def remote(src, dst, i, where):
        return pltpu.make_async_remote_copy(
            src_ref=src, dst_ref=dst, send_sem=w_send.at[i], recv_sem=w_recv.at[i],
            device_id=where, device_id_type=mesh_id,
        )

    near = pl.multiple_of(core * rows2 + bit * rows4, 16)
    far_x = pl.multiple_of(core * rows2 + (1 - bit) * rows4, 16)
    there = (1 - f) * half

    def piece(base, offset):
        return pl.ds(pl.multiple_of(base + offset, 16), rows4)

    kv_cols, q_cols = pl.ds(width_q, 2 * width_k), pl.ds(0, width_q)
    mine = f * half
    gains_copy = remote(gains_ref, gain_far, 0, side)
    kv_y = [
        remote(wk.at[piece(0, near)], wbuf.at[piece(mine, near), pl.ds(width_q, width_k)], 1, side),
        remote(wv.at[piece(0, near)], wbuf.at[piece(mine, near), pl.ds(width_q + width_k, width_k)], 2, side),
    ]
    q_y = [remote(wq.at[piece(0, near)], wbuf.at[piece(mine, near), q_cols], 3, side)]
    o_y = [remote(wo.at[piece(0, near)], obuf.at[piece(mine, near)], 4, side)]

    def forwards(buf, cols, first):
        def part(offset):
            return buf.at[piece(there, offset), cols] if cols is not None else buf.at[piece(there, offset)]

        return [
            remote(part(near), part(near), first, across),
            remote(part(near), part(near), first + 1, mate),
            remote(part(far_x), part(far_x), first + 2, mate),
        ]

    kv_f = forwards(wbuf, kv_cols, 5)
    q_f = forwards(wbuf, q_cols, 8)
    o_f = forwards(obuf, None, 11)
    far_quarter = pl.ds(pl.multiple_of((2 * (1 - f) + core) * quarter, quarter), quarter)

    deep = lax.rem(z, 2)
    above = ax.at_line(top, z + 1 - 2 * deep)

    def gu_rows(base, which=bit):
        return pl.ds(pl.multiple_of(base + which * rows2 + deep * rows4, 16), rows4)

    gu_y = [
        remote(wg.at[gu_rows(0), far_quarter], gubuf.at[gu_rows(mine), pl.ds(0, quarter)], 14, side),
        remote(wu.at[gu_rows(0), far_quarter], gubuf.at[gu_rows(mine), pl.ds(quarter, quarter)], 15, side),
    ]
    gu_x = remote(gubuf.at[gu_rows(there)], gubuf.at[gu_rows(there)], 16, across)
    gu_z = [
        remote(gubuf.at[gu_rows(there, which)], gubuf.at[gu_rows(there, which)], 19 + i, above)
        for i, which in enumerate((bit, 1 - bit))
    ]
    cot_y = remote(cot, cbuf.at[1], 17, side)
    cot_c = remote(cbuf.at[pl.ds(0, 2)], cbuf.at[pl.ds(2, 2)], 18, mate)

    pl.semaphore_wait(barrier, ax.peer_count)
    gains_copy.start()
    for copy in kv_y + q_y:
        copy.start()

    hidden = tokens_ref[...].astype(f32)
    inv = lax.rsqrt(jnp.mean(hidden * hidden, axis=1, keepdims=True) + EPS)
    inv_ref[...] = inv
    gains_copy.wait()
    near_gain, far_gain = gains_ref[0:1, :], gain_far[0:1, :]
    gain = jnp.where(
        f == 0,
        jnp.concatenate([near_gain, far_gain], axis=1),
        jnp.concatenate([far_gain, near_gain], axis=1),
    )
    near_mlp, far_mlp = gains_ref[1:2, :], gain_far[1:2, :]
    gain_ref[0:1, :] = gain
    gain_ref[1:2, :] = jnp.where(
        f == 0,
        jnp.concatenate([near_mlp, far_mlp], axis=1),
        jnp.concatenate([far_mlp, near_mlp], axis=1),
    )
    attn_in = (hidden * inv * gain).astype(bf16)
    attn_in_ref[...] = attn_in

    for copy in kv_y:
        copy.wait()
    kv_f[0].start()
    kv_f[1].start()
    for copy in q_y:
        copy.wait()
    for copy in o_y + gu_y:
        copy.start()
    kv_f[0].wait()
    kv_f[2].start()
    q_f[0].start()
    q_f[1].start()
    for copy in loads[:3]:
        copy.wait()
    kv_f[1].wait()
    kv_f[2].wait()
    kv = jnp.dot(attn_in, wbuf[:, width_q:], preferred_element_type=f32)
    cos_rows, sin_rows = cos_ref[...], sin_ref[...]
    kt = jnp.transpose(kv[:, :width_k])
    k_rot = jnp.concatenate(
        [rotate(kt[HS * g : HS * (g + 1)], cos_rows, sin_rows) for g in range(2 * parts)], axis=0
    )
    own_kv[:, :width_k] = jnp.transpose(k_rot).astype(bf16)
    own_kv[:, width_k:] = kv[:, width_k:].astype(bf16)
    own_at = ax.place_index(place) + (core, f)
    put = pltpu.make_async_copy(own_kv, kv_out.at[own_at], out_sem.at[0])
    put.start()

    def top_copy(k):
        return pltpu.make_async_remote_copy(
            src_ref=own_kv, dst_ref=kv_out.at[own_at],
            send_sem=top_send.at[k - 1], recv_sem=top_recv.at[k - 1],
            device_id=ax.at_line(top, lax.rem(z + k, chunks)), device_id_type=mesh_id,
        )

    for k in range(1, chunks):
        @pl.when(z + k < chunks)
        def _():
            top_copy(k).start()

    lower = ax.lines[:top]
    orders = [lower + [ax.side_axis, ax.core_axis], [ax.side_axis] + lower + [ax.core_axis]]
    stages = len(orders[0])

    def ag_copies(k, stage):
        copies = []
        for kind in range(2):
            index = [None] * (ax.nd + 2)
            index[0] = z - k
            for i, axis in enumerate(orders[kind]):
                index[axis[0]] = slice(None) if i < stage else axis[2]
            region = kv_out.at[tuple(index) + (slice(None), pl.ds(kind * width_k, width_k))]
            axis = orders[kind][stage]
            for i in range(1, axis[1]):
                copies.append(
                    pltpu.make_async_remote_copy(
                        src_ref=region, dst_ref=region,
                        send_sem=ag_send.at[k, kind, stage, i - 1],
                        recv_sem=ag_recv.at[k, kind, stage, i - 1],
                        device_id=axis[3](i)[1], device_id_type=mesh_id,
                    )
                )
        return copies

    def tick(k, stage):
        @pl.when(z >= k)
        def _():
            if stage == 0:
                if k > 0:
                    top_copy(k).wait_recv()
            else:
                for copy in ag_copies(k, stage - 1):
                    copy.wait()
            if stage < stages:
                for copy in ag_copies(k, stage):
                    copy.start()

    put.wait()
    tick(0, 0)
    q_f[0].wait()
    q_f[2].start()
    q_f[1].wait()
    q_f[2].wait()
    back = pltpu.make_async_copy(wbuf, wqkv_out, out_sem.at[1])
    back.start()
    query = jnp.dot(attn_in, wbuf[:, :width_q], preferred_element_type=f32)
    query_t = jnp.transpose(query)
    for h in range(2 * parts * heads):
        qt_ref[HS * h : HS * (h + 1), :] = rotate(
            query_t[HS * h : HS * (h + 1)], cos_rows, sin_rows
        ).astype(bf16)
    m_ref[...] = jnp.full_like(m_ref, NEG)
    l_ref[...] = jnp.zeros_like(l_ref)
    acc_ref[...] = jnp.zeros_like(acc_ref)

    bk = 2 * nf * tq
    per_chunk = math.prod(ax.dims[:top])
    start = ax.me * tq

    def block_copy(j, slot):
        return pltpu.make_async_copy(kv_out.at[ax.place_index(j)], kvb.at[slot], blk_sem.at[slot])

    def attend(k):
        first_block = (z - k) * per_chunk
        count = jnp.minimum(place - first_block + 1, per_chunk)

        @pl.when(z >= k)
        def _():
            block_copy(first_block, 0).start()

            def block(i, carry):
                j = first_block + i
                slot = lax.rem(i, 2)

                @pl.when(i + 1 < count)
                def _():
                    block_copy(j + 1, 1 - slot).start()

                block_copy(j, slot).wait()
                bias = bias_tile((start,), docs, j * bk, bk, tq)
                bias = jnp.concatenate([bias] * heads, axis=1)
                for p in range(parts):
                    kb = kvb[slot, :, :, :, 2 * HS * p : 2 * HS * (p + 1)].reshape(bk, 2 * HS)
                    vb = kvb[slot, :, :, :, width_k + 2 * HS * p : width_k + 2 * HS * (p + 1)]
                    vt = jnp.transpose(vb.reshape(bk, 2 * HS))
                    rows = qt_ref[2 * heads * HS * p : 2 * heads * HS * (p + 1), :] * bf16(1.0 / 8.0)
                    for g in range(2):
                        at = 2 * p + g
                        s = jnp.dot(kb, padded(rows, heads, g), preferred_element_type=f32) + bias
                        m = m_ref[at]
                        new = jnp.maximum(m, jnp.max(s, axis=0, keepdims=True))
                        prob = jnp.exp(s - new)
                        decay = jnp.exp(m - new)
                        m_ref[at] = new
                        l_ref[at] = l_ref[at] * decay + jnp.sum(prob, axis=0, keepdims=True)
                        acc_ref[at] = acc_ref[at] * decay + jnp.dot(
                            vt[HS * g : HS * (g + 1)], prob.astype(bf16), preferred_element_type=f32
                        )
                return carry

            lax.fori_loop(0, count, block, 0)

    for turn in range(1, chunks + stages):
        for k in range(chunks):
            stage = turn - k
            if (k, stage) != (0, 0) and 0 <= stage <= stages:
                tick(k, stage)
        if turn == 4:
            for copy in o_y + gu_y:
                copy.wait()
            o_f[0].start()
            o_f[1].start()
            gu_x.start()
            gu_z[0].start()
        if turn == 3:
            cot_y.start()
        if turn == 6:
            o_f[0].wait()
            o_f[2].start()
            gu_x.wait()
            gu_z[1].start()
        if turn == 5:
            cot_y.wait()
            loads[6].wait()
            cot_c.start()
        if turn >= stages:
            attend(turn - stages)
    for p in range(parts):
        outs = []
        for g in range(2):
            at = 2 * p + g
            out = acc_ref[at] / l_ref[at]
            outs.append(out)
            ot_ref[at] = out
            lse_ref[at] = m_ref[at] + jnp.log(l_ref[at])
        low_ref[:, 2 * heads * HS * p : 2 * heads * HS * (p + 1)] = head_lanes(outs, heads, tq).astype(bf16)

    for k in range(1, chunks):
        @pl.when(z + k < chunks)
        def _():
            top_copy(k).wait_send()
    for copy in loads[3:6]:
        copy.wait()
    backs = [back]
    for waits, src, dst in (
        (o_f[1:], obuf, wo_out), ([cot_c], cbuf, cots_out), (gu_z, gubuf, gu_out)
    ):
        for copy in waits:
            copy.wait()
        backs.append(pltpu.make_async_copy(src, dst, out_sem.at[1 + len(backs)]))
        backs[-1].start()
    for copy in backs:
        copy.wait()


def forward(nctx, nf, docs, tokens, gains, cos_t, sin_t, wq, wk, wv, wo, wg, wu, cot):
    tq, width = tokens.shape
    width_q, width_k = wq.shape[1], wk.shape[1]
    parts = width_k // (2 * HS)
    heads = width_q // HS // (2 * parts)
    hidden_units = wg.shape[1]
    quarter = hidden_units // (2 * nf)
    dims = line_dims(nctx // 2)
    lead = tuple(reversed(dims))
    most = max(dims + [2])
    chunks = dims[-1]
    stages = len(dims) + 1
    bf16, f32 = jnp.bfloat16, jnp.float32
    vmem = pl.BlockSpec(memory_space=pltpu.VMEM)
    smem = pl.BlockSpec(memory_space=pltpu.SMEM)
    hbm = pl.BlockSpec(memory_space=pl.ANY)
    dma = pltpu.SemaphoreType.DMA
    return pl.pallas_call(
        functools.partial(forward_kernel, (nctx, nf, parts, heads, tq)),
        out_shape=[
            jax.ShapeDtypeStruct((width_q, tq), bf16),
            jax.ShapeDtypeStruct(lead + (2, nf, tq, 2 * width_k), bf16),
            jax.ShapeDtypeStruct((tq, width_q), bf16),
            jax.ShapeDtypeStruct((2 * parts, HS, heads * tq), f32),
            jax.ShapeDtypeStruct((2 * parts, 1, heads * tq), f32),
            jax.ShapeDtypeStruct((width, width_q + 2 * width_k), bf16),
            jax.ShapeDtypeStruct((nf * wo.shape[0], wo.shape[1]), bf16),
            jax.ShapeDtypeStruct((width, 2 * quarter), bf16),
            jax.ShapeDtypeStruct((2 * nf, tq, width), bf16),
            jax.ShapeDtypeStruct((tq, width), bf16),
            jax.ShapeDtypeStruct((tq, 1), f32),
            jax.ShapeDtypeStruct((2, width), f32),
        ],
        in_specs=[smem, vmem, vmem, vmem, vmem] + [hbm] * 7,
        out_specs=[vmem, hbm, vmem, vmem, vmem, hbm, hbm, hbm, hbm, vmem, vmem, vmem],
        scratch_shapes=[
            pltpu.VMEM((width, width_q + 2 * width_k), bf16),
            pltpu.VMEM((nf * wo.shape[0], wo.shape[1]), bf16),
            pltpu.VMEM((width, 2 * quarter), bf16),
            pltpu.VMEM((2 * nf, tq, width), bf16),
            pltpu.VMEM(gains.shape, f32),
            pltpu.VMEM((tq, 2 * width_k), bf16),
            pltpu.VMEM((2, 2, nf, tq, 2 * width_k), bf16),
            pltpu.VMEM((2 * parts, 1, heads * tq), f32),
            pltpu.VMEM((2 * parts, 1, heads * tq), f32),
            pltpu.VMEM((2 * parts, HS, heads * tq), f32),
            dma((7,)),
            dma((21,)),
            dma((21,)),
            dma((chunks - 1,)),
            dma((chunks - 1,)),
            dma((chunks, 2, stages, most - 1)),
            dma((chunks, 2, stages, most - 1)),
            dma((2,)),
            dma((5,)),
        ],
        compiler_params=pltpu.CompilerParams(
            collective_id=0, has_side_effects=True, vmem_limit_bytes=60 * 2**20
        ),
        name="forward",
    )(docs, tokens, gains, cos_t, sin_t, wq, wk, wv, wo, wg, wu, cot)


def feed_forward_kernel(plan, tokens_ref, low_ref, attn_in_ref, gains_ref, wo_hbm, gu_hbm, down_hbm, cots_hbm,
                        result_ref, gres_ref, branch_ref, gattn_ref, gmlp_ref, gup_ref, dnp_ref, inputs_out,
                        wo, gu, down, cots, xs, grads, mixed, gm, sums, sent, core_in, side_in, side_out,
                        load_sem, x_send, x_recv, s_send, s_recv, top_send, top_recv,
                        ag_send, ag_recv, out_sem):
    nctx, nf = plan
    ax = Axes(nctx, nf)
    f, core, place = ax.f, ax.core, ax.place
    mesh_id = pl.DeviceIdType.MESH
    bf16, f32 = jnp.bfloat16, jnp.float32
    tq, width = tokens_ref.shape
    quarter = down.shape[0]
    side = ax.side_axis[3](1)[1]
    mate = ax.core_axis[3](1)[1]
    top = ax.nd - 1
    chunks = ax.dims[top]
    z = ax.lines[top][2]

    barrier = pltpu.get_barrier_semaphore()
    for where in ax.peers():
        pl.semaphore_signal(barrier, inc=1, device_id=where, device_id_type=mesh_id)
    loads = [
        pltpu.make_async_copy(src, dst, load_sem.at[i])
        for i, (src, dst) in enumerate((
            (wo_hbm, wo), (cots_hbm, cots),
            (down_hbm.at[pl.ds(pl.multiple_of(core * quarter, quarter), quarter)], down), (gu_hbm, gu),
        ))
    ]
    for copy in loads:
        copy.start()

    def remote(src, dst, sends, recvs, i, where):
        return pltpu.make_async_remote_copy(
            src_ref=src, dst_ref=dst, send_sem=sends.at[i], recv_sem=recvs.at[i],
            device_id=where, device_id_type=mesh_id,
        )

    hidden = tokens_ref[...].astype(f32)
    own_at = ax.place_index(place) + (core,)
    put = pltpu.make_async_copy(attn_in_ref, inputs_out.at[own_at], out_sem.at[0])

    def top_copy(k):
        return pltpu.make_async_remote_copy(
            src_ref=attn_in_ref, dst_ref=inputs_out.at[own_at],
            send_sem=top_send.at[k - 1], recv_sem=top_recv.at[k - 1],
            device_id=ax.at_line(top, lax.rem(z + k, chunks)), device_id_type=mesh_id,
        )

    order = ax.lines[:top] + [ax.core_axis]
    stages = len(order)

    def ag_copies(k, stage):
        index = [None] * (ax.nd + 1)
        index[0] = lax.rem(z + chunks - k, chunks)
        for i, axis in enumerate(order):
            index[axis[0]] = slice(None) if i < stage else axis[2]
        region = inputs_out.at[tuple(index)]
        axis = order[stage]
        return [
            pltpu.make_async_remote_copy(
                src_ref=region, dst_ref=region,
                send_sem=ag_send.at[k, stage, i - 1], recv_sem=ag_recv.at[k, stage, i - 1],
                device_id=axis[3](i)[1], device_id_type=mesh_id,
            )
            for i in range(1, axis[1])
        ]

    def tick(turn):
        for k in range(chunks):
            stage = turn - k
            if not 0 <= stage <= stages:
                continue
            if stage == 0:
                if k > 0:
                    top_copy(k).wait()
                else:
                    put.wait()
            else:
                for copy in ag_copies(k, stage - 1):
                    copy.wait()
            if stage < stages:
                for copy in ag_copies(k, stage):
                    copy.start()

    pl.semaphore_wait(barrier, ax.peer_count)
    put.start()
    top_copy(1).start()
    tick(0)

    loads[0].wait()
    resid = hidden + jnp.dot(low_ref[...], wo[...], preferred_element_type=f32)
    inv = lax.rsqrt(jnp.mean(resid * resid, axis=1, keepdims=True) + EPS)
    normed = resid * inv
    gain = gains_ref[1:2, :]
    xs[0] = (normed * gain).astype(bf16)
    x_side = remote(xs.at[0], xs.at[1], x_send, x_recv, 0, side)
    x_core = remote(xs.at[0], xs.at[2], x_send, x_recv, 1, mate)
    x_far = remote(xs.at[1], xs.at[3], x_send, x_recv, 2, mate)
    x_side.start()
    x_core.start()

    def rows(slot):
        return slice(slot * tq, (slot + 1) * tq)

    for copy in loads[1:3]:
        copy.wait()
    gm[...] = lax.dot_general(
        cots[...].reshape(4 * tq, width), down[...], (((1,), (1,)), ((), ())), preferred_element_type=f32
    )
    loads[3].wait()
    top_copy(2).start()
    step = 256

    def both(ref, a, b, span=slice(None)):
        return jnp.concatenate([ref[a, :, span], ref[b, :, span]], axis=0)

    def compute(a, b):
        x = both(xs, a, b)
        for n in range(quarter // step):
            span = slice(n * step, (n + 1) * step)
            up_span = slice(quarter + n * step, quarter + (n + 1) * step)
            gate = jnp.dot(x, gu[:, span], preferred_element_type=f32)
            up = jnp.dot(x, gu[:, up_span], preferred_element_type=f32)
            sig = jax.nn.sigmoid(gate)
            act = gate * sig
            grad = jnp.concatenate([gm[rows(a), span], gm[rows(b), span]], axis=0)
            mix = (act * up).astype(bf16)
            grad_gate = (grad * up * sig * (1.0 + gate * (1.0 - sig))).astype(bf16)
            grad_up = (grad * act).astype(bf16)
            for i, slot in enumerate((a, b)):
                mixed[slot, :, span] = mix[rows(i)]
                grads[slot, :, span] = grad_gate[rows(i)]
                grads[slot, :, up_span] = grad_up[rows(i)]
        total = lax.dot_general(
            both(grads, a, b), gu[...], (((1,), (1,)), ((), ())), preferred_element_type=f32
        )
        for i, slot in enumerate((a, b)):
            sums[0, slot] = total[rows(i)]

    def outputs(a, b):
        total = jnp.dot(both(mixed, a, b), down[...], preferred_element_type=f32)
        for i, slot in enumerate((a, b)):
            sums[1, slot] = total[rows(i)]

    def to_core(kind, slot):
        i = 2 * kind + slot - 2
        return remote(sent.at[i], core_in.at[i], s_send, s_recv, i, mate)

    def to_side(kind):
        return remote(side_out.at[kind], side_in.at[kind], s_send, s_recv, 4 + kind, side)

    def give_core(kind, slot):
        sent[2 * kind + slot - 2] = sums[kind, slot].astype(bf16)
        to_core(kind, slot).start()

    def give_side(kind):
        to_core(kind, 3).wait()
        side_out[kind] = (sums[kind, 1] + core_in[2 * kind + 1].astype(f32)).astype(bf16)
        to_side(kind).start()

    x_core.wait()
    compute(0, 2)
    give_core(0, 2)
    top_copy(3).start()
    x_side.wait()
    x_far.start()
    tick(1)
    outputs(0, 2)
    give_core(1, 2)
    x_far.wait()
    compute(1, 3)
    give_core(0, 3)
    tick(2)
    outputs(1, 3)
    give_side(0)
    give_core(1, 3)
    flat_x = xs[...].reshape(4 * tq, width)
    pieces = nctx // 2
    unit = quarter // pieces
    tall = max(unit, 256)
    for kind in range(2):
        for n in range(quarter // tall):
            span = slice(kind * quarter + n * tall, kind * quarter + (n + 1) * tall)
            cols = jnp.transpose(jnp.concatenate([grads[s, :, span] for s in range(4)], axis=0))
            part = jnp.dot(cols, flat_x, preferred_element_type=f32).astype(bf16)
            first = n * tall
            while first < (n + 1) * tall:
                piece, at = first // unit, first % unit
                end = min((piece + 1) * unit, (n + 1) * tall)
                gup_ref[static_index(bit_dims(nctx // 2), piece) + (kind, slice(at, at + end - first))] = part[
                    first - n * tall : end - n * tall
                ]
                first = end
        if kind == 0:
            give_side(1)
            tick(3)
    unit = width // pieces
    flat_mixed = mixed[...].reshape(4 * tq, quarter)
    for n in range(width // 384):
        cols = jnp.transpose(jnp.concatenate([cots[s, :, 384 * n : 384 * (n + 1)] for s in range(4)], axis=0))
        part = jnp.dot(cols, flat_mixed, preferred_element_type=f32).astype(bf16)
        first = n * 384
        while first < (n + 1) * 384:
            piece, at = first // unit, first % unit
            end = min((piece + 1) * unit, (n + 1) * 384)
            rows_of = part[first - n * 384 : end - n * 384]
            for c in range(quarter // 128):
                dnp_ref[
                    static_index(bit_dims(nctx // 2), piece)
                    + (slice(c * unit + at, c * unit + at + end - first),)
                ] = rows_of[:, 128 * c : 128 * (c + 1)]
            first = end

    tick(4)
    to_core(0, 2).wait()
    to_side(0).wait()
    grad = sums[0, 0] + core_in[0].astype(f32) + side_in[0].astype(f32)
    product = grad * normed
    gmlp_ref[...] = jnp.sum(product, axis=0, keepdims=True)
    scaled = grad * gain
    mean = jnp.mean(scaled * normed, axis=1, keepdims=True)
    gres = cots[0].astype(f32) + inv * (scaled - normed * mean)
    gres_ref[...] = gres
    branch = gres.astype(bf16)
    branch_ref[...] = branch
    gattn_ref[...] = lax.dot_general(
        branch, wo[...], (((1,), (1,)), ((), ())), preferred_element_type=f32
    ).astype(bf16)
    to_core(1, 2).wait()
    to_side(1).wait()
    result_ref[...] = (resid + sums[1, 0] + core_in[2].astype(f32) + side_in[1].astype(f32)).astype(bf16)
    for turn in range(5, chunks + stages):
        tick(turn)


def static_index(dims, piece):
    return tuple(piece // math.prod(dims[:i]) % dims[i] for i in reversed(range(len(dims))))


def feed_forward(nctx, nf, tokens, low, attn_in, gains, wo, gu, down, cots):
    tq, width = tokens.shape
    quarter = gu.shape[1] // 2
    dims = line_dims(nctx // 2)
    bits = bit_dims(nctx // 2)
    lead = tuple(reversed(dims))
    plane = nctx // 2
    chunks, stages, most = dims[-1], len(dims), max(dims + [2])
    bf16, f32 = jnp.bfloat16, jnp.float32
    vmem = pl.BlockSpec(memory_space=pltpu.VMEM)
    hbm = pl.BlockSpec(memory_space=pl.ANY)
    dma = pltpu.SemaphoreType.DMA
    return pl.pallas_call(
        functools.partial(feed_forward_kernel, (nctx, nf)),
        out_shape=[
            jax.ShapeDtypeStruct((tq, width), bf16),
            jax.ShapeDtypeStruct((tq, width), f32),
            jax.ShapeDtypeStruct((tq, width), bf16),
            jax.ShapeDtypeStruct((tq, width), bf16),
            jax.ShapeDtypeStruct((1, width), f32),
            jax.ShapeDtypeStruct(tuple(bits) + (2, quarter // plane, width), bf16),
            jax.ShapeDtypeStruct(tuple(bits) + (width // plane * (quarter // 128), 128), bf16),
            jax.ShapeDtypeStruct(lead + (2, tq, width), bf16),
        ],
        in_specs=[vmem] * 4 + [hbm] * 4,
        out_specs=[vmem] * 7 + [hbm],
        scratch_shapes=[
            pltpu.VMEM(wo.shape, bf16),
            pltpu.VMEM(gu.shape, bf16),
            pltpu.VMEM((quarter, width), bf16),
            pltpu.VMEM((4, tq, width), bf16),
            pltpu.VMEM((4, tq, width), bf16),
            pltpu.VMEM((4, tq, 2 * quarter), bf16),
            pltpu.VMEM((4, tq, quarter), bf16),
            pltpu.VMEM((4 * tq, quarter), f32),
            pltpu.VMEM((2, 4, tq, width), f32),
            pltpu.VMEM((4, tq, width), bf16),
            pltpu.VMEM((4, tq, width), bf16),
            pltpu.VMEM((2, tq, width), bf16),
            pltpu.VMEM((2, tq, width), bf16),
            dma((4,)),
            dma((4,)),
            dma((4,)),
            dma((6,)),
            dma((6,)),
            dma((chunks - 1,)),
            dma((chunks - 1,)),
            dma((chunks, stages, most - 1)),
            dma((chunks, stages, most - 1)),
            dma((1,)),
        ],
        compiler_params=pltpu.CompilerParams(
            collective_id=2, has_side_effects=True, vmem_limit_bytes=60 * 2**20
        ),
        name="feed_forward",
    )(tokens, low, attn_in, gains, wo, gu, down, cots)


def finish_kernel(*refs):
    count = len(refs) // 2
    for src, dst in zip(refs[:count], refs[count:]):
        dst[...] = src[...]


def finish(*values):
    def whole(x):
        return pl.BlockSpec(x.shape, lambda i: (0,) * len(x.shape))

    return pl.pallas_call(
        finish_kernel,
        grid=(1,),
        out_shape=[jax.ShapeDtypeStruct(x.shape, x.dtype) for x in values],
        in_specs=[whole(x) for x in values],
        out_specs=[whole(x) for x in values],
        compiler_params=pltpu.CompilerParams(vmem_limit_bytes=60 * 2**20),
        name="finish",
    )(*values)


def per_device(
    nctx,
    nf,
    tokens,
    query_weight,
    key_projection,
    value_projection,
    output_weight,
    gate_weight,
    up_weight,
    down_weight,
    norm_attn,
    norm_mlp,
    doc_starts,
    cotangent,
):
    token_rows, width = tokens.shape
    n_tokens = token_rows * nctx * nf
    bf16, f32 = jnp.bfloat16, jnp.float32

    own_device = lax.axis_index(AXES)
    own_index = layout_rows(own_device, token_rows)
    own_begin = doc_begin(own_index, doc_starts)
    cosine_table, sine_table = rope_tables(own_index - own_begin)
    cosine_table, sine_table = cosine_table.T, sine_table.T
    gains = jnp.pad(jnp.stack([norm_attn, norm_mlp]).astype(f32), ((0, 6), (0, 0)))
    (
        query_rot, key_values, attn_low, attn_exact, log_total, qkv_full, output_full, gate_up,
        cotangents, attention_input, inv_attn, gains,
    ) = forward(
        nctx, nf, doc_starts, tokens, gains, cosine_table, sine_table, query_weight, key_projection,
        value_projection, output_weight, gate_weight, up_weight, cotangent,
    )
    key_width = KEY_VALUE_HEADS * HEAD_SIZE
    key_values = key_values.reshape(n_tokens, 2 * key_width)
    result, grad_resid, grad_branch, grad_attn, gain_mlp_partial, gate_up_partial, down_partial, inputs_all = feed_forward(
        nctx, nf, tokens, attn_low, attention_input, gains, output_full, gate_up, down_weight,
        cotangents.reshape(2 * nf, token_rows, width),
    )

    tokens_grad, query_sum, key_sum, value_sum, gain_sums, gate_sum, up_sum, down_sum, output_sum = backward(
        nctx, nf, doc_starts, query_rot, grad_attn, attn_exact, log_total, key_values, qkv_full,
        cosine_table, sine_table, tokens, inv_attn, gains, grad_resid,
        gain_mlp_partial, attn_low, grad_branch, gate_up_partial, down_partial,
        inputs_all.reshape(nctx, token_rows, width),
    )

    gain_sums = gain_sums[: 2 * width // 128].reshape(2, width)
    result, tokens_grad, *sums = finish(
        result, tokens_grad, query_sum, key_sum, value_sum, output_sum, gate_sum, up_sum, down_sum
    )
    return (result, tokens_grad, *(weight.T for weight in sums), gain_sums[0], gain_sums[1])


def solution(mesh):
    return jax.shard_map(
        functools.partial(per_device, mesh.shape["ctx"], mesh.shape["fsdp"]),
        mesh=mesh,
        in_specs=(
            P(("ctx", "fsdp"), None),
            P("fsdp", None),
            P("fsdp", None),
            P("fsdp", None),
            P("fsdp", None),
            P("fsdp", None),
            P("fsdp", None),
            P("fsdp", None),
            P("fsdp"),
            P("fsdp"),
            P(),
            P(("ctx", "fsdp"), None),
        ),
        out_specs=(
            P(("ctx", "fsdp"), None),
            P(("ctx", "fsdp"), None),
            P("fsdp", "ctx"),
            P("fsdp", "ctx"),
            P("fsdp", "ctx"),
            P("fsdp", "ctx"),
            P("fsdp", "ctx"),
            P("fsdp", "ctx"),
            P("fsdp", "ctx"),
            P(),
            P(),
        ),
        check_vma=False,
    )
```

```python
import functools
import math

import jax
import jax.numpy as jnp
from jax import lax
from jax.experimental import pallas as pl
from jax.experimental.pallas import tpu as pltpu
from jax.sharding import PartitionSpec as P

QUERY_HEADS = 18
KEY_VALUE_HEADS = 6
HEAD_SIZE = 64
HS = HEAD_SIZE

EPS = 1e-05
THETA = 10000.0
NEG = -1e30
AXES = ("ctx", "fsdp")


def rope_tables(positions):
    half_dim = HEAD_SIZE // 2
    frequency = jnp.exp(-math.log(THETA) * jnp.arange(half_dim, dtype=jnp.float32) / half_dim)
    angles = positions.astype(jnp.float32)[:, None] * frequency[None, :]
    return (jnp.cos(angles), jnp.sin(angles))


def apply_rotary(values, cosine_table, sine_table):
    half_dim = values.shape[-1] // 2
    first_half = values[..., :half_dim]
    second_half = values[..., half_dim:]
    cos_rows = cosine_table[:, None, :]
    sin_rows = sine_table[:, None, :]
    return jnp.concatenate(
        [
            first_half * cos_rows - second_half * sin_rows,
            second_half * cos_rows + first_half * sin_rows,
        ],
        axis=-1,
    )


def unrotate(values, cosine_table, sine_table):
    half_dim = values.shape[-1] // 2
    first_half = values[..., :half_dim]
    second_half = values[..., half_dim:]
    cos_rows = cosine_table[:, None, :]
    sin_rows = sine_table[:, None, :]
    return jnp.concatenate(
        [
            first_half * cos_rows + second_half * sin_rows,
            second_half * cos_rows - first_half * sin_rows,
        ],
        axis=-1,
    )


def doc_begin(indices, doc_starts):
    marked = jnp.where(indices[:, None] >= doc_starts[None, :], doc_starts[None, :], 0)
    return jnp.max(marked, axis=1)


def layout_rows(device, row_count):
    return device * row_count + jnp.arange(row_count, dtype=jnp.int32)


def heads_rows(natural):
    return jnp.transpose(natural.astype(jnp.float32))
def padded(rows, heads, g):
    top = jnp.concatenate([rows[HS*(heads*g+j):HS*(heads*g+j+1)] for j in range(heads)], axis=1)
    z = jnp.zeros_like(top)
    return jnp.concatenate([top, z] if g == 0 else [z, top], axis=0)
def head_lanes(per_group, heads, tq):
    return jnp.transpose(jnp.concatenate([per_group[g][:, tq*j:tq*(j+1)] for g in range(2) for j in range(heads)], axis=0))
def bias_tile(info, docs, first, bk, tq):
    query = info[0] + lax.broadcasted_iota(jnp.int32, (1, tq), 1)
    begin = jnp.zeros((1, tq), jnp.int32)
    for i in range(docs.shape[0]):
        begin = jnp.maximum(begin, jnp.where(query >= docs[i], docs[i], 0))
    key = first + lax.broadcasted_iota(jnp.int32, (bk, 1), 0)
    return jnp.where((key <= query) & (key >= begin), 0.0, NEG)


def line_dims(count):
    fours = 0
    while count % 4 == 0:
        count //= 4
        fours += 1
    return ([count] if count > 1 else []) + [4] * fours


def rotate_back(rows, cos_rows, sin_rows):
    half_dim = HS // 2
    first, second = rows[:half_dim], rows[half_dim:]
    return jnp.concatenate(
        [first * cos_rows + second * sin_rows, second * cos_rows - first * sin_rows], axis=0
    )


def w_order(lines):
    return [lines[-2]] + lines[1:-2] + [lines[0], lines[-1]]


def bit_dims(count):
    return [2] * (count.bit_length() - 1)


def round_up(value, unit):
    return -(-value // unit) * unit


def backward_kernel(plan, docs, q_ref, do_ref, ot_ref, lse_ref, kv_hbm, w_ref, cos_ref, sin_ref,
                    normed_ref, inv_ref, gain_ref, gres_ref, gmlp_ref, low_ref, branch_ref, gup_hbm, dnp_hbm, inputs_hbm,
                    tokens_ref, query_ref, key_ref, value_ref, gains_out, gate_ref, up_ref, down_ref, out_ref,
                    kvbuf, dkv, acc_ref, gqt_ref, ga_ref, qblk, kvblk, small,
                    load_sem, send_sem, recv_sem, col_send, col_recv, own_sem, credit,
                    wg, wd, wo, brs, lows, halves, fin, fin_in, dsend, din,
                    colq_ref, colkv_ref, gains_ref, cols_acc, half_send, half_in, gain_send, gain_in, in_sem,
                    g_send, g_recv, w_load, w_send, w_recv, top_send, top_recv, fin_send, fin_recv, *recvs):
    nctx, nf, parts, heads, tq, slots = plan
    plane = nctx // 2
    n = nctx * nf
    dims = bit_dims(plane)
    nd = len(dims)
    bk = 2 * nf * tq
    me_c, me_f = lax.axis_index("ctx"), lax.axis_index("fsdp")
    me = me_c * nf + me_f
    core, place = lax.rem(me_c, 2), me_c // 2
    mesh_id = pl.DeviceIdType.MESH
    half_dim = HS // 2

    def target(k):
        other = lax.rem(me + k, n)
        return other, {"ctx": other // nf, "fsdp": lax.rem(other, nf)}

    barrier = pltpu.get_barrier_semaphore()

    def greet(k, carry):
        pl.semaphore_signal(barrier, inc=1, device_id=target(k)[1], device_id_type=mesh_id)
        return carry

    lax.fori_loop(1, n, greet, 0)

    def loads(p):
        s = p % slots
        return [
            pltpu.make_async_copy(
                kv_hbm.at[:, pl.ds((kind * parts + p) * 2 * HS, 2 * HS)],
                kvbuf.at[s, kind], load_sem.at[s, kind],
            )
            for kind in range(2)
        ]

    resident = slots == parts

    def block_loads(p, j):
        slot = lax.rem(j, 2)
        return [
            pltpu.make_async_copy(
                kv_hbm.at[pl.ds(pl.multiple_of(j * bk, bk), bk), pl.ds((kind * parts + p) * 2 * HS, 2 * HS)],
                kvbuf.at[slot, kind], load_sem.at[slot, kind],
            )
            for kind in range(2)
        ]

    if resident:
        for p in range(parts):
            for copy in loads(p):
                copy.start()

    def dim_axis(i):
        stride = math.prod(dims[:i])
        size = dims[i]
        own = lax.rem(place // stride, size)

        def peer(k):
            there = lax.rem(own + k, size)
            return there, {"ctx": (place + (there - own) * stride) * 2 + core, "fsdp": me_f}

        return (nd - 1 - i, size, own, peer)

    core_axis = (nd, 2, core, lambda k: (1 - core, {"ctx": place * 2 + 1 - core, "fsdp": me_f}))
    side_axis = (nd + 1, 2, me_f, lambda k: (1 - me_f, {"ctx": me_c, "fsdp": 1 - me_f}))
    lines = [dim_axis(i) for i in range(nd)]
    orders = [[core_axis, side_axis] + lines, [core_axis, side_axis] + w_order(lines)]
    stages = nd + 2
    wrecvs = recvs[2 * stages :]
    side_at, mate_at = side_axis[3](1)[1], core_axis[3](1)[1]

    low_bits = nd - 2
    arrays = ((wg, gup_hbm, (0,)), (wd, dnp_hbm, ()), (wo, None, ()), (wg, gup_hbm, (1,)))
    w_lines = [lines, w_order(lines), w_order(lines), lines]

    def chunk_at(a, k):
        near, far_line = w_lines[a][nd - 2], w_lines[a][nd - 1]
        far_bit = far_line[2] if k % 2 else 1 - far_line[2]
        near_bit = near[2] if k // 2 else 1 - near[2]
        return far_bit, near_bit

    def w_region(a, k, stage, at):
        index = [slice(None)] * nd
        index[w_lines[a][nd - 1][0]], index[w_lines[a][nd - 2][0]] = chunk_at(a, k)
        for axis in w_lines[a][:stage]:
            index[axis[0]] = axis[2]
        if stage < low_bits:
            index[w_lines[a][stage][0]] = at
        return tuple(index)

    def held(a, index):
        first = w_lines[a][0][0]
        return index if a == 2 else index[:first] + index[first + 1 :] + arrays[a][2]

    def w_copy(a, k, stage):
        buf, far, sub = arrays[a]
        there, where = w_lines[a][stage][3](1)
        index = w_region(a, k, stage, there)
        return pltpu.make_async_remote_copy(
            src_ref=far.at[index + sub] if stage == 0 and a != 2 else buf.at[held(a, index)],
            dst_ref=wrecvs[a * (low_bits + 2) + stage].at[chunk_at(a, k)],
            send_sem=w_send.at[a, k, stage], recv_sem=w_recv.at[a, k, stage],
            device_id=where, device_id_type=mesh_id,
        )

    def near_copy(a, i):
        return pltpu.make_async_remote_copy(
            src_ref=arrays[a][0].at[held(a, w_region(a, i, low_bits, 0))], dst_ref=wrecvs[a * (low_bits + 2) + low_bits].at[i],
            send_sem=top_send.at[a, i], recv_sem=top_recv.at[a, i],
            device_id=w_lines[a][nd - 2][3](1)[1], device_id_type=mesh_id,
        )

    def far_copy(a):
        return pltpu.make_async_remote_copy(
            src_ref=arrays[a][0].at[held(a, w_region(a, 2, low_bits, 0))], dst_ref=wrecvs[a * (low_bits + 2) + low_bits + 1].at[0],
            send_sem=top_send.at[a, 2], recv_sem=top_recv.at[a, 2],
            device_id=w_lines[a][nd - 1][3](1)[1], device_id_type=mesh_id,
        )

    def w_start(which, k):
        for a in which:
            w_copy(a, k, 0).start()

    def w_finish(which, k):
        for a in which:
            buf = arrays[a][0]
            for stage in range(low_bits):
                w_copy(a, k, stage).wait()
                where = held(a, w_region(a, k, stage, w_lines[a][stage][2]))
                got = wrecvs[a * (low_bits + 2) + stage]
                buf[where] = (
                    buf[where].astype(jnp.float32) + got[chunk_at(a, k)].astype(jnp.float32)
                ).astype(buf.dtype)
                if stage + 1 < low_bits:
                    w_copy(a, k, stage + 1).start()
            if k < 2:
                near_copy(a, k).start()
            elif k == 2:
                near_copy(a, 0).wait()
                where = held(a, w_region(a, 2, low_bits, 0))
                buf[where] = (
                    buf[where].astype(jnp.float32)
                    + wrecvs[a * (low_bits + 2) + low_bits][0].astype(jnp.float32)
                ).astype(buf.dtype)
                far_copy(a).start()

    def w_total(a):
        near_copy(a, 1).wait()
        far_copy(a).wait()
        total = arrays[a][0][held(a, w_region(a, 3, low_bits, 0))].astype(jnp.float32)
        total = total + wrecvs[a * (low_bits + 2) + low_bits][1].astype(jnp.float32)
        return total + wrecvs[a * (low_bits + 2) + low_bits + 1][0].astype(jnp.float32)

    w_loads = [
        pltpu.make_async_copy(far.at[(slice(None),) * w_lines[i][0][0] + (w_lines[i][0][2],)], buf, w_load.at[i])
        for i, (buf, far, _) in enumerate(arrays[:2])
    ]
    for copy in w_loads:
        copy.start()
    half = low_ref.shape[1] // nf
    low_all = low_ref[...]
    halves[0] = low_all[:, :half]
    halves[1] = low_all[:, half:]
    lows[0] = halves[me_f]
    brs[0] = branch_ref[...]

    def g_copy(i, src, dst, where):
        return pltpu.make_async_remote_copy(
            src_ref=src, dst_ref=dst, send_sem=g_send.at[i], recv_sem=g_recv.at[i],
            device_id=where, device_id_type=mesh_id,
        )

    low_side = g_copy(0, halves.at[1 - me_f], lows.at[1], side_at)
    br_side = g_copy(1, brs.at[0], brs.at[1], side_at)
    low_core = g_copy(2, lows.at[pl.ds(0, 2)], lows.at[pl.ds(2, 2)], mate_at)
    br_core = g_copy(3, brs.at[pl.ds(0, 2)], brs.at[pl.ds(2, 2)], mate_at)

    def output_partial():
        low_core.wait()
        br_core.wait()
        rows = jnp.transpose(brs[...].reshape(4 * tq, brs.shape[2]))
        unit = brs.shape[2] // nctx
        wo[...] = jnp.zeros_like(wo)
        low_rows = lows[...].reshape(4 * tq, half)
        batch = plane // 4
        for r in range(plane):
            first = 2 * unit * (r % batch)
            if first == 0:
                chunk = 2 * unit * batch
                part = jnp.dot(
                    rows[2 * unit * r : 2 * unit * r + chunk], low_rows, preferred_element_type=jnp.float32
                )
            piece = jnp.where(core == 0, part[first : first + unit], part[first + unit : first + 2 * unit])
            wo[static_index(dims, r) + (slice(0, unit), slice(0, half))] = piece.astype(wo.dtype)

    pl.semaphore_wait(barrier, n - 1)
    low_side.start()
    br_side.start()
    for k in range(4):
        w_start((0, 3, 1) if k < 2 else (1,), k)

    def region(kind, stage, at):
        index = [slice(None)] * (nd + 2)
        for axis in orders[kind][:stage]:
            index[axis[0]] = axis[2]
        index[orders[kind][stage][0]] = at
        return tuple(index)

    def stage_copies(p, kind, stage):
        s = p % slots
        axis = orders[kind][stage]
        copies = []
        for k in range(1, axis[1]):
            there, where = axis[3](k)
            copies.append(
                pltpu.make_async_remote_copy(
                    src_ref=dkv.at[(s, kind) + region(kind, stage, there)],
                    dst_ref=recvs[kind * stages + stage].at[s, k - 1],
                    send_sem=send_sem.at[s, kind, stage, k - 1],
                    recv_sem=recv_sem.at[s, kind, stage, k - 1],
                    device_id=where, device_id_type=mesh_id,
                )
            )
        return copies

    def stage_start(p, stage):
        for kind in range(2):
            for copy in stage_copies(p, kind, stage):
                copy.start()

    finals = {}

    def stage_finish(p, stage):
        s = p % slots
        for kind in range(2):
            axis = orders[kind][stage]
            for copy in stage_copies(p, kind, stage):
                copy.wait()
            where = region(kind, stage, axis[2])
            got = recvs[kind * stages + stage]
            free = [i for i in range(nd + 2) if isinstance(where[i], slice)]

            def add(index, lead):
                total = dkv[(s, kind) + index].astype(jnp.float32)
                for k in range(axis[1] - 1):
                    total = total + got[(s, k) + lead].astype(jnp.float32)
                return total

            if not free:
                finals[p, kind] = add(where, ())
            else:
                size = dkv.shape[2 + free[0]]

                def one(i, carry):
                    index = list(where)
                    index[free[0]] = i
                    index = tuple(index)
                    dkv[(s, kind) + index] = add(index, (i,)).astype(dkv.dtype)
                    return carry

                lax.fori_loop(0, size, one, 0)

    def place_index(j):
        index = []
        for i in reversed(range(nd)):
            index.append(lax.rem(j // math.prod(dims[:i]), dims[i]))
        return tuple(index)

    start = me * tq
    last = (start + tq - 1) // bk + 1

    def compute(p):
        s = p % slots
        span = slice(2 * heads * HS * p, 2 * heads * HS * (p + 1))
        qt = q_ref[span, :].astype(jnp.float32) * (1.0 / 8.0)
        dt = heads_rows(do_ref[:, span])
        qg = [padded(qt, heads, g) for g in range(2)]
        dg = [padded(dt, heads, g) for g in range(2)]
        qrows = jnp.concatenate([jnp.transpose(x) for x in qg], axis=0).astype(jnp.bfloat16)
        drows = jnp.concatenate([jnp.transpose(x) for x in dg], axis=0).astype(jnp.bfloat16)
        delta = [
            jnp.sum(dg[g][HS * g : HS * (g + 1)] * ot_ref[2 * p + g], axis=0, keepdims=True)
            for g in range(2)
        ]
        lse = [lse_ref[2 * p + g] for g in range(2)]
        qg = [x.astype(jnp.bfloat16) for x in qg]
        dg = [x.astype(jnp.bfloat16) for x in dg]
        acc_ref[...] = jnp.zeros_like(acc_ref)
        for copy in loads(p) if resident else block_loads(p, 0):
            if not resident:
                copy.start()
            else:
                copy.wait()

        def zero(j, carry):
            at = place_index(j)
            for kind in range(2):
                dkv[(s, kind) + at] = jnp.zeros((2, nf, tq, 2 * HS), dkv.dtype)
            return carry

        def body(j, carry):
            first = pl.multiple_of(j * bk, bk)
            if resident:
                kb = kvbuf[s, 0, pl.ds(first, bk), :]
                vb = kvbuf[s, 1, pl.ds(first, bk), :]
            else:
                for copy in block_loads(p, j):
                    copy.wait()

                @pl.when(j + 1 < last)
                def _():
                    for copy in block_loads(p, j + 1):
                        copy.start()

                kb, vb = kvbuf[lax.rem(j, 2), 0], kvbuf[lax.rem(j, 2), 1]
            kt = jnp.transpose(kb)
            bias = bias_tile((start,), docs, first, bk, tq)
            bias = jnp.concatenate([bias] * heads, axis=1)
            ps = []
            dss = []
            for g in range(2):
                score = jnp.dot(kb, qg[g], preferred_element_type=jnp.float32)
                prob = jnp.exp(score + (bias - lse[g]))
                dp = jnp.dot(vb, dg[g], preferred_element_type=jnp.float32)
                ds = (prob * (dp - delta[g])).astype(jnp.bfloat16)
                ps.append(prob.astype(jnp.bfloat16))
                dss.append(ds)
                acc_ref[g] += jnp.dot(kt[HS * g : HS * (g + 1)], ds, preferred_element_type=jnp.float32)
            dv = jnp.dot(jnp.concatenate(ps, axis=1), drows, preferred_element_type=jnp.float32)
            dk = jnp.dot(jnp.concatenate(dss, axis=1), qrows, preferred_element_type=jnp.float32)
            at = place_index(j)
            dkv[(s, 0) + at] = dk.astype(dkv.dtype).reshape(2, nf, tq, 2 * HS)
            dkv[(s, 1) + at] = dv.astype(dkv.dtype).reshape(2, nf, tq, 2 * HS)
            return carry

        lax.fori_loop(last, plane, zero, 0)
        lax.fori_loop(0, last, body, 0)
        cos_rows = jnp.concatenate([cos_ref[...]] * heads, axis=1) * (1.0 / 8.0)
        sin_rows = jnp.concatenate([sin_ref[...]] * heads, axis=1) * (1.0 / 8.0)
        for g in range(2):
            back = rotate_back(acc_ref[g], cos_rows, sin_rows).astype(gqt_ref.dtype)
            for j in range(heads):
                h = (2 * p + g) * heads + j
                gqt_ref[HS * h : HS * (h + 1), :] = back[:, tq * j : tq * (j + 1)]

    peers = 2 + sum(size - 1 for size in dims)

    def all_peers():
        found = [core_axis[3](1)[1], side_axis[3](1)[1]]
        for axis in lines:
            found += [axis[3](k)[1] for k in range(1, axis[1])]
        return found

    progress = {}

    def advance(p):
        stage = progress[p]
        stage_finish(p, stage)
        progress[p] = stage + 1
        if stage + 1 < stages:
            stage_start(p, stage + 1)
        else:
            del progress[p]
            if p + slots < parts:
                for where in all_peers():
                    pl.semaphore_signal(credit, inc=1, device_id=where, device_id_type=mesh_id)

    for p in range(parts):
        if p >= slots:
            while p - slots in progress:
                advance(p - slots)
        compute(p)
        if p >= slots:
            pl.semaphore_wait(credit, peers)
        stage_start(p, 0)
        progress[p] = 0
        for older in [o for o in progress if o < p]:
            advance(older)
        if p == 0:
            low_side.wait()
            br_side.wait()
            low_core.start()
            br_core.start()
        if p == 1:
            for copy in w_loads:
                copy.wait()
            for k in range(2):
                w_finish((0, 3), k)
                w_start((0, 3), k + 2)
    for k in range(2):
        w_finish((1,), k)
    output_partial()

    def copies_to(k, which):
        other = lax.rem(me_c + k, nctx)
        where = {"ctx": other, "fsdp": me_f}
        block, out = ((qblk, colq_ref), (kvblk, colkv_ref), (small, gains_ref))[which]
        return pltpu.make_async_remote_copy(
            src_ref=block if which == 2 else block.at[other], dst_ref=out.at[me_c],
            send_sem=col_send.at[which, k], recv_sem=col_recv.at[which, k],
            device_id=where, device_id_type=mesh_id,
        )

    def share(which):
        def one(k, carry):
            copies_to(k, which).start()
            return carry

        block, out = ((qblk, colq_ref), (kvblk, colkv_ref), (small, gains_ref))[which]
        pltpu.make_async_copy(block if which == 2 else block.at[me_c], out.at[me_c], own_sem.at[which]).start()
        lax.fori_loop(1, nctx, one, 0)

    def share_wait(which):
        def one(k, carry):
            copies_to(k, which).wait()
            return carry

        block, out = ((qblk, colq_ref), (kvblk, colkv_ref), (small, gains_ref))[which]
        pltpu.make_async_copy(block if which == 2 else block.at[me_c], out.at[me_c], own_sem.at[which]).wait()
        lax.fori_loop(1, nctx, one, 0)

    width_q = 2 * parts * heads * HS
    width_k = 2 * parts * HS
    cq, ck = width_q // nctx, width_k // nctx
    qblk[...] = jnp.zeros_like(qblk)
    kvblk[...] = jnp.zeros_like(kvblk)
    for i in range(nctx):
        qblk[i, 0:cq, :] = gqt_ref[cq * i : cq * (i + 1), :]
    share(0)
    ga_ref[...] = jnp.dot(w_ref[:, :width_q], gqt_ref[...], preferred_element_type=jnp.float32)
    for k in range(4):
        w_start((2,), k)
    pq, pk = qblk.shape[1], kvblk.shape[1]

    def columns(col_ref, first, count):
        def fetch(i, slot):
            return pltpu.make_async_copy(
                inputs_hbm.at[i], brs.at[slot], in_sem.at[slot]
            )

        fetch(0, 0).start()
        cols_acc[first : first + count, :] = jnp.zeros((count, cols_acc.shape[1]), jnp.float32)

        def one(i, carry):
            slot = lax.rem(i, 2)

            @pl.when(i + 1 < nctx)
            def _():
                fetch(i + 1, 1 - slot).start()

            fetch(i, slot).wait()
            cols_acc[first : first + count, :] += jnp.dot(
                col_ref[i], brs[slot], preferred_element_type=jnp.float32
            )
            return carry

        lax.fori_loop(0, nctx, one, 0)

    per_side = plane // 2
    home = (2 * me_f + core) * per_side + place // 2
    slot = lax.rem(place, 2)

    def home_copy(kind, s):
        return pltpu.make_async_remote_copy(
            src_ref=fin.at[kind, s], dst_ref=fin_in.at[kind, slot],
            send_sem=fin_send.at[kind, s], recv_sem=fin_recv.at[kind, slot],
            device_id={"ctx": home, "fsdp": jnp.int32(s)}, device_id_type=mesh_id,
        )

    def self_copy(kind, s):
        return pltpu.make_async_copy(fin.at[kind, s], fin_in.at[kind, slot], fin_send.at[kind, s])

    def to_homes(kind, a):
        total = w_total(a)
        unit, lanes = fin.shape[2], fin.shape[3]
        blank = jnp.zeros((unit, lanes - half), fin.dtype)
        for s in range(2):
            fin[kind, s] = jnp.concatenate([total[:, half * s : half * (s + 1)].astype(fin.dtype), blank], axis=1)
            at_home = (home == me_c) & (me_f == s)

            @pl.when(jnp.logical_not(at_home))
            def _():
                home_copy(kind, s).start()

            @pl.when(at_home)
            def _():
                self_copy(kind, s).start()

    turn = 0
    while progress:
        for p in list(progress):
            advance(p)
        if turn == 0:
            for k in range(2, 4):
                w_finish((0, 3, 1), k)
        if turn == 1:
            for k in range(2):
                w_finish((2,), k)
        if turn == 2:
            for k in range(2, 4):
                w_finish((2,), k)
        turn += 1

    cos_rows, sin_rows = cos_ref[...], sin_ref[...]
    grads = []
    for kind in range(2):
        rows = []
        for p in range(parts):
            both = jnp.transpose(finals[p, kind])
            for g in range(2):
                one = both[HS * g : HS * (g + 1)]
                rows.append(rotate_back(one, cos_rows, sin_rows) if kind == 0 else one)
        grads.append(jnp.concatenate(rows, axis=0).astype(jnp.bfloat16))
    for i in range(nctx):
        kvblk[i, 0:ck, :] = grads[0][ck * i : ck * (i + 1)]
        kvblk[i, ck : 2 * ck, :] = grads[1][ck * i : ck * (i + 1)]
    share(1)
    grad_t = (
        ga_ref[...]
        + jnp.dot(w_ref[:, width_q : width_q + width_k], grads[0], preferred_element_type=jnp.float32)
        + jnp.dot(w_ref[:, width_q + width_k :], grads[1], preferred_element_type=jnp.float32)
    )
    grad = jnp.transpose(grad_t)
    normed = normed_ref[...].astype(jnp.float32) * inv_ref[...]
    product = grad * normed
    gain_sum = jnp.sum(product, axis=0, keepdims=True)
    lanes = 128
    tiles = gain_sum.shape[1] // lanes
    rows = [gain_sum[:, lanes * i : lanes * (i + 1)] for i in range(tiles)]
    rows += [gmlp_ref[:, lanes * i : lanes * (i + 1)] for i in range(tiles)]
    rows += [jnp.zeros((small.shape[0] - 2 * tiles, lanes), jnp.float32)]
    small[...] = jnp.concatenate(rows, axis=0)
    share(2)
    gain = gain_ref[0:1, :]
    scaled = grad * gain
    mean = jnp.mean(scaled * normed, axis=1, keepdims=True)
    tokens_ref[...] = gres_ref[...] + inv_ref[...] * (scaled - normed * mean)

    to_homes(0, 0)
    share_wait(0)
    columns(colq_ref, 0, pq)

    def give_half(first, count, i):
        rows = slice(first, first + count)
        theirs = jnp.where(me_f == 0, cols_acc[rows, half:], cols_acc[rows, :half]).astype(half_send.dtype)
        side_pad = jnp.zeros((count, half_send.shape[1] - half), half_send.dtype)
        half_send[rows, :] = jnp.concatenate([theirs, side_pad], axis=1)
        span = pl.ds(first, count)
        copy = g_copy(i, half_send.at[span], half_in.at[span], side_at)
        copy.start()
        return copy

    half_q = give_half(0, pq, 5)
    to_homes(1, 3)
    dsum = w_total(1)
    dsend[...] = dsum.astype(dsend.dtype)
    down_copy = g_copy(4, dsend, din, mate_at)
    down_copy.start()
    osum = w_total(2)
    out_ref[...] = osum[: out_ref.shape[0], :half]
    share_wait(1)
    columns(colkv_ref, pq, pk)
    half_kv = give_half(pq, pk, 7)
    share_wait(2)
    gain_total = gains_ref[0]
    for i in range(1, nctx):
        gain_total = gain_total + gains_ref[i]
    gain_send[...] = gain_total
    gain_copy = g_copy(6, gain_send, gain_in, side_at)
    gain_copy.start()
    half_q.wait()
    half_kv.wait()
    own_half = jnp.where(me_f == 0, cols_acc[:, :half], cols_acc[:, half:])
    rows = own_half + half_in[:, :half].astype(jnp.float32)
    query_ref[...] = rows[:cq]
    key_ref[...] = rows[pq : pq + ck]
    value_ref[...] = rows[pq + ck : pq + 2 * ck]
    gain_copy.wait()
    gains_out[...] = gain_send[...] + gain_in[...]
    down_copy.wait()
    cols = down_ref.shape[0]

    def unfold(folded):
        return jnp.concatenate(
            [folded[2 * cols * i : 2 * cols * (i + 1)] for i in range(folded.shape[0] // (2 * cols))], axis=1
        )

    dsum, got = unfold(dsum), unfold(din[...].astype(jnp.float32))
    own_cols = jnp.where(core == 0, dsum[:cols], dsum[cols:])
    far_cols = jnp.where(core == 0, got[:cols], got[cols:])
    down_ref[...] = jnp.where(
        core == 0,
        jnp.concatenate([own_cols, far_cols], axis=1),
        jnp.concatenate([far_cols, own_cols], axis=1),
    )
    owner = me_c // per_side
    for kind in range(2):
        for s in range(2):
            at_home = (home == me_c) & (me_f == s)

            @pl.when(jnp.logical_not(at_home))
            def _():
                home_copy(kind, s).wait_send()

            @pl.when(at_home)
            def _():
                self_copy(kind, s).wait()

        for h in range(2):
            holder = (2 * lax.rem(me_c, per_side) + h) * 2 + lax.rem(owner, 2)

            @pl.when(jnp.logical_not((holder == me_c) & (owner // 2 == me_f)))
            def _():
                pltpu.make_async_remote_copy(
                    src_ref=fin.at[0, 0], dst_ref=fin_in.at[kind, h],
                    send_sem=fin_send.at[0, 0], recv_sem=fin_recv.at[kind, h],
                    device_id={"ctx": home, "fsdp": me_f}, device_id_type=mesh_id,
                ).wait_recv()

    for kind, ref in ((0, gate_ref), (1, up_ref)):
        rows = jnp.concatenate([fin_in[kind, 0], fin_in[kind, 1]], axis=0).astype(jnp.float32)
        ref[...] = rows[:, :half]


def backward(nctx, nf, docs, q, do, ot, lse, kv, w, cos_t, sin_t, normed, inv, gain, gres, gmlp, low, branch, gup, dnp, inputs):
    width_q, tq = q.shape
    n_tokens, width_kv = kv.shape
    n = nctx * nf
    parts = width_kv // (4 * HS)
    heads = width_q // HS // (2 * parts)
    dims = bit_dims(nctx // 2)
    lead = tuple(reversed(dims))
    part_bytes = n_tokens * 2 * HS * 2
    slots = parts if parts * part_bytes * 5 <= 24 * 2**20 else 1
    nd = len(dims)
    bf16, f32 = jnp.bfloat16, jnp.float32
    axes = {"core": (nd, 2), "side": (nd + 1, nf)}
    line = [(nd - 1 - i, dims[i]) for i in range(nd)]
    orders = [
        [axes["core"], axes["side"]] + line,
        [axes["core"], axes["side"]] + w_order(line),
    ]
    recvs = []
    for order in orders:
        left = list(lead) + [2, nf]
        for position, size in order:
            left[position] = None
            recvs.append(
                pltpu.VMEM((slots, size - 1) + tuple(x for x in left if x) + (tq, 2 * HS), bf16)
            )
    model_width = low.shape[1]
    half = model_width // nf
    unit, deep = gup.shape[-2], model_width // (nctx // 2)
    quarter = dnp.shape[-2] // deep * 128
    plane = nctx // 2
    tails = [gup.shape[nd:], dnp.shape[nd:], (round_up(deep // 2, 16), round_up(half, 128))]
    for tail in (tails[0][1:], tails[1], tails[2], tails[0][1:]):
        for stage in range(nd - 2):
            recvs.append(pltpu.VMEM((2,) * (nd - 1 - stage) + tail, bf16))
        recvs += [pltpu.VMEM((2,) + tail, bf16), pltpu.VMEM((1,) + tail, bf16)]
    stages = nd + 2
    most = max(dims + [2])
    pq = round_up(width_q // nctx, 16)
    pk = round_up(2 * (2 * parts * HS) // nctx, 16)
    model = w.shape[0]
    sr = round_up(2 * model // 128, 8)
    vmem = pl.BlockSpec(memory_space=pltpu.VMEM)
    smem = pl.BlockSpec(memory_space=pltpu.SMEM)
    hbm = pl.BlockSpec(memory_space=pl.ANY)
    return pl.pallas_call(
        functools.partial(backward_kernel, (nctx, nf, parts, heads, tq, slots)),
        out_shape=[
            jax.ShapeDtypeStruct((tq, model), f32),
            jax.ShapeDtypeStruct((width_q // nctx, half), f32),
            jax.ShapeDtypeStruct((2 * parts * HS // nctx, half), f32),
            jax.ShapeDtypeStruct((2 * parts * HS // nctx, half), f32),
            jax.ShapeDtypeStruct((sr, 128), f32),
            jax.ShapeDtypeStruct((2 * unit, half), f32),
            jax.ShapeDtypeStruct((2 * unit, half), f32),
            jax.ShapeDtypeStruct((deep // 2, 2 * quarter), f32),
            jax.ShapeDtypeStruct((deep // 2, half), f32),
        ],
        in_specs=[smem, vmem, vmem, vmem, vmem, hbm] + [vmem] * 10 + [hbm] * 3,
        out_specs=[vmem] * 9,
        scratch_shapes=[
            pltpu.VMEM((slots, 2, n_tokens, 2 * HS) if slots == parts else (2, 2, 2 * nf * tq, 2 * HS), bf16),
            pltpu.VMEM((slots, 2) + lead + (2, nf, tq, 2 * HS), bf16),
            pltpu.VMEM((2, HS, heads * tq), f32),
            pltpu.VMEM((width_q, tq), bf16),
            pltpu.VMEM((model, tq), f32),
            pltpu.VMEM((nctx, pq, tq), bf16),
            pltpu.VMEM((nctx, pk, tq), bf16),
            pltpu.VMEM((sr, 128), f32),
            pltpu.SemaphoreType.DMA((max(slots, 2), 2)),
            pltpu.SemaphoreType.DMA((slots, 2, stages, most - 1)),
            pltpu.SemaphoreType.DMA((slots, 2, stages, most - 1)),
            pltpu.SemaphoreType.DMA((3, nctx)),
            pltpu.SemaphoreType.DMA((3, nctx)),
            pltpu.SemaphoreType.DMA((3,)),
            pltpu.SemaphoreType.REGULAR,
            pltpu.VMEM(lead[:-1] + tails[0], bf16),
            pltpu.VMEM(lead[:-1] + tails[1], bf16),
            pltpu.VMEM(lead + tails[2], bf16),
            pltpu.VMEM((4,) + branch.shape, bf16),
            pltpu.VMEM((4, tq, half), bf16),
            pltpu.VMEM((2, tq, half), bf16),
            pltpu.VMEM((2, 2, unit, round_up(half, 128)), bf16),
            pltpu.VMEM((2, 2, unit, round_up(half, 128)), bf16),
            pltpu.VMEM(tails[1], bf16),
            pltpu.VMEM(tails[1], bf16),
            pltpu.VMEM((nctx, pq, tq), bf16),
            pltpu.VMEM((nctx, pk, tq), bf16),
            pltpu.VMEM((nctx, sr, 128), f32),
            pltpu.VMEM((pq + pk, model), f32),
            pltpu.VMEM((pq + pk, round_up(half, 128)), bf16),
            pltpu.VMEM((pq + pk, round_up(half, 128)), bf16),
            pltpu.VMEM((sr, 128), f32),
            pltpu.VMEM((sr, 128), f32),
            pltpu.SemaphoreType.DMA((2,)),
            pltpu.SemaphoreType.DMA((8,)),
            pltpu.SemaphoreType.DMA((8,)),
            pltpu.SemaphoreType.DMA((2,)),
            pltpu.SemaphoreType.DMA((4, 4, max(nd - 2, 1))),
            pltpu.SemaphoreType.DMA((4, 4, max(nd - 2, 1))),
            pltpu.SemaphoreType.DMA((4, 3)),
            pltpu.SemaphoreType.DMA((4, 3)),
            pltpu.SemaphoreType.DMA((2, 2)),
            pltpu.SemaphoreType.DMA((2, 2)),
        ]
        + recvs,
        compiler_params=pltpu.CompilerParams(
            collective_id=1, has_side_effects=True, vmem_limit_bytes=63 * 2**20
        ),
        cost_estimate=pl.CostEstimate(flops=10**10, bytes_accessed=3 * 10**7, transcendentals=10**7),
        name="backward",
    )(docs, q, do, ot, lse, kv, w, cos_t, sin_t, normed, inv, gain, gres, gmlp, low, branch, gup, dnp, inputs)


def rotate(rows, cos_rows, sin_rows):
    half_dim = HS // 2
    first, second = rows[:half_dim], rows[half_dim:]
    return jnp.concatenate(
        [first * cos_rows - second * sin_rows, second * cos_rows + first * sin_rows], axis=0
    )


class Axes:
    def __init__(self, nctx, nf):
        self.ctx, self.f = lax.axis_index("ctx"), lax.axis_index("fsdp")
        self.core, self.place = lax.rem(self.ctx, 2), self.ctx // 2
        self.me = self.ctx * nf + self.f
        self.dims = line_dims(nctx // 2)
        self.nd = len(self.dims)
        ctx, f, core, place = self.ctx, self.f, self.core, self.place
        self.core_axis = (self.nd, 2, core, lambda k: (1 - core, {"ctx": place * 2 + 1 - core, "fsdp": f}))
        self.side_axis = (self.nd + 1, 2, f, lambda k: (1 - f, {"ctx": ctx, "fsdp": 1 - f}))
        self.lines = [self.line(i) for i in range(self.nd)]
        self.peer_count = 2 + sum(size - 1 for size in self.dims)

    def at_line(self, i, there):
        stride = math.prod(self.dims[:i])
        own = lax.rem(self.place // stride, self.dims[i])
        return {"ctx": (self.place + (there - own) * stride) * 2 + self.core, "fsdp": self.f}

    def line(self, i):
        size = self.dims[i]
        own = lax.rem(self.place // math.prod(self.dims[:i]), size)

        def peer(k):
            there = lax.rem(own + k, size)
            return there, self.at_line(i, there)

        return (self.nd - 1 - i, size, own, peer)

    def peers(self):
        found = [self.core_axis[3](1)[1], self.side_axis[3](1)[1]]
        for axis in self.lines:
            found += [axis[3](k)[1] for k in range(1, axis[1])]
        return found

    def place_index(self, j):
        return tuple(
            lax.rem(j // math.prod(self.dims[:i]), self.dims[i]) for i in reversed(range(self.nd))
        )


def forward_kernel(plan, docs, tokens_ref, norm_attn_ref, norm_mlp_ref, cos_ref, sin_ref, wq, wk, wv, wo, wg, wu, cot,
                   qt_ref, kv_out, low_ref, ot_ref, lse_ref, wqkv_out, wo_out, gu_out, cots_out,
                   attn_in_ref, inv_ref, gain_ref,
                   wbuf, obuf, gubuf, cbuf, gains_ref, gain_far, own_kv, kvb, m_ref, l_ref, acc_ref,
                   load_sem, w_send, w_recv, top_send, top_recv, ag_send, ag_recv, blk_sem, out_sem):
    nctx, nf, parts, heads, tq = plan
    ax = Axes(nctx, nf)
    f, core, place = ax.f, ax.core, ax.place
    mesh_id = pl.DeviceIdType.MESH
    bf16, f32 = jnp.bfloat16, jnp.float32
    width = tokens_ref.shape[1]
    half = width // nf
    width_q, width_k = 2 * parts * heads * HS, 2 * parts * HS
    rows4, rows2 = half // 4, half // 2
    quarter = gu_out.shape[1] // 2
    side = ax.side_axis[3](1)[1]
    mate = ax.core_axis[3](1)[1]
    low = ax.lines[0]
    bit = lax.rem(low[2], 2)
    across = ax.at_line(0, low[2] + 1 - 2 * bit)
    top = ax.nd - 1
    chunks = ax.dims[top]
    z = ax.lines[top][2]

    barrier = pltpu.get_barrier_semaphore()
    for where in ax.peers():
        pl.semaphore_signal(barrier, inc=1, device_id=where, device_id_type=mesh_id)

    def local(src, dst, i):
        return pltpu.make_async_copy(src, dst, load_sem.at[i])

    own_rows = pl.ds(pl.multiple_of(f * half, half), half)
    own_quarter = pl.ds(pl.multiple_of((2 * f + core) * quarter, quarter), quarter)
    loads = [
        local(wk, wbuf.at[own_rows, pl.ds(width_q, width_k)], 0),
        local(wv, wbuf.at[own_rows, pl.ds(width_q + width_k, width_k)], 1),
        local(wq, wbuf.at[own_rows, pl.ds(0, width_q)], 2),
        local(wo, obuf.at[own_rows], 3),
        local(wg.at[:, own_quarter], gubuf.at[own_rows, pl.ds(0, quarter)], 4),
        local(wu.at[:, own_quarter], gubuf.at[own_rows, pl.ds(quarter, quarter)], 5),
        local(cot, cbuf.at[0], 6),
    ]
    for copy in loads:
        copy.start()

    def remote(src, dst, i, where):
        return pltpu.make_async_remote_copy(
            src_ref=src, dst_ref=dst, send_sem=w_send.at[i], recv_sem=w_recv.at[i],
            device_id=where, device_id_type=mesh_id,
        )

    near = pl.multiple_of(core * rows2 + bit * rows4, 16)
    far_x = pl.multiple_of(core * rows2 + (1 - bit) * rows4, 16)
    there = (1 - f) * half

    def piece(base, offset):
        return pl.ds(pl.multiple_of(base + offset, 16), rows4)

    kv_cols, q_cols = pl.ds(width_q, 2 * width_k), pl.ds(0, width_q)
    mine = f * half
    gains_copy = remote(gains_ref, gain_far, 0, side)
    kv_y = [
        remote(wk.at[piece(0, near)], wbuf.at[piece(mine, near), pl.ds(width_q, width_k)], 1, side),
        remote(wv.at[piece(0, near)], wbuf.at[piece(mine, near), pl.ds(width_q + width_k, width_k)], 2, side),
    ]
    q_y = [remote(wq.at[piece(0, near)], wbuf.at[piece(mine, near), q_cols], 3, side)]
    o_y = [remote(wo.at[piece(0, near)], obuf.at[piece(mine, near)], 4, side)]

    def forwards(buf, cols, first):
        def part(offset):
            return buf.at[piece(there, offset), cols] if cols is not None else buf.at[piece(there, offset)]

        return [
            remote(part(near), part(near), first, across),
            remote(part(near), part(near), first + 1, mate),
            remote(part(far_x), part(far_x), first + 2, mate),
        ]

    kv_f = forwards(wbuf, kv_cols, 5)
    q_f = forwards(wbuf, q_cols, 8)
    o_f = forwards(obuf, None, 11)
    far_quarter = pl.ds(pl.multiple_of((2 * (1 - f) + core) * quarter, quarter), quarter)

    deep = lax.rem(z, 2)
    above = ax.at_line(top, z + 1 - 2 * deep)

    def gu_rows(base, which=bit):
        return pl.ds(pl.multiple_of(base + which * rows2 + deep * rows4, 16), rows4)

    gu_y = [
        remote(wg.at[gu_rows(0), far_quarter], gubuf.at[gu_rows(mine), pl.ds(0, quarter)], 14, side),
        remote(wu.at[gu_rows(0), far_quarter], gubuf.at[gu_rows(mine), pl.ds(quarter, quarter)], 15, side),
    ]
    gu_x = remote(gubuf.at[gu_rows(there)], gubuf.at[gu_rows(there)], 16, across)
    gu_z = [
        remote(gubuf.at[gu_rows(there, which)], gubuf.at[gu_rows(there, which)], 19 + i, above)
        for i, which in enumerate((bit, 1 - bit))
    ]
    cot_y = remote(cot, cbuf.at[1], 17, side)
    cot_c = remote(cbuf.at[pl.ds(0, 2)], cbuf.at[pl.ds(2, 2)], 18, mate)

    gains_ref[...] = jnp.zeros_like(gains_ref)
    gains_ref[0:1, :] = norm_attn_ref[...].astype(f32)
    gains_ref[1:2, :] = norm_mlp_ref[...].astype(f32)
    pl.semaphore_wait(barrier, ax.peer_count)
    gains_copy.start()
    for copy in kv_y + q_y:
        copy.start()

    hidden = tokens_ref[...].astype(f32)
    inv = lax.rsqrt(jnp.mean(hidden * hidden, axis=1, keepdims=True) + EPS)
    inv_ref[...] = inv
    gains_copy.wait()
    near_gain, far_gain = gains_ref[0:1, :], gain_far[0:1, :]
    gain = jnp.where(
        f == 0,
        jnp.concatenate([near_gain, far_gain], axis=1),
        jnp.concatenate([far_gain, near_gain], axis=1),
    )
    near_mlp, far_mlp = gains_ref[1:2, :], gain_far[1:2, :]
    gain_ref[0:1, :] = gain
    gain_ref[1:2, :] = jnp.where(
        f == 0,
        jnp.concatenate([near_mlp, far_mlp], axis=1),
        jnp.concatenate([far_mlp, near_mlp], axis=1),
    )
    attn_in = (hidden * inv * gain).astype(bf16)
    attn_in_ref[...] = attn_in

    for copy in kv_y:
        copy.wait()
    kv_f[0].start()
    kv_f[1].start()
    for copy in q_y:
        copy.wait()
    for copy in o_y + gu_y:
        copy.start()
    kv_f[0].wait()
    kv_f[2].start()
    q_f[0].start()
    q_f[1].start()
    for copy in loads[:3]:
        copy.wait()
    kv_f[1].wait()
    kv_f[2].wait()
    kv = jnp.dot(attn_in, wbuf[:, width_q:], preferred_element_type=f32)
    cos_rows, sin_rows = cos_ref[...], sin_ref[...]
    kt = jnp.transpose(kv[:, :width_k])
    k_rot = jnp.concatenate(
        [rotate(kt[HS * g : HS * (g + 1)], cos_rows, sin_rows) for g in range(2 * parts)], axis=0
    )
    own_kv[:, :width_k] = jnp.transpose(k_rot).astype(bf16)
    own_kv[:, width_k:] = kv[:, width_k:].astype(bf16)
    own_at = ax.place_index(place) + (core, f)
    put = pltpu.make_async_copy(own_kv, kv_out.at[own_at], out_sem.at[0])
    put.start()

    def top_copy(k):
        return pltpu.make_async_remote_copy(
            src_ref=own_kv, dst_ref=kv_out.at[own_at],
            send_sem=top_send.at[k - 1], recv_sem=top_recv.at[k - 1],
            device_id=ax.at_line(top, lax.rem(z + k, chunks)), device_id_type=mesh_id,
        )

    for k in range(1, chunks):
        @pl.when(z + k < chunks)
        def _():
            top_copy(k).start()

    lower = ax.lines[:top]
    orders = [lower + [ax.side_axis, ax.core_axis], [ax.side_axis] + lower + [ax.core_axis]]
    stages = len(orders[0])

    def ag_copies(k, stage):
        copies = []
        for kind in range(2):
            index = [None] * (ax.nd + 2)
            index[0] = z - k
            for i, axis in enumerate(orders[kind]):
                index[axis[0]] = slice(None) if i < stage else axis[2]
            region = kv_out.at[tuple(index) + (slice(None), pl.ds(kind * width_k, width_k))]
            axis = orders[kind][stage]
            for i in range(1, axis[1]):
                copies.append(
                    pltpu.make_async_remote_copy(
                        src_ref=region, dst_ref=region,
                        send_sem=ag_send.at[k, kind, stage, i - 1],
                        recv_sem=ag_recv.at[k, kind, stage, i - 1],
                        device_id=axis[3](i)[1], device_id_type=mesh_id,
                    )
                )
        return copies

    def tick(k, stage):
        @pl.when(z >= k)
        def _():
            if stage == 0:
                if k > 0:
                    top_copy(k).wait_recv()
            else:
                for copy in ag_copies(k, stage - 1):
                    copy.wait()
            if stage < stages:
                for copy in ag_copies(k, stage):
                    copy.start()

    put.wait()
    tick(0, 0)
    q_f[0].wait()
    q_f[2].start()
    q_f[1].wait()
    q_f[2].wait()
    back = pltpu.make_async_copy(wbuf, wqkv_out, out_sem.at[1])
    back.start()
    query = jnp.dot(attn_in, wbuf[:, :width_q], preferred_element_type=f32)
    query_t = jnp.transpose(query)
    for h in range(2 * parts * heads):
        qt_ref[HS * h : HS * (h + 1), :] = rotate(
            query_t[HS * h : HS * (h + 1)], cos_rows, sin_rows
        ).astype(bf16)
    m_ref[...] = jnp.full_like(m_ref, NEG)
    l_ref[...] = jnp.zeros_like(l_ref)
    acc_ref[...] = jnp.zeros_like(acc_ref)

    bk = 2 * nf * tq
    per_chunk = math.prod(ax.dims[:top])
    start = ax.me * tq

    def block_copy(j, slot):
        return pltpu.make_async_copy(kv_out.at[ax.place_index(j)], kvb.at[slot], blk_sem.at[slot])

    def attend(k):
        first_block = (z - k) * per_chunk
        count = jnp.minimum(place - first_block + 1, per_chunk)

        @pl.when(z >= k)
        def _():
            block_copy(first_block, 0).start()

            def block(i, carry):
                j = first_block + i
                slot = lax.rem(i, 2)

                @pl.when(i + 1 < count)
                def _():
                    block_copy(j + 1, 1 - slot).start()

                block_copy(j, slot).wait()
                bias = bias_tile((start,), docs, j * bk, bk, tq)
                bias = jnp.concatenate([bias] * heads, axis=1)
                for p in range(parts):
                    kb = kvb[slot, :, :, :, 2 * HS * p : 2 * HS * (p + 1)].reshape(bk, 2 * HS)
                    vb = kvb[slot, :, :, :, width_k + 2 * HS * p : width_k + 2 * HS * (p + 1)]
                    vt = jnp.transpose(vb.reshape(bk, 2 * HS))
                    rows = qt_ref[2 * heads * HS * p : 2 * heads * HS * (p + 1), :] * bf16(1.0 / 8.0)
                    for g in range(2):
                        at = 2 * p + g
                        s = jnp.dot(kb, padded(rows, heads, g), preferred_element_type=f32) + bias
                        m = m_ref[at]
                        new = jnp.maximum(m, jnp.max(s, axis=0, keepdims=True))
                        prob = jnp.exp(s - new)
                        decay = jnp.exp(m - new)
                        m_ref[at] = new
                        l_ref[at] = l_ref[at] * decay + jnp.sum(prob, axis=0, keepdims=True)
                        acc_ref[at] = acc_ref[at] * decay + jnp.dot(
                            vt[HS * g : HS * (g + 1)], prob.astype(bf16), preferred_element_type=f32
                        )
                return carry

            lax.fori_loop(0, count, block, 0)

    for turn in range(1, chunks + stages):
        for k in range(chunks):
            stage = turn - k
            if (k, stage) != (0, 0) and 0 <= stage <= stages:
                tick(k, stage)
        if turn == 4:
            for copy in o_y + gu_y:
                copy.wait()
            o_f[0].start()
            o_f[1].start()
            gu_x.start()
            gu_z[0].start()
        if turn == 3:
            cot_y.start()
        if turn == 6:
            o_f[0].wait()
            o_f[2].start()
            gu_x.wait()
            gu_z[1].start()
        if turn == 5:
            cot_y.wait()
            loads[6].wait()
            cot_c.start()
        if turn >= stages:
            attend(turn - stages)
    for p in range(parts):
        outs = []
        for g in range(2):
            at = 2 * p + g
            out = acc_ref[at] / l_ref[at]
            outs.append(out)
            ot_ref[at] = out
            lse_ref[at] = m_ref[at] + jnp.log(l_ref[at])
        low_ref[:, 2 * heads * HS * p : 2 * heads * HS * (p + 1)] = head_lanes(outs, heads, tq).astype(bf16)

    for k in range(1, chunks):
        @pl.when(z + k < chunks)
        def _():
            top_copy(k).wait_send()
    for copy in loads[3:6]:
        copy.wait()
    backs = [back]
    for waits, src, dst in (
        (o_f[1:], obuf, wo_out), ([cot_c], cbuf, cots_out), (gu_z, gubuf, gu_out)
    ):
        for copy in waits:
            copy.wait()
        backs.append(pltpu.make_async_copy(src, dst, out_sem.at[1 + len(backs)]))
        backs[-1].start()
    for copy in backs:
        copy.wait()


def forward(nctx, nf, docs, tokens, norm_attn, norm_mlp, cos_t, sin_t, wq, wk, wv, wo, wg, wu, cot):
    tq, width = tokens.shape
    width_q, width_k = wq.shape[1], wk.shape[1]
    parts = width_k // (2 * HS)
    heads = width_q // HS // (2 * parts)
    hidden_units = wg.shape[1]
    quarter = hidden_units // (2 * nf)
    dims = line_dims(nctx // 2)
    lead = tuple(reversed(dims))
    most = max(dims + [2])
    chunks = dims[-1]
    stages = len(dims) + 1
    bf16, f32 = jnp.bfloat16, jnp.float32
    vmem = pl.BlockSpec(memory_space=pltpu.VMEM)
    smem = pl.BlockSpec(memory_space=pltpu.SMEM)
    hbm = pl.BlockSpec(memory_space=pl.ANY)
    dma = pltpu.SemaphoreType.DMA
    return pl.pallas_call(
        functools.partial(forward_kernel, (nctx, nf, parts, heads, tq)),
        out_shape=[
            jax.ShapeDtypeStruct((width_q, tq), bf16),
            jax.ShapeDtypeStruct(lead + (2, nf, tq, 2 * width_k), bf16),
            jax.ShapeDtypeStruct((tq, width_q), bf16),
            jax.ShapeDtypeStruct((2 * parts, HS, heads * tq), f32),
            jax.ShapeDtypeStruct((2 * parts, 1, heads * tq), f32),
            jax.ShapeDtypeStruct((width, width_q + 2 * width_k), bf16),
            jax.ShapeDtypeStruct((nf * wo.shape[0], wo.shape[1]), bf16),
            jax.ShapeDtypeStruct((width, 2 * quarter), bf16),
            jax.ShapeDtypeStruct((2 * nf, tq, width), bf16),
            jax.ShapeDtypeStruct((tq, width), bf16),
            jax.ShapeDtypeStruct((tq, 1), f32),
            jax.ShapeDtypeStruct((2, width), f32),
        ],
        in_specs=[smem, vmem, vmem, vmem, vmem, vmem] + [hbm] * 7,
        out_specs=[vmem, hbm, vmem, vmem, vmem, hbm, hbm, hbm, hbm, vmem, vmem, vmem],
        scratch_shapes=[
            pltpu.VMEM((width, width_q + 2 * width_k), bf16),
            pltpu.VMEM((nf * wo.shape[0], wo.shape[1]), bf16),
            pltpu.VMEM((width, 2 * quarter), bf16),
            pltpu.VMEM((2 * nf, tq, width), bf16),
            pltpu.VMEM((8, norm_attn.shape[1]), f32),
            pltpu.VMEM((8, norm_attn.shape[1]), f32),
            pltpu.VMEM((tq, 2 * width_k), bf16),
            pltpu.VMEM((2, 2, nf, tq, 2 * width_k), bf16),
            pltpu.VMEM((2 * parts, 1, heads * tq), f32),
            pltpu.VMEM((2 * parts, 1, heads * tq), f32),
            pltpu.VMEM((2 * parts, HS, heads * tq), f32),
            dma((7,)),
            dma((21,)),
            dma((21,)),
            dma((chunks - 1,)),
            dma((chunks - 1,)),
            dma((chunks, 2, stages, most - 1)),
            dma((chunks, 2, stages, most - 1)),
            dma((2,)),
            dma((5,)),
        ],
        compiler_params=pltpu.CompilerParams(
            collective_id=0, has_side_effects=True, vmem_limit_bytes=60 * 2**20
        ),
        name="forward",
    )(docs, tokens, norm_attn, norm_mlp, cos_t, sin_t, wq, wk, wv, wo, wg, wu, cot)


def feed_forward_kernel(plan, tokens_ref, low_ref, attn_in_ref, gains_ref, wo_hbm, gu_hbm, down_hbm, cots_hbm,
                        result_ref, gres_ref, branch_ref, gattn_ref, gmlp_ref, gup_ref, dnp_ref, inputs_out,
                        wo, gu, down, cots, xs, grads, mixed, gm, sums, sent, core_in, side_in, side_out,
                        load_sem, x_send, x_recv, s_send, s_recv, top_send, top_recv,
                        ag_send, ag_recv, out_sem):
    nctx, nf = plan
    ax = Axes(nctx, nf)
    f, core, place = ax.f, ax.core, ax.place
    mesh_id = pl.DeviceIdType.MESH
    bf16, f32 = jnp.bfloat16, jnp.float32
    tq, width = tokens_ref.shape
    quarter = down.shape[0]
    side = ax.side_axis[3](1)[1]
    mate = ax.core_axis[3](1)[1]
    top = ax.nd - 1
    chunks = ax.dims[top]
    z = ax.lines[top][2]

    barrier = pltpu.get_barrier_semaphore()
    for where in ax.peers():
        pl.semaphore_signal(barrier, inc=1, device_id=where, device_id_type=mesh_id)
    loads = [
        pltpu.make_async_copy(src, dst, load_sem.at[i])
        for i, (src, dst) in enumerate((
            (wo_hbm, wo), (cots_hbm, cots),
            (down_hbm.at[pl.ds(pl.multiple_of(core * quarter, quarter), quarter)], down), (gu_hbm, gu),
        ))
    ]
    for copy in loads:
        copy.start()

    def remote(src, dst, sends, recvs, i, where):
        return pltpu.make_async_remote_copy(
            src_ref=src, dst_ref=dst, send_sem=sends.at[i], recv_sem=recvs.at[i],
            device_id=where, device_id_type=mesh_id,
        )

    hidden = tokens_ref[...].astype(f32)
    own_at = ax.place_index(place) + (core,)
    put = pltpu.make_async_copy(attn_in_ref, inputs_out.at[own_at], out_sem.at[0])

    def top_copy(k):
        return pltpu.make_async_remote_copy(
            src_ref=attn_in_ref, dst_ref=inputs_out.at[own_at],
            send_sem=top_send.at[k - 1], recv_sem=top_recv.at[k - 1],
            device_id=ax.at_line(top, lax.rem(z + k, chunks)), device_id_type=mesh_id,
        )

    order = ax.lines[:top] + [ax.core_axis]
    stages = len(order)

    def ag_copies(k, stage):
        index = [None] * (ax.nd + 1)
        index[0] = lax.rem(z + chunks - k, chunks)
        for i, axis in enumerate(order):
            index[axis[0]] = slice(None) if i < stage else axis[2]
        region = inputs_out.at[tuple(index)]
        axis = order[stage]
        return [
            pltpu.make_async_remote_copy(
                src_ref=region, dst_ref=region,
                send_sem=ag_send.at[k, stage, i - 1], recv_sem=ag_recv.at[k, stage, i - 1],
                device_id=axis[3](i)[1], device_id_type=mesh_id,
            )
            for i in range(1, axis[1])
        ]

    def tick(turn):
        for k in range(chunks):
            stage = turn - k
            if not 0 <= stage <= stages:
                continue
            if stage == 0:
                if k > 0:
                    top_copy(k).wait()
                else:
                    put.wait()
            else:
                for copy in ag_copies(k, stage - 1):
                    copy.wait()
            if stage < stages:
                for copy in ag_copies(k, stage):
                    copy.start()

    pl.semaphore_wait(barrier, ax.peer_count)
    put.start()
    top_copy(1).start()
    tick(0)

    loads[0].wait()
    resid = hidden + jnp.dot(low_ref[...], wo[...], preferred_element_type=f32)
    inv = lax.rsqrt(jnp.mean(resid * resid, axis=1, keepdims=True) + EPS)
    normed = resid * inv
    gain = gains_ref[1:2, :]
    xs[0] = (normed * gain).astype(bf16)
    x_side = remote(xs.at[0], xs.at[1], x_send, x_recv, 0, side)
    x_core = remote(xs.at[0], xs.at[2], x_send, x_recv, 1, mate)
    x_far = remote(xs.at[1], xs.at[3], x_send, x_recv, 2, mate)
    x_side.start()
    x_core.start()

    def rows(slot):
        return slice(slot * tq, (slot + 1) * tq)

    for copy in loads[1:3]:
        copy.wait()
    gm[...] = lax.dot_general(
        cots[...].reshape(4 * tq, width), down[...], (((1,), (1,)), ((), ())), preferred_element_type=f32
    )
    loads[3].wait()
    top_copy(2).start()
    step = 256

    def both(ref, a, b, span=slice(None)):
        return jnp.concatenate([ref[a, :, span], ref[b, :, span]], axis=0)

    def compute(a, b):
        x = both(xs, a, b)
        for n in range(quarter // step):
            span = slice(n * step, (n + 1) * step)
            up_span = slice(quarter + n * step, quarter + (n + 1) * step)
            gate = jnp.dot(x, gu[:, span], preferred_element_type=f32)
            up = jnp.dot(x, gu[:, up_span], preferred_element_type=f32)
            sig = jax.nn.sigmoid(gate)
            act = gate * sig
            grad = jnp.concatenate([gm[rows(a), span], gm[rows(b), span]], axis=0)
            mix = (act * up).astype(bf16)
            grad_gate = (grad * up * sig * (1.0 + gate * (1.0 - sig))).astype(bf16)
            grad_up = (grad * act).astype(bf16)
            for i, slot in enumerate((a, b)):
                mixed[slot, :, span] = mix[rows(i)]
                grads[slot, :, span] = grad_gate[rows(i)]
                grads[slot, :, up_span] = grad_up[rows(i)]
        total = lax.dot_general(
            both(grads, a, b), gu[...], (((1,), (1,)), ((), ())), preferred_element_type=f32
        )
        for i, slot in enumerate((a, b)):
            sums[0, slot] = total[rows(i)]

    def outputs(a, b):
        total = jnp.dot(both(mixed, a, b), down[...], preferred_element_type=f32)
        for i, slot in enumerate((a, b)):
            sums[1, slot] = total[rows(i)]

    def to_core(kind, slot):
        i = 2 * kind + slot - 2
        return remote(sent.at[i], core_in.at[i], s_send, s_recv, i, mate)

    def to_side(kind):
        return remote(side_out.at[kind], side_in.at[kind], s_send, s_recv, 4 + kind, side)

    def give_core(kind, slot):
        sent[2 * kind + slot - 2] = sums[kind, slot].astype(bf16)
        to_core(kind, slot).start()

    def give_side(kind):
        to_core(kind, 3).wait()
        side_out[kind] = (sums[kind, 1] + core_in[2 * kind + 1].astype(f32)).astype(bf16)
        to_side(kind).start()

    x_core.wait()
    compute(0, 2)
    give_core(0, 2)
    top_copy(3).start()
    x_side.wait()
    x_far.start()
    tick(1)
    outputs(0, 2)
    give_core(1, 2)
    x_far.wait()
    compute(1, 3)
    give_core(0, 3)
    tick(2)
    outputs(1, 3)
    give_side(0)
    give_core(1, 3)
    flat_x = xs[...].reshape(4 * tq, width)
    pieces = nctx // 2
    unit = quarter // pieces
    tall = max(unit, 256)
    for kind in range(2):
        for n in range(quarter // tall):
            span = slice(kind * quarter + n * tall, kind * quarter + (n + 1) * tall)
            cols = jnp.transpose(jnp.concatenate([grads[s, :, span] for s in range(4)], axis=0))
            part = jnp.dot(cols, flat_x, preferred_element_type=f32).astype(bf16)
            first = n * tall
            while first < (n + 1) * tall:
                piece, at = first // unit, first % unit
                end = min((piece + 1) * unit, (n + 1) * tall)
                gup_ref[static_index(bit_dims(nctx // 2), piece) + (kind, slice(at, at + end - first))] = part[
                    first - n * tall : end - n * tall
                ]
                first = end
        if kind == 0:
            give_side(1)
            tick(3)
    unit = width // pieces
    flat_mixed = mixed[...].reshape(4 * tq, quarter)
    for n in range(width // 384):
        cols = jnp.transpose(jnp.concatenate([cots[s, :, 384 * n : 384 * (n + 1)] for s in range(4)], axis=0))
        part = jnp.dot(cols, flat_mixed, preferred_element_type=f32).astype(bf16)
        first = n * 384
        while first < (n + 1) * 384:
            piece, at = first // unit, first % unit
            end = min((piece + 1) * unit, (n + 1) * 384)
            rows_of = part[first - n * 384 : end - n * 384]
            for c in range(quarter // 128):
                dnp_ref[
                    static_index(bit_dims(nctx // 2), piece)
                    + (slice(c * unit + at, c * unit + at + end - first),)
                ] = rows_of[:, 128 * c : 128 * (c + 1)]
            first = end

    tick(4)
    to_core(0, 2).wait()
    to_side(0).wait()
    grad = sums[0, 0] + core_in[0].astype(f32) + side_in[0].astype(f32)
    product = grad * normed
    gmlp_ref[...] = jnp.sum(product, axis=0, keepdims=True)
    scaled = grad * gain
    mean = jnp.mean(scaled * normed, axis=1, keepdims=True)
    gres = cots[0].astype(f32) + inv * (scaled - normed * mean)
    gres_ref[...] = gres
    branch = gres.astype(bf16)
    branch_ref[...] = branch
    gattn_ref[...] = lax.dot_general(
        branch, wo[...], (((1,), (1,)), ((), ())), preferred_element_type=f32
    ).astype(bf16)
    to_core(1, 2).wait()
    to_side(1).wait()
    result_ref[...] = (resid + sums[1, 0] + core_in[2].astype(f32) + side_in[1].astype(f32)).astype(bf16)
    for turn in range(5, chunks + stages):
        tick(turn)


def static_index(dims, piece):
    return tuple(piece // math.prod(dims[:i]) % dims[i] for i in reversed(range(len(dims))))


def feed_forward(nctx, nf, tokens, low, attn_in, gains, wo, gu, down, cots):
    tq, width = tokens.shape
    quarter = gu.shape[1] // 2
    dims = line_dims(nctx // 2)
    bits = bit_dims(nctx // 2)
    lead = tuple(reversed(dims))
    plane = nctx // 2
    chunks, stages, most = dims[-1], len(dims), max(dims + [2])
    bf16, f32 = jnp.bfloat16, jnp.float32
    vmem = pl.BlockSpec(memory_space=pltpu.VMEM)
    hbm = pl.BlockSpec(memory_space=pl.ANY)
    dma = pltpu.SemaphoreType.DMA
    return pl.pallas_call(
        functools.partial(feed_forward_kernel, (nctx, nf)),
        out_shape=[
            jax.ShapeDtypeStruct((tq, width), bf16),
            jax.ShapeDtypeStruct((tq, width), f32),
            jax.ShapeDtypeStruct((tq, width), bf16),
            jax.ShapeDtypeStruct((tq, width), bf16),
            jax.ShapeDtypeStruct((1, width), f32),
            jax.ShapeDtypeStruct(tuple(bits) + (2, quarter // plane, width), bf16),
            jax.ShapeDtypeStruct(tuple(bits) + (width // plane * (quarter // 128), 128), bf16),
            jax.ShapeDtypeStruct(lead + (2, tq, width), bf16),
        ],
        in_specs=[vmem] * 4 + [hbm] * 4,
        out_specs=[vmem] * 7 + [hbm],
        scratch_shapes=[
            pltpu.VMEM(wo.shape, bf16),
            pltpu.VMEM(gu.shape, bf16),
            pltpu.VMEM((quarter, width), bf16),
            pltpu.VMEM((4, tq, width), bf16),
            pltpu.VMEM((4, tq, width), bf16),
            pltpu.VMEM((4, tq, 2 * quarter), bf16),
            pltpu.VMEM((4, tq, quarter), bf16),
            pltpu.VMEM((4 * tq, quarter), f32),
            pltpu.VMEM((2, 4, tq, width), f32),
            pltpu.VMEM((4, tq, width), bf16),
            pltpu.VMEM((4, tq, width), bf16),
            pltpu.VMEM((2, tq, width), bf16),
            pltpu.VMEM((2, tq, width), bf16),
            dma((4,)),
            dma((4,)),
            dma((4,)),
            dma((6,)),
            dma((6,)),
            dma((chunks - 1,)),
            dma((chunks - 1,)),
            dma((chunks, stages, most - 1)),
            dma((chunks, stages, most - 1)),
            dma((1,)),
        ],
        compiler_params=pltpu.CompilerParams(
            collective_id=2, has_side_effects=True, vmem_limit_bytes=60 * 2**20
        ),
        name="feed_forward",
    )(tokens, low, attn_in, gains, wo, gu, down, cots)


def finish_kernel(*refs):
    count = len(refs) // 2
    for src, dst in zip(refs[:count], refs[count:]):
        dst[...] = src[...]


def finish(*values):
    def whole(x):
        return pl.BlockSpec(x.shape, lambda i: (0,) * len(x.shape))

    return pl.pallas_call(
        finish_kernel,
        grid=(1,),
        out_shape=[jax.ShapeDtypeStruct(x.shape, x.dtype) for x in values],
        in_specs=[whole(x) for x in values],
        out_specs=[whole(x) for x in values],
        compiler_params=pltpu.CompilerParams(vmem_limit_bytes=60 * 2**20),
        name="finish",
    )(*values)


def per_device(
    nctx,
    nf,
    tokens,
    query_weight,
    key_projection,
    value_projection,
    output_weight,
    gate_weight,
    up_weight,
    down_weight,
    norm_attn,
    norm_mlp,
    doc_starts,
    cotangent,
):
    token_rows, width = tokens.shape
    n_tokens = token_rows * nctx * nf
    bf16, f32 = jnp.bfloat16, jnp.float32

    own_device = lax.axis_index(AXES)
    own_index = layout_rows(own_device, token_rows)
    own_begin = doc_begin(own_index, doc_starts)
    cosine_table, sine_table = rope_tables(own_index - own_begin)
    cosine_table, sine_table = cosine_table.T, sine_table.T
    (
        query_rot, key_values, attn_low, attn_exact, log_total, qkv_full, output_full, gate_up,
        cotangents, attention_input, inv_attn, gains,
    ) = forward(
        nctx, nf, doc_starts, tokens, norm_attn[None], norm_mlp[None], cosine_table, sine_table, query_weight, key_projection,
        value_projection, output_weight, gate_weight, up_weight, cotangent,
    )
    key_width = KEY_VALUE_HEADS * HEAD_SIZE
    key_values = key_values.reshape(n_tokens, 2 * key_width)
    result, grad_resid, grad_branch, grad_attn, gain_mlp_partial, gate_up_partial, down_partial, inputs_all = feed_forward(
        nctx, nf, tokens, attn_low, attention_input, gains, output_full, gate_up, down_weight,
        cotangents.reshape(2 * nf, token_rows, width),
    )

    tokens_grad, query_sum, key_sum, value_sum, gain_sums, gate_sum, up_sum, down_sum, output_sum = backward(
        nctx, nf, doc_starts, query_rot, grad_attn, attn_exact, log_total, key_values, qkv_full,
        cosine_table, sine_table, tokens, inv_attn, gains, grad_resid,
        gain_mlp_partial, attn_low, grad_branch, gate_up_partial, down_partial,
        inputs_all.reshape(nctx, token_rows, width),
    )

    gain_sums = gain_sums[: 2 * width // 128].reshape(2, width)
    result, tokens_grad, *sums = finish(
        result, tokens_grad, query_sum, key_sum, value_sum, output_sum, gate_sum, up_sum, down_sum
    )
    return (result, tokens_grad, *(weight.T for weight in sums), gain_sums[0], gain_sums[1])


def solution(mesh):
    return jax.shard_map(
        functools.partial(per_device, mesh.shape["ctx"], mesh.shape["fsdp"]),
        mesh=mesh,
        in_specs=(
            P(("ctx", "fsdp"), None),
            P("fsdp", None),
            P("fsdp", None),
            P("fsdp", None),
            P("fsdp", None),
            P("fsdp", None),
            P("fsdp", None),
            P("fsdp", None),
            P("fsdp"),
            P("fsdp"),
            P(),
            P(("ctx", "fsdp"), None),
        ),
        out_specs=(
            P(("ctx", "fsdp"), None),
            P(("ctx", "fsdp"), None),
            P("fsdp", "ctx"),
            P("fsdp", "ctx"),
            P("fsdp", "ctx"),
            P("fsdp", "ctx"),
            P("fsdp", "ctx"),
            P("fsdp", "ctx"),
            P("fsdp", "ctx"),
            P(),
            P(),
        ),
        check_vma=False,
    )
```

```python
import functools
import math

import jax
import jax.numpy as jnp
from jax import lax
from jax.experimental import pallas as pl
from jax.experimental.pallas import tpu as pltpu
from jax.sharding import PartitionSpec as P

QUERY_HEADS = 18
KEY_VALUE_HEADS = 6
HEAD_SIZE = 64
HS = HEAD_SIZE

EPS = 1e-05
THETA = 10000.0
NEG = -1e30
AXES = ("ctx", "fsdp")


def rope_tables(positions):
    half_dim = HEAD_SIZE // 2
    frequency = jnp.exp(-math.log(THETA) * jnp.arange(half_dim, dtype=jnp.float32) / half_dim)
    angles = positions.astype(jnp.float32)[:, None] * frequency[None, :]
    return (jnp.cos(angles), jnp.sin(angles))


def apply_rotary(values, cosine_table, sine_table):
    half_dim = values.shape[-1] // 2
    first_half = values[..., :half_dim]
    second_half = values[..., half_dim:]
    cos_rows = cosine_table[:, None, :]
    sin_rows = sine_table[:, None, :]
    return jnp.concatenate(
        [
            first_half * cos_rows - second_half * sin_rows,
            second_half * cos_rows + first_half * sin_rows,
        ],
        axis=-1,
    )


def unrotate(values, cosine_table, sine_table):
    half_dim = values.shape[-1] // 2
    first_half = values[..., :half_dim]
    second_half = values[..., half_dim:]
    cos_rows = cosine_table[:, None, :]
    sin_rows = sine_table[:, None, :]
    return jnp.concatenate(
        [
            first_half * cos_rows + second_half * sin_rows,
            second_half * cos_rows - first_half * sin_rows,
        ],
        axis=-1,
    )


def doc_begin(indices, doc_starts):
    marked = jnp.where(indices[:, None] >= doc_starts[None, :], doc_starts[None, :], 0)
    return jnp.max(marked, axis=1)


def layout_rows(device, row_count):
    return device * row_count + jnp.arange(row_count, dtype=jnp.int32)


def heads_rows(natural):
    return jnp.transpose(natural.astype(jnp.float32))
def padded(rows, heads, g):
    top = jnp.concatenate([rows[HS*(heads*g+j):HS*(heads*g+j+1)] for j in range(heads)], axis=1)
    z = jnp.zeros_like(top)
    return jnp.concatenate([top, z] if g == 0 else [z, top], axis=0)
def head_lanes(per_group, heads, tq):
    return jnp.transpose(jnp.concatenate([per_group[g][:, tq*j:tq*(j+1)] for g in range(2) for j in range(heads)], axis=0))
def bias_tile(info, docs, first, bk, tq):
    query = info[0] + lax.broadcasted_iota(jnp.int32, (1, tq), 1)
    begin = jnp.zeros((1, tq), jnp.int32)
    for i in range(docs.shape[0]):
        begin = jnp.maximum(begin, jnp.where(query >= docs[i], docs[i], 0))
    key = first + lax.broadcasted_iota(jnp.int32, (bk, 1), 0)
    return jnp.where((key <= query) & (key >= begin), 0.0, NEG)


def line_dims(count):
    fours = 0
    while count % 4 == 0:
        count //= 4
        fours += 1
    return ([count] if count > 1 else []) + [4] * fours


def rotate_back(rows, cos_rows, sin_rows):
    half_dim = HS // 2
    first, second = rows[:half_dim], rows[half_dim:]
    return jnp.concatenate(
        [first * cos_rows + second * sin_rows, second * cos_rows - first * sin_rows], axis=0
    )


def w_order(lines):
    return [lines[-2]] + lines[1:-2] + [lines[0], lines[-1]]


def bit_dims(count):
    return [2] * (count.bit_length() - 1)


def round_up(value, unit):
    return -(-value // unit) * unit


def backward_kernel(plan, docs, q_ref, do_ref, ot_ref, lse_ref, kv_hbm, w_ref, cos_ref, sin_ref,
                    normed_ref, inv_ref, gain_ref, gres_ref, gmlp_ref, low_ref, branch_ref, gup_hbm, dnp_hbm, inputs_hbm,
                    tokens_ref, query_ref, key_ref, value_ref, gains_out, gate_ref, up_ref, down_ref, out_ref,
                    kvbuf, dkv, acc_ref, gqt_ref, ga_ref, qblk, kvblk, small,
                    load_sem, send_sem, recv_sem, col_send, col_recv, own_sem, credit,
                    wg, wd, wo, brs, lows, halves, fin, fin_in, dsend, din,
                    colq_ref, colkv_ref, gains_ref, cols_acc, half_send, half_in, gain_send, gain_in, in_sem,
                    g_send, g_recv, w_load, w_send, w_recv, top_send, top_recv, fin_send, fin_recv, *recvs):
    nctx, nf, parts, heads, tq, slots = plan
    plane = nctx // 2
    n = nctx * nf
    dims = bit_dims(plane)
    nd = len(dims)
    bk = 2 * nf * tq
    me_c, me_f = lax.axis_index("ctx"), lax.axis_index("fsdp")
    me = me_c * nf + me_f
    core, place = lax.rem(me_c, 2), me_c // 2
    mesh_id = pl.DeviceIdType.MESH
    half_dim = HS // 2

    def target(k):
        other = lax.rem(me + k, n)
        return other, {"ctx": other // nf, "fsdp": lax.rem(other, nf)}

    barrier = pltpu.get_barrier_semaphore()

    def greet(k, carry):
        pl.semaphore_signal(barrier, inc=1, device_id=target(k)[1], device_id_type=mesh_id)
        return carry

    lax.fori_loop(1, n, greet, 0)

    def loads(p):
        s = p % slots
        return [
            pltpu.make_async_copy(
                kv_hbm.at[:, pl.ds((kind * parts + p) * 2 * HS, 2 * HS)],
                kvbuf.at[s, kind], load_sem.at[s, kind],
            )
            for kind in range(2)
        ]

    resident = slots == parts

    def block_loads(p, j):
        slot = lax.rem(j, 2)
        return [
            pltpu.make_async_copy(
                kv_hbm.at[pl.ds(pl.multiple_of(j * bk, bk), bk), pl.ds((kind * parts + p) * 2 * HS, 2 * HS)],
                kvbuf.at[slot, kind], load_sem.at[slot, kind],
            )
            for kind in range(2)
        ]

    if resident:
        for p in range(parts):
            for copy in loads(p):
                copy.start()

    def dim_axis(i):
        stride = math.prod(dims[:i])
        size = dims[i]
        own = lax.rem(place // stride, size)

        def peer(k):
            there = lax.rem(own + k, size)
            return there, {"ctx": (place + (there - own) * stride) * 2 + core, "fsdp": me_f}

        return (nd - 1 - i, size, own, peer)

    core_axis = (nd, 2, core, lambda k: (1 - core, {"ctx": place * 2 + 1 - core, "fsdp": me_f}))
    side_axis = (nd + 1, 2, me_f, lambda k: (1 - me_f, {"ctx": me_c, "fsdp": 1 - me_f}))
    lines = [dim_axis(i) for i in range(nd)]
    orders = [[core_axis, side_axis] + lines, [core_axis, side_axis] + w_order(lines)]
    stages = nd + 2
    wrecvs = recvs[2 * stages :]
    side_at, mate_at = side_axis[3](1)[1], core_axis[3](1)[1]

    low_bits = nd - 2
    arrays = ((wg, gup_hbm, (0,)), (wd, dnp_hbm, ()), (wo, None, ()), (wg, gup_hbm, (1,)))
    w_lines = [lines, w_order(lines), w_order(lines), lines]

    def chunk_at(a, k):
        near, far_line = w_lines[a][nd - 2], w_lines[a][nd - 1]
        far_bit = far_line[2] if k % 2 else 1 - far_line[2]
        near_bit = near[2] if k // 2 else 1 - near[2]
        return far_bit, near_bit

    def w_region(a, k, stage, at):
        index = [slice(None)] * nd
        index[w_lines[a][nd - 1][0]], index[w_lines[a][nd - 2][0]] = chunk_at(a, k)
        for axis in w_lines[a][:stage]:
            index[axis[0]] = axis[2]
        if stage < low_bits:
            index[w_lines[a][stage][0]] = at
        return tuple(index)

    def held(a, index):
        first = w_lines[a][0][0]
        return index if a == 2 else index[:first] + index[first + 1 :] + arrays[a][2]

    def w_copy(a, k, stage):
        buf, far, sub = arrays[a]
        there, where = w_lines[a][stage][3](1)
        index = w_region(a, k, stage, there)
        return pltpu.make_async_remote_copy(
            src_ref=far.at[index + sub] if stage == 0 and a != 2 else buf.at[held(a, index)],
            dst_ref=wrecvs[a * (low_bits + 2) + stage].at[chunk_at(a, k)],
            send_sem=w_send.at[a, k, stage], recv_sem=w_recv.at[a, k, stage],
            device_id=where, device_id_type=mesh_id,
        )

    def near_copy(a, i):
        return pltpu.make_async_remote_copy(
            src_ref=arrays[a][0].at[held(a, w_region(a, i, low_bits, 0))], dst_ref=wrecvs[a * (low_bits + 2) + low_bits].at[i],
            send_sem=top_send.at[a, i], recv_sem=top_recv.at[a, i],
            device_id=w_lines[a][nd - 2][3](1)[1], device_id_type=mesh_id,
        )

    def far_copy(a):
        return pltpu.make_async_remote_copy(
            src_ref=arrays[a][0].at[held(a, w_region(a, 2, low_bits, 0))], dst_ref=wrecvs[a * (low_bits + 2) + low_bits + 1].at[0],
            send_sem=top_send.at[a, 2], recv_sem=top_recv.at[a, 2],
            device_id=w_lines[a][nd - 1][3](1)[1], device_id_type=mesh_id,
        )

    def w_start(which, k):
        for a in which:
            w_copy(a, k, 0).start()

    def w_finish(which, k):
        for a in which:
            buf = arrays[a][0]
            for stage in range(low_bits):
                w_copy(a, k, stage).wait()
                where = held(a, w_region(a, k, stage, w_lines[a][stage][2]))
                got = wrecvs[a * (low_bits + 2) + stage]
                buf[where] = (
                    buf[where].astype(jnp.float32) + got[chunk_at(a, k)].astype(jnp.float32)
                ).astype(buf.dtype)
                if stage + 1 < low_bits:
                    w_copy(a, k, stage + 1).start()
            if k < 2:
                near_copy(a, k).start()
            elif k == 2:
                near_copy(a, 0).wait()
                where = held(a, w_region(a, 2, low_bits, 0))
                buf[where] = (
                    buf[where].astype(jnp.float32)
                    + wrecvs[a * (low_bits + 2) + low_bits][0].astype(jnp.float32)
                ).astype(buf.dtype)
                far_copy(a).start()

    def w_total(a):
        near_copy(a, 1).wait()
        far_copy(a).wait()
        total = arrays[a][0][held(a, w_region(a, 3, low_bits, 0))].astype(jnp.float32)
        total = total + wrecvs[a * (low_bits + 2) + low_bits][1].astype(jnp.float32)
        return total + wrecvs[a * (low_bits + 2) + low_bits + 1][0].astype(jnp.float32)

    w_loads = [
        pltpu.make_async_copy(far.at[(slice(None),) * w_lines[i][0][0] + (w_lines[i][0][2],)], buf, w_load.at[i])
        for i, (buf, far, _) in enumerate(arrays[:2])
    ]
    for copy in w_loads:
        copy.start()
    half = low_ref.shape[1] // nf
    low_all = low_ref[...]
    halves[0] = low_all[:, :half]
    halves[1] = low_all[:, half:]
    lows[0] = halves[me_f]
    brs[0] = branch_ref[...]

    def g_copy(i, src, dst, where):
        return pltpu.make_async_remote_copy(
            src_ref=src, dst_ref=dst, send_sem=g_send.at[i], recv_sem=g_recv.at[i],
            device_id=where, device_id_type=mesh_id,
        )

    low_side = g_copy(0, halves.at[1 - me_f], lows.at[1], side_at)
    br_side = g_copy(1, brs.at[0], brs.at[1], side_at)
    low_core = g_copy(2, lows.at[pl.ds(0, 2)], lows.at[pl.ds(2, 2)], mate_at)
    br_core = g_copy(3, brs.at[pl.ds(0, 2)], brs.at[pl.ds(2, 2)], mate_at)

    def output_partial():
        low_core.wait()
        br_core.wait()
        rows = jnp.transpose(brs[...].reshape(4 * tq, brs.shape[2]))
        unit = brs.shape[2] // nctx
        wo[...] = jnp.zeros_like(wo)
        low_rows = lows[...].reshape(4 * tq, half)
        batch = plane // 4
        for r in range(plane):
            first = 2 * unit * (r % batch)
            if first == 0:
                chunk = 2 * unit * batch
                part = jnp.dot(
                    rows[2 * unit * r : 2 * unit * r + chunk], low_rows, preferred_element_type=jnp.float32
                )
            piece = jnp.where(core == 0, part[first : first + unit], part[first + unit : first + 2 * unit])
            wo[static_index(dims, r) + (slice(0, unit), slice(0, half))] = piece.astype(wo.dtype)

    pl.semaphore_wait(barrier, n - 1)
    low_side.start()
    br_side.start()
    for k in range(4):
        w_start((0, 3, 1) if k < 2 else (1,), k)

    def region(kind, stage, at):
        index = [slice(None)] * (nd + 2)
        for axis in orders[kind][:stage]:
            index[axis[0]] = axis[2]
        index[orders[kind][stage][0]] = at
        return tuple(index)

    def stage_copies(p, kind, stage):
        s = p % slots
        axis = orders[kind][stage]
        copies = []
        for k in range(1, axis[1]):
            there, where = axis[3](k)
            copies.append(
                pltpu.make_async_remote_copy(
                    src_ref=dkv.at[(s, kind) + region(kind, stage, there)],
                    dst_ref=recvs[kind * stages + stage].at[s, k - 1],
                    send_sem=send_sem.at[s, kind, stage, k - 1],
                    recv_sem=recv_sem.at[s, kind, stage, k - 1],
                    device_id=where, device_id_type=mesh_id,
                )
            )
        return copies

    def stage_start(p, stage):
        for kind in range(2):
            for copy in stage_copies(p, kind, stage):
                copy.start()

    finals = {}

    def stage_finish(p, stage):
        s = p % slots
        for kind in range(2):
            axis = orders[kind][stage]
            for copy in stage_copies(p, kind, stage):
                copy.wait()
            where = region(kind, stage, axis[2])
            got = recvs[kind * stages + stage]
            free = [i for i in range(nd + 2) if isinstance(where[i], slice)]

            def add(index, lead):
                total = dkv[(s, kind) + index].astype(jnp.float32)
                for k in range(axis[1] - 1):
                    total = total + got[(s, k) + lead].astype(jnp.float32)
                return total

            if not free:
                finals[p, kind] = add(where, ())
            else:
                size = dkv.shape[2 + free[0]]

                def one(i, carry):
                    index = list(where)
                    index[free[0]] = i
                    index = tuple(index)
                    dkv[(s, kind) + index] = add(index, (i,)).astype(dkv.dtype)
                    return carry

                lax.fori_loop(0, size, one, 0)

    def place_index(j):
        index = []
        for i in reversed(range(nd)):
            index.append(lax.rem(j // math.prod(dims[:i]), dims[i]))
        return tuple(index)

    start = me * tq
    last = (start + tq - 1) // bk + 1

    def compute(p):
        s = p % slots
        span = slice(2 * heads * HS * p, 2 * heads * HS * (p + 1))
        qt = q_ref[span, :].astype(jnp.float32) * (1.0 / 8.0)
        dt = heads_rows(do_ref[:, span])
        qg = [padded(qt, heads, g) for g in range(2)]
        dg = [padded(dt, heads, g) for g in range(2)]
        qrows = jnp.concatenate([jnp.transpose(x) for x in qg], axis=0).astype(jnp.bfloat16)
        drows = jnp.concatenate([jnp.transpose(x) for x in dg], axis=0).astype(jnp.bfloat16)
        delta = [
            jnp.sum(dg[g][HS * g : HS * (g + 1)] * ot_ref[2 * p + g], axis=0, keepdims=True)
            for g in range(2)
        ]
        lse = [lse_ref[2 * p + g] for g in range(2)]
        qg = [x.astype(jnp.bfloat16) for x in qg]
        dg = [x.astype(jnp.bfloat16) for x in dg]
        acc_ref[...] = jnp.zeros_like(acc_ref)
        for copy in loads(p) if resident else block_loads(p, 0):
            if not resident:
                copy.start()
            else:
                copy.wait()

        def zero(j, carry):
            at = place_index(j)
            for kind in range(2):
                dkv[(s, kind) + at] = jnp.zeros((2, nf, tq, 2 * HS), dkv.dtype)
            return carry

        def body(j, carry):
            first = pl.multiple_of(j * bk, bk)
            if resident:
                kb = kvbuf[s, 0, pl.ds(first, bk), :]
                vb = kvbuf[s, 1, pl.ds(first, bk), :]
            else:
                for copy in block_loads(p, j):
                    copy.wait()

                @pl.when(j + 1 < last)
                def _():
                    for copy in block_loads(p, j + 1):
                        copy.start()

                kb, vb = kvbuf[lax.rem(j, 2), 0], kvbuf[lax.rem(j, 2), 1]
            kt = jnp.transpose(kb)
            bias = bias_tile((start,), docs, first, bk, tq)
            bias = jnp.concatenate([bias] * heads, axis=1)
            ps = []
            dss = []
            for g in range(2):
                score = jnp.dot(kb, qg[g], preferred_element_type=jnp.float32)
                prob = jnp.exp(score + (bias - lse[g]))
                dp = jnp.dot(vb, dg[g], preferred_element_type=jnp.float32)
                ds = (prob * (dp - delta[g])).astype(jnp.bfloat16)
                ps.append(prob.astype(jnp.bfloat16))
                dss.append(ds)
                acc_ref[g] += jnp.dot(kt[HS * g : HS * (g + 1)], ds, preferred_element_type=jnp.float32)
            dv = jnp.dot(jnp.concatenate(ps, axis=1), drows, preferred_element_type=jnp.float32)
            dk = jnp.dot(jnp.concatenate(dss, axis=1), qrows, preferred_element_type=jnp.float32)
            at = place_index(j)
            dkv[(s, 0) + at] = dk.astype(dkv.dtype).reshape(2, nf, tq, 2 * HS)
            dkv[(s, 1) + at] = dv.astype(dkv.dtype).reshape(2, nf, tq, 2 * HS)
            return carry

        lax.fori_loop(last, plane, zero, 0)
        lax.fori_loop(0, last, body, 0)
        cos_rows = jnp.concatenate([cos_ref[...]] * heads, axis=1) * (1.0 / 8.0)
        sin_rows = jnp.concatenate([sin_ref[...]] * heads, axis=1) * (1.0 / 8.0)
        for g in range(2):
            back = rotate_back(acc_ref[g], cos_rows, sin_rows).astype(gqt_ref.dtype)
            for j in range(heads):
                h = (2 * p + g) * heads + j
                gqt_ref[HS * h : HS * (h + 1), :] = back[:, tq * j : tq * (j + 1)]

    peers = 2 + sum(size - 1 for size in dims)

    def all_peers():
        found = [core_axis[3](1)[1], side_axis[3](1)[1]]
        for axis in lines:
            found += [axis[3](k)[1] for k in range(1, axis[1])]
        return found

    progress = {}

    def advance(p):
        stage = progress[p]
        stage_finish(p, stage)
        progress[p] = stage + 1
        if stage + 1 < stages:
            stage_start(p, stage + 1)
        else:
            del progress[p]
            if p + slots < parts:
                for where in all_peers():
                    pl.semaphore_signal(credit, inc=1, device_id=where, device_id_type=mesh_id)

    for p in range(parts):
        if p >= slots:
            while p - slots in progress:
                advance(p - slots)
        compute(p)
        if p >= slots:
            pl.semaphore_wait(credit, peers)
        stage_start(p, 0)
        progress[p] = 0
        for older in [o for o in progress if o < p]:
            advance(older)
        if p == 0:
            low_side.wait()
            br_side.wait()
            low_core.start()
            br_core.start()
        if p == 1:
            for copy in w_loads:
                copy.wait()
            for k in range(2):
                w_finish((0, 3), k)
                w_start((0, 3), k + 2)
    for k in range(2):
        w_finish((1,), k)
    output_partial()

    def copies_to(k, which):
        other = lax.rem(me_c + k, nctx)
        where = {"ctx": other, "fsdp": me_f}
        block, out = ((qblk, colq_ref), (kvblk, colkv_ref), (small, gains_ref))[which]
        return pltpu.make_async_remote_copy(
            src_ref=block if which == 2 else block.at[other], dst_ref=out.at[me_c],
            send_sem=col_send.at[which, k], recv_sem=col_recv.at[which, k],
            device_id=where, device_id_type=mesh_id,
        )

    def share(which):
        def one(k, carry):
            copies_to(k, which).start()
            return carry

        block, out = ((qblk, colq_ref), (kvblk, colkv_ref), (small, gains_ref))[which]
        pltpu.make_async_copy(block if which == 2 else block.at[me_c], out.at[me_c], own_sem.at[which]).start()
        lax.fori_loop(1, nctx, one, 0)

    def share_wait(which):
        def one(k, carry):
            copies_to(k, which).wait()
            return carry

        block, out = ((qblk, colq_ref), (kvblk, colkv_ref), (small, gains_ref))[which]
        pltpu.make_async_copy(block if which == 2 else block.at[me_c], out.at[me_c], own_sem.at[which]).wait()
        lax.fori_loop(1, nctx, one, 0)

    width_q = 2 * parts * heads * HS
    width_k = 2 * parts * HS
    cq, ck = width_q // nctx, width_k // nctx
    qblk[...] = jnp.zeros_like(qblk)
    kvblk[...] = jnp.zeros_like(kvblk)
    for i in range(nctx):
        qblk[i, 0:cq, :] = gqt_ref[cq * i : cq * (i + 1), :]
    share(0)
    ga_ref[...] = jnp.dot(w_ref[:, :width_q], gqt_ref[...], preferred_element_type=jnp.float32)
    for k in range(4):
        w_start((2,), k)
    pq, pk = qblk.shape[1], kvblk.shape[1]

    def columns(col_ref, first, count):
        def fetch(i, slot):
            return pltpu.make_async_copy(
                inputs_hbm.at[i], brs.at[slot], in_sem.at[slot]
            )

        fetch(0, 0).start()
        cols_acc[first : first + count, :] = jnp.zeros((count, cols_acc.shape[1]), jnp.float32)

        def one(i, carry):
            slot = lax.rem(i, 2)

            @pl.when(i + 1 < nctx)
            def _():
                fetch(i + 1, 1 - slot).start()

            fetch(i, slot).wait()
            cols_acc[first : first + count, :] += jnp.dot(
                col_ref[i], brs[slot], preferred_element_type=jnp.float32
            )
            return carry

        lax.fori_loop(0, nctx, one, 0)

    per_side = plane // 2
    home = (2 * me_f + core) * per_side + place // 2
    slot = lax.rem(place, 2)

    def home_copy(kind, s):
        return pltpu.make_async_remote_copy(
            src_ref=fin.at[kind, s], dst_ref=fin_in.at[kind, slot],
            send_sem=fin_send.at[kind, s], recv_sem=fin_recv.at[kind, slot],
            device_id={"ctx": home, "fsdp": jnp.int32(s)}, device_id_type=mesh_id,
        )

    def self_copy(kind, s):
        return pltpu.make_async_copy(fin.at[kind, s], fin_in.at[kind, slot], fin_send.at[kind, s])

    def to_homes(kind, a):
        total = w_total(a)
        unit, lanes = fin.shape[2], fin.shape[3]
        blank = jnp.zeros((unit, lanes - half), fin.dtype)
        for s in range(2):
            fin[kind, s] = jnp.concatenate([total[:, half * s : half * (s + 1)].astype(fin.dtype), blank], axis=1)
            at_home = (home == me_c) & (me_f == s)

            @pl.when(jnp.logical_not(at_home))
            def _():
                home_copy(kind, s).start()

            @pl.when(at_home)
            def _():
                self_copy(kind, s).start()

    turn = 0
    while progress:
        for p in list(progress):
            advance(p)
        if turn == 0:
            for k in range(2, 4):
                w_finish((0, 3, 1), k)
        if turn == 1:
            for k in range(2):
                w_finish((2,), k)
        if turn == 2:
            for k in range(2, 4):
                w_finish((2,), k)
        turn += 1

    cos_rows, sin_rows = cos_ref[...], sin_ref[...]
    grads = []
    for kind in range(2):
        rows = []
        for p in range(parts):
            both = jnp.transpose(finals[p, kind])
            for g in range(2):
                one = both[HS * g : HS * (g + 1)]
                rows.append(rotate_back(one, cos_rows, sin_rows) if kind == 0 else one)
        grads.append(jnp.concatenate(rows, axis=0).astype(jnp.bfloat16))
    for i in range(nctx):
        kvblk[i, 0:ck, :] = grads[0][ck * i : ck * (i + 1)]
        kvblk[i, ck : 2 * ck, :] = grads[1][ck * i : ck * (i + 1)]
    share(1)
    grad_t = (
        ga_ref[...]
        + jnp.dot(w_ref[:, width_q : width_q + width_k], grads[0], preferred_element_type=jnp.float32)
        + jnp.dot(w_ref[:, width_q + width_k :], grads[1], preferred_element_type=jnp.float32)
    )
    grad = jnp.transpose(grad_t)
    normed = normed_ref[...].astype(jnp.float32) * inv_ref[...]
    product = grad * normed
    gain_sum = jnp.sum(product, axis=0, keepdims=True)
    lanes = 128
    tiles = gain_sum.shape[1] // lanes
    rows = [gain_sum[:, lanes * i : lanes * (i + 1)] for i in range(tiles)]
    rows += [gmlp_ref[:, lanes * i : lanes * (i + 1)] for i in range(tiles)]
    rows += [jnp.zeros((small.shape[0] - 2 * tiles, lanes), jnp.float32)]
    small[...] = jnp.concatenate(rows, axis=0)
    share(2)
    gain = gain_ref[0:1, :]
    scaled = grad * gain
    mean = jnp.mean(scaled * normed, axis=1, keepdims=True)
    tokens_ref[...] = gres_ref[...] + inv_ref[...] * (scaled - normed * mean)

    to_homes(0, 0)
    to_homes(1, 3)
    share_wait(0)
    columns(colq_ref, 0, pq)

    def give_half(first, count, i):
        rows = slice(first, first + count)
        theirs = jnp.where(me_f == 0, cols_acc[rows, half:], cols_acc[rows, :half]).astype(half_send.dtype)
        side_pad = jnp.zeros((count, half_send.shape[1] - half), half_send.dtype)
        half_send[rows, :] = jnp.concatenate([theirs, side_pad], axis=1)
        span = pl.ds(first, count)
        copy = g_copy(i, half_send.at[span], half_in.at[span], side_at)
        copy.start()
        return copy

    half_q = give_half(0, pq, 5)
    dsum = w_total(1)
    dsend[...] = dsum.astype(dsend.dtype)
    down_copy = g_copy(4, dsend, din, mate_at)
    down_copy.start()
    osum = w_total(2)
    out_ref[...] = osum[: out_ref.shape[0], :half]
    share_wait(1)
    columns(colkv_ref, pq, pk)
    half_kv = give_half(pq, pk, 7)
    share_wait(2)
    gain_total = gains_ref[0]
    for i in range(1, nctx):
        gain_total = gain_total + gains_ref[i]
    gain_send[...] = gain_total
    gain_copy = g_copy(6, gain_send, gain_in, side_at)
    gain_copy.start()
    half_q.wait()
    half_kv.wait()
    own_half = jnp.where(me_f == 0, cols_acc[:, :half], cols_acc[:, half:])
    rows = own_half + half_in[:, :half].astype(jnp.float32)
    query_ref[...] = rows[:cq]
    key_ref[...] = rows[pq : pq + ck]
    value_ref[...] = rows[pq + ck : pq + 2 * ck]
    gain_copy.wait()
    gains_out[...] = gain_send[...] + gain_in[...]
    down_copy.wait()
    cols = down_ref.shape[0]

    def unfold(folded):
        return jnp.concatenate(
            [folded[2 * cols * i : 2 * cols * (i + 1)] for i in range(folded.shape[0] // (2 * cols))], axis=1
        )

    dsum, got = unfold(dsum), unfold(din[...].astype(jnp.float32))
    own_cols = jnp.where(core == 0, dsum[:cols], dsum[cols:])
    far_cols = jnp.where(core == 0, got[:cols], got[cols:])
    down_ref[...] = jnp.where(
        core == 0,
        jnp.concatenate([own_cols, far_cols], axis=1),
        jnp.concatenate([far_cols, own_cols], axis=1),
    )
    owner = me_c // per_side
    for kind in range(2):
        for s in range(2):
            at_home = (home == me_c) & (me_f == s)

            @pl.when(jnp.logical_not(at_home))
            def _():
                home_copy(kind, s).wait_send()

            @pl.when(at_home)
            def _():
                self_copy(kind, s).wait()

        for h in range(2):
            holder = (2 * lax.rem(me_c, per_side) + h) * 2 + lax.rem(owner, 2)

            @pl.when(jnp.logical_not((holder == me_c) & (owner // 2 == me_f)))
            def _():
                pltpu.make_async_remote_copy(
                    src_ref=fin.at[0, 0], dst_ref=fin_in.at[kind, h],
                    send_sem=fin_send.at[0, 0], recv_sem=fin_recv.at[kind, h],
                    device_id={"ctx": home, "fsdp": me_f}, device_id_type=mesh_id,
                ).wait_recv()

    for kind, ref in ((0, gate_ref), (1, up_ref)):
        rows = jnp.concatenate([fin_in[kind, 0], fin_in[kind, 1]], axis=0).astype(jnp.float32)
        ref[...] = rows[:, :half]


def backward(nctx, nf, docs, q, do, ot, lse, kv, w, cos_t, sin_t, normed, inv, gain, gres, gmlp, low, branch, gup, dnp, inputs):
    width_q, tq = q.shape
    n_tokens, width_kv = kv.shape
    n = nctx * nf
    parts = width_kv // (4 * HS)
    heads = width_q // HS // (2 * parts)
    dims = bit_dims(nctx // 2)
    lead = tuple(reversed(dims))
    part_bytes = n_tokens * 2 * HS * 2
    slots = parts if parts * part_bytes * 5 <= 24 * 2**20 else 1
    nd = len(dims)
    bf16, f32 = jnp.bfloat16, jnp.float32
    axes = {"core": (nd, 2), "side": (nd + 1, nf)}
    line = [(nd - 1 - i, dims[i]) for i in range(nd)]
    orders = [
        [axes["core"], axes["side"]] + line,
        [axes["core"], axes["side"]] + w_order(line),
    ]
    recvs = []
    for order in orders:
        left = list(lead) + [2, nf]
        for position, size in order:
            left[position] = None
            recvs.append(
                pltpu.VMEM((slots, size - 1) + tuple(x for x in left if x) + (tq, 2 * HS), bf16)
            )
    model_width = low.shape[1]
    half = model_width // nf
    unit, deep = gup.shape[-2], model_width // (nctx // 2)
    quarter = dnp.shape[-2] // deep * 128
    plane = nctx // 2
    tails = [gup.shape[nd:], dnp.shape[nd:], (round_up(deep // 2, 16), round_up(half, 128))]
    for tail in (tails[0][1:], tails[1], tails[2], tails[0][1:]):
        for stage in range(nd - 2):
            recvs.append(pltpu.VMEM((2,) * (nd - 1 - stage) + tail, bf16))
        recvs += [pltpu.VMEM((2,) + tail, bf16), pltpu.VMEM((1,) + tail, bf16)]
    stages = nd + 2
    most = max(dims + [2])
    pq = round_up(width_q // nctx, 16)
    pk = round_up(2 * (2 * parts * HS) // nctx, 16)
    model = w.shape[0]
    sr = round_up(2 * model // 128, 8)
    vmem = pl.BlockSpec(memory_space=pltpu.VMEM)
    smem = pl.BlockSpec(memory_space=pltpu.SMEM)
    hbm = pl.BlockSpec(memory_space=pl.ANY)
    return pl.pallas_call(
        functools.partial(backward_kernel, (nctx, nf, parts, heads, tq, slots)),
        out_shape=[
            jax.ShapeDtypeStruct((tq, model), f32),
            jax.ShapeDtypeStruct((width_q // nctx, half), f32),
            jax.ShapeDtypeStruct((2 * parts * HS // nctx, half), f32),
            jax.ShapeDtypeStruct((2 * parts * HS // nctx, half), f32),
            jax.ShapeDtypeStruct((sr, 128), f32),
            jax.ShapeDtypeStruct((2 * unit, half), f32),
            jax.ShapeDtypeStruct((2 * unit, half), f32),
            jax.ShapeDtypeStruct((deep // 2, 2 * quarter), f32),
            jax.ShapeDtypeStruct((deep // 2, half), f32),
        ],
        in_specs=[smem, vmem, vmem, vmem, vmem, hbm] + [vmem] * 10 + [hbm] * 3,
        out_specs=[vmem] * 9,
        scratch_shapes=[
            pltpu.VMEM((slots, 2, n_tokens, 2 * HS) if slots == parts else (2, 2, 2 * nf * tq, 2 * HS), bf16),
            pltpu.VMEM((slots, 2) + lead + (2, nf, tq, 2 * HS), bf16),
            pltpu.VMEM((2, HS, heads * tq), f32),
            pltpu.VMEM((width_q, tq), bf16),
            pltpu.VMEM((model, tq), f32),
            pltpu.VMEM((nctx, pq, tq), bf16),
            pltpu.VMEM((nctx, pk, tq), bf16),
            pltpu.VMEM((sr, 128), f32),
            pltpu.SemaphoreType.DMA((max(slots, 2), 2)),
            pltpu.SemaphoreType.DMA((slots, 2, stages, most - 1)),
            pltpu.SemaphoreType.DMA((slots, 2, stages, most - 1)),
            pltpu.SemaphoreType.DMA((3, nctx)),
            pltpu.SemaphoreType.DMA((3, nctx)),
            pltpu.SemaphoreType.DMA((3,)),
            pltpu.SemaphoreType.REGULAR,
            pltpu.VMEM(lead[:-1] + tails[0], bf16),
            pltpu.VMEM(lead[:-1] + tails[1], bf16),
            pltpu.VMEM(lead + tails[2], bf16),
            pltpu.VMEM((4,) + branch.shape, bf16),
            pltpu.VMEM((4, tq, half), bf16),
            pltpu.VMEM((2, tq, half), bf16),
            pltpu.VMEM((2, 2, unit, round_up(half, 128)), bf16),
            pltpu.VMEM((2, 2, unit, round_up(half, 128)), bf16),
            pltpu.VMEM(tails[1], bf16),
            pltpu.VMEM(tails[1], bf16),
            pltpu.VMEM((nctx, pq, tq), bf16),
            pltpu.VMEM((nctx, pk, tq), bf16),
            pltpu.VMEM((nctx, sr, 128), f32),
            pltpu.VMEM((pq + pk, model), f32),
            pltpu.VMEM((pq + pk, round_up(half, 128)), bf16),
            pltpu.VMEM((pq + pk, round_up(half, 128)), bf16),
            pltpu.VMEM((sr, 128), f32),
            pltpu.VMEM((sr, 128), f32),
            pltpu.SemaphoreType.DMA((2,)),
            pltpu.SemaphoreType.DMA((8,)),
            pltpu.SemaphoreType.DMA((8,)),
            pltpu.SemaphoreType.DMA((2,)),
            pltpu.SemaphoreType.DMA((4, 4, max(nd - 2, 1))),
            pltpu.SemaphoreType.DMA((4, 4, max(nd - 2, 1))),
            pltpu.SemaphoreType.DMA((4, 3)),
            pltpu.SemaphoreType.DMA((4, 3)),
            pltpu.SemaphoreType.DMA((2, 2)),
            pltpu.SemaphoreType.DMA((2, 2)),
        ]
        + recvs,
        compiler_params=pltpu.CompilerParams(
            collective_id=1, has_side_effects=True, vmem_limit_bytes=63 * 2**20
        ),
        cost_estimate=pl.CostEstimate(flops=10**10, bytes_accessed=3 * 10**7, transcendentals=10**7),
        name="backward",
    )(docs, q, do, ot, lse, kv, w, cos_t, sin_t, normed, inv, gain, gres, gmlp, low, branch, gup, dnp, inputs)


def rotate(rows, cos_rows, sin_rows):
    half_dim = HS // 2
    first, second = rows[:half_dim], rows[half_dim:]
    return jnp.concatenate(
        [first * cos_rows - second * sin_rows, second * cos_rows + first * sin_rows], axis=0
    )


class Axes:
    def __init__(self, nctx, nf):
        self.ctx, self.f = lax.axis_index("ctx"), lax.axis_index("fsdp")
        self.core, self.place = lax.rem(self.ctx, 2), self.ctx // 2
        self.me = self.ctx * nf + self.f
        self.dims = line_dims(nctx // 2)
        self.nd = len(self.dims)
        ctx, f, core, place = self.ctx, self.f, self.core, self.place
        self.core_axis = (self.nd, 2, core, lambda k: (1 - core, {"ctx": place * 2 + 1 - core, "fsdp": f}))
        self.side_axis = (self.nd + 1, 2, f, lambda k: (1 - f, {"ctx": ctx, "fsdp": 1 - f}))
        self.lines = [self.line(i) for i in range(self.nd)]
        self.peer_count = 2 + sum(size - 1 for size in self.dims)

    def at_line(self, i, there):
        stride = math.prod(self.dims[:i])
        own = lax.rem(self.place // stride, self.dims[i])
        return {"ctx": (self.place + (there - own) * stride) * 2 + self.core, "fsdp": self.f}

    def line(self, i):
        size = self.dims[i]
        own = lax.rem(self.place // math.prod(self.dims[:i]), size)

        def peer(k):
            there = lax.rem(own + k, size)
            return there, self.at_line(i, there)

        return (self.nd - 1 - i, size, own, peer)

    def peers(self):
        found = [self.core_axis[3](1)[1], self.side_axis[3](1)[1]]
        for axis in self.lines:
            found += [axis[3](k)[1] for k in range(1, axis[1])]
        return found

    def place_index(self, j):
        return tuple(
            lax.rem(j // math.prod(self.dims[:i]), self.dims[i]) for i in reversed(range(self.nd))
        )


def forward_kernel(plan, docs, tokens_ref, norm_attn_ref, norm_mlp_ref, cos_ref, sin_ref, wq, wk, wv, wo, wg, wu, cot,
                   qt_ref, kv_out, low_ref, ot_ref, lse_ref, wqkv_out, wo_out, gu_out, cots_out,
                   attn_in_ref, inv_ref, gain_ref,
                   wbuf, obuf, gubuf, cbuf, gains_ref, gain_far, own_kv, kvb, m_ref, l_ref, acc_ref,
                   load_sem, w_send, w_recv, top_send, top_recv, ag_send, ag_recv, blk_sem, out_sem):
    nctx, nf, parts, heads, tq = plan
    ax = Axes(nctx, nf)
    f, core, place = ax.f, ax.core, ax.place
    mesh_id = pl.DeviceIdType.MESH
    bf16, f32 = jnp.bfloat16, jnp.float32
    width = tokens_ref.shape[1]
    half = width // nf
    width_q, width_k = 2 * parts * heads * HS, 2 * parts * HS
    rows4, rows2 = half // 4, half // 2
    quarter = gu_out.shape[1] // 2
    side = ax.side_axis[3](1)[1]
    mate = ax.core_axis[3](1)[1]
    low = ax.lines[0]
    bit = lax.rem(low[2], 2)
    across = ax.at_line(0, low[2] + 1 - 2 * bit)
    top = ax.nd - 1
    chunks = ax.dims[top]
    z = ax.lines[top][2]

    barrier = pltpu.get_barrier_semaphore()
    for where in ax.peers():
        pl.semaphore_signal(barrier, inc=1, device_id=where, device_id_type=mesh_id)

    def local(src, dst, i):
        return pltpu.make_async_copy(src, dst, load_sem.at[i])

    own_rows = pl.ds(pl.multiple_of(f * half, half), half)
    own_quarter = pl.ds(pl.multiple_of((2 * f + core) * quarter, quarter), quarter)
    loads = [
        local(wk, wbuf.at[own_rows, pl.ds(width_q, width_k)], 0),
        local(wv, wbuf.at[own_rows, pl.ds(width_q + width_k, width_k)], 1),
        local(wq, wbuf.at[own_rows, pl.ds(0, width_q)], 2),
        local(wo, obuf.at[own_rows], 3),
        local(wg.at[:, own_quarter], gubuf.at[own_rows, pl.ds(0, quarter)], 4),
        local(wu.at[:, own_quarter], gubuf.at[own_rows, pl.ds(quarter, quarter)], 5),
        local(cot, cbuf.at[0], 6),
    ]
    for copy in loads:
        copy.start()

    def remote(src, dst, i, where):
        return pltpu.make_async_remote_copy(
            src_ref=src, dst_ref=dst, send_sem=w_send.at[i], recv_sem=w_recv.at[i],
            device_id=where, device_id_type=mesh_id,
        )

    near = pl.multiple_of(core * rows2 + bit * rows4, 16)
    far_x = pl.multiple_of(core * rows2 + (1 - bit) * rows4, 16)
    there = (1 - f) * half

    def piece(base, offset):
        return pl.ds(pl.multiple_of(base + offset, 16), rows4)

    kv_cols, q_cols = pl.ds(width_q, 2 * width_k), pl.ds(0, width_q)
    mine = f * half
    gains_copy = remote(gains_ref, gain_far, 0, side)
    kv_y = [
        remote(wk.at[piece(0, near)], wbuf.at[piece(mine, near), pl.ds(width_q, width_k)], 1, side),
        remote(wv.at[piece(0, near)], wbuf.at[piece(mine, near), pl.ds(width_q + width_k, width_k)], 2, side),
    ]
    q_y = [remote(wq.at[piece(0, near)], wbuf.at[piece(mine, near), q_cols], 3, side)]
    o_y = [remote(wo.at[piece(0, near)], obuf.at[piece(mine, near)], 4, side)]

    def forwards(buf, cols, first):
        def part(offset):
            return buf.at[piece(there, offset), cols] if cols is not None else buf.at[piece(there, offset)]

        return [
            remote(part(near), part(near), first, across),
            remote(part(near), part(near), first + 1, mate),
            remote(part(far_x), part(far_x), first + 2, mate),
        ]

    kv_f = forwards(wbuf, kv_cols, 5)
    q_f = forwards(wbuf, q_cols, 8)
    o_f = forwards(obuf, None, 11)
    far_quarter = pl.ds(pl.multiple_of((2 * (1 - f) + core) * quarter, quarter), quarter)

    deep = lax.rem(z, 2)
    above = ax.at_line(top, z + 1 - 2 * deep)

    def gu_rows(base, which=bit):
        return pl.ds(pl.multiple_of(base + which * rows2 + deep * rows4, 16), rows4)

    gu_y = [
        remote(wg.at[gu_rows(0), far_quarter], gubuf.at[gu_rows(mine), pl.ds(0, quarter)], 14, side),
        remote(wu.at[gu_rows(0), far_quarter], gubuf.at[gu_rows(mine), pl.ds(quarter, quarter)], 15, side),
    ]
    gu_x = remote(gubuf.at[gu_rows(there)], gubuf.at[gu_rows(there)], 16, across)
    gu_z = [
        remote(gubuf.at[gu_rows(there, which)], gubuf.at[gu_rows(there, which)], 19 + i, above)
        for i, which in enumerate((bit, 1 - bit))
    ]
    cot_y = remote(cot, cbuf.at[1], 17, side)
    cot_c = remote(cbuf.at[pl.ds(0, 2)], cbuf.at[pl.ds(2, 2)], 18, mate)

    gains_ref[...] = jnp.zeros_like(gains_ref)
    gains_ref[0:1, :] = norm_attn_ref[...].astype(f32)
    gains_ref[1:2, :] = norm_mlp_ref[...].astype(f32)
    pl.semaphore_wait(barrier, ax.peer_count)
    gains_copy.start()
    for copy in kv_y + q_y:
        copy.start()

    hidden = tokens_ref[...].astype(f32)
    inv = lax.rsqrt(jnp.mean(hidden * hidden, axis=1, keepdims=True) + EPS)
    inv_ref[...] = inv
    gains_copy.wait()
    near_gain, far_gain = gains_ref[0:1, :], gain_far[0:1, :]
    gain = jnp.where(
        f == 0,
        jnp.concatenate([near_gain, far_gain], axis=1),
        jnp.concatenate([far_gain, near_gain], axis=1),
    )
    near_mlp, far_mlp = gains_ref[1:2, :], gain_far[1:2, :]
    gain_ref[0:1, :] = gain
    gain_ref[1:2, :] = jnp.where(
        f == 0,
        jnp.concatenate([near_mlp, far_mlp], axis=1),
        jnp.concatenate([far_mlp, near_mlp], axis=1),
    )
    attn_in = (hidden * inv * gain).astype(bf16)
    attn_in_ref[...] = attn_in

    for copy in kv_y:
        copy.wait()
    kv_f[0].start()
    kv_f[1].start()
    for copy in q_y:
        copy.wait()
    for copy in o_y + gu_y:
        copy.start()
    kv_f[0].wait()
    kv_f[2].start()
    q_f[0].start()
    q_f[1].start()
    for copy in loads[:3]:
        copy.wait()
    kv_f[1].wait()
    kv_f[2].wait()
    kv = jnp.dot(attn_in, wbuf[:, width_q:], preferred_element_type=f32)
    cos_rows, sin_rows = cos_ref[...], sin_ref[...]
    kt = jnp.transpose(kv[:, :width_k])
    k_rot = jnp.concatenate(
        [rotate(kt[HS * g : HS * (g + 1)], cos_rows, sin_rows) for g in range(2 * parts)], axis=0
    )
    own_kv[:, :width_k] = jnp.transpose(k_rot).astype(bf16)
    own_kv[:, width_k:] = kv[:, width_k:].astype(bf16)
    own_at = ax.place_index(place) + (core, f)
    put = pltpu.make_async_copy(own_kv, kv_out.at[own_at], out_sem.at[0])
    put.start()

    def top_copy(k):
        return pltpu.make_async_remote_copy(
            src_ref=own_kv, dst_ref=kv_out.at[own_at],
            send_sem=top_send.at[k - 1], recv_sem=top_recv.at[k - 1],
            device_id=ax.at_line(top, lax.rem(z + k, chunks)), device_id_type=mesh_id,
        )

    for k in range(1, chunks):
        @pl.when(z + k < chunks)
        def _():
            top_copy(k).start()

    lower = ax.lines[:top]
    orders = [lower + [ax.side_axis, ax.core_axis], [ax.side_axis] + lower + [ax.core_axis]]
    stages = len(orders[0])

    def ag_copies(k, stage):
        copies = []
        for kind in range(2):
            index = [None] * (ax.nd + 2)
            index[0] = z - k
            for i, axis in enumerate(orders[kind]):
                index[axis[0]] = slice(None) if i < stage else axis[2]
            region = kv_out.at[tuple(index) + (slice(None), pl.ds(kind * width_k, width_k))]
            axis = orders[kind][stage]
            for i in range(1, axis[1]):
                copies.append(
                    pltpu.make_async_remote_copy(
                        src_ref=region, dst_ref=region,
                        send_sem=ag_send.at[k, kind, stage, i - 1],
                        recv_sem=ag_recv.at[k, kind, stage, i - 1],
                        device_id=axis[3](i)[1], device_id_type=mesh_id,
                    )
                )
        return copies

    def tick(k, stage):
        @pl.when(z >= k)
        def _():
            if stage == 0:
                if k > 0:
                    top_copy(k).wait_recv()
            else:
                for copy in ag_copies(k, stage - 1):
                    copy.wait()
            if stage < stages:
                for copy in ag_copies(k, stage):
                    copy.start()

    put.wait()
    tick(0, 0)
    q_f[0].wait()
    q_f[2].start()
    q_f[1].wait()
    q_f[2].wait()
    back = pltpu.make_async_copy(wbuf, wqkv_out, out_sem.at[1])
    back.start()
    query = jnp.dot(attn_in, wbuf[:, :width_q], preferred_element_type=f32)
    query_t = jnp.transpose(query)
    for h in range(2 * parts * heads):
        qt_ref[HS * h : HS * (h + 1), :] = rotate(
            query_t[HS * h : HS * (h + 1)], cos_rows, sin_rows
        ).astype(bf16)
    m_ref[...] = jnp.full_like(m_ref, NEG)
    l_ref[...] = jnp.zeros_like(l_ref)
    acc_ref[...] = jnp.zeros_like(acc_ref)

    bk = 2 * nf * tq
    per_chunk = math.prod(ax.dims[:top])
    start = ax.me * tq

    def block_copy(j, slot):
        return pltpu.make_async_copy(kv_out.at[ax.place_index(j)], kvb.at[slot], blk_sem.at[slot])

    def attend(k):
        first_block = (z - k) * per_chunk
        count = jnp.minimum(place - first_block + 1, per_chunk)

        @pl.when(z >= k)
        def _():
            block_copy(first_block, 0).start()

            def block(i, carry):
                j = first_block + i
                slot = lax.rem(i, 2)

                @pl.when(i + 1 < count)
                def _():
                    block_copy(j + 1, 1 - slot).start()

                block_copy(j, slot).wait()
                bias = bias_tile((start,), docs, j * bk, bk, tq)
                bias = jnp.concatenate([bias] * heads, axis=1)
                for p in range(parts):
                    kb = kvb[slot, :, :, :, 2 * HS * p : 2 * HS * (p + 1)].reshape(bk, 2 * HS)
                    vb = kvb[slot, :, :, :, width_k + 2 * HS * p : width_k + 2 * HS * (p + 1)]
                    vt = jnp.transpose(vb.reshape(bk, 2 * HS))
                    rows = qt_ref[2 * heads * HS * p : 2 * heads * HS * (p + 1), :] * bf16(1.0 / 8.0)
                    for g in range(2):
                        at = 2 * p + g
                        s = jnp.dot(kb, padded(rows, heads, g), preferred_element_type=f32) + bias
                        m = m_ref[at]
                        new = jnp.maximum(m, jnp.max(s, axis=0, keepdims=True))
                        prob = jnp.exp(s - new)
                        decay = jnp.exp(m - new)
                        m_ref[at] = new
                        l_ref[at] = l_ref[at] * decay + jnp.sum(prob, axis=0, keepdims=True)
                        acc_ref[at] = acc_ref[at] * decay + jnp.dot(
                            vt[HS * g : HS * (g + 1)], prob.astype(bf16), preferred_element_type=f32
                        )
                return carry

            lax.fori_loop(0, count, block, 0)

    for turn in range(1, chunks + stages):
        for k in range(chunks):
            stage = turn - k
            if (k, stage) != (0, 0) and 0 <= stage <= stages:
                tick(k, stage)
        if turn == 4:
            for copy in o_y + gu_y:
                copy.wait()
            o_f[0].start()
            o_f[1].start()
            gu_x.start()
            gu_z[0].start()
        if turn == 3:
            cot_y.start()
        if turn == 6:
            o_f[0].wait()
            o_f[2].start()
            gu_x.wait()
            gu_z[1].start()
        if turn == 5:
            cot_y.wait()
            loads[6].wait()
            cot_c.start()
        if turn >= stages:
            attend(turn - stages)
    for p in range(parts):
        outs = []
        for g in range(2):
            at = 2 * p + g
            out = acc_ref[at] / l_ref[at]
            outs.append(out)
            ot_ref[at] = out
            lse_ref[at] = m_ref[at] + jnp.log(l_ref[at])
        low_ref[:, 2 * heads * HS * p : 2 * heads * HS * (p + 1)] = head_lanes(outs, heads, tq).astype(bf16)

    for k in range(1, chunks):
        @pl.when(z + k < chunks)
        def _():
            top_copy(k).wait_send()
    for copy in loads[3:6]:
        copy.wait()
    backs = [back]
    for waits, src, dst in (
        (o_f[1:], obuf, wo_out), ([cot_c], cbuf, cots_out), (gu_z, gubuf, gu_out)
    ):
        for copy in waits:
            copy.wait()
        backs.append(pltpu.make_async_copy(src, dst, out_sem.at[1 + len(backs)]))
        backs[-1].start()
    for copy in backs:
        copy.wait()


def forward(nctx, nf, docs, tokens, norm_attn, norm_mlp, cos_t, sin_t, wq, wk, wv, wo, wg, wu, cot):
    tq, width = tokens.shape
    width_q, width_k = wq.shape[1], wk.shape[1]
    parts = width_k // (2 * HS)
    heads = width_q // HS // (2 * parts)
    hidden_units = wg.shape[1]
    quarter = hidden_units // (2 * nf)
    dims = line_dims(nctx // 2)
    lead = tuple(reversed(dims))
    most = max(dims + [2])
    chunks = dims[-1]
    stages = len(dims) + 1
    bf16, f32 = jnp.bfloat16, jnp.float32
    vmem = pl.BlockSpec(memory_space=pltpu.VMEM)
    smem = pl.BlockSpec(memory_space=pltpu.SMEM)
    hbm = pl.BlockSpec(memory_space=pl.ANY)
    dma = pltpu.SemaphoreType.DMA
    return pl.pallas_call(
        functools.partial(forward_kernel, (nctx, nf, parts, heads, tq)),
        out_shape=[
            jax.ShapeDtypeStruct((width_q, tq), bf16),
            jax.ShapeDtypeStruct(lead + (2, nf, tq, 2 * width_k), bf16),
            jax.ShapeDtypeStruct((tq, width_q), bf16),
            jax.ShapeDtypeStruct((2 * parts, HS, heads * tq), f32),
            jax.ShapeDtypeStruct((2 * parts, 1, heads * tq), f32),
            jax.ShapeDtypeStruct((width, width_q + 2 * width_k), bf16),
            jax.ShapeDtypeStruct((nf * wo.shape[0], wo.shape[1]), bf16),
            jax.ShapeDtypeStruct((width, 2 * quarter), bf16),
            jax.ShapeDtypeStruct((2 * nf, tq, width), bf16),
            jax.ShapeDtypeStruct((tq, width), bf16),
            jax.ShapeDtypeStruct((tq, 1), f32),
            jax.ShapeDtypeStruct((2, width), f32),
        ],
        in_specs=[smem, vmem, vmem, vmem, vmem, vmem] + [hbm] * 7,
        out_specs=[vmem, hbm, vmem, vmem, vmem, hbm, hbm, hbm, hbm, vmem, vmem, vmem],
        scratch_shapes=[
            pltpu.VMEM((width, width_q + 2 * width_k), bf16),
            pltpu.VMEM((nf * wo.shape[0], wo.shape[1]), bf16),
            pltpu.VMEM((width, 2 * quarter), bf16),
            pltpu.VMEM((2 * nf, tq, width), bf16),
            pltpu.VMEM((8, norm_attn.shape[1]), f32),
            pltpu.VMEM((8, norm_attn.shape[1]), f32),
            pltpu.VMEM((tq, 2 * width_k), bf16),
            pltpu.VMEM((2, 2, nf, tq, 2 * width_k), bf16),
            pltpu.VMEM((2 * parts, 1, heads * tq), f32),
            pltpu.VMEM((2 * parts, 1, heads * tq), f32),
            pltpu.VMEM((2 * parts, HS, heads * tq), f32),
            dma((7,)),
            dma((21,)),
            dma((21,)),
            dma((chunks - 1,)),
            dma((chunks - 1,)),
            dma((chunks, 2, stages, most - 1)),
            dma((chunks, 2, stages, most - 1)),
            dma((2,)),
            dma((5,)),
        ],
        compiler_params=pltpu.CompilerParams(
            collective_id=0, has_side_effects=True, vmem_limit_bytes=60 * 2**20
        ),
        name="forward",
    )(docs, tokens, norm_attn, norm_mlp, cos_t, sin_t, wq, wk, wv, wo, wg, wu, cot)


def feed_forward_kernel(plan, tokens_ref, low_ref, attn_in_ref, gains_ref, wo_hbm, gu_hbm, down_hbm, cots_hbm,
                        result_ref, gres_ref, branch_ref, gattn_ref, gmlp_ref, gup_ref, dnp_ref, inputs_out,
                        wo, gu, down, cots, xs, grads, mixed, gm, sums, sent, core_in, side_in, side_out,
                        load_sem, x_send, x_recv, s_send, s_recv, top_send, top_recv,
                        ag_send, ag_recv, out_sem):
    nctx, nf = plan
    ax = Axes(nctx, nf)
    f, core, place = ax.f, ax.core, ax.place
    mesh_id = pl.DeviceIdType.MESH
    bf16, f32 = jnp.bfloat16, jnp.float32
    tq, width = tokens_ref.shape
    quarter = down.shape[0]
    side = ax.side_axis[3](1)[1]
    mate = ax.core_axis[3](1)[1]
    top = ax.nd - 1
    chunks = ax.dims[top]
    z = ax.lines[top][2]

    barrier = pltpu.get_barrier_semaphore()
    for where in ax.peers():
        pl.semaphore_signal(barrier, inc=1, device_id=where, device_id_type=mesh_id)
    loads = [
        pltpu.make_async_copy(src, dst, load_sem.at[i])
        for i, (src, dst) in enumerate((
            (wo_hbm, wo), (cots_hbm, cots),
            (down_hbm.at[pl.ds(pl.multiple_of(core * quarter, quarter), quarter)], down), (gu_hbm, gu),
        ))
    ]
    for copy in loads:
        copy.start()

    def remote(src, dst, sends, recvs, i, where):
        return pltpu.make_async_remote_copy(
            src_ref=src, dst_ref=dst, send_sem=sends.at[i], recv_sem=recvs.at[i],
            device_id=where, device_id_type=mesh_id,
        )

    hidden = tokens_ref[...].astype(f32)
    own_at = ax.place_index(place) + (core,)
    put = pltpu.make_async_copy(attn_in_ref, inputs_out.at[own_at], out_sem.at[0])

    def top_copy(k):
        return pltpu.make_async_remote_copy(
            src_ref=attn_in_ref, dst_ref=inputs_out.at[own_at],
            send_sem=top_send.at[k - 1], recv_sem=top_recv.at[k - 1],
            device_id=ax.at_line(top, lax.rem(z + k, chunks)), device_id_type=mesh_id,
        )

    order = ax.lines[:top] + [ax.core_axis]
    stages = len(order)

    def ag_copies(k, stage):
        index = [None] * (ax.nd + 1)
        index[0] = lax.rem(z + chunks - k, chunks)
        for i, axis in enumerate(order):
            index[axis[0]] = slice(None) if i < stage else axis[2]
        region = inputs_out.at[tuple(index)]
        axis = order[stage]
        return [
            pltpu.make_async_remote_copy(
                src_ref=region, dst_ref=region,
                send_sem=ag_send.at[k, stage, i - 1], recv_sem=ag_recv.at[k, stage, i - 1],
                device_id=axis[3](i)[1], device_id_type=mesh_id,
            )
            for i in range(1, axis[1])
        ]

    def tick(turn):
        for k in range(chunks):
            stage = turn - k
            if not 0 <= stage <= stages:
                continue
            if stage == 0:
                if k > 0:
                    top_copy(k).wait()
                else:
                    put.wait()
            else:
                for copy in ag_copies(k, stage - 1):
                    copy.wait()
            if stage < stages:
                for copy in ag_copies(k, stage):
                    copy.start()

    pl.semaphore_wait(barrier, ax.peer_count)
    put.start()
    top_copy(1).start()
    tick(0)

    loads[0].wait()
    resid = hidden + jnp.dot(low_ref[...], wo[...], preferred_element_type=f32)
    inv = lax.rsqrt(jnp.mean(resid * resid, axis=1, keepdims=True) + EPS)
    normed = resid * inv
    gain = gains_ref[1:2, :]
    xs[0] = (normed * gain).astype(bf16)
    x_side = remote(xs.at[0], xs.at[1], x_send, x_recv, 0, side)
    x_core = remote(xs.at[0], xs.at[2], x_send, x_recv, 1, mate)
    x_far = remote(xs.at[1], xs.at[3], x_send, x_recv, 2, mate)
    x_side.start()
    x_core.start()

    def rows(slot):
        return slice(slot * tq, (slot + 1) * tq)

    for copy in loads[1:3]:
        copy.wait()
    gm[...] = lax.dot_general(
        cots[...].reshape(4 * tq, width), down[...], (((1,), (1,)), ((), ())), preferred_element_type=f32
    )
    loads[3].wait()
    top_copy(2).start()
    step = 256

    def both(ref, a, b, span=slice(None)):
        return jnp.concatenate([ref[a, :, span], ref[b, :, span]], axis=0)

    def compute(a, b):
        x = both(xs, a, b)
        for n in range(quarter // step):
            span = slice(n * step, (n + 1) * step)
            up_span = slice(quarter + n * step, quarter + (n + 1) * step)
            gate = jnp.dot(x, gu[:, span], preferred_element_type=f32)
            up = jnp.dot(x, gu[:, up_span], preferred_element_type=f32)
            sig = jax.nn.sigmoid(gate)
            act = gate * sig
            grad = jnp.concatenate([gm[rows(a), span], gm[rows(b), span]], axis=0)
            mix = (act * up).astype(bf16)
            grad_gate = (grad * up * sig * (1.0 + gate * (1.0 - sig))).astype(bf16)
            grad_up = (grad * act).astype(bf16)
            for i, slot in enumerate((a, b)):
                mixed[slot, :, span] = mix[rows(i)]
                grads[slot, :, span] = grad_gate[rows(i)]
                grads[slot, :, up_span] = grad_up[rows(i)]
        total = lax.dot_general(
            both(grads, a, b), gu[...], (((1,), (1,)), ((), ())), preferred_element_type=f32
        )
        for i, slot in enumerate((a, b)):
            sums[0, slot] = total[rows(i)]

    def outputs(a, b):
        total = jnp.dot(both(mixed, a, b), down[...], preferred_element_type=f32)
        for i, slot in enumerate((a, b)):
            sums[1, slot] = total[rows(i)]

    def to_core(kind, slot):
        i = 2 * kind + slot - 2
        return remote(sent.at[i], core_in.at[i], s_send, s_recv, i, mate)

    def to_side(kind):
        return remote(side_out.at[kind], side_in.at[kind], s_send, s_recv, 4 + kind, side)

    def give_core(kind, slot):
        sent[2 * kind + slot - 2] = sums[kind, slot].astype(bf16)
        to_core(kind, slot).start()

    def give_side(kind):
        to_core(kind, 3).wait()
        side_out[kind] = (sums[kind, 1] + core_in[2 * kind + 1].astype(f32)).astype(bf16)
        to_side(kind).start()

    x_core.wait()
    compute(0, 2)
    give_core(0, 2)
    top_copy(3).start()
    x_side.wait()
    x_far.start()
    tick(1)
    outputs(0, 2)
    give_core(1, 2)
    x_far.wait()
    compute(1, 3)
    give_core(0, 3)
    tick(2)
    outputs(1, 3)
    give_side(0)
    give_core(1, 3)
    flat_x = xs[...].reshape(4 * tq, width)
    pieces = nctx // 2
    unit = quarter // pieces
    tall = max(unit, 256)
    for kind in range(2):
        for n in range(quarter // tall):
            span = slice(kind * quarter + n * tall, kind * quarter + (n + 1) * tall)
            cols = jnp.transpose(jnp.concatenate([grads[s, :, span] for s in range(4)], axis=0))
            part = jnp.dot(cols, flat_x, preferred_element_type=f32).astype(bf16)
            first = n * tall
            while first < (n + 1) * tall:
                piece, at = first // unit, first % unit
                end = min((piece + 1) * unit, (n + 1) * tall)
                gup_ref[static_index(bit_dims(nctx // 2), piece) + (kind, slice(at, at + end - first))] = part[
                    first - n * tall : end - n * tall
                ]
                first = end
        if kind == 0:
            give_side(1)
            tick(3)
    unit = width // pieces
    flat_mixed = mixed[...].reshape(4 * tq, quarter)
    for n in range(width // 384):
        cols = jnp.transpose(jnp.concatenate([cots[s, :, 384 * n : 384 * (n + 1)] for s in range(4)], axis=0))
        part = jnp.dot(cols, flat_mixed, preferred_element_type=f32).astype(bf16)
        first = n * 384
        while first < (n + 1) * 384:
            piece, at = first // unit, first % unit
            end = min((piece + 1) * unit, (n + 1) * 384)
            rows_of = part[first - n * 384 : end - n * 384]
            for c in range(quarter // 128):
                dnp_ref[
                    static_index(bit_dims(nctx // 2), piece)
                    + (slice(c * unit + at, c * unit + at + end - first),)
                ] = rows_of[:, 128 * c : 128 * (c + 1)]
            first = end

    tick(4)
    to_core(0, 2).wait()
    to_side(0).wait()
    grad = sums[0, 0] + core_in[0].astype(f32) + side_in[0].astype(f32)
    product = grad * normed
    gmlp_ref[...] = jnp.sum(product, axis=0, keepdims=True)
    scaled = grad * gain
    mean = jnp.mean(scaled * normed, axis=1, keepdims=True)
    gres = cots[0].astype(f32) + inv * (scaled - normed * mean)
    gres_ref[...] = gres
    branch = gres.astype(bf16)
    branch_ref[...] = branch
    gattn_ref[...] = lax.dot_general(
        branch, wo[...], (((1,), (1,)), ((), ())), preferred_element_type=f32
    ).astype(bf16)
    to_core(1, 2).wait()
    to_side(1).wait()
    result_ref[...] = (resid + sums[1, 0] + core_in[2].astype(f32) + side_in[1].astype(f32)).astype(bf16)
    for turn in range(5, chunks + stages):
        tick(turn)


def static_index(dims, piece):
    return tuple(piece // math.prod(dims[:i]) % dims[i] for i in reversed(range(len(dims))))


def feed_forward(nctx, nf, tokens, low, attn_in, gains, wo, gu, down, cots):
    tq, width = tokens.shape
    quarter = gu.shape[1] // 2
    dims = line_dims(nctx // 2)
    bits = bit_dims(nctx // 2)
    lead = tuple(reversed(dims))
    plane = nctx // 2
    chunks, stages, most = dims[-1], len(dims), max(dims + [2])
    bf16, f32 = jnp.bfloat16, jnp.float32
    vmem = pl.BlockSpec(memory_space=pltpu.VMEM)
    hbm = pl.BlockSpec(memory_space=pl.ANY)
    dma = pltpu.SemaphoreType.DMA
    return pl.pallas_call(
        functools.partial(feed_forward_kernel, (nctx, nf)),
        out_shape=[
            jax.ShapeDtypeStruct((tq, width), bf16),
            jax.ShapeDtypeStruct((tq, width), f32),
            jax.ShapeDtypeStruct((tq, width), bf16),
            jax.ShapeDtypeStruct((tq, width), bf16),
            jax.ShapeDtypeStruct((1, width), f32),
            jax.ShapeDtypeStruct(tuple(bits) + (2, quarter // plane, width), bf16),
            jax.ShapeDtypeStruct(tuple(bits) + (width // plane * (quarter // 128), 128), bf16),
            jax.ShapeDtypeStruct(lead + (2, tq, width), bf16),
        ],
        in_specs=[vmem] * 4 + [hbm] * 4,
        out_specs=[vmem] * 7 + [hbm],
        scratch_shapes=[
            pltpu.VMEM(wo.shape, bf16),
            pltpu.VMEM(gu.shape, bf16),
            pltpu.VMEM((quarter, width), bf16),
            pltpu.VMEM((4, tq, width), bf16),
            pltpu.VMEM((4, tq, width), bf16),
            pltpu.VMEM((4, tq, 2 * quarter), bf16),
            pltpu.VMEM((4, tq, quarter), bf16),
            pltpu.VMEM((4 * tq, quarter), f32),
            pltpu.VMEM((2, 4, tq, width), f32),
            pltpu.VMEM((4, tq, width), bf16),
            pltpu.VMEM((4, tq, width), bf16),
            pltpu.VMEM((2, tq, width), bf16),
            pltpu.VMEM((2, tq, width), bf16),
            dma((4,)),
            dma((4,)),
            dma((4,)),
            dma((6,)),
            dma((6,)),
            dma((chunks - 1,)),
            dma((chunks - 1,)),
            dma((chunks, stages, most - 1)),
            dma((chunks, stages, most - 1)),
            dma((1,)),
        ],
        compiler_params=pltpu.CompilerParams(
            collective_id=2, has_side_effects=True, vmem_limit_bytes=60 * 2**20
        ),
        name="feed_forward",
    )(tokens, low, attn_in, gains, wo, gu, down, cots)


def finish_kernel(*refs):
    count = len(refs) // 2
    for src, dst in zip(refs[:count], refs[count:]):
        dst[...] = src[...]


def finish(*values):
    def whole(x):
        return pl.BlockSpec(x.shape, lambda i: (0,) * len(x.shape))

    return pl.pallas_call(
        finish_kernel,
        grid=(1,),
        out_shape=[jax.ShapeDtypeStruct(x.shape, x.dtype) for x in values],
        in_specs=[whole(x) for x in values],
        out_specs=[whole(x) for x in values],
        compiler_params=pltpu.CompilerParams(vmem_limit_bytes=60 * 2**20),
        name="finish",
    )(*values)


def per_device(
    nctx,
    nf,
    tokens,
    query_weight,
    key_projection,
    value_projection,
    output_weight,
    gate_weight,
    up_weight,
    down_weight,
    norm_attn,
    norm_mlp,
    doc_starts,
    cotangent,
):
    token_rows, width = tokens.shape
    n_tokens = token_rows * nctx * nf
    bf16, f32 = jnp.bfloat16, jnp.float32

    own_device = lax.axis_index(AXES)
    own_index = layout_rows(own_device, token_rows)
    own_begin = doc_begin(own_index, doc_starts)
    cosine_table, sine_table = rope_tables(own_index - own_begin)
    cosine_table, sine_table = cosine_table.T, sine_table.T
    (
        query_rot, key_values, attn_low, attn_exact, log_total, qkv_full, output_full, gate_up,
        cotangents, attention_input, inv_attn, gains,
    ) = forward(
        nctx, nf, doc_starts, tokens, norm_attn[None], norm_mlp[None], cosine_table, sine_table, query_weight, key_projection,
        value_projection, output_weight, gate_weight, up_weight, cotangent,
    )
    key_width = KEY_VALUE_HEADS * HEAD_SIZE
    key_values = key_values.reshape(n_tokens, 2 * key_width)
    result, grad_resid, grad_branch, grad_attn, gain_mlp_partial, gate_up_partial, down_partial, inputs_all = feed_forward(
        nctx, nf, tokens, attn_low, attention_input, gains, output_full, gate_up, down_weight,
        cotangents.reshape(2 * nf, token_rows, width),
    )

    tokens_grad, query_sum, key_sum, value_sum, gain_sums, gate_sum, up_sum, down_sum, output_sum = backward(
        nctx, nf, doc_starts, query_rot, grad_attn, attn_exact, log_total, key_values, qkv_full,
        cosine_table, sine_table, tokens, inv_attn, gains, grad_resid,
        gain_mlp_partial, attn_low, grad_branch, gate_up_partial, down_partial,
        inputs_all.reshape(nctx, token_rows, width),
    )

    gain_sums = gain_sums[: 2 * width // 128].reshape(2, width)
    result, tokens_grad, *sums = finish(
        result, tokens_grad, query_sum, key_sum, value_sum, output_sum, gate_sum, up_sum, down_sum
    )
    return (result, tokens_grad, *(weight.T for weight in sums), gain_sums[0], gain_sums[1])


def solution(mesh):
    return jax.shard_map(
        functools.partial(per_device, mesh.shape["ctx"], mesh.shape["fsdp"]),
        mesh=mesh,
        in_specs=(
            P(("ctx", "fsdp"), None),
            P("fsdp", None),
            P("fsdp", None),
            P("fsdp", None),
            P("fsdp", None),
            P("fsdp", None),
            P("fsdp", None),
            P("fsdp", None),
            P("fsdp"),
            P("fsdp"),
            P(),
            P(("ctx", "fsdp"), None),
        ),
        out_specs=(
            P(("ctx", "fsdp"), None),
            P(("ctx", "fsdp"), None),
            P("fsdp", "ctx"),
            P("fsdp", "ctx"),
            P("fsdp", "ctx"),
            P("fsdp", "ctx"),
            P("fsdp", "ctx"),
            P("fsdp", "ctx"),
            P("fsdp", "ctx"),
            P(),
            P(),
        ),
        check_vma=False,
    )
```
